32 devices in a mesh: dp: 8 (over z, x), expert: 4 (over y, core).
Axes of the slice: x: 2, y: 2, z: 4, core: 2. Of those that a mesh axis runs over, the one named last changes fastest.
Arguments:
- tokens: bfloat16 [4096, 1536], P(('dp', 'expert')), may hold values from -6 to 6
- cotangent: bfloat16 [4096, 1536], P(('dp', 'expert')), may hold values from -6 to 6
- routes: int32 [4096, 8], P(('dp', 'expert')), may hold values from 0 to 39, all different within a row; in each aligned block of 128 rows (0 to 127, 128 to 255, ...) at most 32 rows name the same one
- weight_qkv: float32 [1536, 2560], P(('dp', 'expert')), may hold values from -0.15625 to 0.15625
- moment_qkv: float32 [1536, 2560], P(('dp', 'expert')), may hold values from -128 to 128
- square_qkv: float32 [1536, 2560], P(('dp', 'expert')), may hold values from 1925.12 to 7782.4
- weight_out: float32 [1536, 1536], P(('dp', 'expert')), may hold values from -2.5 to 2.5
- moment_out: float32 [1536, 1536], P(('dp', 'expert')), may hold values from -5 to 5
- square_out: float32 [1536, 1536], P(('dp', 'expert')), may hold values from 0.53248 to 2.17088
- weight_router: float32 [1536, 40], P(('dp', 'expert')), may hold values from -0.078125 to 0.078125
- moment_router: float32 [1536, 40], P(('dp', 'expert')), may hold values from -128 to 128
- square_router: float32 [1536, 40], P(('dp', 'expert')), may hold values from 1925.12 to 7782.4
- gains: float32 [2, 1536], P(None, ('dp', 'expert')), may hold values from 0.5 to 1.5
- moment_gains: float32 [2, 1536], P(None, ('dp', 'expert')), may hold values from -80 to 80
- square_gains: float32 [2, 1536], P(None, ('dp', 'expert')), may hold values from 860.16 to 3440.64
- weight_gate_up: float32 [40, 1536, 1024], P('expert', 'dp'), may hold values from -0.15625 to 0.15625
- moment_gate_up: float32 [40, 1536, 1024], P('expert', 'dp'), may hold values from -6 to 6
- square_gate_up: float32 [40, 1536, 1024], P('expert', 'dp'), may hold values from 3.6864 to 14.7456
- weight_down: float32 [40, 512, 1536], P('expert', 'dp'), may hold values from -3 to 3
- moment_down: float32 [40, 512, 1536], P('expert', 'dp'), may hold values from -0.75 to 0.75
- square_down: float32 [40, 512, 1536], P('expert', 'dp'), may hold values from 0.0118784 to 0.0475136
Outputs:
- layer_out: bfloat16 [4096, 1536], P(('dp', 'expert'))
- token_grad: float32 [4096, 1536], P(('dp', 'expert'))
- new_weight_qkv: float32 [1536, 2560], P(('dp', 'expert'))
- new_moment_qkv: float32 [1536, 2560], P(('dp', 'expert'))
- new_square_qkv: float32 [1536, 2560], P(('dp', 'expert'))
- new_weight_out: float32 [1536, 1536], P(('dp', 'expert'))
- new_moment_out: float32 [1536, 1536], P(('dp', 'expert'))
- new_square_out: float32 [1536, 1536], P(('dp', 'expert'))
- new_weight_router: float32 [1536, 40], P(('dp', 'expert'))
- new_moment_router: float32 [1536, 40], P(('dp', 'expert'))
- new_square_router: float32 [1536, 40], P(('dp', 'expert'))
- new_gains: float32 [2, 1536], P(None, ('dp', 'expert'))
- new_moment_gains: float32 [2, 1536], P(None, ('dp', 'expert'))
- new_square_gains: float32 [2, 1536], P(None, ('dp', 'expert'))
- new_weight_gate_up: float32 [40, 1536, 1024], P('expert', 'dp')
- new_moment_gate_up: float32 [40, 1536, 1024], P('expert', 'dp')
- new_square_gate_up: float32 [40, 1536, 1024], P('expert', 'dp')
- new_weight_down: float32 [40, 512, 1536], P('expert', 'dp')
- new_moment_down: float32 [40, 512, 1536], P('expert', 'dp')
- new_square_down: float32 [40, 512, 1536], P('expert', 'dp')
The draws below stay inside these ranges and needn't reach their ends.
Inputs may be any that keep to these rules, and one draw needn't show every extreme that they name: `routes`: each row names 8 different experts. Among the rows of one device, no expert is named by more than 32 rows, and in every draw some device has an expert named by exactly 32.
All inputs are finite; a program needn't handle non-finite values.
Results may differ from the reference program's by a relative error of at most 0.02.
Values may be sent and summed in bfloat16 or wider, within the bound.
No kernel may reach another device: no remote copies, remote signals or barrier semaphores. Data moves between devices by JAX's collectives and lax.ppermute only.
A program may use at most 320 MiB of HBM per device.

```python
import math
import jax
import jax.numpy as jnp
import numpy as np
from jax import lax

D = 1536
QUERY_HEADS = 24
KEY_VALUE_HEADS = 8
HEAD_SIZE = 64
FF = 512
EXPERTS = 40
TOPK = 8
TOK_DEV = 128
STEP = 10
CAP = 32
QKV = 2560
TOKENS = 4096
N_DP = 8
N_EXPERT = 4


def block_levels(rng, dims, shards, low, high):
    level, own = 1.0, jax.random.fold_in(rng, 6)
    for axis_at, shards_of in shards:
        draws = jnp.exp(jax.random.uniform(jax.random.fold_in(own, axis_at), (shards_of,), jnp.float32, low / len(shards), high / len(shards)))
        level = level * jnp.repeat(draws, dims[axis_at] // shards_of).reshape([-1 if axis == axis_at else 1 for axis in range(len(dims))])
    return level


def assign_block(stream_key, own, number, rows, number_of, top, most, lean):
    order = jax.random.permutation(stream_key, number_of)
    heavy_load, common = load_shares(number_of, rows * top, most, lean, True), load_shares(number_of, rows * top, most, lean, False)
    places = jnp.arange(number_of)

    def named(sizes, offset_by):
        used = int((sizes > 0).sum())
        fixed = max(1, used // 4)
        shifted = fixed + (places - fixed + offset_by * (used - fixed)) % max(1, number_of - fixed)
        return jnp.zeros((number_of,), jnp.int32).at[order[jnp.where(places < fixed, places, shifted)]].set(jnp.asarray(sizes, jnp.int32))

    sizes = jnp.where(number % 4 == 0, named(heavy_load, number // 4), named(common, number - number // 4 - 1))
    mixed = jax.random.permutation(jax.random.fold_in(own, 3), number_of)
    giver, sink = mixed[0:number_of // 2 * 2:2], mixed[1:number_of // 2 * 2:2]
    slack = jnp.minimum(sizes[giver] - 1, most - sizes[sink]) // 2
    slack = jnp.where((giver == order[0]) | (sink == order[0]) | (sizes[sink] == 0), 0, jnp.maximum(slack, 0))
    shifted = jax.random.randint(jax.random.fold_in(own, 4), (number_of // 2,), 0, 1 << 20) % (slack + 1)
    sizes = sizes.at[giver].add(-shifted).at[sink].add(shifted)
    members = jnp.searchsorted(jnp.cumsum(sizes), jnp.arange(rows * top), side="right").astype(jnp.int32)
    grid = members.reshape(top, rows).T
    grid = grid[jax.random.permutation(jax.random.fold_in(own, 1), rows)]
    offset_by = jax.random.randint(jax.random.fold_in(own, 2), (rows, 1), 0, top)
    return jnp.take_along_axis(grid, (jnp.arange(top)[None, :] + offset_by) % top, axis=1)


def load_shares(number_of, total, bound, skew, full):
    portions = [(1 << 20) // math.isqrt(standing ** skew) + 1 for standing in range(1, number_of + 1)]
    largest = bound if full else min(bound, max(-(-total // number_of), total * portions[0] // sum(portions)))
    least = 1 if total - largest >= number_of - 1 else 0
    given, surplus = [largest] + [least] * (number_of - 1), total - largest - least * (number_of - 1)
    while surplus > 0:
        movable = [i for i in range(1, number_of) if given[i] < largest] or [i for i in range(1, number_of) if given[i] < bound]
        whole, budget = sum([portions[i] for i in movable]), surplus
        for i in movable:
            addition = min(bound - given[i], max(1, budget * portions[i] // whole), surplus)
            given[i] = given[i] + addition
            surplus = surplus - addition
    return np.array(given)


def noise(rng, extent, deviation, most, pieces=(), kind=jnp.bfloat16):
    array = deviation * jax.random.normal(rng, extent, jnp.float32)
    if pieces:
        array = array * block_levels(rng, extent, pieces, -0.22, 0.18)
    return jnp.clip(array, -most, most).astype(kind)


def setup_inputs(seed: int = 0) -> dict:
    key_of = jax.random.split(jax.random.key(seed), 22)
    tokens = noise(key_of[0], (TOKENS, D), 1.0, 6.0, ((0, 32),))
    cotangent = noise(key_of[1], (TOKENS, D), 1.0, 6.0, ((0, 32),))
    routes_keys = jax.random.split(jax.random.fold_in(key_of[2], 1), TOKENS // TOK_DEV)
    routes_turns = jax.random.permutation(jax.random.fold_in(key_of[2], 3), TOKENS // TOK_DEV)
    routes = jax.vmap(lambda own, number: assign_block(jax.random.fold_in(key_of[2], 2), own, number, TOK_DEV, EXPERTS, TOPK, CAP, 1))(routes_keys, routes_turns).reshape((TOKENS, TOPK))
    weight_qkv = noise(key_of[3], (D, QKV), D ** -0.5, 0.15625, ((0, 32),), jnp.float32)
    moment_qkv = noise(key_of[4], (D, QKV), (0.33 * TOKENS ** 0.5), 128.0, ((0, 32),), jnp.float32)
    square_qkv = jnp.clip(jnp.exp(math.log(7782.4) - 1.3968765 * jax.random.uniform(key_of[5], (D, QKV), jnp.float32) ** block_levels(key_of[5], (D, QKV), ((0, 32),), -0.2, 0.2)), 1925.12, 7782.4)
    weight_out = noise(key_of[6], (QUERY_HEADS * HEAD_SIZE, D), (max(4, QUERY_HEADS * HEAD_SIZE // 256)) ** -0.5, 2.5, ((0, 32),), jnp.float32)
    moment_out = noise(key_of[7], (QUERY_HEADS * HEAD_SIZE, D), (0.0055 * TOKENS ** 0.5), 5.0, ((0, 32),), jnp.float32)
    square_out = jnp.clip(jnp.exp(math.log(2.17088) - 1.4053426 * jax.random.uniform(key_of[8], (QUERY_HEADS * HEAD_SIZE, D), jnp.float32) ** block_levels(key_of[8], (QUERY_HEADS * HEAD_SIZE, D), ((0, 32),), -0.2, 0.2)), 0.53248, 2.17088)
    weight_router = noise(key_of[9], (D, EXPERTS), (4 * D) ** -0.5, 0.078125, ((0, 32),), jnp.float32)
    moment_router = noise(key_of[10], (D, EXPERTS), (0.33 * TOKENS ** 0.5), 128.0, ((0, 32),), jnp.float32)
    square_router = jnp.clip(jnp.exp(math.log(7782.4) - 1.3968765 * jax.random.uniform(key_of[11], (D, EXPERTS), jnp.float32) ** block_levels(key_of[11], (D, EXPERTS), ((0, 32),), -0.2, 0.2)), 1925.12, 7782.4)
    gains = jnp.clip(1.0 + 0.1 * jax.random.normal(key_of[12], (2, D), jnp.float32), 0.5, 1.5)
    moment_gains = noise(key_of[13], (2, D), (0.22 * TOKENS ** 0.5), 80.0, ((1, 32),), jnp.float32)
    square_gains = jnp.clip(jnp.exp(math.log(3440.64) - 1.3862944 * jax.random.uniform(key_of[14], (2, D), jnp.float32) ** block_levels(key_of[14], (2, D), ((1, 32),), -0.2, 0.2)), 860.16, 3440.64)
    weight_gate_up = noise(key_of[15], (EXPERTS, D, 2 * FF), D ** -0.5, 0.15625, ((0, 4), (1, 8)), jnp.float32)
    moment_gate_up = noise(key_of[16], (EXPERTS, D, 2 * FF), (0.014 * TOKENS ** 0.5), 6.0, ((0, 4), (1, 8)), jnp.float32)
    square_gate_up = jnp.clip(jnp.exp(math.log(14.7456) - 1.3862944 * jax.random.uniform(key_of[17], (EXPERTS, D, 2 * FF), jnp.float32) ** block_levels(key_of[17], (EXPERTS, D, 2 * FF), ((0, 4), (1, 8)), -0.2, 0.2)), 3.6864, 14.7456)
    weight_down = noise(key_of[18], (EXPERTS, FF, D), (max(2, FF // 128)) ** -0.5, 3.0, ((0, 4), (1, 8)), jnp.float32)
    moment_down = noise(key_of[19], (EXPERTS, FF, D), (0.0008 * TOKENS ** 0.5), 0.75, ((0, 4), (1, 8)), jnp.float32)
    square_down = jnp.clip(jnp.exp(math.log(0.0475136) - 1.3862944 * jax.random.uniform(key_of[20], (EXPERTS, FF, D), jnp.float32) ** block_levels(key_of[20], (EXPERTS, FF, D), ((0, 4), (1, 8)), -0.2, 0.2)), 0.0118784, 0.0475136)
    return dict(tokens=tokens, cotangent=cotangent, routes=routes, weight_qkv=weight_qkv, moment_qkv=moment_qkv, square_qkv=square_qkv, weight_out=weight_out, moment_out=moment_out, square_out=square_out, weight_router=weight_router, moment_router=moment_router, square_router=square_router, gains=gains, moment_gains=moment_gains, square_gains=square_gains, weight_gate_up=weight_gate_up, moment_gate_up=moment_gate_up, square_gate_up=square_gate_up, weight_down=weight_down, moment_down=moment_down, square_down=square_down)


@jax.custom_vjp
def lower_precision(v):
    return lax.optimization_barrier(v.astype(jnp.bfloat16)).astype(jnp.float32)

@jax.custom_vjp
def low_back(v):
    return v

def low_keep(v):
    return (lower_precision(v), None)

def low_pass(kept, grad):
    return (grad,)

def back_keep(v):
    return (v, None)

def back_low(kept, grad):
    return (lower_precision(grad),)
lower_precision.defvjp(low_keep, low_pass)
low_back.defvjp(back_keep, back_low)
norm_eps = 1e-06
residual_scale = 0.22
score_scale = 0.125
beta_one = 0.9
beta_two = 0.95
adam_eps = 1e-08
weight_decay = 0.1
highest = lax.Precision.HIGHEST

def rotary_tables(sequence_length, size):
    half = size // 2
    places = jnp.arange(sequence_length).astype(jnp.float32)[:, None]
    inverse = 10000.0 ** (-jnp.arange(half).astype(jnp.float32) * 2.0 / size)
    angles = places * inverse[None, :]
    return (jnp.cos(angles)[:, None, :], jnp.sin(angles)[:, None, :])

def apply_rotation(values, cosine_lookup, sine_lookup):
    half = values.shape[-1] // 2
    first = values[..., :half]
    second = values[..., half:]
    return jnp.concatenate([first * cosine_lookup - second * sine_lookup, second * cosine_lookup + first * sine_lookup], axis=-1)

def rms_norm(values, gain):
    factor = lax.rsqrt(lax.optimization_barrier(jnp.mean(values * values, axis=-1, keepdims=True)) + norm_eps)
    return values * factor * gain

def destinations(route_rows, capacity, expert_count):
    flat_ids = route_rows.reshape(-1).astype(jnp.int32)
    matches = (flat_ids[:, None] == jnp.arange(expert_count).astype(jnp.int32)[None, :]).astype(jnp.int32)
    earlier = jnp.cumsum(matches, axis=0) - matches
    slot_index = lax.optimization_barrier(jnp.sum(earlier * matches, axis=1))
    return (flat_ids * capacity + slot_index).astype(jnp.int32)

def sequence_forward(lowered, tokens_seq, route_seq):
    qkv_w, out_w, router_w, gain_w, gate_up_w, down_w = lowered
    sequence_length = tokens_seq.shape[0]
    head_groups = QUERY_HEADS // KEY_VALUE_HEADS
    hidden_one = lower_precision(rms_norm(tokens_seq, gain_w[0]))
    joined_heads = low_back(jnp.dot(hidden_one, qkv_w, precision=highest))
    query_rows = joined_heads[:, :QUERY_HEADS * HEAD_SIZE].reshape(sequence_length, QUERY_HEADS, HEAD_SIZE)
    every_key = joined_heads[:, QUERY_HEADS * HEAD_SIZE:QUERY_HEADS * HEAD_SIZE + KEY_VALUE_HEADS * HEAD_SIZE].reshape(sequence_length, KEY_VALUE_HEADS, HEAD_SIZE)
    every_value = joined_heads[:, QUERY_HEADS * HEAD_SIZE + KEY_VALUE_HEADS * HEAD_SIZE:].reshape(sequence_length, KEY_VALUE_HEADS, HEAD_SIZE)
    cosine_lookup, sine_lookup = rotary_tables(sequence_length, HEAD_SIZE)
    query_rotated = lower_precision(apply_rotation(query_rows, cosine_lookup, sine_lookup)).reshape(sequence_length, KEY_VALUE_HEADS, head_groups, HEAD_SIZE)
    key_rot = lower_precision(apply_rotation(every_key, cosine_lookup, sine_lookup))
    value_low = lower_precision(every_value)
    scores = low_back(jnp.einsum('skgd,tkd->kgst', query_rotated, key_rot, precision=highest) * score_scale)
    causal = jnp.arange(sequence_length)[:, None] >= jnp.arange(sequence_length)[None, :]
    scores = jnp.where(causal, scores, -1e+30)
    peak = lax.optimization_barrier(jnp.max(scores, axis=-1, keepdims=True))
    expo = jnp.exp(scores - peak)
    probs = lower_precision(expo / lax.optimization_barrier(jnp.sum(expo, axis=-1, keepdims=True)))
    heads = jnp.einsum('kgst,tkd->skgd', probs, value_low, precision=highest).reshape(sequence_length, QUERY_HEADS * HEAD_SIZE)
    attended = lower_precision(low_back(heads))
    mid = tokens_seq + residual_scale * low_back(jnp.dot(attended, out_w, precision=highest))
    hidden_two = lower_precision(rms_norm(mid, gain_w[1]))
    logits = low_back(jnp.dot(hidden_two, router_w, precision=highest))
    chosen = jnp.take_along_axis(logits, route_seq, axis=1)
    gates = jax.nn.softmax(chosen, axis=-1)
    destination = destinations(route_seq, CAP, EXPERTS)
    flat_rows = jnp.repeat(hidden_two, TOPK, axis=0)
    buffer = jnp.zeros((EXPERTS * CAP, D), jnp.float32).at[destination].set(flat_rows)
    expert_in = low_back(buffer.reshape(EXPERTS, CAP, D))
    gate_up_act = low_back(jnp.einsum('ecd,edf->ecf', expert_in, gate_up_w, precision=highest))
    hidden = lower_precision(jax.nn.silu(gate_up_act[..., :FF]) * gate_up_act[..., FF:])
    expert_out = lower_precision(low_back(jnp.einsum('ecf,efd->ecd', hidden, down_w, precision=highest)))
    picked = expert_out.reshape(EXPERTS * CAP, D)[destination].reshape(sequence_length, TOPK, D)
    mixed = lax.optimization_barrier(jnp.sum(gates[..., None] * picked, axis=1))
    return mid + residual_scale * mixed

def adam_step(weight, moment, square, grad, rate, decay):
    moment = beta_one * moment + (1.0 - beta_one) * grad
    square = beta_two * square + (1.0 - beta_two) * grad * grad
    fixed_one = moment / (1.0 - beta_one ** STEP)
    fixed_two = square / (1.0 - beta_two ** STEP)
    weight = weight - rate * (fixed_one / (jnp.sqrt(fixed_two) + adam_eps) + decay * weight)
    return (weight, moment, square)

def reference(tokens, cotangent, routes, weight_qkv, moment_qkv, square_qkv, weight_out, moment_out, square_out, weight_router, moment_router, square_router, gains, moment_gains, square_gains, weight_gate_up, moment_gate_up, square_gate_up, weight_down, moment_down, square_down):
    count = N_DP * N_EXPERT
    per_step = math.gcd(count, max(1, 2048 // TOK_DEV))
    total_steps = count // per_step
    inputs = tokens.astype(jnp.float32).reshape(total_steps, per_step, TOK_DEV, D)
    grads_in = cotangent.astype(jnp.float32).reshape(total_steps, per_step, TOK_DEV, D)
    route_blocks = routes.reshape(total_steps, per_step, TOK_DEV, TOPK)
    masters = (weight_qkv, weight_out, weight_router, gains, weight_gate_up, weight_down)

    def apply_layer(master_set, block_in, block_routes):
        lowered = tuple((lower_precision(item) for item in master_set))
        return jax.vmap(sequence_forward, in_axes=(None, 0, 0))(lowered, block_in, block_routes)

    def one_block(total, block):
        block_in, block_grad, block_routes = block

        def closed(master_set, values):
            return apply_layer(master_set, values, block_routes)
        result, pull = jax.vjp(closed, masters, block_in)
        weight_grads, input_grad = pull(block_grad)
        total = jax.tree.map(jnp.add, total, weight_grads)
        return (total, (result, input_grad))
    start = tuple((jnp.zeros_like(item) for item in masters))
    sums, (results, input_grads) = lax.scan(one_block, start, (inputs, grads_in, route_blocks))
    layer_out = results.reshape(TOKENS, D).astype(jnp.bfloat16)
    token_grad = input_grads.reshape(TOKENS, D)
    rates = (D ** (-0.5), max(4, QUERY_HEADS * HEAD_SIZE // 256) ** (-0.5), (4 * D) ** (-0.5), 0.75, D ** (-0.5), max(2, FF // 128) ** (-0.5))
    decays = (weight_decay, weight_decay, weight_decay, 0.0, weight_decay, weight_decay)
    moments = (moment_qkv, moment_out, moment_router, moment_gains, moment_gate_up, moment_down)
    squares = (square_qkv, square_out, square_router, square_gains, square_gate_up, square_down)
    updated = []
    for index in range(6):
        updated.extend(adam_step(masters[index], moments[index], squares[index], sums[index], rates[index], decays[index]))
    return (layer_out, token_grad, updated[0], updated[1], updated[2], updated[3], updated[4], updated[5], updated[6], updated[7], updated[8], updated[9], updated[10], updated[11], updated[12], updated[13], updated[14], updated[15], updated[16], updated[17])
```

```python
import jax
import jax.numpy as jnp
from jax import lax
from jax.sharding import Mesh, PartitionSpec as P

D = 1536
QUERY_HEADS = 24
KEY_VALUE_HEADS = 8
HEAD_SIZE = 64
FF = 512
EXPERTS = 40
TOPK = 8
STEP = 10
QKV = 2560
LANES = 128

norm_eps = 1e-06
residual_scale = 0.22
score_scale = 0.125
beta_one = 0.9
beta_two = 0.95
adam_eps = 1e-08
weight_decay = 0.1

f32 = jnp.float32
bf16 = jnp.bfloat16
ALL = ("z", "x", "y", "core")
PLANE = ("z", "x")
SAME_CORE = ("z", "x", "y")


def rotary_tables(sequence_length, size):
    half = size // 2
    places = jnp.arange(sequence_length).astype(f32)[:, None]
    inverse = 10000.0 ** (-jnp.arange(half).astype(f32) * 2.0 / size)
    angles = places * inverse[None, :]
    return (jnp.cos(angles)[:, None, :], jnp.sin(angles)[:, None, :])


def apply_rotation(values, cosine_lookup, sine_lookup):
    half = values.shape[-1] // 2
    first = values[..., :half]
    second = values[..., half:]
    return jnp.concatenate(
        [
            first * cosine_lookup - second * sine_lookup,
            second * cosine_lookup + first * sine_lookup,
        ],
        axis=-1,
    )


def attention_scores(query_rotated, key_rot, causal):
    scores = (
        jnp.einsum("skgd,tkd->kgst", query_rotated, key_rot, preferred_element_type=f32)
        * score_scale
    )
    return jnp.where(causal, scores, -1e30)


def norm_backward(grad_normed, values, factor, gain):
    scaled = grad_normed * gain
    grad_gain = jnp.sum(grad_normed * values * factor, axis=0)
    value_gradient = factor * scaled - values * factor * factor * factor * jnp.mean(
        scaled * values, axis=-1, keepdims=True
    )
    return (value_gradient, grad_gain)


def adam_step(weight, moment, square, grad, rate, decay):
    moment = beta_one * moment + (1.0 - beta_one) * grad
    square = beta_two * square + (1.0 - beta_two) * grad * grad
    fixed_one = moment / (1.0 - beta_one**STEP)
    fixed_two = square / (1.0 - beta_two**STEP)
    weight = weight - rate * (fixed_one / (jnp.sqrt(fixed_two) + adam_eps) + decay * weight)
    return (weight, moment, square)


def dot(a, b):
    return jnp.dot(a, b, preferred_element_type=f32)


def dot_nt(a, b):
    return lax.dot_general(a, b, (((1,), (1,)), ((), ())), preferred_element_type=f32)


def dot_tn(a, b):
    return lax.dot_general(a, b, (((0,), (0,)), ((), ())), preferred_element_type=f32)


def pad_lanes(values):
    extra = -values.shape[-1] % LANES
    return jnp.pad(values, ((0, 0), (0, extra)))


def swap_core(values):
    return lax.ppermute(values, "core", [(0, 1), (1, 0)])


def make_shards(sizes):
    nz, nx, ny = sizes
    planes = nz * nx
    per_group = EXPERTS // (2 * ny)
    whole = per_group // planes
    spare = per_group - whole * planes
    piece = FF // planes

    def pack_gate_up(weights):
        rows = weights.shape[1]
        parts = []
        if whole:
            full = weights[: whole * planes].reshape(planes, whole, rows, 2, FF)
            full = full.transpose(0, 2, 3, 1, 4).reshape(planes, rows, 2, whole * FF)
            parts.append(full)
        if spare:
            cut = weights[whole * planes :].reshape(spare, rows, 2, planes, piece)
            cut = cut.transpose(3, 1, 2, 0, 4).reshape(planes, rows, 2, spare * piece)
            parts.append(cut)
        return jnp.concatenate([p.reshape(planes, rows, -1) for p in parts], axis=2)

    def unpack_gate_up(packed):
        rows = packed.shape[1]
        parts = []
        at = 0
        if whole:
            full = packed[:, :, : 2 * whole * FF].reshape(planes, rows, 2, whole, FF)
            full = full.transpose(0, 3, 1, 2, 4).reshape(planes * whole, rows, 2 * FF)
            parts.append(full)
            at = 2 * whole * FF
        if spare:
            cut = packed[:, :, at:].reshape(planes, rows, 2, spare, piece)
            cut = cut.transpose(3, 1, 2, 0, 4).reshape(spare, rows, 2 * FF)
            parts.append(cut)
        return jnp.concatenate(parts, axis=0)

    wide = whole * FF
    narrow = spare * piece
    units = wide + narrow

    def split_gate_up(values):
        gate = [values[:, :wide], values[:, 2 * wide : 2 * wide + narrow]]
        up = [values[:, wide : 2 * wide], values[:, 2 * wide + narrow :]]
        return jnp.concatenate(gate, axis=1), jnp.concatenate(up, axis=1)

    def join_gate_up(gate, up):
        return jnp.concatenate(
            [gate[:, :wide], up[:, :wide], gate[:, wide:], up[:, wide:]], axis=1
        )

    def expert_ids(group, place):
        base = group * per_group
        first = [(base + place * whole + i, FF) for i in range(whole)]
        return first + [(base + whole * planes + i, piece) for i in range(spare)]

    def spread(columns, widths):
        rows = columns[0].shape[0]
        return jnp.concatenate(
            [jnp.broadcast_to(c[:, None], (rows, w)) for c, w in zip(columns, widths)], axis=1
        )

    def all_to_all_plane(values):
        return lax.all_to_all(values, PLANE, split_axis=0, concat_axis=0, tiled=True)

    def shards(
        tokens,
        cotangent,
        routes,
        weight_qkv,
        moment_qkv,
        square_qkv,
        weight_out,
        moment_out,
        square_out,
        weight_router,
        moment_router,
        square_router,
        gains,
        moment_gains,
        square_gains,
        weight_gate_up,
        moment_gate_up,
        square_gate_up,
        weight_down,
        moment_down,
        square_down,
    ):
        sequence_length = tokens.shape[0]
        head_groups = QUERY_HEADS // KEY_VALUE_HEADS
        place = lax.axis_index(PLANE)
        row = lax.axis_index("y")
        core = lax.axis_index("core")

        small = pad_lanes(jnp.concatenate([weight_router, gains.T], axis=1))
        first_pack = jnp.concatenate([weight_qkv, small], axis=1).astype(bf16)
        first_all = lax.all_gather(first_pack, ALL, axis=0, tiled=True)
        out_w = lax.all_gather(weight_out.astype(bf16), ALL, axis=0, tiled=True)
        qkv_w = first_all[:, :QKV]
        router_w = first_all[:, QKV : QKV + EXPERTS]
        gain_one = first_all[:, QKV + EXPERTS].astype(f32)
        gain_two = first_all[:, QKV + EXPERTS + 1].astype(f32)

        gate_up_own = all_to_all_plane(pack_gate_up(weight_gate_up.astype(bf16))).reshape(D, -1)
        down_low = weight_down.astype(bf16)
        down_parts = []
        if whole:
            got = all_to_all_plane(down_low[: whole * planes].reshape(planes, whole, piece, D))
            down_parts.append(got.transpose(1, 0, 2, 3).reshape(wide, D))
        if spare:
            down_parts.append(down_low[whole * planes :].reshape(narrow, D))
        down_own = jnp.concatenate(down_parts, axis=0)
        gate_up_other = swap_core(gate_up_own)
        down_other = swap_core(down_own)

        cot_all = lax.all_gather(cotangent, SAME_CORE, axis=0, tiled=True)

        inputs = tokens.astype(f32)
        factor_one = lax.rsqrt(jnp.mean(inputs * inputs, axis=-1, keepdims=True) + norm_eps)
        hidden_one = (inputs * factor_one * gain_one).astype(bf16)
        joined_heads = dot(hidden_one, qkv_w)
        query_rows = joined_heads[:, : QUERY_HEADS * HEAD_SIZE].reshape(
            sequence_length, QUERY_HEADS, HEAD_SIZE
        )
        every_key = joined_heads[
            :, QUERY_HEADS * HEAD_SIZE : QUERY_HEADS * HEAD_SIZE + KEY_VALUE_HEADS * HEAD_SIZE
        ].reshape(sequence_length, KEY_VALUE_HEADS, HEAD_SIZE)
        every_value = joined_heads[
            :, QUERY_HEADS * HEAD_SIZE + KEY_VALUE_HEADS * HEAD_SIZE :
        ].reshape(sequence_length, KEY_VALUE_HEADS, HEAD_SIZE)
        cosine_lookup, sine_lookup = rotary_tables(sequence_length, HEAD_SIZE)
        query_rotated = (
            apply_rotation(query_rows, cosine_lookup, sine_lookup)
            .astype(bf16)
            .reshape(sequence_length, KEY_VALUE_HEADS, head_groups, HEAD_SIZE)
        )
        key_rot = apply_rotation(every_key, cosine_lookup, sine_lookup).astype(bf16)
        value_low = every_value.astype(bf16)
        causal = jnp.arange(sequence_length)[:, None] >= jnp.arange(sequence_length)[None, :]
        scores = attention_scores(query_rotated, key_rot, causal)
        peak = jnp.max(scores, axis=-1, keepdims=True)
        expo = jnp.exp(scores - peak)
        totals = jnp.sum(expo, axis=-1, keepdims=True)
        probs = expo / totals
        prob_low = probs.astype(bf16)
        heads = jnp.einsum("kgst,tkd->skgd", prob_low, value_low, preferred_element_type=f32)
        attended = heads.reshape(sequence_length, QUERY_HEADS * HEAD_SIZE).astype(bf16)
        mid = inputs + residual_scale * dot(attended, out_w)
        factor_two = lax.rsqrt(jnp.mean(mid * mid, axis=-1, keepdims=True) + norm_eps)
        hidden_two = (mid * factor_two * gain_two).astype(bf16)
        logits = dot(hidden_two, router_w)
        named = jnp.any(
            routes[..., None] == jnp.arange(EXPERTS, dtype=routes.dtype)[None, None, :], axis=1
        )
        shown = jnp.where(named, logits, -jnp.inf)
        raised = jnp.exp(shown - jnp.max(shown, axis=-1, keepdims=True))
        gates = raised / jnp.sum(raised, axis=-1, keepdims=True)

        gate_high = gates.astype(bf16)
        gate_rest = (gates - gate_high.astype(f32)).astype(bf16)
        sent = jnp.concatenate(
            [hidden_two, pad_lanes(jnp.concatenate([gate_high, gate_rest], axis=1))], axis=1
        )
        sent_all = lax.all_gather(sent, SAME_CORE, axis=0, tiled=True)
        rows_all = sent_all[:, :D]
        gates_all = sent_all[:, D : D + EXPERTS].astype(f32) + sent_all[
            :, D + EXPERTS : D + 2 * EXPERTS
        ].astype(f32)

        numbers = jnp.arange(EXPERTS)
        mixed_part = 0.0
        grad_two_part = 0.0
        dgate_part = 0.0
        grads = []
        for gate_up_w, down_w, group in (
            (gate_up_own, down_own, row * 2 + core),
            (gate_up_other, down_other, row * 2 + 1 - core),
        ):
            ids = expert_ids(group, place)
            widths = [w for _, w in ids]
            gate_cols = [
                jnp.sum(jnp.where(numbers[None, :] == e, gates_all, 0.0), axis=1) for e, _ in ids
            ]
            gate_wide = spread(gate_cols, widths)
            gate_part, up_part = split_gate_up(dot(rows_all, gate_up_w))
            squash = jax.nn.sigmoid(gate_part)
            swish = gate_part * squash
            hidden = swish * up_part
            gated = (hidden * gate_wide).astype(bf16)
            mixed_part = mixed_part + dot(gated, down_w)
            reach = residual_scale * dot_nt(cot_all, down_w)
            product = hidden * reach
            at = 0
            for e, width in ids:
                total = jnp.sum(product[:, at : at + width], axis=1, keepdims=True)
                dgate_part = dgate_part + jnp.where(numbers[None, :] == e, total, 0.0)
                at += width
            grad_hidden = reach * gate_wide
            grad_gate = grad_hidden * up_part * squash * (1.0 + gate_part * (1.0 - squash))
            grad_up = grad_hidden * swish
            grad_both = join_gate_up(grad_gate, grad_up).astype(bf16)
            grad_two_part = grad_two_part + dot_nt(grad_both, gate_up_w)
            grads.append(
                (
                    dot_tn(rows_all, grad_both),
                    residual_scale * dot_tn(gated, cot_all),
                )
            )

        mixed_sent = jnp.concatenate([mixed_part, pad_lanes(dgate_part)], axis=1).astype(bf16)
        grad_two = lax.psum_scatter(
            grad_two_part.astype(bf16), SAME_CORE, scatter_dimension=0, tiled=True
        ).astype(f32)
        mixed_got = lax.psum_scatter(
            mixed_sent, SAME_CORE, scatter_dimension=0, tiled=True
        ).astype(f32)
        layer_out = (mid + residual_scale * mixed_got[:, :D]).astype(bf16)
        grad_gates = mixed_got[:, D : D + EXPERTS]

        (own_gate_up, own_down), (other_gate_up, other_down) = grads
        sum_gate_up = own_gate_up + swap_core(other_gate_up.astype(bf16)).astype(f32)
        sum_down = own_down + swap_core(other_down.astype(bf16)).astype(f32)
        home_gate_up = unpack_gate_up(
            all_to_all_plane(sum_gate_up.astype(bf16).reshape(planes, D // planes, -1))
        ).astype(f32)
        down_parts = []
        if whole:
            back = sum_down[:wide].astype(bf16).reshape(whole, planes, piece, D)
            back = all_to_all_plane(back.transpose(1, 0, 2, 3))
            down_parts.append(back.reshape(planes * whole, piece, D).astype(f32))
        if spare:
            down_parts.append(sum_down[wide:].reshape(spare, piece, D))
        home_down = jnp.concatenate(down_parts, axis=0)

        grad_out = cotangent.astype(f32)
        grad_chosen = gates * (grad_gates - jnp.sum(gates * grad_gates, axis=-1, keepdims=True))
        grad_logits = grad_chosen.astype(bf16)
        grad_router = dot_tn(hidden_two, grad_logits)
        grad_two = grad_two + dot_nt(grad_logits, router_w)
        grad_mid, grad_gain_two = norm_backward(grad_two, mid, factor_two, gain_two)
        grad_mid = grad_out + grad_mid
        grad_att = (residual_scale * grad_mid).astype(bf16)
        grad_out_w = dot_tn(attended, grad_att)
        grad_heads = (
            dot_nt(grad_att, out_w)
            .astype(bf16)
            .reshape(sequence_length, KEY_VALUE_HEADS, head_groups, HEAD_SIZE)
        )
        grad_probs = jnp.einsum(
            "skgd,tkd->kgst", grad_heads, value_low, preferred_element_type=f32
        )
        value_gradient = jnp.einsum(
            "kgst,skgd->tkd", prob_low, grad_heads, preferred_element_type=f32
        )
        row_dot = jnp.sum(probs * grad_probs, axis=-1, keepdims=True)
        grad_scores = (probs * (grad_probs - row_dot)).astype(bf16)
        grad_qrot = (
            jnp.einsum("kgst,tkd->skgd", grad_scores, key_rot, preferred_element_type=f32)
            * score_scale
        )
        grad_krot = (
            jnp.einsum("kgst,skgd->tkd", grad_scores, query_rotated, preferred_element_type=f32)
            * score_scale
        )
        grad_queries = apply_rotation(
            grad_qrot.reshape(sequence_length, QUERY_HEADS, HEAD_SIZE), cosine_lookup, -sine_lookup
        )
        key_gradient = apply_rotation(grad_krot, cosine_lookup, -sine_lookup)
        grad_joined = jnp.concatenate(
            [
                grad_queries.reshape(sequence_length, QUERY_HEADS * HEAD_SIZE),
                key_gradient.reshape(sequence_length, KEY_VALUE_HEADS * HEAD_SIZE),
                value_gradient.reshape(sequence_length, KEY_VALUE_HEADS * HEAD_SIZE),
            ],
            axis=1,
        ).astype(bf16)
        grad_qkv_w = dot_tn(hidden_one, grad_joined)
        grad_one = dot_nt(grad_joined, qkv_w)
        grad_inputs, grad_gain_one = norm_backward(grad_one, inputs, factor_one, gain_one)
        token_grad = grad_mid + grad_inputs

        out_sent = jnp.concatenate(
            [
                grad_out_w,
                pad_lanes(jnp.concatenate([grad_router, grad_gain_two[:, None]], axis=1)),
            ],
            axis=1,
        ).astype(bf16)
        out_got = lax.psum_scatter(out_sent, ALL, scatter_dimension=0, tiled=True).astype(f32)
        qkv_sent = jnp.concatenate(
            [grad_qkv_w, pad_lanes(grad_gain_one[:, None])], axis=1
        ).astype(bf16)
        qkv_got = lax.psum_scatter(qkv_sent, ALL, scatter_dimension=0, tiled=True).astype(f32)
        sum_out = out_got[:, : QUERY_HEADS * HEAD_SIZE]
        sum_router = out_got[:, D : D + EXPERTS]
        sum_qkv = qkv_got[:, :QKV]
        sum_gains = jnp.stack([qkv_got[:, QKV], out_got[:, D + EXPERTS]], axis=0)

        new_gate_up = adam_step(
            weight_gate_up, moment_gate_up, square_gate_up, home_gate_up, D ** (-0.5), weight_decay
        )
        new_down = adam_step(
            weight_down,
            moment_down,
            square_down,
            home_down,
            max(2, FF // 128) ** (-0.5),
            weight_decay,
        )
        new_qkv = adam_step(weight_qkv, moment_qkv, square_qkv, sum_qkv, D ** (-0.5), weight_decay)
        new_out = adam_step(
            weight_out,
            moment_out,
            square_out,
            sum_out,
            max(4, QUERY_HEADS * HEAD_SIZE // 256) ** (-0.5),
            weight_decay,
        )
        new_router = adam_step(
            weight_router, moment_router, square_router, sum_router, (4 * D) ** (-0.5), weight_decay
        )
        new_gains = adam_step(gains, moment_gains, square_gains, sum_gains, 0.75, 0.0)
        return (
            layer_out,
            token_grad,
            *new_qkv,
            *new_out,
            *new_router,
            *new_gains,
            *new_gate_up,
            *new_down,
        )

    return shards


def solution(mesh):
    n_dp, n_expert = mesh.shape["dp"], mesh.shape["expert"]
    nz = 4
    nx, ny = n_dp // nz, n_expert // 2
    fine = Mesh(mesh.devices.reshape(nz, nx, ny, 2), ALL)
    rows = P(ALL, None)
    columns = P(None, ALL)
    experts = P(("y", "core"), ("z", "x"), None)
    dense = (rows,) * 9 + (columns,) * 3 + (experts,) * 6
    return jax.shard_map(
        make_shards((nz, nx, ny)),
        mesh=fine,
        in_specs=(rows,) * 3 + dense,
        out_specs=(rows,) * 2 + dense,
        check_vma=False,
    )
```

```python
import jax
import jax.numpy as jnp
import numpy as np
from jax import lax
from jax.sharding import Mesh, PartitionSpec as P

D = 1536
QUERY_HEADS = 24
KEY_VALUE_HEADS = 8
HEAD_SIZE = 64
FF = 512
EXPERTS = 40
TOPK = 8
STEP = 10
QKV = 2560
LANES = 128
HEADS_WIDTH = QUERY_HEADS * HEAD_SIZE
KEYS_WIDTH = KEY_VALUE_HEADS * HEAD_SIZE

norm_eps = 1e-06
residual_scale = 0.22
score_scale = 0.125
beta_one = 0.9
beta_two = 0.95
adam_eps = 1e-08
weight_decay = 0.1

f32 = jnp.float32
bf16 = jnp.bfloat16
ALL = ("z", "x", "y", "core")
PLANE = ("z", "x")


def rotary_tables(sequence_length, size):
    half = size // 2
    places = jnp.arange(sequence_length).astype(f32)[:, None]
    inverse = 10000.0 ** (-jnp.arange(half).astype(f32) * 2.0 / size)
    angles = places * inverse[None, :]
    return (jnp.cos(angles)[:, None, :], jnp.sin(angles)[:, None, :])


def apply_rotation(values, cosine_lookup, sine_lookup):
    half = values.shape[-1] // 2
    first = values[..., :half]
    second = values[..., half:]
    return jnp.concatenate(
        [
            first * cosine_lookup - second * sine_lookup,
            second * cosine_lookup + first * sine_lookup,
        ],
        axis=-1,
    )


def attention_scores(query_rotated, key_rot, causal):
    scores = (
        jnp.einsum("skgd,tkd->kgst", query_rotated, key_rot, preferred_element_type=f32)
        * score_scale
    )
    return jnp.where(causal, scores, -1e30)


def norm_backward(grad_normed, values, factor, gain):
    scaled = grad_normed * gain
    grad_gain = jnp.sum(grad_normed * values * factor, axis=0)
    value_gradient = factor * scaled - values * factor * factor * factor * jnp.mean(
        scaled * values, axis=-1, keepdims=True
    )
    return (value_gradient, grad_gain)


def adam_step(weight, moment, square, grad, rate, decay):
    moment = beta_one * moment + (1.0 - beta_one) * grad
    square = beta_two * square + (1.0 - beta_two) * grad * grad
    fixed_one = moment / (1.0 - beta_one**STEP)
    fixed_two = square / (1.0 - beta_two**STEP)
    weight = weight - rate * (fixed_one / (jnp.sqrt(fixed_two) + adam_eps) + decay * weight)
    return (weight, moment, square)


def dot(a, b):
    return jnp.dot(a, b, preferred_element_type=f32)


def dot_nt(a, b):
    return lax.dot_general(a, b, (((1,), (1,)), ((), ())), preferred_element_type=f32)


def dot_tn(a, b):
    return lax.dot_general(a, b, (((0,), (0,)), ((), ())), preferred_element_type=f32)


def pad_lanes(values):
    extra = -values.shape[-1] % LANES
    return jnp.pad(values, ((0, 0), (0, extra)))


def swap_core(values):
    return lax.ppermute(values, "core", [(0, 1), (1, 0)])


def ring_order(n):
    return [0] + list(range(1, n, 2)) + list(range(n - 2 + n % 2, 0, -2))


def home_table(n):
    order = ring_order(n)
    place = {chip: at for at, chip in enumerate(order)}
    return np.array([[order[(place[i] - s) % n] for s in range(n)] for i in range(n)], np.int32)


def make_shards(sizes):
    nz, nx, ny = sizes
    length = {"z": nz, "x": nx, "y": ny}
    planes = nz * nx
    per_group = EXPERTS // (2 * ny)
    whole = per_group // planes
    spare = per_group - whole * planes
    piece = FF // planes
    wide = whole * FF
    narrow = spare * piece

    def onward(values, axis):
        order = ring_order(length[axis])
        pairs = [(order[i], order[(i + 1) % len(order)]) for i in range(len(order))]
        return lax.ppermute(values, axis, pairs)

    def backward(values, axis):
        order = ring_order(length[axis])
        pairs = [(order[(i + 1) % len(order)], order[i]) for i in range(len(order))]
        return lax.ppermute(values, axis, pairs)

    def gather(own, second, third):
        rows = own.shape[0]
        found = {}
        block = own
        for sz in range(nz):
            if sz:
                block = onward(block, "z")
            line = [block]
            for _ in range(length[second] - 1):
                line.append(onward(line[-1], second))
            pack = jnp.concatenate(line, axis=0)
            for s3 in range(length[third]):
                if s3:
                    pack = onward(pack, third)
                for s2 in range(length[second]):
                    at = {"z": sz, second: s2, third: s3}
                    found[at["z"], at["y"], at["x"]] = pack[s2 * rows : (s2 + 1) * rows]
        return found

    def scatter(parts, second, third):
        total = None
        for sz in reversed(range(nz)):
            line = None
            for s3 in reversed(range(length[third])):
                blocks = []
                for s2 in range(length[second]):
                    at = {"z": sz, second: s2, third: s3}
                    blocks.append(parts[at["z"], at["y"], at["x"]])
                mine = jnp.concatenate(blocks, axis=0)
                line = mine if line is None else add_low(backward(line, third), mine)
            rows = line.shape[0] // length[second]
            one = None
            for s2 in reversed(range(length[second])):
                mine = line[s2 * rows : (s2 + 1) * rows]
                one = mine if one is None else add_low(backward(one, second), mine)
            total = one if total is None else add_low(backward(total, "z"), one)
        return total

    def add_low(a, b):
        return (a.astype(f32) + b.astype(f32)).astype(bf16)

    offsets = [(sz, sy, sx) for sz in range(nz) for sy in range(ny) for sx in range(nx)]

    def in_order(found, some=None):
        return jnp.concatenate([found[o] for o in (some or offsets)], axis=0)

    def cut(values, some=None):
        some = some or offsets
        rows = values.shape[0] // len(some)
        return {o: values[i * rows : (i + 1) * rows] for i, o in enumerate(some)}

    def gather_weights(left, right):
        whole_parts = []
        for own, second, third in ((left, "x", "y"), (right, "y", "x")):
            found = gather(own, second, third)
            groups = []
            for sz in range(nz):
                groups.append(in_order(found, [o for o in offsets if o[0] == sz]))
            others = [swap_core(g) for g in groups]
            whole_parts.append(jnp.concatenate(groups + others, axis=0))
        return whole_parts

    def scatter_weights(left, right):
        sums = []
        for values, second, third in ((left, "x", "y"), (right, "y", "x")):
            half = values.shape[0] // 2
            both = add_low(swap_core(values[half:]), values[:half])
            sums.append(scatter(cut(both), second, third).astype(f32))
        return sums

    def row_order():
        block = jnp.zeros((1, 1, 1, 1), jnp.int32)
        for axis, n, shape in (
            ("z", nz, (1, nz, 1, 1)),
            ("x", nx, (1, 1, 1, nx)),
            ("y", ny, (1, 1, ny, 1)),
            ("core", 2, (2, 1, 1, 1)),
        ):
            table = jnp.asarray(home_table(n))
            here = jnp.arange(n)[:, None] == lax.axis_index(axis)
            home = jnp.sum(jnp.where(here, table, 0), axis=0)
            block = block * n + home.reshape(shape)
        block = block.reshape(-1, 1)
        rows = D // block.shape[0]
        kept = (block * rows + jnp.arange(rows)[None, :]).reshape(1, D)
        return (jnp.arange(D)[:, None] == kept).astype(bf16)

    def all_to_all_plane(values):
        return lax.all_to_all(values, PLANE, split_axis=0, concat_axis=0, tiled=True)

    def send_experts(gate_up, down):
        rows = gate_up.shape[1]
        sets = []
        if whole:
            full = gate_up[: whole * planes].reshape(planes, whole, rows, 2, FF)
            full = full.transpose(0, 2, 3, 1, 4).reshape(planes, rows, 2 * wide)
            low = down[: whole * planes].reshape(planes, whole, piece, D)
            low = all_to_all_plane(low).transpose(1, 0, 2, 3).reshape(wide, D)
            sets.append((all_to_all_plane(full).reshape(D, 2 * wide), low))
        if spare:
            part = gate_up[whole * planes :].reshape(spare, rows, 2, planes, piece)
            part = part.transpose(3, 1, 2, 0, 4).reshape(planes, rows, 2 * narrow)
            part = all_to_all_plane(part).reshape(D, 2 * narrow)
            sets.append((part, down[whole * planes :].reshape(narrow, D)))
        return sets

    def return_experts(sets):
        rows = D // planes
        gate_up, down = [], []
        at = 0
        if whole:
            full, low = sets[at]
            at += 1
            full = all_to_all_plane(full.astype(bf16).reshape(planes, rows, 2 * wide))
            full = full.reshape(planes, rows, 2, whole, FF).transpose(0, 3, 1, 2, 4)
            gate_up.append(full.reshape(whole * planes, rows, 2 * FF).astype(f32))
            low = low.astype(bf16).reshape(whole, planes, piece, D).transpose(1, 0, 2, 3)
            down.append(all_to_all_plane(low).reshape(whole * planes, piece, D).astype(f32))
        if spare:
            part, low = sets[at]
            part = all_to_all_plane(part.astype(bf16).reshape(planes, rows, 2 * narrow))
            part = part.reshape(planes, rows, 2, spare, piece).transpose(3, 1, 2, 0, 4)
            gate_up.append(part.reshape(spare, rows, 2 * FF).astype(f32))
            down.append(low.reshape(spare, piece, D))
        return jnp.concatenate(gate_up, axis=0), jnp.concatenate(down, axis=0)

    def unit_experts(group, place):
        base = group * per_group
        sets = []
        if whole:
            sets.append(base + place * whole + jnp.arange(wide) // FF)
        if spare:
            sets.append(base + whole * planes + jnp.arange(narrow) // piece)
        return sets

    def shards(
        tokens,
        cotangent,
        routes,
        weight_qkv,
        moment_qkv,
        square_qkv,
        weight_out,
        moment_out,
        square_out,
        weight_router,
        moment_router,
        square_router,
        gains,
        moment_gains,
        square_gains,
        weight_gate_up,
        moment_gate_up,
        square_gate_up,
        weight_down,
        moment_down,
        square_down,
    ):
        sequence_length = tokens.shape[0]
        half_rows = sequence_length // 2
        head_groups = QUERY_HEADS // KEY_VALUE_HEADS
        place = lax.axis_index(PLANE)
        group = lax.axis_index("y") * 2 + lax.axis_index("core")
        partner = lax.axis_index("y") * 2 + 1 - lax.axis_index("core")

        small = pad_lanes(jnp.concatenate([weight_router, gains.T], axis=1))
        qkv_low = weight_qkv.astype(bf16)
        out_low = weight_out.astype(bf16)
        first_left = jnp.concatenate([qkv_low[:, : QKV // 2], small.astype(bf16)], axis=1)
        left_all, qkv_right = gather_weights(first_left, qkv_low[:, QKV // 2 :])
        out_low, left_all, qkv_right = lax.optimization_barrier((out_low, left_all, qkv_right))
        qkv_left, small_all = left_all[:, : QKV // 2], left_all[:, QKV // 2 :]
        out_left, out_right = gather_weights(out_low[:, : D // 2], out_low[:, D // 2 :])

        own_sets = send_experts(weight_gate_up.astype(bf16), weight_down.astype(bf16))
        other_sets = [(swap_core(a), swap_core(b)) for a, b in own_sets]

        order = row_order()
        tokens_own = dot(tokens, order)
        inputs = tokens.astype(f32)
        factor_one = lax.rsqrt(jnp.mean(inputs * inputs, axis=-1, keepdims=True) + norm_eps)
        gain_one = small_all[:, EXPERTS].astype(f32)
        small_here = dot(order, small_all)
        gain_two = small_here[:, EXPERTS + 1]
        router_w = small_here[:, :EXPERTS].astype(bf16)
        hidden_one = (tokens_own * factor_one * gain_one).astype(bf16)
        joined_heads = jnp.concatenate([dot(hidden_one, qkv_left), dot(hidden_one, qkv_right)], axis=1)
        query_rows = joined_heads[:, :HEADS_WIDTH].reshape(sequence_length, QUERY_HEADS, HEAD_SIZE)
        every_key = joined_heads[:, HEADS_WIDTH : HEADS_WIDTH + KEYS_WIDTH].reshape(
            sequence_length, KEY_VALUE_HEADS, HEAD_SIZE
        )
        every_value = joined_heads[:, HEADS_WIDTH + KEYS_WIDTH :].reshape(
            sequence_length, KEY_VALUE_HEADS, HEAD_SIZE
        )
        cosine_lookup, sine_lookup = rotary_tables(sequence_length, HEAD_SIZE)
        query_rotated = (
            apply_rotation(query_rows, cosine_lookup, sine_lookup)
            .astype(bf16)
            .reshape(sequence_length, KEY_VALUE_HEADS, head_groups, HEAD_SIZE)
        )
        key_rot = apply_rotation(every_key, cosine_lookup, sine_lookup).astype(bf16)
        value_low = every_value.astype(bf16)
        causal = jnp.arange(sequence_length)[:, None] >= jnp.arange(sequence_length)[None, :]
        scores = attention_scores(query_rotated, key_rot, causal)
        peak = jnp.max(scores, axis=-1, keepdims=True)
        expo = jnp.exp(scores - peak)
        totals = jnp.sum(expo, axis=-1, keepdims=True)
        probs = expo / totals
        prob_low = probs.astype(bf16)
        heads = jnp.einsum("kgst,tkd->skgd", prob_low, value_low, preferred_element_type=f32)
        attended = heads.reshape(sequence_length, HEADS_WIDTH).astype(bf16)
        attended = dot(attended, order).astype(bf16)
        mid = inputs + residual_scale * jnp.concatenate(
            [dot(attended, out_left), dot(attended, out_right)], axis=1
        )
        factor_two = lax.rsqrt(jnp.mean(mid * mid, axis=-1, keepdims=True) + norm_eps)
        hidden_two = (mid * factor_two * gain_two).astype(bf16)
        logits = dot(hidden_two, router_w)
        named = jnp.any(
            routes[..., None] == jnp.arange(EXPERTS, dtype=routes.dtype)[None, None, :], axis=1
        )
        shown = jnp.where(named, logits, -jnp.inf)
        raised = jnp.exp(shown - jnp.max(shown, axis=-1, keepdims=True))
        gates = raised / jnp.sum(raised, axis=-1, keepdims=True)

        gate_high = gates.astype(bf16)
        gate_rest = (gates - gate_high.astype(f32)).astype(bf16)
        sent = jnp.concatenate(
            [hidden_two, pad_lanes(jnp.concatenate([gate_high, gate_rest], axis=1))], axis=1
        )
        sent_parts = [
            gather(sent[:half_rows], "x", "y"),
            gather(sent[half_rows:], "y", "x"),
        ]
        rows_all = jnp.concatenate([b[:, :D] for p in sent_parts for b in [p[o] for o in offsets]], axis=0)
        gates_all = jnp.concatenate([b[:, D:] for p in sent_parts for b in [p[o] for o in offsets]], axis=0)

        cot_own, rows_all, gates_all = lax.optimization_barrier((cotangent, rows_all, gates_all))
        cot_parts = [
            gather(cot_own[:half_rows], "x", "y"),
            gather(cot_own[half_rows:], "y", "x"),
        ]
        cot_all = jnp.concatenate([in_order(p) for p in cot_parts], axis=0)

        numbers = jnp.arange(LANES)
        mixed_part = 0.0
        grad_two_part = 0.0
        dgate_part = 0.0
        grads = []
        for sets, whose in ((own_sets, group), (other_sets, partner)):
            set_grads = []
            for (gate_up_w, down_w), behind in zip(sets, unit_experts(whose, place)):
                width = down_w.shape[0]
                belongs = numbers[:, None] == behind[None, :]
                twice = belongs | (numbers[:, None] == behind[None, :] + EXPERTS)
                gate_wide = dot(gates_all, twice.astype(bf16))
                gate_up_act = dot(rows_all, gate_up_w)
                gate_part, up_part = gate_up_act[:, :width], gate_up_act[:, width:]
                squash = jax.nn.sigmoid(gate_part)
                swish = gate_part * squash
                hidden = swish * up_part
                gated = (hidden * gate_wide).astype(bf16)
                mixed_part = mixed_part + dot(gated, down_w)
                reach = residual_scale * dot_nt(cot_all, down_w)
                dgate_part = dgate_part + dot_nt((hidden * reach).astype(bf16), belongs.astype(bf16))
                grad_hidden = reach * gate_wide
                grad_gate = grad_hidden * up_part * squash * (1.0 + gate_part * (1.0 - squash))
                grad_up = grad_hidden * swish
                grad_both = jnp.concatenate([grad_gate, grad_up], axis=1).astype(bf16)
                grad_two_part = grad_two_part + dot_nt(grad_both, gate_up_w)
                set_grads.append(
                    (dot_tn(rows_all, grad_both), residual_scale * dot_tn(gated, cot_all))
                )
            grads.append(set_grads)

        def scatter_tokens(values):
            top, low = values[: values.shape[0] // 2], values[values.shape[0] // 2 :]
            sums = [scatter(cut(top), "x", "y"), scatter(cut(low), "y", "x")]
            return jnp.concatenate(sums, axis=0).astype(f32)

        two_got = scatter_tokens(
            jnp.concatenate([grad_two_part.astype(bf16), dgate_part.astype(bf16)], axis=1)
        )
        mixed_low, two_got = lax.optimization_barrier((mixed_part.astype(bf16), two_got))
        grad_two, grad_gates = two_got[:, :D], two_got[:, D : D + EXPERTS]
        mixed = scatter_tokens(mixed_low)
        layer_out = (mid + residual_scale * mixed).astype(bf16)

        sum_sets = []
        for (own_a, own_b), (other_a, other_b) in zip(*grads):
            sum_a = own_a + swap_core(other_a.astype(bf16)).astype(f32)
            sum_b = own_b + swap_core(other_b.astype(bf16)).astype(f32)
            sum_sets.append((sum_a, sum_b))
        home_gate_up, home_down = return_experts(sum_sets)

        grad_out = cotangent.astype(f32)
        grad_chosen = gates * (grad_gates - jnp.sum(gates * grad_gates, axis=-1, keepdims=True))
        grad_logits = grad_chosen.astype(bf16)
        grad_router = dot_tn(dot(hidden_two, order).astype(bf16), grad_logits)
        grad_two = grad_two + dot_nt(grad_logits, router_w)
        grad_mid, grad_gain_two = norm_backward(grad_two, mid, factor_two, gain_two)
        grad_gain_two = dot_tn(order, grad_gain_two.astype(bf16)[:, None])
        grad_mid = grad_out + grad_mid
        grad_att = (residual_scale * grad_mid).astype(bf16)
        grad_heads = (
            dot_nt(grad_att[:, : D // 2], out_left) + dot_nt(grad_att[:, D // 2 :], out_right)
        ).astype(bf16)
        grad_heads = (
            dot_nt(grad_heads, order)
            .astype(bf16)
            .reshape(sequence_length, KEY_VALUE_HEADS, head_groups, HEAD_SIZE)
        )
        grad_probs = jnp.einsum(
            "skgd,tkd->kgst", grad_heads, value_low, preferred_element_type=f32
        )
        value_gradient = jnp.einsum(
            "kgst,skgd->tkd", prob_low, grad_heads, preferred_element_type=f32
        )
        row_dot = jnp.sum(probs * grad_probs, axis=-1, keepdims=True)
        grad_scores = (probs * (grad_probs - row_dot)).astype(bf16)
        grad_qrot = (
            jnp.einsum("kgst,tkd->skgd", grad_scores, key_rot, preferred_element_type=f32)
            * score_scale
        )
        grad_krot = (
            jnp.einsum("kgst,skgd->tkd", grad_scores, query_rotated, preferred_element_type=f32)
            * score_scale
        )
        grad_queries = apply_rotation(
            grad_qrot.reshape(sequence_length, QUERY_HEADS, HEAD_SIZE), cosine_lookup, -sine_lookup
        )
        key_gradient = apply_rotation(grad_krot, cosine_lookup, -sine_lookup)
        grad_joined = jnp.concatenate(
            [
                grad_queries.reshape(sequence_length, HEADS_WIDTH),
                key_gradient.reshape(sequence_length, KEYS_WIDTH),
                value_gradient.reshape(sequence_length, KEYS_WIDTH),
            ],
            axis=1,
        ).astype(bf16)
        joined_left, joined_right = grad_joined[:, : QKV // 2], grad_joined[:, QKV // 2 :]
        grad_one = dot_nt(joined_left, qkv_left) + dot_nt(joined_right, qkv_right)
        grad_inputs, grad_gain_one = norm_backward(grad_one, tokens_own, factor_one, gain_one)
        grad_inputs = lax.dot_general(
            grad_inputs,
            order.astype(f32),
            (((1,), (1,)), ((), ())),
            precision=lax.Precision.HIGHEST,
            preferred_element_type=f32,
        )
        token_grad = grad_mid + grad_inputs

        small_sent = pad_lanes(jnp.concatenate([grad_router, grad_gain_two], axis=1))
        out_got, out_rest = scatter_weights(
            jnp.concatenate([dot_tn(attended, grad_att[:, : D // 2]), small_sent], axis=1).astype(bf16),
            dot_tn(attended, grad_att[:, D // 2 :]).astype(bf16),
        )
        gain_sent = pad_lanes(grad_gain_one[:, None])
        qkv_got, qkv_rest = scatter_weights(
            jnp.concatenate([dot_tn(hidden_one, joined_left), gain_sent], axis=1).astype(bf16),
            dot_tn(hidden_one, joined_right).astype(bf16),
        )
        sum_out = jnp.concatenate([out_got[:, : D // 2], out_rest], axis=1)
        sum_router = out_got[:, D // 2 : D // 2 + EXPERTS]
        sum_qkv = jnp.concatenate([qkv_got[:, : QKV // 2], qkv_rest], axis=1)
        sum_gains = jnp.stack([qkv_got[:, QKV // 2], out_got[:, D // 2 + EXPERTS]], axis=0)

        new_gate_up = adam_step(
            weight_gate_up, moment_gate_up, square_gate_up, home_gate_up, D ** (-0.5), weight_decay
        )
        new_down = adam_step(
            weight_down,
            moment_down,
            square_down,
            home_down,
            max(2, FF // 128) ** (-0.5),
            weight_decay,
        )
        new_qkv = adam_step(weight_qkv, moment_qkv, square_qkv, sum_qkv, D ** (-0.5), weight_decay)
        new_out = adam_step(
            weight_out,
            moment_out,
            square_out,
            sum_out,
            max(4, QUERY_HEADS * HEAD_SIZE // 256) ** (-0.5),
            weight_decay,
        )
        new_router = adam_step(
            weight_router, moment_router, square_router, sum_router, (4 * D) ** (-0.5), weight_decay
        )
        new_gains = adam_step(gains, moment_gains, square_gains, sum_gains, 0.75, 0.0)
        return (
            layer_out,
            token_grad,
            *new_qkv,
            *new_out,
            *new_router,
            *new_gains,
            *new_gate_up,
            *new_down,
        )

    return shards


def solution(mesh):
    n_dp, n_expert = mesh.shape["dp"], mesh.shape["expert"]
    nz = 4
    nx, ny = n_dp // nz, n_expert // 2
    fine = Mesh(mesh.devices.reshape(nz, nx, ny, 2), ALL)
    rows = P(ALL, None)
    columns = P(None, ALL)
    experts = P(("y", "core"), ("z", "x"), None)
    dense = (rows,) * 9 + (columns,) * 3 + (experts,) * 6
    return jax.shard_map(
        make_shards((nz, nx, ny)),
        mesh=fine,
        in_specs=(rows,) * 3 + dense,
        out_specs=(rows,) * 2 + dense,
        check_vma=False,
    )
```

```python
import jax
import jax.numpy as jnp
import numpy as np
from jax import lax
from jax.sharding import Mesh, PartitionSpec as P

D = 1536
QUERY_HEADS = 24
KEY_VALUE_HEADS = 8
HEAD_SIZE = 64
FF = 512
EXPERTS = 40
TOPK = 8
STEP = 10
QKV = 2560
LANES = 128
HEADS_WIDTH = QUERY_HEADS * HEAD_SIZE
KEYS_WIDTH = KEY_VALUE_HEADS * HEAD_SIZE

norm_eps = 1e-06
residual_scale = 0.22
score_scale = 0.125
beta_one = 0.9
beta_two = 0.95
adam_eps = 1e-08
weight_decay = 0.1

f32 = jnp.float32
bf16 = jnp.bfloat16
ALL = ("z", "x", "y", "core")
PLANE = ("z", "x")
SAME_CORE = ("z", "x", "y")


def rotary_tables(sequence_length, size):
    half = size // 2
    places = jnp.arange(sequence_length).astype(f32)[:, None]
    inverse = 10000.0 ** (-jnp.arange(half).astype(f32) * 2.0 / size)
    angles = places * inverse[None, :]
    return (jnp.cos(angles)[:, None, :], jnp.sin(angles)[:, None, :])


def apply_rotation(values, cosine_lookup, sine_lookup):
    half = values.shape[-1] // 2
    first = values[..., :half]
    second = values[..., half:]
    return jnp.concatenate(
        [
            first * cosine_lookup - second * sine_lookup,
            second * cosine_lookup + first * sine_lookup,
        ],
        axis=-1,
    )


def attention_scores(query_rotated, key_rot, causal):
    scores = (
        jnp.einsum("skgd,tkd->kgst", query_rotated, key_rot, preferred_element_type=f32)
        * score_scale
    )
    return jnp.where(causal, scores, -1e30)


def norm_backward(grad_normed, values, factor, gain):
    scaled = grad_normed * gain
    grad_gain = jnp.sum(grad_normed * values * factor, axis=0)
    value_gradient = factor * scaled - values * factor * factor * factor * jnp.mean(
        scaled * values, axis=-1, keepdims=True
    )
    return (value_gradient, grad_gain)


def adam_step(weight, moment, square, grad, rate, decay):
    moment = beta_one * moment + (1.0 - beta_one) * grad
    square = beta_two * square + (1.0 - beta_two) * grad * grad
    fixed_one = moment / (1.0 - beta_one**STEP)
    fixed_two = square / (1.0 - beta_two**STEP)
    weight = weight - rate * (fixed_one / (jnp.sqrt(fixed_two) + adam_eps) + decay * weight)
    return (weight, moment, square)


def dot(a, b):
    return jnp.dot(a, b, preferred_element_type=f32)


def dot_nt(a, b):
    return lax.dot_general(a, b, (((1,), (1,)), ((), ())), preferred_element_type=f32)


def dot_tn(a, b):
    return lax.dot_general(a, b, (((0,), (0,)), ((), ())), preferred_element_type=f32)


def pad_lanes(values):
    extra = -values.shape[-1] % LANES
    return jnp.pad(values, ((0, 0), (0, extra)))


def swap_core(values):
    return lax.ppermute(values, "core", [(0, 1), (1, 0)])


def ring_order(n):
    return [0] + list(range(1, n, 2)) + list(range(n - 2 + n % 2, 0, -2))


def home_table(n):
    order = ring_order(n)
    place = {chip: at for at, chip in enumerate(order)}
    return np.array([[order[(place[i] - s) % n] for s in range(n)] for i in range(n)], np.int32)


def make_shards(sizes):
    nz, nx, ny = sizes
    length = {"z": nz, "x": nx, "y": ny}
    planes = nz * nx
    per_group = EXPERTS // (2 * ny)
    whole = per_group // planes
    spare = per_group - whole * planes
    piece = FF // planes
    wide = whole * FF
    narrow = spare * piece

    rings = {axis: ring_order(n) for axis, n in length.items()}
    places = {axis: i for i, axis in enumerate(("z", "x", "y", "core"))}
    shape = (nz, nx, ny, 2)

    def pairs_of(axes, step):
        pairs = []
        for at in np.ndindex(*shape):
            axis = axes[at[3]]
            ring = rings[axis]
            to = list(at)
            to[places[axis]] = ring[(ring.index(at[places[axis]]) + step) % len(ring)]
            pairs.append(
                (int(np.ravel_multi_index(at, shape)), int(np.ravel_multi_index(to, shape)))
            )
        return pairs

    def move(values, axes, step):
        return lax.ppermute(values, ALL, pairs_of(axes, step))

    def homes(axis):
        n = length[axis]
        here = jnp.arange(n)[:, None] == lax.axis_index(axis)
        row = jnp.sum(jnp.where(here, jnp.asarray(home_table(n)), 0), axis=0)
        return [row[s] for s in range(n)]

    def add_low(a, b):
        return (a.astype(f32) + b.astype(f32)).astype(bf16)

    def pick(values, index, axis):
        return lax.dynamic_index_in_dim(values, index, axis, keepdims=False)

    def gather_rows(own):
        rows, columns = own.shape
        half = rows // 2
        line = [own]
        for _ in range(nz - 1):
            line.append(move(line[-1], "zz", 1))
        hx, hy, hz = homes("x"), homes("y"), homes("z")
        result = jnp.zeros((nz * nx * ny * rows, columns), own.dtype)
        for part, second, third in ((0, "x", "y"), (1, "y", "x")):
            pack = jnp.concatenate([b[part * half : (part + 1) * half] for b in line], axis=0)
            seconds = [pack]
            for _ in range(length[second] - 1):
                seconds.append(move(seconds[-1], second * 2, 1))
            pack = jnp.concatenate(seconds, axis=0)
            for s3 in range(length[third]):
                if s3:
                    pack = move(pack, third * 2, 1)
                for s2 in range(length[second]):
                    for sz in range(nz):
                        x, y = (hx[s2], hy[s3]) if second == "x" else (hx[s3], hy[s2])
                        at = ((hz[sz] * nx + x) * ny + y) * rows + part * half
                        first = (s2 * nz + sz) * half
                        result = lax.dynamic_update_slice(
                            result, pack[first : first + half], (at, 0)
                        )
        return result

    def scatter_rows(values):
        columns = values.shape[1]
        rows = values.shape[0] // (nz * nx * ny)
        half = rows // 2
        grid = values.reshape(nz, nx * ny * rows, columns)
        home = {"x": homes("x"), "y": homes("y"), "z": homes("z")}
        sets = [range(nz)[i : i + 2] for i in range(0, nz, 2)]
        total = None
        for group in reversed(sets):
            planes_of = [
                pick(grid, home["z"][s], 0).reshape(nx, ny, 2, half, columns) for s in group
            ]
            done = []
            for part, second, third in ((0, "x", "y"), (1, "y", "x")):
                axis3 = 1 if third == "y" else 0
                acc = None
                for s in reversed(range(length[third])):
                    mine = jnp.stack(
                        [pick(p[:, :, part], home[third][s], axis3) for p in planes_of]
                    )
                    acc = mine if acc is None else add_low(move(acc, third * 2, -1), mine)
                two = None
                for s in reversed(range(length[second])):
                    mine = pick(acc, home[second][s], 1)
                    two = mine if two is None else add_low(move(two, second * 2, -1), mine)
                done.append(two)
            both = jnp.concatenate(done, axis=1)
            for i in reversed(range(len(group))):
                total = both[i] if total is None else add_low(move(total, "zz", -1), both[i])
        return total.astype(f32)

    def gather_halves(own):
        rows, columns = own.shape
        half = columns // 2
        core = lax.axis_index("core")
        left, right = own[:, :half], own[:, half:]
        kept = jnp.where(core == 0, left, right)
        came = swap_core(jnp.where(core == 0, right, left))
        chip = jnp.where(
            core == 0, jnp.concatenate([kept, came], axis=0), jnp.concatenate([came, kept], axis=0)
        )
        line = [chip]
        for _ in range(nz - 1):
            line.append(move(line[-1], "zz", 1))
        seconds = [jnp.concatenate(line, axis=0)]
        for _ in range(nx - 1):
            seconds.append(move(seconds[-1], "xy", 1))
        pack = jnp.concatenate(seconds, axis=0)
        hx, hy, hz = homes("x"), homes("y"), homes("z")
        result = jnp.zeros((nz * nx * ny * 2 * rows, half), own.dtype)
        for s3 in range(nx):
            if s3:
                pack = move(pack, "yx", 1)
            for s2 in range(nx):
                x = jnp.where(core == 0, hx[s2], hx[s3])
                y = jnp.where(core == 0, hy[s3], hy[s2])
                for sz in range(nz):
                    at = ((hz[sz] * nx + x) * ny + y) * 2 * rows
                    first = (s2 * nz + sz) * 2 * rows
                    result = lax.dynamic_update_slice(
                        result, pack[first : first + 2 * rows], (at, 0)
                    )
        return result, swap_core(result)

    def scatter_halves(left, right):
        core = lax.axis_index("core")
        columns = left.shape[1]
        rows = left.shape[0] // (nz * nx * ny * 2)
        came = swap_core(jnp.where(core == 0, right, left))
        both = add_low(came, jnp.where(core == 0, left, right))
        grid = both.reshape(nz, nx, ny, 2 * rows, columns)
        hx, hy, hz = homes("x"), homes("y"), homes("z")
        acc = None
        for s in reversed(range(nx)):
            mine = jnp.where(core == 0, pick(grid, hy[s], 2), pick(grid, hx[s], 1))
            acc = mine if acc is None else add_low(move(acc, "yx", -1), mine)
        two = None
        for s in reversed(range(nx)):
            mine = pick(acc, jnp.where(core == 0, hx[s], hy[s]), 1)
            two = mine if two is None else add_low(move(two, "xy", -1), mine)
        total = None
        for s in reversed(range(nz)):
            mine = pick(two, hz[s], 0)
            total = mine if total is None else add_low(move(total, "zz", -1), mine)
        total = total.reshape(2, rows, columns)
        kept = pick(total, core, 0)
        came = swap_core(pick(total, 1 - core, 0))
        return (
            jnp.where(core == 0, kept, came).astype(f32),
            jnp.where(core == 0, came, kept).astype(f32),
        )

    def all_to_all_plane(values):
        return lax.all_to_all(values, PLANE, split_axis=0, concat_axis=0, tiled=True)

    def send_experts(gate_up, down):
        rows = gate_up.shape[1]
        sets = []
        if whole:
            full = gate_up[: whole * planes].reshape(planes, whole, rows, 2, FF)
            full = full.transpose(0, 2, 3, 1, 4).reshape(planes, rows, 2 * wide)
            low = down[: whole * planes].reshape(planes, whole, piece, D)
            low = all_to_all_plane(low).transpose(1, 0, 2, 3).reshape(wide, D)
            sets.append((all_to_all_plane(full).reshape(D, 2 * wide), low))
        if spare:
            part = gate_up[whole * planes :].reshape(spare, rows, 2, planes, piece)
            part = part.transpose(3, 1, 2, 0, 4).reshape(planes, rows, 2 * narrow)
            part = all_to_all_plane(part).reshape(D, 2 * narrow)
            sets.append((part, down[whole * planes :].reshape(narrow, D)))
        return sets

    def return_experts(sets):
        rows = D // planes
        gate_up, down = [], []
        at = 0
        if whole:
            full, low = sets[at]
            at += 1
            full = all_to_all_plane(full.astype(bf16).reshape(planes, rows, 2 * wide))
            full = full.reshape(planes, rows, 2, whole, FF).transpose(0, 3, 1, 2, 4)
            gate_up.append(full.reshape(whole * planes, rows, 2 * FF).astype(f32))
            low = low.astype(bf16).reshape(whole, planes, piece, D).transpose(1, 0, 2, 3)
            down.append(all_to_all_plane(low).reshape(whole * planes, piece, D).astype(f32))
        if spare:
            part, low = sets[at]
            part = all_to_all_plane(part.astype(bf16).reshape(planes, rows, 2 * narrow))
            part = part.reshape(planes, rows, 2, spare, piece).transpose(3, 1, 2, 0, 4)
            gate_up.append(part.reshape(spare, rows, 2 * FF).astype(f32))
            down.append(low.reshape(spare, piece, D))
        return jnp.concatenate(gate_up, axis=0), jnp.concatenate(down, axis=0)

    def unit_experts(group, place):
        base = group * per_group
        sets = []
        if whole:
            sets.append(base + place * whole + jnp.arange(wide) // FF)
        if spare:
            sets.append(base + whole * planes + jnp.arange(narrow) // piece)
        return sets

    def shards(
        tokens,
        cotangent,
        routes,
        weight_qkv,
        moment_qkv,
        square_qkv,
        weight_out,
        moment_out,
        square_out,
        weight_router,
        moment_router,
        square_router,
        gains,
        moment_gains,
        square_gains,
        weight_gate_up,
        moment_gate_up,
        square_gate_up,
        weight_down,
        moment_down,
        square_down,
    ):
        sequence_length = tokens.shape[0]
        head_groups = QUERY_HEADS // KEY_VALUE_HEADS
        place = lax.axis_index(PLANE)
        group = lax.axis_index("y") * 2 + lax.axis_index("core")
        partner = lax.axis_index("y") * 2 + 1 - lax.axis_index("core")

        own_sets = send_experts(weight_gate_up.astype(bf16), weight_down.astype(bf16))
        other_sets = [(swap_core(a), swap_core(b)) for a, b in own_sets]

        small = pad_lanes(jnp.concatenate([weight_router, gains.T], axis=1))
        first_pack = jnp.concatenate([weight_qkv, small], axis=1).astype(bf16)
        first_all = lax.all_gather(first_pack, ALL, axis=0, tiled=True)
        out_mine, out_other = gather_halves(weight_out.astype(bf16))
        first_all, out_mine, out_other = lax.optimization_barrier((first_all, out_mine, out_other))
        qkv_w = first_all[:, :QKV]
        router_w = first_all[:, QKV : QKV + EXPERTS]
        gain_one = first_all[:, QKV + EXPERTS].astype(f32)
        gain_two = first_all[:, QKV + EXPERTS + 1].astype(f32)
        cot_all = gather_rows(cotangent)

        inputs = tokens.astype(f32)
        factor_one = lax.rsqrt(jnp.mean(inputs * inputs, axis=-1, keepdims=True) + norm_eps)
        hidden_one = (inputs * factor_one * gain_one).astype(bf16)
        joined_heads = dot(hidden_one, qkv_w)
        query_rows = joined_heads[:, :HEADS_WIDTH].reshape(sequence_length, QUERY_HEADS, HEAD_SIZE)
        every_key = joined_heads[:, HEADS_WIDTH : HEADS_WIDTH + KEYS_WIDTH].reshape(
            sequence_length, KEY_VALUE_HEADS, HEAD_SIZE
        )
        every_value = joined_heads[:, HEADS_WIDTH + KEYS_WIDTH :].reshape(
            sequence_length, KEY_VALUE_HEADS, HEAD_SIZE
        )
        cosine_lookup, sine_lookup = rotary_tables(sequence_length, HEAD_SIZE)
        query_rotated = (
            apply_rotation(query_rows, cosine_lookup, sine_lookup)
            .astype(bf16)
            .reshape(sequence_length, KEY_VALUE_HEADS, head_groups, HEAD_SIZE)
        )
        key_rot = apply_rotation(every_key, cosine_lookup, sine_lookup).astype(bf16)
        value_low = every_value.astype(bf16)
        causal = jnp.arange(sequence_length)[:, None] >= jnp.arange(sequence_length)[None, :]
        scores = attention_scores(query_rotated, key_rot, causal)
        peak = jnp.max(scores, axis=-1, keepdims=True)
        expo = jnp.exp(scores - peak)
        totals = jnp.sum(expo, axis=-1, keepdims=True)
        probs = expo / totals
        prob_low = probs.astype(bf16)
        heads = jnp.einsum("kgst,tkd->skgd", prob_low, value_low, preferred_element_type=f32)
        attended = heads.reshape(sequence_length, HEADS_WIDTH).astype(bf16)
        core = lax.axis_index("core")
        projected = [dot(attended, out_mine), dot(attended, out_other)]
        mid = inputs + residual_scale * jnp.where(
            core == 0,
            jnp.concatenate(projected, axis=1),
            jnp.concatenate(projected[::-1], axis=1),
        )
        factor_two = lax.rsqrt(jnp.mean(mid * mid, axis=-1, keepdims=True) + norm_eps)
        hidden_two = (mid * factor_two * gain_two).astype(bf16)
        logits = dot(hidden_two, router_w)
        named = jnp.any(
            routes[..., None] == jnp.arange(EXPERTS, dtype=routes.dtype)[None, None, :], axis=1
        )
        shown = jnp.where(named, logits, -jnp.inf)
        raised = jnp.exp(shown - jnp.max(shown, axis=-1, keepdims=True))
        gates = raised / jnp.sum(raised, axis=-1, keepdims=True)

        gate_high = gates.astype(bf16)
        gate_rest = (gates - gate_high.astype(f32)).astype(bf16)
        sent = jnp.concatenate(
            [hidden_two, pad_lanes(jnp.concatenate([gate_high, gate_rest], axis=1))], axis=1
        )
        sent_all = lax.all_gather(sent, SAME_CORE, axis=0, tiled=True)
        rows_all = sent_all[:, :D]
        gates_all = sent_all[:, D:]

        numbers = jnp.arange(LANES)
        mixed_part = 0.0
        grad_two_part = 0.0
        dgate_part = 0.0
        grads = []
        for sets, whose in ((own_sets, group), (other_sets, partner)):
            set_grads = []
            for (gate_up_w, down_w), behind in zip(sets, unit_experts(whose, place)):
                width = down_w.shape[0]
                belongs = numbers[:, None] == behind[None, :]
                twice = belongs | (numbers[:, None] == behind[None, :] + EXPERTS)
                gate_wide = dot(gates_all, twice.astype(bf16))
                gate_up_act = dot(rows_all, gate_up_w)
                gate_part, up_part = gate_up_act[:, :width], gate_up_act[:, width:]
                squash = jax.nn.sigmoid(gate_part)
                swish = gate_part * squash
                hidden = swish * up_part
                gated = (hidden * gate_wide).astype(bf16)
                mixed_part = mixed_part + dot(gated, down_w)
                reach = residual_scale * dot_nt(cot_all, down_w)
                dgate_part = dgate_part + dot_nt((hidden * reach).astype(bf16), belongs.astype(bf16))
                grad_hidden = reach * gate_wide
                grad_gate = grad_hidden * up_part * squash * (1.0 + gate_part * (1.0 - squash))
                grad_up = grad_hidden * swish
                grad_both = jnp.concatenate([grad_gate, grad_up], axis=1).astype(bf16)
                grad_two_part = grad_two_part + dot_nt(grad_both, gate_up_w)
                set_grads.append(
                    (dot_tn(rows_all, grad_both), residual_scale * dot_tn(gated, cot_all))
                )
            grads.append(set_grads)

        grad_gates = lax.psum_scatter(
            dgate_part.astype(bf16), SAME_CORE, scatter_dimension=0, tiled=True
        )[:, :EXPERTS].astype(f32)
        grad_two = scatter_rows(grad_two_part.astype(bf16))
        mixed = lax.psum_scatter(
            mixed_part.astype(bf16), SAME_CORE, scatter_dimension=0, tiled=True
        ).astype(f32)
        layer_out = (mid + residual_scale * mixed).astype(bf16)

        sum_sets = []
        for (own_a, own_b), (other_a, other_b) in zip(*grads):
            sum_a = own_a + swap_core(other_a.astype(bf16)).astype(f32)
            sum_b = own_b + swap_core(other_b.astype(bf16)).astype(f32)
            sum_sets.append((sum_a, sum_b))
        home_gate_up, home_down = return_experts(sum_sets)

        grad_out = cotangent.astype(f32)
        grad_chosen = gates * (grad_gates - jnp.sum(gates * grad_gates, axis=-1, keepdims=True))
        grad_logits = grad_chosen.astype(bf16)
        grad_router = dot_tn(hidden_two, grad_logits)
        grad_two = grad_two + dot_nt(grad_logits, router_w)
        grad_mid, grad_gain_two = norm_backward(grad_two, mid, factor_two, gain_two)
        grad_mid = grad_out + grad_mid
        grad_att = (residual_scale * grad_mid).astype(bf16)
        att_left, att_right = grad_att[:, : D // 2], grad_att[:, D // 2 :]
        grad_heads = (
            (
                dot_nt(jnp.where(core == 0, att_left, att_right), out_mine)
                + dot_nt(jnp.where(core == 0, att_right, att_left), out_other)
            )
            .astype(bf16)
            .reshape(sequence_length, KEY_VALUE_HEADS, head_groups, HEAD_SIZE)
        )
        out_left, out_right = scatter_halves(
            dot_tn(attended, att_left).astype(bf16), dot_tn(attended, att_right).astype(bf16)
        )
        grad_probs = jnp.einsum(
            "skgd,tkd->kgst", grad_heads, value_low, preferred_element_type=f32
        )
        value_gradient = jnp.einsum(
            "kgst,skgd->tkd", prob_low, grad_heads, preferred_element_type=f32
        )
        row_dot = jnp.sum(probs * grad_probs, axis=-1, keepdims=True)
        grad_scores = (probs * (grad_probs - row_dot)).astype(bf16)
        grad_qrot = (
            jnp.einsum("kgst,tkd->skgd", grad_scores, key_rot, preferred_element_type=f32)
            * score_scale
        )
        grad_krot = (
            jnp.einsum("kgst,skgd->tkd", grad_scores, query_rotated, preferred_element_type=f32)
            * score_scale
        )
        grad_queries = apply_rotation(
            grad_qrot.reshape(sequence_length, QUERY_HEADS, HEAD_SIZE), cosine_lookup, -sine_lookup
        )
        key_gradient = apply_rotation(grad_krot, cosine_lookup, -sine_lookup)
        grad_joined = jnp.concatenate(
            [
                grad_queries.reshape(sequence_length, HEADS_WIDTH),
                key_gradient.reshape(sequence_length, KEYS_WIDTH),
                value_gradient.reshape(sequence_length, KEYS_WIDTH),
            ],
            axis=1,
        ).astype(bf16)
        grad_one = dot_nt(grad_joined, qkv_w)
        grad_inputs, grad_gain_one = norm_backward(grad_one, inputs, factor_one, gain_one)
        token_grad = grad_mid + grad_inputs
        small_sent = pad_lanes(
            jnp.concatenate([grad_router, grad_gain_one[:, None], grad_gain_two[:, None]], axis=1)
        )
        qkv_left, qkv_right = scatter_halves(
            jnp.concatenate(
                [dot_tn(hidden_one, grad_joined[:, : QKV // 2]), small_sent], axis=1
            ).astype(bf16),
            jnp.concatenate(
                [dot_tn(hidden_one, grad_joined[:, QKV // 2 :]), jnp.zeros_like(small_sent)], axis=1
            ).astype(bf16),
        )
        sum_out = jnp.concatenate([out_left, out_right], axis=1)
        sum_qkv = jnp.concatenate([qkv_left[:, : QKV // 2], qkv_right[:, : QKV // 2]], axis=1)
        sum_router = qkv_left[:, QKV // 2 : QKV // 2 + EXPERTS]
        sum_gains = qkv_left[:, QKV // 2 + EXPERTS : QKV // 2 + EXPERTS + 2].T

        new_gate_up = adam_step(
            weight_gate_up, moment_gate_up, square_gate_up, home_gate_up, D ** (-0.5), weight_decay
        )
        new_down = adam_step(
            weight_down,
            moment_down,
            square_down,
            home_down,
            max(2, FF // 128) ** (-0.5),
            weight_decay,
        )
        new_qkv = adam_step(weight_qkv, moment_qkv, square_qkv, sum_qkv, D ** (-0.5), weight_decay)
        new_out = adam_step(
            weight_out,
            moment_out,
            square_out,
            sum_out,
            max(4, QUERY_HEADS * HEAD_SIZE // 256) ** (-0.5),
            weight_decay,
        )
        new_router = adam_step(
            weight_router, moment_router, square_router, sum_router, (4 * D) ** (-0.5), weight_decay
        )
        new_gains = adam_step(gains, moment_gains, square_gains, sum_gains, 0.75, 0.0)
        return (
            layer_out,
            token_grad,
            *new_qkv,
            *new_out,
            *new_router,
            *new_gains,
            *new_gate_up,
            *new_down,
        )

    return shards


def solution(mesh):
    n_dp, n_expert = mesh.shape["dp"], mesh.shape["expert"]
    nz = 4
    nx, ny = n_dp // nz, n_expert // 2
    fine = Mesh(mesh.devices.reshape(nz, nx, ny, 2), ALL)
    rows = P(ALL, None)
    columns = P(None, ALL)
    experts = P(("y", "core"), ("z", "x"), None)
    dense = (rows,) * 9 + (columns,) * 3 + (experts,) * 6
    return jax.shard_map(
        make_shards((nz, nx, ny)),
        mesh=fine,
        in_specs=(rows,) * 3 + dense,
        out_specs=(rows,) * 2 + dense,
        check_vma=False,
    )
```

```python
import jax
import jax.numpy as jnp
import numpy as np
from jax import lax
from jax.experimental import pallas as pl
from jax.experimental.pallas import tpu as pltpu
from jax.sharding import Mesh, PartitionSpec as P

D = 1536
QUERY_HEADS = 24
KEY_VALUE_HEADS = 8
HEAD_SIZE = 64
FF = 512
EXPERTS = 40
TOPK = 8
STEP = 10
QKV = 2560
LANES = 128
HEADS_WIDTH = QUERY_HEADS * HEAD_SIZE
KEYS_WIDTH = KEY_VALUE_HEADS * HEAD_SIZE

norm_eps = 1e-06
residual_scale = 0.22
score_scale = 0.125
beta_one = 0.9
beta_two = 0.95
adam_eps = 1e-08
weight_decay = 0.1

f32 = jnp.float32
bf16 = jnp.bfloat16
ALL = ("z", "x", "y", "core")
PLANE = ("z", "x")
SAME_CORE = ("z", "x", "y")


def rotary_tables(sequence_length, size):
    half = size // 2
    places = jnp.arange(sequence_length).astype(f32)[:, None]
    inverse = 10000.0 ** (-jnp.arange(half).astype(f32) * 2.0 / size)
    angles = places * inverse[None, :]
    return (jnp.cos(angles)[:, None, :], jnp.sin(angles)[:, None, :])


def apply_rotation(values, cosine_lookup, sine_lookup):
    half = values.shape[-1] // 2
    first = values[..., :half]
    second = values[..., half:]
    return jnp.concatenate(
        [
            first * cosine_lookup - second * sine_lookup,
            second * cosine_lookup + first * sine_lookup,
        ],
        axis=-1,
    )


def attention_scores(query_rotated, key_rot, causal):
    scores = (
        jnp.einsum("skgd,tkd->kgst", query_rotated, key_rot, preferred_element_type=f32)
        * score_scale
    )
    return jnp.where(causal, scores, -1e30)


def norm_backward(grad_normed, values, factor, gain):
    scaled = grad_normed * gain
    grad_gain = jnp.sum(grad_normed * values * factor, axis=0)
    value_gradient = factor * scaled - values * factor * factor * factor * jnp.mean(
        scaled * values, axis=-1, keepdims=True
    )
    return (value_gradient, grad_gain)


def adam_step(weight, moment, square, grad, rate, decay):
    moment = beta_one * moment + (1.0 - beta_one) * grad
    square = beta_two * square + (1.0 - beta_two) * grad * grad
    fixed_one = moment / (1.0 - beta_one**STEP)
    fixed_two = square / (1.0 - beta_two**STEP)
    weight = weight - rate * (fixed_one / (jnp.sqrt(fixed_two) + adam_eps) + decay * weight)
    return (weight, moment, square)


def dot(a, b):
    return jnp.dot(a, b, preferred_element_type=f32)


def dot_nt(a, b):
    return lax.dot_general(a, b, (((1,), (1,)), ((), ())), preferred_element_type=f32)


def dot_tn(a, b):
    return lax.dot_general(a, b, (((0,), (0,)), ((), ())), preferred_element_type=f32)


def pad_lanes(values):
    extra = -values.shape[-1] % LANES
    return jnp.pad(values, ((0, 0), (0, extra)))


def swap_core(values):
    return lax.ppermute(values, "core", [(0, 1), (1, 0)])


def after(values, first):
    return lax.optimization_barrier((values, first))[0]


def ring_order(n):
    return [0] + list(range(1, n, 2)) + list(range(n - 2 + n % 2, 0, -2))


def home_table(n):
    order = ring_order(n)
    place = {chip: at for at, chip in enumerate(order)}
    return np.array([[order[(place[i] - s) % n] for s in range(n)] for i in range(n)], np.int32)


def make_shards(sizes):
    nz, nx, ny = sizes
    length = {"z": nz, "x": nx, "y": ny}
    planes = nz * nx
    per_group = EXPERTS // (2 * ny)
    whole = per_group // planes
    spare = per_group - whole * planes
    piece = FF // planes
    wide = whole * FF
    narrow = spare * piece
    narrow_pad = narrow + -narrow % LANES
    units = wide + narrow_pad

    rings = {axis: ring_order(n) for axis, n in length.items()}
    places = {axis: i for i, axis in enumerate(("z", "x", "y", "core"))}
    shape = (nz, nx, ny, 2)

    def pairs_of(axes, step):
        pairs = []
        for at in np.ndindex(*shape):
            axis = axes[at[3]]
            ring = rings[axis]
            to = list(at)
            to[places[axis]] = ring[(ring.index(at[places[axis]]) + step) % len(ring)]
            pairs.append(
                (int(np.ravel_multi_index(at, shape)), int(np.ravel_multi_index(to, shape)))
            )
        return pairs

    def move(values, axes, step):
        return lax.ppermute(values, ALL, pairs_of(axes, step))

    def homes(axis):
        n = length[axis]
        here = jnp.arange(n)[:, None] == lax.axis_index(axis)
        row = jnp.sum(jnp.where(here, jnp.asarray(home_table(n)), 0), axis=0)
        return [row[s] for s in range(n)]

    def add_low(a, b):
        return (a.astype(f32) + b.astype(f32)).astype(bf16)

    def pick(values, index, axis):
        return lax.dynamic_index_in_dim(values, index, axis, keepdims=False)

    def gather_rows(own):
        rows, columns = own.shape
        half = rows // 2
        line = [own]
        for _ in range(nz - 1):
            line.append(move(line[-1], "zz", 1))
        hx, hy, hz = homes("x"), homes("y"), homes("z")
        result = jnp.zeros((nz * nx * ny * 2, half, columns), own.dtype)
        for part, second, third in ((0, "x", "y"), (1, "y", "x")):
            pack = jnp.concatenate([b[part * half : (part + 1) * half] for b in line], axis=0)
            seconds = [pack]
            for _ in range(length[second] - 1):
                seconds.append(move(seconds[-1], second * 2, 1))
            pack = jnp.concatenate(seconds, axis=0)
            for s3 in range(length[third]):
                if s3:
                    pack = move(pack, third * 2, 1)
                for s2 in range(length[second]):
                    for sz in range(nz):
                        x, y = (hx[s2], hy[s3]) if second == "x" else (hx[s3], hy[s2])
                        at = ((hz[sz] * nx + x) * ny + y) * 2 + part
                        first = (s2 * nz + sz) * half
                        result = lax.dynamic_update_slice(
                            result, pack[None, first : first + half], (at, 0, 0)
                        )
        return result.reshape(nz * nx * ny * rows, columns)

    def scatter_rows(values):
        columns = values.shape[1]
        rows = values.shape[0] // (nz * nx * ny)
        half = rows // 2
        grid = values.reshape(nz, nx * ny * rows, columns)
        home = {"x": homes("x"), "y": homes("y"), "z": homes("z")}
        sets = [range(nz)[i : i + 2] for i in range(0, nz, 2)]
        total = None
        for group in reversed(sets):
            planes_of = [
                pick(grid, home["z"][s], 0).reshape(nx, ny, 2, half, columns) for s in group
            ]
            done = []
            for part, second, third in ((0, "x", "y"), (1, "y", "x")):
                axis3 = 1 if third == "y" else 0
                acc = None
                for s in reversed(range(length[third])):
                    mine = jnp.stack(
                        [pick(p[:, :, part], home[third][s], axis3) for p in planes_of]
                    )
                    acc = mine if acc is None else add_low(move(acc, third * 2, -1), mine)
                two = None
                for s in reversed(range(length[second])):
                    mine = pick(acc, home[second][s], 1)
                    two = mine if two is None else add_low(move(two, second * 2, -1), mine)
                done.append(two)
            both = jnp.concatenate(done, axis=1)
            for i in reversed(range(len(group))):
                total = both[i] if total is None else add_low(move(total, "zz", -1), both[i])
        return total.astype(f32)

    def gather_halves(own):
        rows, columns = own.shape
        half = columns // 2
        core = lax.axis_index("core")
        left, right = own[:, :half], own[:, half:]
        kept = jnp.where(core == 0, left, right)
        came = swap_core(jnp.where(core == 0, right, left))
        chip = jnp.where(
            core == 0, jnp.concatenate([kept, came], axis=0), jnp.concatenate([came, kept], axis=0)
        )
        line = [chip]
        for _ in range(nz - 1):
            line.append(move(line[-1], "zz", 1))
        seconds = [jnp.concatenate(line, axis=0)]
        for _ in range(nx - 1):
            seconds.append(move(seconds[-1], "xy", 1))
        pack = jnp.concatenate(seconds, axis=0)
        hx, hy, hz = homes("x"), homes("y"), homes("z")
        result = jnp.zeros((nz * nx * ny, 2 * rows, half), own.dtype)
        for s3 in range(nx):
            if s3:
                pack = move(pack, "yx", 1)
            for s2 in range(nx):
                x = jnp.where(core == 0, hx[s2], hx[s3])
                y = jnp.where(core == 0, hy[s3], hy[s2])
                for sz in range(nz):
                    at = (hz[sz] * nx + x) * ny + y
                    first = (s2 * nz + sz) * 2 * rows
                    result = lax.dynamic_update_slice(
                        result, pack[None, first : first + 2 * rows], (at, 0, 0)
                    )
        result = result.reshape(nz * nx * ny * 2 * rows, half)
        return result, swap_core(result)

    def scatter_halves(left, right):
        core = lax.axis_index("core")
        columns = left.shape[1]
        rows = left.shape[0] // (nz * nx * ny * 2)
        came = swap_core(jnp.where(core == 0, right, left))
        both = add_low(came, jnp.where(core == 0, left, right))
        grid = both.reshape(nz, nx, ny, 2 * rows, columns)
        hx, hy, hz = homes("x"), homes("y"), homes("z")
        acc = None
        for s in reversed(range(nx)):
            mine = jnp.where(core == 0, pick(grid, hy[s], 2), pick(grid, hx[s], 1))
            acc = mine if acc is None else add_low(move(acc, "yx", -1), mine)
        two = None
        for s in reversed(range(nx)):
            mine = pick(acc, jnp.where(core == 0, hx[s], hy[s]), 1)
            two = mine if two is None else add_low(move(two, "xy", -1), mine)
        total = None
        for s in reversed(range(nz)):
            mine = pick(two, hz[s], 0)
            total = mine if total is None else add_low(move(total, "zz", -1), mine)
        total = total.reshape(2, rows, columns)
        kept = pick(total, core, 0)
        came = swap_core(pick(total, 1 - core, 0))
        return (
            jnp.where(core == 0, kept, came).astype(f32),
            jnp.where(core == 0, came, kept).astype(f32),
        )

    def all_to_all_plane(values):
        return lax.all_to_all(values, PLANE, split_axis=0, concat_axis=0, tiled=True)

    def pack_down(low):
        across = D // wide
        low = low.reshape(planes, piece, across, wide).transpose(0, 2, 1, 3)
        return low.reshape(planes, D // planes, wide)

    def unpack_down(low):
        across = D // wide
        low = low.reshape(planes, across, piece, wide).transpose(0, 2, 1, 3)
        return low.reshape(planes, piece, D)

    def send_experts(gate_up, down):
        rows = D // planes
        parts = []
        if whole:
            parts.append(gate_up[:planes])
        part = gate_up[whole * planes :].reshape(spare, rows, 2, planes, piece)
        part = part.transpose(3, 1, 2, 0, 4).reshape(planes, rows, 2, narrow)
        part = jnp.pad(part, ((0, 0), (0, 0), (0, 0), (0, narrow_pad - narrow)))
        parts.append(part.reshape(planes, rows, 2 * narrow_pad))
        if whole:
            parts.append(pack_down(down[:planes]))
        packed = all_to_all_plane(jnp.concatenate(parts, axis=2)).reshape(D, -1)
        return packed, jnp.pad(
            down[whole * planes :].reshape(narrow, D), ((0, narrow_pad - narrow), (0, 0))
        )

    def down_of(packed, spare_down):
        if not whole:
            return spare_down
        low = packed[:, 2 * units :].reshape(planes, D // planes, wide)
        return jnp.concatenate([unpack_down(low).reshape(wide, D), spare_down], axis=0)

    def pack_grads(grad_gate_up, grad_down):
        if not whole:
            return grad_gate_up, grad_down
        low = pack_down(grad_down[:wide].reshape(planes, piece, D)).reshape(D, wide)
        return jnp.concatenate([grad_gate_up, low], axis=1), grad_down[wide:]

    def return_experts(packed, spare_down):
        rows = D // planes
        home = all_to_all_plane(packed.reshape(planes, rows, -1))
        gate_up, down = [], []
        if whole:
            gate_up.append(home[:, :, : 2 * wide])
            down.append(unpack_down(home[:, :, 2 * units :]).astype(f32))
        part = home[:, :, 2 * wide : 2 * units].reshape(planes, rows, 2, narrow_pad)
        part = part[..., :narrow].reshape(planes, rows, 2, spare, piece).transpose(3, 1, 2, 0, 4)
        gate_up.append(part.reshape(spare, rows, 2 * FF))
        down.append(spare_down[:narrow].reshape(spare, piece, D))
        return jnp.concatenate(gate_up, axis=0).astype(f32), jnp.concatenate(down, axis=0)

    def unit_experts(group, place):
        base = group * per_group
        sets = []
        if whole:
            sets.append(jnp.full((wide,), base + place))
        behind = base + whole * planes + jnp.arange(narrow_pad) // piece
        sets.append(jnp.where(jnp.arange(narrow_pad) < narrow, behind, -1))
        return jnp.concatenate(sets)

    def columns_of():
        pieces = []
        for first in range(0, wide, 256):
            pieces.append((first, wide + first, first, min(256, wide - first)))
        pieces.append((2 * wide, 2 * wide + narrow_pad, wide, narrow_pad))
        return pieces

    def expert_kernel(
        rows_ref, gates_ref, reach_ref, own_ref, other_ref, twice_ref, once_ref,
        gated_ref, grad_ref, dgate_ref, two_ref,
    ):
        rows = rows_ref[...]
        gates = gates_ref[...]
        dgate = jnp.zeros(dgate_ref.shape, f32)
        for k, weights in enumerate((own_ref, other_ref)):
            for gate_at, up_at, unit_at, width in columns_of():
                unit = pl.ds(k * units + unit_at, width)
                gate_part = jnp.dot(
                    rows, weights[:, pl.ds(gate_at, width)], preferred_element_type=f32
                )
                up_part = jnp.dot(
                    rows, weights[:, pl.ds(up_at, width)], preferred_element_type=f32
                )
                gate_wide = jnp.dot(gates, twice_ref[:, unit], preferred_element_type=f32)
                reach = reach_ref[:, unit]
                squash = 1.0 / (1.0 + jnp.exp(-gate_part))
                swish = gate_part * squash
                hidden = swish * up_part
                gated_ref[:, unit] = (hidden * gate_wide).astype(bf16)
                dgate += dot_nt((hidden * reach).astype(bf16), once_ref[:, unit])
                grad_hidden = reach * gate_wide
                grad_gate = grad_hidden * up_part * squash * (1.0 + gate_part * (1.0 - squash))
                grad_ref[:, pl.ds(k * 2 * units + gate_at, width)] = grad_gate.astype(bf16)
                grad_ref[:, pl.ds(k * 2 * units + up_at, width)] = (grad_hidden * swish).astype(
                    bf16
                )
        dgate_ref[...] = dgate.astype(bf16)
        two_ref[...] = (
            dot_nt(grad_ref[:, : 2 * units], own_ref[...])
            + dot_nt(grad_ref[:, 2 * units :], other_ref[...])
        ).astype(bf16)

    def run_experts(rows_all, gates_all, reach, own, other, twice, once):
        count = rows_all.shape[0]
        tile = 512

        def by_rows(columns):
            return pl.BlockSpec((tile, columns), lambda i: (i, 0))

        def fixed(rows, columns):
            return pl.BlockSpec((rows, columns), lambda i: (0, 0), pipeline_mode=pl.Buffered(1))

        return pl.pallas_call(
            expert_kernel,
            grid=(count // tile,),
            in_specs=[
                by_rows(D),
                by_rows(LANES),
                by_rows(2 * units),
                fixed(D, 2 * units),
                fixed(D, 2 * units),
                fixed(LANES, 2 * units),
                fixed(LANES, 2 * units),
            ],
            out_specs=[by_rows(2 * units), by_rows(4 * units), by_rows(LANES), by_rows(D)],
            out_shape=[
                jax.ShapeDtypeStruct((count, 2 * units), bf16),
                jax.ShapeDtypeStruct((count, 4 * units), bf16),
                jax.ShapeDtypeStruct((count, LANES), bf16),
                jax.ShapeDtypeStruct((count, D), bf16),
            ],
            compiler_params=pltpu.CompilerParams(vmem_limit_bytes=60 * 2**20),
        )(rows_all, gates_all, reach, own, other, twice, once)

    def shards(
        tokens,
        cotangent,
        routes,
        weight_qkv,
        moment_qkv,
        square_qkv,
        weight_out,
        moment_out,
        square_out,
        weight_router,
        moment_router,
        square_router,
        gains,
        moment_gains,
        square_gains,
        weight_gate_up,
        moment_gate_up,
        square_gate_up,
        weight_down,
        moment_down,
        square_down,
    ):
        sequence_length = tokens.shape[0]
        head_groups = QUERY_HEADS // KEY_VALUE_HEADS
        place = lax.axis_index(PLANE)
        group = lax.axis_index("y") * 2 + lax.axis_index("core")
        partner = lax.axis_index("y") * 2 + 1 - lax.axis_index("core")

        small = pad_lanes(jnp.concatenate([weight_router, gains.T], axis=1))
        first_pack = jnp.concatenate([weight_qkv, small], axis=1).astype(bf16)
        first_all = lax.all_gather(first_pack, ALL, axis=0, tiled=True)

        own, own_spare = send_experts(weight_gate_up.astype(bf16), weight_down.astype(bf16))

        out_mine, out_other = gather_halves(weight_out.astype(bf16))
        qkv_w = first_all[:, :QKV]
        router_w = first_all[:, QKV : QKV + EXPERTS]
        gain_one = first_all[:, QKV + EXPERTS].astype(f32)
        gain_two = first_all[:, QKV + EXPERTS + 1].astype(f32)

        inputs = tokens.astype(f32)
        factor_one = lax.rsqrt(jnp.mean(inputs * inputs, axis=-1, keepdims=True) + norm_eps)
        hidden_one = (inputs * factor_one * gain_one).astype(bf16)
        joined_heads = dot(hidden_one, qkv_w)
        query_rows = joined_heads[:, :HEADS_WIDTH].reshape(sequence_length, QUERY_HEADS, HEAD_SIZE)
        every_key = joined_heads[:, HEADS_WIDTH : HEADS_WIDTH + KEYS_WIDTH].reshape(
            sequence_length, KEY_VALUE_HEADS, HEAD_SIZE
        )
        every_value = joined_heads[:, HEADS_WIDTH + KEYS_WIDTH :].reshape(
            sequence_length, KEY_VALUE_HEADS, HEAD_SIZE
        )
        cosine_lookup, sine_lookup = rotary_tables(sequence_length, HEAD_SIZE)
        query_rotated = (
            apply_rotation(query_rows, cosine_lookup, sine_lookup)
            .astype(bf16)
            .reshape(sequence_length, KEY_VALUE_HEADS, head_groups, HEAD_SIZE)
        )
        key_rot = apply_rotation(every_key, cosine_lookup, sine_lookup).astype(bf16)
        value_low = every_value.astype(bf16)
        causal = jnp.arange(sequence_length)[:, None] >= jnp.arange(sequence_length)[None, :]
        scores = attention_scores(query_rotated, key_rot, causal)
        peak = jnp.max(scores, axis=-1, keepdims=True)
        expo = jnp.exp(scores - peak)
        totals = jnp.sum(expo, axis=-1, keepdims=True)
        probs = expo / totals
        prob_low = probs.astype(bf16)
        heads = jnp.einsum("kgst,tkd->skgd", prob_low, value_low, preferred_element_type=f32)
        attended = heads.reshape(sequence_length, HEADS_WIDTH).astype(bf16)
        core = lax.axis_index("core")
        projected = [dot(attended, out_mine), dot(attended, out_other)]
        mid = inputs + residual_scale * jnp.where(
            core == 0,
            jnp.concatenate(projected, axis=1),
            jnp.concatenate(projected[::-1], axis=1),
        )
        factor_two = lax.rsqrt(jnp.mean(mid * mid, axis=-1, keepdims=True) + norm_eps)
        hidden_two = (mid * factor_two * gain_two).astype(bf16)
        logits = dot(hidden_two, router_w)
        named = jnp.any(
            routes[..., None] == jnp.arange(EXPERTS, dtype=routes.dtype)[None, None, :], axis=1
        )
        shown = jnp.where(named, logits, -jnp.inf)
        raised = jnp.exp(shown - jnp.max(shown, axis=-1, keepdims=True))
        gates = raised / jnp.sum(raised, axis=-1, keepdims=True)

        gate_high = gates.astype(bf16)
        gate_rest = (gates - gate_high.astype(f32)).astype(bf16)
        sent = jnp.concatenate(
            [hidden_two, pad_lanes(jnp.concatenate([gate_high, gate_rest], axis=1))], axis=1
        )
        sent_all = lax.all_gather(sent, SAME_CORE, axis=0, tiled=True)
        cot_all = gather_rows(after(cotangent, sent))
        own = after(own, sent)
        other, other_spare = swap_core(own), swap_core(own_spare)
        down_own, down_other = down_of(own, own_spare), down_of(other, other_spare)
        rows_all = sent_all[:, :D]
        gates_all = sent_all[:, D:]

        behind = jnp.concatenate([unit_experts(group, place), unit_experts(partner, place)])
        numbers = jnp.arange(LANES)[:, None]
        real = behind[None, :] >= 0
        once = (numbers == behind[None, :]) & real
        twice = once | ((numbers == behind[None, :] + EXPERTS) & real)
        reach = residual_scale * jnp.concatenate(
            [dot_nt(cot_all, down_own), dot_nt(cot_all, down_other)], axis=1
        )
        gated, grad_both, dgate_part, grad_two_part = run_experts(
            rows_all, gates_all, reach, own, other, twice.astype(bf16), once.astype(bf16)
        )
        mixed_part = dot(gated[:, :units], down_own) + dot(gated[:, units:], down_other)

        grad_gates = lax.psum_scatter(
            dgate_part, SAME_CORE, scatter_dimension=0, tiled=True
        )[:, :EXPERTS].astype(f32)
        grad_two = scatter_rows(grad_two_part)
        mixed = lax.psum_scatter(
            mixed_part.astype(bf16), SAME_CORE, scatter_dimension=0, tiled=True
        ).astype(f32)
        layer_out = (mid + residual_scale * mixed).astype(bf16)

        other_packed, other_rest = pack_grads(
            dot_tn(rows_all, grad_both[:, 2 * units :]).astype(bf16),
            (residual_scale * dot_tn(gated[:, units:], cot_all)).astype(bf16),
        )
        came_packed, came_rest = swap_core(other_packed), swap_core(other_rest)
        own_packed, own_rest = pack_grads(
            dot_tn(rows_all, grad_both[:, : 2 * units]),
            residual_scale * dot_tn(gated[:, :units], cot_all),
        )
        home_gate_up, home_down = return_experts(
            (own_packed + came_packed.astype(f32)).astype(bf16), own_rest + came_rest.astype(f32)
        )

        grad_out = cotangent.astype(f32)
        grad_chosen = gates * (grad_gates - jnp.sum(gates * grad_gates, axis=-1, keepdims=True))
        grad_logits = grad_chosen.astype(bf16)
        grad_router = dot_tn(hidden_two, grad_logits)
        grad_two = grad_two + dot_nt(grad_logits, router_w)
        grad_mid, grad_gain_two = norm_backward(grad_two, mid, factor_two, gain_two)
        grad_mid = grad_out + grad_mid
        grad_att = (residual_scale * grad_mid).astype(bf16)
        att_left, att_right = grad_att[:, : D // 2], grad_att[:, D // 2 :]
        grad_heads = (
            (
                dot_nt(jnp.where(core == 0, att_left, att_right), out_mine)
                + dot_nt(jnp.where(core == 0, att_right, att_left), out_other)
            )
            .astype(bf16)
            .reshape(sequence_length, KEY_VALUE_HEADS, head_groups, HEAD_SIZE)
        )
        out_left, out_right = scatter_halves(
            dot_tn(attended, att_left).astype(bf16), dot_tn(attended, att_right).astype(bf16)
        )
        grad_probs = jnp.einsum(
            "skgd,tkd->kgst", grad_heads, value_low, preferred_element_type=f32
        )
        value_gradient = jnp.einsum(
            "kgst,skgd->tkd", prob_low, grad_heads, preferred_element_type=f32
        )
        row_dot = jnp.sum(probs * grad_probs, axis=-1, keepdims=True)
        grad_scores = (probs * (grad_probs - row_dot)).astype(bf16)
        grad_qrot = (
            jnp.einsum("kgst,tkd->skgd", grad_scores, key_rot, preferred_element_type=f32)
            * score_scale
        )
        grad_krot = (
            jnp.einsum("kgst,skgd->tkd", grad_scores, query_rotated, preferred_element_type=f32)
            * score_scale
        )
        grad_queries = apply_rotation(
            grad_qrot.reshape(sequence_length, QUERY_HEADS, HEAD_SIZE), cosine_lookup, -sine_lookup
        )
        key_gradient = apply_rotation(grad_krot, cosine_lookup, -sine_lookup)
        grad_joined = jnp.concatenate(
            [
                grad_queries.reshape(sequence_length, HEADS_WIDTH),
                key_gradient.reshape(sequence_length, KEYS_WIDTH),
                value_gradient.reshape(sequence_length, KEYS_WIDTH),
            ],
            axis=1,
        ).astype(bf16)
        grad_one = dot_nt(grad_joined, qkv_w)
        grad_inputs, grad_gain_one = norm_backward(grad_one, inputs, factor_one, gain_one)
        token_grad = grad_mid + grad_inputs
        small_sent = pad_lanes(
            jnp.concatenate([grad_router, grad_gain_one[:, None], grad_gain_two[:, None]], axis=1)
        )
        qkv_left, qkv_right = scatter_halves(
            jnp.concatenate(
                [dot_tn(hidden_one, grad_joined[:, : QKV // 2]), small_sent], axis=1
            ).astype(bf16),
            jnp.concatenate(
                [dot_tn(hidden_one, grad_joined[:, QKV // 2 :]), jnp.zeros_like(small_sent)], axis=1
            ).astype(bf16),
        )
        sum_out = jnp.concatenate([out_left, out_right], axis=1)
        sum_qkv = jnp.concatenate([qkv_left[:, : QKV // 2], qkv_right[:, : QKV // 2]], axis=1)
        sum_router = qkv_left[:, QKV // 2 : QKV // 2 + EXPERTS]
        sum_gains = qkv_left[:, QKV // 2 + EXPERTS : QKV // 2 + EXPERTS + 2].T

        new_gate_up = adam_step(
            weight_gate_up, moment_gate_up, square_gate_up, home_gate_up, D ** (-0.5), weight_decay
        )
        new_down = adam_step(
            weight_down,
            moment_down,
            square_down,
            home_down,
            max(2, FF // 128) ** (-0.5),
            weight_decay,
        )
        new_qkv = adam_step(weight_qkv, moment_qkv, square_qkv, sum_qkv, D ** (-0.5), weight_decay)
        new_out = adam_step(
            weight_out,
            moment_out,
            square_out,
            sum_out,
            max(4, QUERY_HEADS * HEAD_SIZE // 256) ** (-0.5),
            weight_decay,
        )
        new_router = adam_step(
            weight_router, moment_router, square_router, sum_router, (4 * D) ** (-0.5), weight_decay
        )
        new_gains = adam_step(gains, moment_gains, square_gains, sum_gains, 0.75, 0.0)
        return (
            layer_out,
            token_grad,
            *new_qkv,
            *new_out,
            *new_router,
            *new_gains,
            *new_gate_up,
            *new_down,
        )

    return shards


def solution(mesh):
    n_dp, n_expert = mesh.shape["dp"], mesh.shape["expert"]
    nz = 4
    nx, ny = n_dp // nz, n_expert // 2
    fine = Mesh(mesh.devices.reshape(nz, nx, ny, 2), ALL)
    rows = P(ALL, None)
    columns = P(None, ALL)
    experts = P(("y", "core"), ("z", "x"), None)
    dense = (rows,) * 9 + (columns,) * 3 + (experts,) * 6
    return jax.shard_map(
        make_shards((nz, nx, ny)),
        mesh=fine,
        in_specs=(rows,) * 3 + dense,
        out_specs=(rows,) * 2 + dense,
        check_vma=False,
    )
```

```python
import functools

import jax
import jax.numpy as jnp
import numpy as np
from jax import lax
from jax.experimental import pallas as pl
from jax.experimental.pallas import tpu as pltpu
from jax.sharding import Mesh, PartitionSpec as P

D = 1536
QUERY_HEADS = 24
KEY_VALUE_HEADS = 8
HEAD_SIZE = 64
FF = 512
EXPERTS = 40
TOPK = 8
STEP = 10
QKV = 2560
LANES = 128
HEADS_WIDTH = QUERY_HEADS * HEAD_SIZE
KEYS_WIDTH = KEY_VALUE_HEADS * HEAD_SIZE

norm_eps = 1e-06
residual_scale = 0.22
score_scale = 0.125
beta_one = 0.9
beta_two = 0.95
adam_eps = 1e-08
weight_decay = 0.1

f32 = jnp.float32
bf16 = jnp.bfloat16
ALL = ("z", "x", "y", "core")
PLANE = ("z", "x")


def rotary_tables(sequence_length, size):
    half = size // 2
    places = jnp.arange(sequence_length).astype(f32)[:, None]
    inverse = 10000.0 ** (-jnp.arange(half).astype(f32) * 2.0 / size)
    angles = places * inverse[None, :]
    return (jnp.cos(angles)[:, None, :], jnp.sin(angles)[:, None, :])


def apply_rotation(values, cosine_lookup, sine_lookup):
    half = values.shape[-1] // 2
    first = values[..., :half]
    second = values[..., half:]
    return jnp.concatenate(
        [
            first * cosine_lookup - second * sine_lookup,
            second * cosine_lookup + first * sine_lookup,
        ],
        axis=-1,
    )


def attention_scores(query_rotated, key_rot, causal):
    scores = (
        jnp.einsum("skgd,tkd->kgst", query_rotated, key_rot, preferred_element_type=f32)
        * score_scale
    )
    return jnp.where(causal, scores, -1e30)


def norm_backward(grad_normed, values, factor, gain):
    scaled = grad_normed * gain
    grad_gain = jnp.sum(grad_normed * values * factor, axis=0)
    value_gradient = factor * scaled - values * factor * factor * factor * jnp.mean(
        scaled * values, axis=-1, keepdims=True
    )
    return (value_gradient, grad_gain)


def adam_step(weight, moment, square, grad, rate, decay):
    moment = beta_one * moment + (1.0 - beta_one) * grad
    square = beta_two * square + (1.0 - beta_two) * grad * grad
    fixed_one = moment / (1.0 - beta_one**STEP)
    fixed_two = square / (1.0 - beta_two**STEP)
    weight = weight - rate * (fixed_one / (jnp.sqrt(fixed_two) + adam_eps) + decay * weight)
    return (weight, moment, square)


def dot(a, b):
    return jnp.dot(a, b, preferred_element_type=f32)


def dot_nt(a, b):
    return lax.dot_general(a, b, (((1,), (1,)), ((), ())), preferred_element_type=f32)


def dot_tn(a, b):
    return lax.dot_general(a, b, (((0,), (0,)), ((), ())), preferred_element_type=f32)


def pad_lanes(values):
    extra = -values.shape[-1] % LANES
    return jnp.pad(values, ((0, 0), (0, extra)))


def swap_core(values):
    return lax.ppermute(values, "core", [(0, 1), (1, 0)])


def keep_kernel(*refs):
    pass


def after(values, *first):
    anywhere = pl.BlockSpec(memory_space=pl.ANY)
    return pl.pallas_call(
        keep_kernel,
        in_specs=[anywhere] * (1 + len(first)),
        out_specs=anywhere,
        out_shape=jax.ShapeDtypeStruct(values.shape, values.dtype),
        input_output_aliases={0: 0},
    )(values, *first)


def ring_order(n):
    return [0] + list(range(1, n, 2)) + list(range(n - 2 + n % 2, 0, -2))


def home_table(n):
    order = ring_order(n)
    place = {chip: at for at, chip in enumerate(order)}
    return np.array([[order[(place[i] - s) % n] for s in range(n)] for i in range(n)], np.int32)


def make_shards(sizes):
    nz, nx, ny = sizes
    length = {"z": nz, "x": nx, "y": ny}
    planes = nz * nx
    per_group = EXPERTS // (2 * ny)
    whole = per_group // planes
    spare = per_group - whole * planes
    piece = FF // planes
    wide = whole * FF
    narrow = spare * piece
    narrow_pad = narrow + -narrow % LANES
    units = wide + narrow_pad

    rings = {axis: ring_order(n) for axis, n in length.items()}
    places = {axis: i for i, axis in enumerate(("z", "x", "y", "core"))}
    shape = (nz, nx, ny, 2)

    def pairs_of(axes, step):
        pairs = []
        for at in np.ndindex(*shape):
            axis = axes[at[3]]
            ring = rings[axis]
            to = list(at)
            to[places[axis]] = ring[(ring.index(at[places[axis]]) + step) % len(ring)]
            pairs.append(
                (int(np.ravel_multi_index(at, shape)), int(np.ravel_multi_index(to, shape)))
            )
        return pairs

    def move(values, axes, step):
        return lax.ppermute(values, ALL, pairs_of(axes, step))

    def homes(axis):
        n = length[axis]
        here = jnp.arange(n)[:, None] == lax.axis_index(axis)
        row = jnp.sum(jnp.where(here, jnp.asarray(home_table(n)), 0), axis=0)
        return [row[s] for s in range(n)]

    def add_low(a, b):
        return (a.astype(f32) + b.astype(f32)).astype(bf16)

    def pick(values, index, axis):
        return lax.dynamic_index_in_dim(values, index, axis, keepdims=False)

    sets = [tuple(range(nz))[i : i + nz // 2] for i in range(0, nz, nz // 2)]
    parts = ((0, "x", "y"), (1, "y", "x"))

    def line_of(own):
        line = [own]
        for _ in range(nz - 1):
            line.append(move(line[-1], "zz", 1))
        return line

    def gather_set(line, chosen):
        half = line[0].shape[0] // 2
        packs = [
            jnp.concatenate([line[s][part * half : (part + 1) * half] for s in chosen], axis=0)
            for part, _, _ in parts
        ]
        for level in (1, 2):
            grown = []
            for pack, names in zip(packs, parts):
                axis = names[level]
                steps = [pack]
                for _ in range(length[axis] - 1):
                    steps.append(move(steps[-1], axis * 2, 1))
                grown.append(jnp.concatenate(steps, axis=0))
            packs = grown
        return jnp.concatenate(packs, axis=0)

    def scatter_set(values):
        count = values.shape[0] // 2
        packs = [values[:count], values[count:]]
        for level in (2, 1):
            summed = []
            for pack, names in zip(packs, parts):
                n = length[names[level]]
                rows = pack.shape[0] // n
                acc = None
                for s in reversed(range(n)):
                    mine = pack[s * rows : (s + 1) * rows]
                    acc = mine if acc is None else add_low(move(acc, names[level] * 2, -1), mine)
                summed.append(acc)
            packs = summed
        half = packs[0].shape[0] // (nz // 2)
        return [
            jnp.concatenate([p[s * half : (s + 1) * half] for p in packs], axis=0)
            for s in range(nz // 2)
        ]

    def sum_line(blocks):
        total = blocks[-1]
        for mine in reversed(blocks[:-1]):
            total = add_low(move(total, "zz", -1), mine)
        return total.astype(f32)

    def chip_half(own):
        half = own.shape[1] // 2
        core = lax.axis_index("core")
        left, right = own[:, :half], own[:, half:]
        kept = jnp.where(core == 0, left, right)
        came = swap_core(jnp.where(core == 0, right, left))
        return jnp.where(
            core == 0, jnp.concatenate([kept, came], axis=0), jnp.concatenate([came, kept], axis=0)
        )

    def gather_halves(line):
        rows, half = line[0].shape
        core = lax.axis_index("core")
        seconds = [jnp.concatenate(line, axis=0)]
        for _ in range(nx - 1):
            seconds.append(move(seconds[-1], "xy", 1))
        pack = jnp.concatenate(seconds, axis=0)
        hx, hy, hz = homes("x"), homes("y"), homes("z")
        result = jnp.zeros((nz * nx * ny, rows, half), pack.dtype)
        for s3 in range(nx):
            if s3:
                pack = move(pack, "yx", 1)
            for s2 in range(nx):
                x = jnp.where(core == 0, hx[s2], hx[s3])
                y = jnp.where(core == 0, hy[s3], hy[s2])
                for sz in range(nz):
                    at = (hz[sz] * nx + x) * ny + y
                    first = (s2 * nz + sz) * rows
                    result = lax.dynamic_update_slice(
                        result, pack[None, first : first + rows], (at, 0, 0)
                    )
        result = result.reshape(nz * nx * ny * rows, half)
        return result, swap_core(result)

    def scatter_halves(left, right):
        core = lax.axis_index("core")
        columns = left.shape[1]
        rows = left.shape[0] // (nz * nx * ny * 2)
        came = swap_core(jnp.where(core == 0, right, left))
        both = add_low(came, jnp.where(core == 0, left, right))
        grid = both.reshape(nz, nx, ny, 2 * rows, columns)
        hx, hy, hz = homes("x"), homes("y"), homes("z")
        acc = None
        for s in reversed(range(nx)):
            mine = jnp.where(core == 0, pick(grid, hy[s], 2), pick(grid, hx[s], 1))
            acc = mine if acc is None else add_low(move(acc, "yx", -1), mine)
        two = None
        for s in reversed(range(nx)):
            mine = pick(acc, jnp.where(core == 0, hx[s], hy[s]), 1)
            two = mine if two is None else add_low(move(two, "xy", -1), mine)
        total = None
        for s in reversed(range(nz)):
            mine = pick(two, hz[s], 0)
            total = mine if total is None else add_low(move(total, "zz", -1), mine)
        total = total.reshape(2, rows, columns)
        kept = pick(total, core, 0)
        came = swap_core(pick(total, 1 - core, 0))
        return (
            jnp.where(core == 0, kept, came).astype(f32),
            jnp.where(core == 0, came, kept).astype(f32),
        )

    def all_to_all_plane(values):
        return lax.all_to_all(values, PLANE, split_axis=0, concat_axis=0, tiled=True)

    rows_home = D // planes
    across = rows_home // piece
    rest = 2 * narrow_pad + wide

    def cut_spare(part):
        part = part.reshape(spare, rows_home, 2, planes, piece)
        part = part.transpose(3, 1, 2, 0, 4).reshape(planes, rows_home, 2, narrow)
        part = jnp.pad(part, ((0, 0), (0, 0), (0, 0), (0, narrow_pad - narrow)))
        return part.reshape(planes, rows_home, 2 * narrow_pad)

    def join_spare(part):
        part = part.reshape(planes, rows_home, 2, narrow_pad)[..., :narrow]
        part = part.reshape(planes, rows_home, 2, spare, piece).transpose(3, 1, 2, 0, 4)
        return part.reshape(spare, rows_home, 2 * FF)

    def lanes(values, first, width=piece):
        return values[:, first : first + width]

    def pack_kernel(gate_up_ref, spare_ref, down_ref, spare_down_ref, full_ref, rest_ref, low_ref):
        step = pl.program_id(0)
        full_ref[0] = gate_up_ref[0].astype(bf16)
        for j in range(across):
            rest_ref[step, pl.ds(j * piece, piece), pl.ds(2 * narrow_pad, wide)] = down_ref[
                0, :, pl.ds(j * wide, wide)
            ].astype(bf16)

        @pl.when(step == 0)
        def _():
            for to in range(planes):
                taken = [
                    lanes(spare_ref[s], g * FF + to * piece) for g in range(2) for s in range(spare)
                ]
                rest_ref[to, :, pl.ds(0, 2 * narrow)] = jnp.concatenate(taken, axis=1).astype(bf16)
            for s in range(spare):
                low_ref[pl.ds(s * piece, piece), :] = spare_down_ref[s].astype(bf16)

    def pack_experts(gate_up, down):
        if not whole:
            low = down.astype(bf16).reshape(narrow, D)
            low = jnp.pad(low, ((0, narrow_pad - narrow), (0, 0)))
            return None, cut_spare(gate_up.astype(bf16)), low
        return pl.pallas_call(
            pack_kernel,
            grid=(planes,),
            in_specs=[
                pl.BlockSpec((1, rows_home, 2 * FF), lambda i: (i, 0, 0)),
                pl.BlockSpec((spare, rows_home, 2 * FF), lambda i: (planes // spare, 0, 0)),
                pl.BlockSpec((1, piece, D), lambda i: (i, 0, 0)),
                pl.BlockSpec((spare, piece, D), lambda i: (planes // spare, 0, 0)),
            ],
            out_specs=[
                pl.BlockSpec((1, rows_home, 2 * FF), lambda i: (i, 0, 0)),
                pl.BlockSpec((planes, rows_home, rest), lambda i: (0, 0, 0)),
                pl.BlockSpec((narrow, D), lambda i: (0, 0)),
            ],
            out_shape=[
                jax.ShapeDtypeStruct((planes, rows_home, 2 * FF), bf16),
                jax.ShapeDtypeStruct((planes, rows_home, rest), bf16),
                jax.ShapeDtypeStruct((narrow, D), bf16),
            ],
            compiler_params=pltpu.CompilerParams(vmem_limit_bytes=48 * 2**20),
        )(gate_up, gate_up, down, down)

    def down_of(packed, low):
        if not whole:
            return low
        mine = packed[:, 2 * narrow_pad :].reshape(planes, across, piece, wide)
        mine = mine.transpose(0, 2, 1, 3).reshape(wide, D)
        return jnp.concatenate([mine, low], axis=0)

    def combine_kernel(a_ref, came_a_ref, b_ref, came_b_ref, c_ref, came_c_ref, full_ref, rest_ref, low_ref):
        total = a_ref[...].astype(f32) + came_a_ref[...].astype(f32)
        full_ref[0] = total[:, : 2 * wide].astype(bf16)
        rest_ref[0, :, pl.ds(0, 2 * narrow_pad)] = total[:, 2 * wide :].astype(bf16)
        total = residual_scale * (b_ref[...].astype(f32) + came_b_ref[...].astype(f32))
        for j in range(across):
            rest_ref[0, pl.ds(j * piece, piece), pl.ds(2 * narrow_pad, wide)] = total[
                :, j * wide : (j + 1) * wide
            ].astype(bf16)
        low_ref[...] = residual_scale * (c_ref[...].astype(f32) + came_c_ref[...].astype(f32))

    def combine_grads(gate_up, came_gate_up, down, came_down):
        if not whole:
            total = (gate_up.astype(f32) + came_gate_up.astype(f32)).astype(bf16)
            low = residual_scale * (down.astype(f32) + came_down.astype(f32))
            return None, total.reshape(planes, rows_home, rest), low
        return pl.pallas_call(
            combine_kernel,
            grid=(planes,),
            in_specs=[pl.BlockSpec((rows_home, 2 * units), lambda i: (i, 0))] * 2
            + [pl.BlockSpec((piece, D), lambda i: (i, 0))] * 2
            + [pl.BlockSpec((narrow, D), lambda i: (wide // narrow, 0))] * 2,
            out_specs=[
                pl.BlockSpec((1, rows_home, 2 * FF), lambda i: (i, 0, 0)),
                pl.BlockSpec((1, rows_home, rest), lambda i: (i, 0, 0)),
                pl.BlockSpec((narrow, D), lambda i: (0, 0)),
            ],
            out_shape=[
                jax.ShapeDtypeStruct((planes, rows_home, 2 * FF), bf16),
                jax.ShapeDtypeStruct((planes, rows_home, rest), bf16),
                jax.ShapeDtypeStruct((narrow, D), f32),
            ],
            compiler_params=pltpu.CompilerParams(vmem_limit_bytes=48 * 2**20),
        )(gate_up, came_gate_up, down, came_down, down, came_down)

    gate_up_rate = D ** (-0.5)
    down_rate = max(2, FF // 128) ** (-0.5)

    def full_kernel(home_ref, w_ref, m_ref, s_ref, *outs):
        done = adam_step(
            w_ref[0], m_ref[0], s_ref[0], home_ref[0].astype(f32), gate_up_rate, weight_decay
        )
        for ref, value in zip(outs, done):
            ref[0] = value

    def spare_kernel(home_ref, w_ref, m_ref, s_ref, a_ref, b_ref, c_ref, *outs):
        for s in range(spare):

            @pl.when(pl.program_id(0) == s)
            def _():
                grad = jnp.concatenate(
                    [
                        lanes(home_ref[p], g * narrow_pad + s * piece)
                        for g in range(2)
                        for p in range(planes)
                    ],
                    axis=1,
                ).astype(f32)
                done = adam_step(w_ref[0], m_ref[0], s_ref[0], grad, gate_up_rate, weight_decay)
                for ref, value in zip(outs, done):
                    ref[0] = value

    def down_kernel(home_ref, low_ref, w_ref, m_ref, s_ref, *outs):
        def update(grad):
            done = adam_step(w_ref[0], m_ref[0], s_ref[0], grad, down_rate, weight_decay)
            for ref, value in zip(outs, done):
                ref[0] = value

        @pl.when(pl.program_id(0) < planes)
        def _():
            update(
                jnp.concatenate(
                    [
                        home_ref[0, pl.ds(j * piece, piece), pl.ds(2 * narrow_pad, wide)]
                        for j in range(across)
                    ],
                    axis=1,
                ).astype(f32)
            )

        @pl.when(pl.program_id(0) >= planes)
        def _():
            update(low_ref[...])

    def update_experts(home_full, home_rest, low, gate_up, down):
        if not whole:
            grad = join_spare(home_rest).astype(f32)
            return (
                adam_step(*gate_up, grad, gate_up_rate, weight_decay),
                adam_step(
                    *down, low[:narrow].reshape(spare, piece, D), down_rate, weight_decay
                ),
            )
        params = pltpu.CompilerParams(vmem_limit_bytes=48 * 2**20)
        shapes = [jax.ShapeDtypeStruct(gate_up[0].shape, f32)] * 3
        one = pl.BlockSpec((1, rows_home, 2 * FF), lambda i: (i, 0, 0))
        last = pl.BlockSpec((1, rows_home, 2 * FF), lambda i: (planes + i, 0, 0))
        new_gate_up = pl.pallas_call(
            full_kernel,
            grid=(planes,),
            in_specs=[one] * 4,
            out_specs=[one] * 3,
            out_shape=shapes,
            compiler_params=params,
        )(home_full, *gate_up)
        new_gate_up = pl.pallas_call(
            spare_kernel,
            grid=(spare,),
            in_specs=[pl.BlockSpec((planes, rows_home, 2 * narrow_pad), lambda i: (0, 0, 0))]
            + [last] * 3
            + [pl.BlockSpec(memory_space=pl.ANY)] * 3,
            out_specs=[last] * 3,
            out_shape=shapes,
            input_output_aliases={4: 0, 5: 1, 6: 2},
            compiler_params=params,
        )(home_rest, *gate_up, *new_gate_up)
        row = pl.BlockSpec((1, piece, D), lambda i: (i, 0, 0))
        new_down = pl.pallas_call(
            down_kernel,
            grid=(per_group,),
            in_specs=[
                pl.BlockSpec((1, rows_home, rest), lambda i: (jnp.minimum(i, planes - 1), 0, 0)),
                pl.BlockSpec((piece, D), lambda i: (jnp.maximum(i - planes, 0), 0)),
            ]
            + [row] * 3,
            out_specs=[row] * 3,
            out_shape=[jax.ShapeDtypeStruct(down[0].shape, f32)] * 3,
            compiler_params=params,
        )(home_rest, low, *down)
        return new_gate_up, new_down

    def unit_experts(group, place):
        base = group * per_group
        sets = []
        if whole:
            sets.append(jnp.full((wide,), base + place))
        behind = base + whole * planes + jnp.arange(narrow_pad) // piece
        sets.append(jnp.where(jnp.arange(narrow_pad) < narrow, behind, -1))
        return jnp.concatenate(sets)

    def columns_of():
        pieces = []
        for first in range(0, wide, 256):
            pieces.append((True, first, wide + first, first, min(256, wide - first)))
        pieces.append((False, 0, narrow_pad, wide, narrow_pad))
        return pieces

    def expert_kernel(first_call, *refs):
        count = 2 if whole else 1
        rows_ref, gates_ref, reach_ref = refs[:3]
        weights = (refs[3 : 3 + count], refs[3 + count : 3 + 2 * count])
        twice_ref, once_ref = refs[3 + 2 * count : 5 + 2 * count]
        gated_ref, grad_ref, two_ref = refs[5 + 2 * count + (0 if first_call else 2) :]
        rows = rows_ref[...]
        gates = gates_ref[...]
        dgate = jnp.zeros((rows.shape[0], LANES), f32)
        two = jnp.zeros((rows.shape[0], D), f32)
        for k in range(2):
            for in_full, gate_at, up_at, unit_at, width in columns_of():
                held = weights[k][0 if in_full else -1]
                unit = pl.ds(k * units + unit_at, width)
                at = 2 * (k * units + unit_at)
                gate_w = held[:, pl.ds(gate_at, width)]
                up_w = held[:, pl.ds(up_at, width)]
                gate_part = jnp.dot(rows, gate_w, preferred_element_type=f32)
                up_part = jnp.dot(rows, up_w, preferred_element_type=f32)
                gate_wide = jnp.dot(gates, twice_ref[:, unit], preferred_element_type=f32)
                reach = reach_ref[:, unit]
                squash = 1.0 / (1.0 + jnp.exp(-gate_part))
                swish = gate_part * squash
                hidden = swish * up_part
                gated_ref[:, unit] = (hidden * gate_wide).astype(bf16)
                dgate += dot_nt((hidden * reach).astype(bf16), once_ref[:, unit])
                grad_hidden = reach * gate_wide
                grad_gate = grad_hidden * up_part * squash * (1.0 + gate_part * (1.0 - squash))
                base = k * 2 * units + (0 if in_full else 2 * wide)
                grad_ref[:, pl.ds(base + gate_at, width)] = grad_gate.astype(bf16)
                grad_ref[:, pl.ds(base + up_at, width)] = (grad_hidden * swish).astype(bf16)
        for k in range(2):
            at = k * 2 * units
            if whole:
                two += dot_nt(grad_ref[:, pl.ds(at, 2 * wide)], weights[k][0][...])
            two += dot_nt(
                grad_ref[:, pl.ds(at + 2 * wide, 2 * narrow_pad)],
                weights[k][-1][:, pl.ds(0, 2 * narrow_pad)],
            )
        two_ref[:, pl.ds(0, D)] = two.astype(bf16)
        two_ref[:, pl.ds(D, LANES)] = dgate.astype(bf16)

    def run_experts(at, sent, reach, own, other, twice, once, before):
        count = sent.shape[0]
        total = reach.shape[0]
        tile = min(512, count)
        first = at * (count // tile)

        def by_rows(columns, offset=0, column=0):
            return pl.BlockSpec((tile, columns), lambda i: (i + offset, column))

        def fixed(rows, columns):
            return pl.BlockSpec((rows, columns), lambda i: (0, 0), pipeline_mode=pl.Buffered(1))

        held = []
        for full, more in (own, other):
            if whole:
                held.append((full, fixed(D, 2 * wide)))
            held.append((more, fixed(D, 2 * narrow_pad)))
        kept = list(before) if before else []
        return pl.pallas_call(
            functools.partial(expert_kernel, not kept),
            grid=(count // tile,),
            in_specs=[by_rows(D), by_rows(LANES, 0, D // LANES), by_rows(2 * units, first)]
            + [spec for _, spec in held]
            + [fixed(LANES, 2 * units)] * 2
            + [pl.BlockSpec(memory_space=pl.ANY)] * len(kept),
            out_specs=[
                by_rows(2 * units, first),
                by_rows(4 * units, first),
                by_rows(D + LANES),
            ],
            out_shape=[
                jax.ShapeDtypeStruct((total, 2 * units), bf16),
                jax.ShapeDtypeStruct((total, 4 * units), bf16),
                jax.ShapeDtypeStruct((count, D + LANES), bf16),
            ],
            input_output_aliases={5 + len(held) + i: i for i in range(len(kept))},
            compiler_params=pltpu.CompilerParams(vmem_limit_bytes=60 * 2**20),
        )(sent, sent, reach, *[w for w, _ in held], twice, once, *kept)

    def shards(
        tokens,
        cotangent,
        routes,
        weight_qkv,
        moment_qkv,
        square_qkv,
        weight_out,
        moment_out,
        square_out,
        weight_router,
        moment_router,
        square_router,
        gains,
        moment_gains,
        square_gains,
        weight_gate_up,
        moment_gate_up,
        square_gate_up,
        weight_down,
        moment_down,
        square_down,
    ):
        sequence_length = tokens.shape[0]
        head_groups = QUERY_HEADS // KEY_VALUE_HEADS
        place = lax.axis_index(PLANE)
        group = lax.axis_index("y") * 2 + lax.axis_index("core")
        partner = lax.axis_index("y") * 2 + 1 - lax.axis_index("core")

        small = pad_lanes(jnp.concatenate([weight_router, gains.T], axis=1))
        first_pack = jnp.concatenate([weight_qkv, small], axis=1).astype(bf16)
        first_all = lax.all_gather(first_pack, ALL, axis=0, tiled=True)

        full, more, low_own = pack_experts(weight_gate_up, weight_down)
        out_line = line_of(chip_half(weight_out.astype(bf16)))
        cot_line = line_of(cotangent)
        more = after(more, out_line[-1], cot_line[-1])
        more_own = all_to_all_plane(more).reshape(D, -1)
        out_mine, out_other = gather_halves(out_line)
        cot_all = jnp.concatenate([gather_set(cot_line, s) for s in sets], axis=0)

        qkv_w = first_all[:, :QKV]
        router_w = first_all[:, QKV : QKV + EXPERTS]
        gain_one = first_all[:, QKV + EXPERTS].astype(f32)
        gain_two = first_all[:, QKV + EXPERTS + 1].astype(f32)

        inputs = tokens.astype(f32)
        factor_one = lax.rsqrt(jnp.mean(inputs * inputs, axis=-1, keepdims=True) + norm_eps)
        hidden_one = (inputs * factor_one * gain_one).astype(bf16)
        joined_heads = dot(hidden_one, qkv_w)
        query_rows = joined_heads[:, :HEADS_WIDTH].reshape(sequence_length, QUERY_HEADS, HEAD_SIZE)
        every_key = joined_heads[:, HEADS_WIDTH : HEADS_WIDTH + KEYS_WIDTH].reshape(
            sequence_length, KEY_VALUE_HEADS, HEAD_SIZE
        )
        every_value = joined_heads[:, HEADS_WIDTH + KEYS_WIDTH :].reshape(
            sequence_length, KEY_VALUE_HEADS, HEAD_SIZE
        )
        cosine_lookup, sine_lookup = rotary_tables(sequence_length, HEAD_SIZE)
        query_rotated = (
            apply_rotation(query_rows, cosine_lookup, sine_lookup)
            .astype(bf16)
            .reshape(sequence_length, KEY_VALUE_HEADS, head_groups, HEAD_SIZE)
        )
        key_rot = apply_rotation(every_key, cosine_lookup, sine_lookup).astype(bf16)
        value_low = every_value.astype(bf16)
        causal = jnp.arange(sequence_length)[:, None] >= jnp.arange(sequence_length)[None, :]
        scores = attention_scores(query_rotated, key_rot, causal)
        peak = jnp.max(scores, axis=-1, keepdims=True)
        expo = jnp.exp(scores - peak)
        totals = jnp.sum(expo, axis=-1, keepdims=True)
        probs = expo / totals
        prob_low = probs.astype(bf16)
        heads = jnp.einsum("kgst,tkd->skgd", prob_low, value_low, preferred_element_type=f32)
        attended = heads.reshape(sequence_length, HEADS_WIDTH).astype(bf16)
        core = lax.axis_index("core")
        projected = [dot(attended, out_mine), dot(attended, out_other)]
        mid = inputs + residual_scale * jnp.where(
            core == 0,
            jnp.concatenate(projected, axis=1),
            jnp.concatenate(projected[::-1], axis=1),
        )
        factor_two = lax.rsqrt(jnp.mean(mid * mid, axis=-1, keepdims=True) + norm_eps)
        hidden_two = (mid * factor_two * gain_two).astype(bf16)
        logits = dot(hidden_two, router_w)
        named = jnp.any(
            routes[..., None] == jnp.arange(EXPERTS, dtype=routes.dtype)[None, None, :], axis=1
        )
        shown = jnp.where(named, logits, -jnp.inf)
        raised = jnp.exp(shown - jnp.max(shown, axis=-1, keepdims=True))
        gates = raised / jnp.sum(raised, axis=-1, keepdims=True)

        gate_high = gates.astype(bf16)
        gate_rest = (gates - gate_high.astype(f32)).astype(bf16)
        sent = jnp.concatenate(
            [hidden_two, pad_lanes(jnp.concatenate([gate_high, gate_rest], axis=1))], axis=1
        )
        sent_line = line_of(sent)
        more_own = after(more_own, sent)
        own = [None, more_own]
        if whole:
            own[0] = all_to_all_plane(after(full, sent_line[-1])).reshape(D, -1)
        more_other, low_other = swap_core(more_own), swap_core(low_own)
        down_own, down_other = down_of(more_own, low_own), down_of(more_other, low_other)
        reach = residual_scale * jnp.concatenate(
            [dot_nt(cot_all, down_own), dot_nt(cot_all, down_other)], axis=1
        )
        sent_sets = [gather_set(sent_line, s) for s in sets]
        other = [None, more_other]
        if whole:
            own[0] = after(own[0], sent_sets[-1])
            other[0] = swap_core(own[0])
        rows_all = jnp.concatenate([s[:, :D] for s in sent_sets], axis=0)

        behind = jnp.concatenate([unit_experts(group, place), unit_experts(partner, place)])
        numbers = jnp.arange(LANES)[:, None]
        real = behind[None, :] >= 0
        once = ((numbers == behind[None, :]) & real).astype(bf16)
        twice = once + ((numbers == behind[None, :] + EXPERTS) & real).astype(bf16)
        kept = None
        two_blocks = []
        for at, sent_set in enumerate(sent_sets):
            *kept, two = run_experts(at, sent_set, reach, own, other, twice, once, kept)
            two_blocks += scatter_set(two)
        gated, grad_both = kept
        two_sum = sum_line(two_blocks)
        grad_two, grad_gates = two_sum[:, :D], two_sum[:, D : D + EXPERTS]
        mixed = (dot(gated[:, :units], down_own) + dot(gated[:, units:], down_other)).astype(bf16)
        mixed = after(mixed, two_blocks[0])
        half = mixed.shape[0] // 2
        mixed = sum_line(scatter_set(mixed[:half]) + scatter_set(mixed[half:]))
        layer_out = (mid + residual_scale * mixed).astype(bf16)

        came_gate_up = swap_core(dot_tn(rows_all, grad_both[:, 2 * units :]).astype(bf16))
        came_down = swap_core(dot_tn(gated[:, units:], cot_all).astype(bf16))
        full, more, low = combine_grads(
            dot_tn(rows_all, grad_both[:, : 2 * units]).astype(bf16),
            came_gate_up,
            dot_tn(gated[:, :units], cot_all).astype(bf16),
            came_down,
        )
        home_full = all_to_all_plane(after(full, two_sum)) if whole else None
        home_rest = all_to_all_plane(after(more, two_sum))

        grad_out = cotangent.astype(f32)
        grad_chosen = gates * (grad_gates - jnp.sum(gates * grad_gates, axis=-1, keepdims=True))
        grad_logits = grad_chosen.astype(bf16)
        grad_router = dot_tn(hidden_two, grad_logits)
        grad_two = grad_two + dot_nt(grad_logits, router_w)
        grad_mid, grad_gain_two = norm_backward(grad_two, mid, factor_two, gain_two)
        grad_mid = grad_out + grad_mid
        grad_att = (residual_scale * grad_mid).astype(bf16)
        att_left, att_right = grad_att[:, : D // 2], grad_att[:, D // 2 :]
        grad_heads = (
            (
                dot_nt(jnp.where(core == 0, att_left, att_right), out_mine)
                + dot_nt(jnp.where(core == 0, att_right, att_left), out_other)
            )
            .astype(bf16)
            .reshape(sequence_length, KEY_VALUE_HEADS, head_groups, HEAD_SIZE)
        )
        out_left, out_right = scatter_halves(
            dot_tn(attended, att_left).astype(bf16), dot_tn(attended, att_right).astype(bf16)
        )
        grad_probs = jnp.einsum(
            "skgd,tkd->kgst", grad_heads, value_low, preferred_element_type=f32
        )
        value_gradient = jnp.einsum(
            "kgst,skgd->tkd", prob_low, grad_heads, preferred_element_type=f32
        )
        row_dot = jnp.sum(probs * grad_probs, axis=-1, keepdims=True)
        grad_scores = (probs * (grad_probs - row_dot)).astype(bf16)
        grad_qrot = (
            jnp.einsum("kgst,tkd->skgd", grad_scores, key_rot, preferred_element_type=f32)
            * score_scale
        )
        grad_krot = (
            jnp.einsum("kgst,skgd->tkd", grad_scores, query_rotated, preferred_element_type=f32)
            * score_scale
        )
        grad_queries = apply_rotation(
            grad_qrot.reshape(sequence_length, QUERY_HEADS, HEAD_SIZE), cosine_lookup, -sine_lookup
        )
        key_gradient = apply_rotation(grad_krot, cosine_lookup, -sine_lookup)
        grad_joined = jnp.concatenate(
            [
                grad_queries.reshape(sequence_length, HEADS_WIDTH),
                key_gradient.reshape(sequence_length, KEYS_WIDTH),
                value_gradient.reshape(sequence_length, KEYS_WIDTH),
            ],
            axis=1,
        ).astype(bf16)
        grad_one = dot_nt(grad_joined, qkv_w)
        grad_inputs, grad_gain_one = norm_backward(grad_one, inputs, factor_one, gain_one)
        token_grad = grad_mid + grad_inputs
        small_sent = pad_lanes(
            jnp.concatenate([grad_router, grad_gain_one[:, None], grad_gain_two[:, None]], axis=1)
        )
        qkv_left, qkv_right = scatter_halves(
            jnp.concatenate(
                [dot_tn(hidden_one, grad_joined[:, : QKV // 2]), small_sent], axis=1
            ).astype(bf16),
            jnp.concatenate(
                [dot_tn(hidden_one, grad_joined[:, QKV // 2 :]), jnp.zeros_like(small_sent)], axis=1
            ).astype(bf16),
        )
        sum_out = jnp.concatenate([out_left, out_right], axis=1)
        sum_qkv = jnp.concatenate([qkv_left[:, : QKV // 2], qkv_right[:, : QKV // 2]], axis=1)
        sum_router = qkv_left[:, QKV // 2 : QKV // 2 + EXPERTS]
        sum_gains = qkv_left[:, QKV // 2 + EXPERTS : QKV // 2 + EXPERTS + 2].T

        new_gate_up, new_down = update_experts(
            home_full,
            home_rest,
            low,
            (weight_gate_up, moment_gate_up, square_gate_up),
            (weight_down, moment_down, square_down),
        )
        new_qkv = adam_step(weight_qkv, moment_qkv, square_qkv, sum_qkv, D ** (-0.5), weight_decay)
        new_out = adam_step(
            weight_out,
            moment_out,
            square_out,
            sum_out,
            max(4, QUERY_HEADS * HEAD_SIZE // 256) ** (-0.5),
            weight_decay,
        )
        new_router = adam_step(
            weight_router, moment_router, square_router, sum_router, (4 * D) ** (-0.5), weight_decay
        )
        new_gains = adam_step(gains, moment_gains, square_gains, sum_gains, 0.75, 0.0)
        return (
            layer_out,
            token_grad,
            *new_qkv,
            *new_out,
            *new_router,
            *new_gains,
            *new_gate_up,
            *new_down,
        )

    return shards


def solution(mesh):
    n_dp, n_expert = mesh.shape["dp"], mesh.shape["expert"]
    nz = 4
    nx, ny = n_dp // nz, n_expert // 2
    fine = Mesh(mesh.devices.reshape(nz, nx, ny, 2), ALL)
    rows = P(ALL, None)
    columns = P(None, ALL)
    experts = P(("y", "core"), ("z", "x"), None)
    dense = (rows,) * 9 + (columns,) * 3 + (experts,) * 6
    return jax.shard_map(
        make_shards((nz, nx, ny)),
        mesh=fine,
        in_specs=(rows,) * 3 + dense,
        out_specs=(rows,) * 2 + dense,
        check_vma=False,
    )
```

```python
import functools

import jax
import jax.numpy as jnp
import numpy as np
from jax import lax
from jax.experimental import pallas as pl
from jax.experimental.pallas import tpu as pltpu
from jax.sharding import Mesh, PartitionSpec as P

D = 1536
QUERY_HEADS = 24
KEY_VALUE_HEADS = 8
HEAD_SIZE = 64
FF = 512
EXPERTS = 40
TOPK = 8
STEP = 10
QKV = 2560
LANES = 128
HEADS_WIDTH = QUERY_HEADS * HEAD_SIZE
KEYS_WIDTH = KEY_VALUE_HEADS * HEAD_SIZE

norm_eps = 1e-06
residual_scale = 0.22
score_scale = 0.125
beta_one = 0.9
beta_two = 0.95
adam_eps = 1e-08
weight_decay = 0.1

f32 = jnp.float32
bf16 = jnp.bfloat16
ALL = ("z", "x", "y", "core")
PLANE = ("z", "x")


def rotary_tables(sequence_length, size):
    half = size // 2
    places = jnp.arange(sequence_length).astype(f32)[:, None]
    inverse = 10000.0 ** (-jnp.arange(half).astype(f32) * 2.0 / size)
    angles = places * inverse[None, :]
    return (jnp.cos(angles)[:, None, :], jnp.sin(angles)[:, None, :])


def apply_rotation(values, cosine_lookup, sine_lookup):
    half = values.shape[-1] // 2
    first = values[..., :half]
    second = values[..., half:]
    return jnp.concatenate(
        [
            first * cosine_lookup - second * sine_lookup,
            second * cosine_lookup + first * sine_lookup,
        ],
        axis=-1,
    )


def attention_scores(query_rotated, key_rot, causal):
    scores = (
        jnp.einsum("skgd,tkd->kgst", query_rotated, key_rot, preferred_element_type=f32)
        * score_scale
    )
    return jnp.where(causal, scores, -1e30)


def norm_backward(grad_normed, values, factor, gain):
    scaled = grad_normed * gain
    grad_gain = jnp.sum(grad_normed * values * factor, axis=0)
    value_gradient = factor * scaled - values * factor * factor * factor * jnp.mean(
        scaled * values, axis=-1, keepdims=True
    )
    return (value_gradient, grad_gain)


def adam_step(weight, moment, square, grad, rate, decay):
    moment = beta_one * moment + (1.0 - beta_one) * grad
    square = beta_two * square + (1.0 - beta_two) * grad * grad
    fixed_one = moment / (1.0 - beta_one**STEP)
    fixed_two = square / (1.0 - beta_two**STEP)
    weight = weight - rate * (fixed_one / (jnp.sqrt(fixed_two) + adam_eps) + decay * weight)
    return (weight, moment, square)


def dot(a, b):
    return jnp.dot(a, b, preferred_element_type=f32)


def dot_nt(a, b):
    return lax.dot_general(a, b, (((1,), (1,)), ((), ())), preferred_element_type=f32)


def dot_tn(a, b):
    return lax.dot_general(a, b, (((0,), (0,)), ((), ())), preferred_element_type=f32)


def pad_lanes(values):
    extra = -values.shape[-1] % LANES
    return jnp.pad(values, ((0, 0), (0, extra)))


def swap_core(values):
    return lax.ppermute(values, "core", [(0, 1), (1, 0)])


def keep_kernel(*refs):
    pass


def ring_order(n):
    return [0] + list(range(1, n, 2)) + list(range(n - 2 + n % 2, 0, -2))


def home_table(n):
    order = ring_order(n)
    place = {chip: at for at, chip in enumerate(order)}
    return np.array([[order[(place[i] - s) % n] for s in range(n)] for i in range(n)], np.int32)


def make_shards(sizes):
    nz, nx, ny = sizes
    length = {"z": nz, "x": nx, "y": ny}
    planes = nz * nx
    per_group = EXPERTS // (2 * ny)
    whole = per_group // planes
    spare = per_group - whole * planes
    piece = FF // planes
    wide = whole * FF
    narrow = spare * piece
    narrow_pad = narrow + -narrow % LANES
    units = wide + narrow_pad

    rings = {axis: ring_order(n) for axis, n in length.items()}
    places = {axis: i for i, axis in enumerate(("z", "x", "y", "core"))}
    shape = (nz, nx, ny, 2)

    def pairs_of(axes, step):
        pairs = []
        for at in np.ndindex(*shape):
            axis = axes[at[3]]
            ring = rings[axis]
            to = list(at)
            to[places[axis]] = ring[(ring.index(at[places[axis]]) + step) % len(ring)]
            pairs.append(
                (int(np.ravel_multi_index(at, shape)), int(np.ravel_multi_index(to, shape)))
            )
        return pairs

    def move(values, axes, step):
        return lax.ppermute(values, ALL, pairs_of(axes, step))

    def row_order():
        found = {}
        for axis, n, form in (("z", nz, (1, 1, nz, 1)), ("x", nx, (1, nx, 1, 1)), ("y", ny, (ny, 1, 1, 1))):
            here = jnp.arange(n)[:, None] == lax.axis_index(axis)
            row = jnp.sum(jnp.where(here, jnp.asarray(home_table(n)), 0), axis=0)
            found[axis] = row.reshape(form)
        block = ((found["z"] * nx + found["x"]) * ny + found["y"]) * 2 + jnp.arange(2)
        block = block.reshape(-1, 1)
        rows = D // block.shape[0]
        kept = (block * rows + jnp.arange(rows)[None, :]).reshape(1, D)
        return (jnp.arange(D)[:, None] == kept).astype(bf16)

    def add_low(a, b):
        return (a.astype(f32) + b.astype(f32)).astype(bf16)

    sets = [tuple(range(nz))[i : i + nz // 2] for i in range(0, nz, nz // 2)]
    parts = ((0, "x", "y"), (1, "y", "x"))

    def line_of(own):
        line = [own]
        for _ in range(nz - 1):
            line.append(move(line[-1], "zz", 1))
        return line

    def gather_set(line, chosen):
        half = line[0].shape[0] // 2
        packs = [
            jnp.concatenate([line[s][part * half : (part + 1) * half] for s in chosen], axis=0)
            for part, _, _ in parts
        ]
        for level in (1, 2):
            grown = []
            for pack, names in zip(packs, parts):
                axis = names[level]
                steps = [pack]
                for _ in range(length[axis] - 1):
                    steps.append(move(steps[-1], axis * 2, 1))
                grown.append(jnp.concatenate(steps, axis=0))
            packs = grown
        return jnp.concatenate(packs, axis=0)

    def sum_level(packs, level):
        summed = []
        for pack, names in zip(packs, parts):
            n = length[names[level]]
            rows = pack.shape[0] // n
            acc = None
            for s in reversed(range(n)):
                mine = pack[s * rows : (s + 1) * rows]
                acc = mine if acc is None else add_low(move(acc, names[level] * 2, -1), mine)
            summed.append(acc)
        return summed

    def scatter_first(values):
        count = values.shape[0] // 2
        return sum_level([values[:count], values[count:]], 2)

    def scatter_second(packs):
        packs = sum_level(packs, 1)
        half = packs[0].shape[0] // (nz // 2)
        return [
            jnp.concatenate([p[s * half : (s + 1) * half] for p in packs], axis=0)
            for s in range(nz // 2)
        ]

    def sum_line(blocks):
        total = blocks[-1]
        for mine in reversed(blocks[:-1]):
            total = add_low(move(total, "zz", -1), mine)
        return total.astype(f32)

    def chip_half(own):
        half = own.shape[1] // 2
        core = lax.axis_index("core")
        left, right = own[:, :half], own[:, half:]
        kept = jnp.where(core == 0, left, right)
        came = swap_core(jnp.where(core == 0, right, left))
        return jnp.where(
            core == 0, jnp.concatenate([kept, came], axis=0), jnp.concatenate([came, kept], axis=0)
        )

    def gather_halves(line):
        rows, half = line[0].shape
        steps = [jnp.concatenate(line, axis=0)]
        for _ in range(nx - 1):
            steps.append(move(steps[-1], "xy", 1))
        packs = [jnp.concatenate(steps, axis=0)]
        for _ in range(nx - 1):
            packs.append(move(packs[-1], "yx", 1))
        result = jnp.concatenate(packs, axis=0).reshape(nx, nx, nz * rows, half)
        result = jnp.where(lax.axis_index("core") == 0, result, result.swapaxes(0, 1))
        result = result.reshape(nz * nx * ny * rows, half)
        return result, swap_core(result)

    def scatter_halves(left, right):
        core = lax.axis_index("core")
        columns = left.shape[1]
        rows = left.shape[0] // (nz * nx * ny * 2)
        came = swap_core(jnp.where(core == 0, right, left))
        both = add_low(came, jnp.where(core == 0, left, right))
        grid = both.reshape(ny, nx, nz * 2 * rows, columns)
        acc = None
        for s in reversed(range(nx)):
            mine = jnp.where(core == 0, grid[s], grid[:, s])
            acc = mine if acc is None else add_low(move(acc, "yx", -1), mine)
        two = None
        for s in reversed(range(nx)):
            mine = acc[s]
            two = mine if two is None else add_low(move(two, "xy", -1), mine)
        total = None
        for s in reversed(range(nz)):
            mine = two[s * 2 * rows : (s + 1) * 2 * rows]
            total = mine if total is None else add_low(move(total, "zz", -1), mine)
        kept = jnp.where(core == 0, total[:rows], total[rows:])
        came = swap_core(jnp.where(core == 0, total[rows:], total[:rows]))
        return (
            jnp.where(core == 0, kept, came).astype(f32),
            jnp.where(core == 0, came, kept).astype(f32),
        )

    def after(values, *first):
        if not whole:
            return values
        anywhere = pl.BlockSpec(memory_space=pl.ANY)
        return pl.pallas_call(
            keep_kernel,
            in_specs=[anywhere] * (1 + len(first)),
            out_specs=anywhere,
            out_shape=jax.ShapeDtypeStruct(values.shape, values.dtype),
            input_output_aliases={0: 0},
        )(values, *first)

    def all_to_all_plane(values):
        return lax.all_to_all(values, PLANE, split_axis=0, concat_axis=0, tiled=True)

    rows_home = D // planes
    across = rows_home // piece
    rest = 2 * narrow_pad + wide

    def cut_spare(part):
        part = part.reshape(spare, rows_home, 2, planes, piece)
        part = part.transpose(3, 1, 2, 0, 4).reshape(planes, rows_home, 2, narrow)
        part = jnp.pad(part, ((0, 0), (0, 0), (0, 0), (0, narrow_pad - narrow)))
        return part.reshape(planes, rows_home, 2 * narrow_pad)

    def join_spare(part):
        part = part.reshape(planes, rows_home, 2, narrow_pad)[..., :narrow]
        part = part.reshape(planes, rows_home, 2, spare, piece).transpose(3, 1, 2, 0, 4)
        return part.reshape(spare, rows_home, 2 * FF)

    def lanes(values, first, width=piece):
        return values[:, first : first + width]

    def pack_kernel(gate_up_ref, spare_ref, down_ref, spare_down_ref, full_ref, rest_ref, low_ref):
        step = pl.program_id(0)
        full_ref[0] = gate_up_ref[0].astype(bf16)
        for j in range(across):
            rest_ref[step, pl.ds(j * piece, piece), pl.ds(2 * narrow_pad, wide)] = down_ref[
                0, :, pl.ds(j * wide, wide)
            ].astype(bf16)

        @pl.when(step == 0)
        def _():
            for to in range(planes):
                taken = [
                    lanes(spare_ref[s], g * FF + to * piece) for g in range(2) for s in range(spare)
                ]
                rest_ref[to, :, pl.ds(0, 2 * narrow)] = jnp.concatenate(taken, axis=1).astype(bf16)
            for s in range(spare):
                low_ref[pl.ds(s * piece, piece), :] = spare_down_ref[s].astype(bf16)

    def pack_experts(gate_up, down):
        if not whole:
            low = down.astype(bf16).reshape(narrow, D)
            low = jnp.pad(low, ((0, narrow_pad - narrow), (0, 0)))
            return None, cut_spare(gate_up.astype(bf16)), low
        return pl.pallas_call(
            pack_kernel,
            grid=(planes,),
            in_specs=[
                pl.BlockSpec((1, rows_home, 2 * FF), lambda i: (i, 0, 0)),
                pl.BlockSpec((spare, rows_home, 2 * FF), lambda i: (planes // spare, 0, 0)),
                pl.BlockSpec((1, piece, D), lambda i: (i, 0, 0)),
                pl.BlockSpec((spare, piece, D), lambda i: (planes // spare, 0, 0)),
            ],
            out_specs=[
                pl.BlockSpec((1, rows_home, 2 * FF), lambda i: (i, 0, 0)),
                pl.BlockSpec((planes, rows_home, rest), lambda i: (0, 0, 0)),
                pl.BlockSpec((narrow, D), lambda i: (0, 0)),
            ],
            out_shape=[
                jax.ShapeDtypeStruct((planes, rows_home, 2 * FF), bf16),
                jax.ShapeDtypeStruct((planes, rows_home, rest), bf16),
                jax.ShapeDtypeStruct((narrow, D), bf16),
            ],
            cost_estimate=pl.CostEstimate(flops=0, bytes_accessed=2**24, transcendentals=0),
            compiler_params=pltpu.CompilerParams(vmem_limit_bytes=48 * 2**20),
        )(gate_up, gate_up, down, down)

    def down_of(packed, low):
        if not whole:
            return low
        mine = packed[:, 2 * narrow_pad :].reshape(planes, across, piece, wide)
        mine = mine.transpose(0, 2, 1, 3).reshape(wide, D)
        return jnp.concatenate([mine, low], axis=0)

    def combine_kernel(a_ref, came_a_ref, b_ref, came_b_ref, c_ref, came_c_ref, full_ref, rest_ref, low_ref):
        total = a_ref[...].astype(f32) + came_a_ref[...].astype(f32)
        full_ref[0] = total[:, : 2 * wide].astype(bf16)
        rest_ref[0, :, pl.ds(0, 2 * narrow_pad)] = total[:, 2 * wide :].astype(bf16)
        total = residual_scale * (b_ref[...].astype(f32) + came_b_ref[...].astype(f32))
        for j in range(across):
            rest_ref[0, pl.ds(j * piece, piece), pl.ds(2 * narrow_pad, wide)] = total[
                :, j * wide : (j + 1) * wide
            ].astype(bf16)
        low_ref[...] = residual_scale * (c_ref[...].astype(f32) + came_c_ref[...].astype(f32))

    def combine_grads(gate_up, came_gate_up, down, came_down):
        if not whole:
            total = (gate_up.astype(f32) + came_gate_up.astype(f32)).astype(bf16)
            low = residual_scale * (down.astype(f32) + came_down.astype(f32))
            return None, total.reshape(planes, rows_home, rest), low
        return pl.pallas_call(
            combine_kernel,
            grid=(planes,),
            in_specs=[pl.BlockSpec((rows_home, 2 * units), lambda i: (i, 0))] * 2
            + [pl.BlockSpec((piece, D), lambda i: (i, 0))] * 2
            + [pl.BlockSpec((narrow, D), lambda i: (wide // narrow, 0))] * 2,
            out_specs=[
                pl.BlockSpec((1, rows_home, 2 * FF), lambda i: (i, 0, 0)),
                pl.BlockSpec((1, rows_home, rest), lambda i: (i, 0, 0)),
                pl.BlockSpec((narrow, D), lambda i: (0, 0)),
            ],
            out_shape=[
                jax.ShapeDtypeStruct((planes, rows_home, 2 * FF), bf16),
                jax.ShapeDtypeStruct((planes, rows_home, rest), bf16),
                jax.ShapeDtypeStruct((narrow, D), f32),
            ],
            cost_estimate=pl.CostEstimate(flops=0, bytes_accessed=2**24, transcendentals=0),
            compiler_params=pltpu.CompilerParams(vmem_limit_bytes=48 * 2**20),
        )(gate_up, came_gate_up, down, came_down, down, came_down)

    gate_up_rate = D ** (-0.5)
    down_rate = max(2, FF // 128) ** (-0.5)

    def full_kernel(home_ref, w_ref, m_ref, s_ref, *outs):
        done = adam_step(
            w_ref[0], m_ref[0], s_ref[0], home_ref[0].astype(f32), gate_up_rate, weight_decay
        )
        for ref, value in zip(outs, done):
            ref[0] = value

    def spare_kernel(home_ref, w_ref, m_ref, s_ref, a_ref, b_ref, c_ref, *outs):
        for s in range(spare):

            @pl.when(pl.program_id(0) == s)
            def _():
                grad = jnp.concatenate(
                    [
                        lanes(home_ref[p], g * narrow_pad + s * piece)
                        for g in range(2)
                        for p in range(planes)
                    ],
                    axis=1,
                ).astype(f32)
                done = adam_step(w_ref[0], m_ref[0], s_ref[0], grad, gate_up_rate, weight_decay)
                for ref, value in zip(outs, done):
                    ref[0] = value

    def down_kernel(home_ref, low_ref, w_ref, m_ref, s_ref, *outs):
        def update(grad):
            done = adam_step(w_ref[0], m_ref[0], s_ref[0], grad, down_rate, weight_decay)
            for ref, value in zip(outs, done):
                ref[0] = value

        @pl.when(pl.program_id(0) < planes)
        def _():
            update(
                jnp.concatenate(
                    [
                        home_ref[0, pl.ds(j * piece, piece), pl.ds(2 * narrow_pad, wide)]
                        for j in range(across)
                    ],
                    axis=1,
                ).astype(f32)
            )

        @pl.when(pl.program_id(0) >= planes)
        def _():
            update(low_ref[...])

    def update_experts(home_full, home_rest, low, gate_up, down):
        if not whole:
            grad = join_spare(home_rest).astype(f32)
            return (
                adam_step(*gate_up, grad, gate_up_rate, weight_decay),
                adam_step(
                    *down, low[:narrow].reshape(spare, piece, D), down_rate, weight_decay
                ),
            )
        params = pltpu.CompilerParams(vmem_limit_bytes=48 * 2**20)
        shapes = [jax.ShapeDtypeStruct(gate_up[0].shape, f32)] * 3
        one = pl.BlockSpec((1, rows_home, 2 * FF), lambda i: (i, 0, 0))
        last = pl.BlockSpec((1, rows_home, 2 * FF), lambda i: (planes + i, 0, 0))
        new_gate_up = pl.pallas_call(
            full_kernel,
            grid=(planes,),
            in_specs=[one] * 4,
            out_specs=[one] * 3,
            cost_estimate=pl.CostEstimate(flops=0, bytes_accessed=2**25, transcendentals=0),
            out_shape=shapes,
            compiler_params=params,
        )(home_full, *gate_up)
        new_gate_up = pl.pallas_call(
            spare_kernel,
            grid=(spare,),
            in_specs=[pl.BlockSpec((planes, rows_home, 2 * narrow_pad), lambda i: (0, 0, 0))]
            + [last] * 3
            + [pl.BlockSpec(memory_space=pl.ANY)] * 3,
            out_specs=[last] * 3,
            out_shape=shapes,
            input_output_aliases={4: 0, 5: 1, 6: 2},
            compiler_params=params,
        )(home_rest, *gate_up, *new_gate_up)
        row = pl.BlockSpec((1, piece, D), lambda i: (i, 0, 0))
        new_down = pl.pallas_call(
            down_kernel,
            grid=(per_group,),
            in_specs=[
                pl.BlockSpec((1, rows_home, rest), lambda i: (jnp.minimum(i, planes - 1), 0, 0)),
                pl.BlockSpec((piece, D), lambda i: (jnp.maximum(i - planes, 0), 0)),
            ]
            + [row] * 3,
            out_specs=[row] * 3,
            cost_estimate=pl.CostEstimate(flops=0, bytes_accessed=2**24, transcendentals=0),
            out_shape=[jax.ShapeDtypeStruct(down[0].shape, f32)] * 3,
            compiler_params=params,
        )(home_rest, low, *down)
        return new_gate_up, new_down

    def unit_experts(group, place):
        base = group * per_group
        sets = []
        if whole:
            sets.append(jnp.full((wide,), base + place))
        behind = base + whole * planes + jnp.arange(narrow_pad) // piece
        sets.append(jnp.where(jnp.arange(narrow_pad) < narrow, behind, -1))
        return jnp.concatenate(sets)

    def columns_of():
        pieces = []
        for first in range(0, wide, 256):
            pieces.append((True, first, wide + first, first, min(256, wide - first)))
        pieces.append((False, 0, narrow_pad, wide, narrow_pad))
        return pieces

    def expert_kernel(first_call, *refs):
        count = 2 if whole else 1
        rows_ref, gates_ref = refs[:2]
        reaches = refs[2:4]
        weights = (refs[4 : 4 + count], refs[4 + count : 4 + 2 * count])
        twice_ref, once_ref = refs[4 + 2 * count : 6 + 2 * count]
        gated_ref, grad_ref, two_ref = refs[6 + 2 * count + (0 if first_call else 2) :]
        rows = rows_ref[...]
        gates = gates_ref[...]
        dgate = jnp.zeros((rows.shape[0], LANES), f32)
        two = jnp.zeros((rows.shape[0], D), f32)
        for k in range(2):
            for in_full, gate_at, up_at, unit_at, width in columns_of():
                held = weights[k][0 if in_full else -1]
                unit = pl.ds(k * units + unit_at, width)
                gate_w = held[:, pl.ds(gate_at, width)]
                up_w = held[:, pl.ds(up_at, width)]
                gate_part = jnp.dot(rows, gate_w, preferred_element_type=f32)
                up_part = jnp.dot(rows, up_w, preferred_element_type=f32)
                gate_wide = jnp.dot(gates, twice_ref[:, unit], preferred_element_type=f32)
                reach = residual_scale * reaches[k][:, pl.ds(unit_at, width)]
                squash = 1.0 / (1.0 + jnp.exp(-gate_part))
                swish = gate_part * squash
                hidden = swish * up_part
                gated_ref[:, unit] = (hidden * gate_wide).astype(bf16)
                dgate += dot_nt((hidden * reach).astype(bf16), once_ref[:, unit])
                grad_hidden = reach * gate_wide
                grad_gate = grad_hidden * up_part * squash * (1.0 + gate_part * (1.0 - squash))
                base = k * 2 * units + (0 if in_full else 2 * wide)
                grad_ref[:, pl.ds(base + gate_at, width)] = grad_gate.astype(bf16)
                grad_ref[:, pl.ds(base + up_at, width)] = (grad_hidden * swish).astype(bf16)
        for k in range(2):
            at = k * 2 * units
            if whole:
                two += dot_nt(grad_ref[:, pl.ds(at, 2 * wide)], weights[k][0][...])
            two += dot_nt(
                grad_ref[:, pl.ds(at + 2 * wide, 2 * narrow_pad)],
                weights[k][-1][:, pl.ds(0, 2 * narrow_pad)],
            )
        two_ref[:, pl.ds(0, D)] = two.astype(bf16)
        two_ref[:, pl.ds(D, LANES)] = dgate.astype(bf16)

    def run_experts(at, sent, reach, own, other, twice, once, before):
        count = sent.shape[0]
        total = reach[0].shape[0]
        tile = min(512, count)
        first = at * (count // tile)

        def by_rows(columns, offset=0, column=0):
            return pl.BlockSpec((tile, columns), lambda i: (i + offset, column))

        def fixed(rows, columns):
            return pl.BlockSpec((rows, columns), lambda i: (0, 0), pipeline_mode=pl.Buffered(1))

        held = []
        for full, more in (own, other):
            if whole:
                held.append((full, fixed(D, 2 * wide)))
            held.append((more, fixed(D, 2 * narrow_pad)))
        kept = list(before) if before else []
        return pl.pallas_call(
            functools.partial(expert_kernel, not kept),
            grid=(count // tile,),
            in_specs=[by_rows(D), by_rows(LANES, 0, D // LANES)]
            + [by_rows(units, first)] * 2
            + [spec for _, spec in held]
            + [fixed(LANES, 2 * units)] * 2
            + [pl.BlockSpec(memory_space=pl.ANY)] * len(kept),
            out_specs=[
                by_rows(2 * units, first),
                by_rows(4 * units, first),
                by_rows(D + LANES),
            ],
            out_shape=[
                jax.ShapeDtypeStruct((total, 2 * units), bf16),
                jax.ShapeDtypeStruct((total, 4 * units), bf16),
                jax.ShapeDtypeStruct((count, D + LANES), bf16),
            ],
            input_output_aliases={6 + len(held) + i: i for i in range(len(kept))},
            cost_estimate=pl.CostEstimate(
                flops=16 * count * D * units, bytes_accessed=2**25, transcendentals=2 * count * units
            ),
            compiler_params=pltpu.CompilerParams(vmem_limit_bytes=60 * 2**20),
        )(sent, sent, *reach, *[w for w, _ in held], twice, once, *kept)

    def shards(
        tokens,
        cotangent,
        routes,
        weight_qkv,
        moment_qkv,
        square_qkv,
        weight_out,
        moment_out,
        square_out,
        weight_router,
        moment_router,
        square_router,
        gains,
        moment_gains,
        square_gains,
        weight_gate_up,
        moment_gate_up,
        square_gate_up,
        weight_down,
        moment_down,
        square_down,
    ):
        sequence_length = tokens.shape[0]
        head_groups = QUERY_HEADS // KEY_VALUE_HEADS
        place = lax.axis_index(PLANE)
        group = lax.axis_index("y") * 2 + lax.axis_index("core")
        partner = lax.axis_index("y") * 2 + 1 - lax.axis_index("core")

        small = pad_lanes(jnp.concatenate([weight_router, gains.T], axis=1))
        first_pack = jnp.concatenate([weight_qkv, small], axis=1).astype(bf16)
        first_all = lax.all_gather(first_pack, ALL, axis=0, tiled=True)

        full, more, low_own = pack_experts(weight_gate_up, weight_down)
        out_line = line_of(chip_half(weight_out.astype(bf16)))
        cot_line = line_of(cotangent)
        more = after(more, out_line[-1], cot_line[-1])
        more_own = all_to_all_plane(more).reshape(D, -1)
        out_mine, out_other = gather_halves(out_line)
        order = row_order()

        qkv_w = first_all[:, :QKV]
        router_w = first_all[:, QKV : QKV + EXPERTS]
        gain_one = first_all[:, QKV + EXPERTS].astype(f32)
        gain_two = first_all[:, QKV + EXPERTS + 1].astype(f32)

        inputs = tokens.astype(f32)
        factor_one = lax.rsqrt(jnp.mean(inputs * inputs, axis=-1, keepdims=True) + norm_eps)
        hidden_one = (inputs * factor_one * gain_one).astype(bf16)
        joined_heads = dot(hidden_one, qkv_w)
        cot_line = [after(b, joined_heads) for b in cot_line]
        cot_all = jnp.concatenate([gather_set(cot_line, s) for s in sets], axis=0)
        hidden_here = dot(hidden_one, order).astype(bf16)
        query_rows = joined_heads[:, :HEADS_WIDTH].reshape(sequence_length, QUERY_HEADS, HEAD_SIZE)
        every_key = joined_heads[:, HEADS_WIDTH : HEADS_WIDTH + KEYS_WIDTH].reshape(
            sequence_length, KEY_VALUE_HEADS, HEAD_SIZE
        )
        every_value = joined_heads[:, HEADS_WIDTH + KEYS_WIDTH :].reshape(
            sequence_length, KEY_VALUE_HEADS, HEAD_SIZE
        )
        cosine_lookup, sine_lookup = rotary_tables(sequence_length, HEAD_SIZE)
        query_rotated = (
            apply_rotation(query_rows, cosine_lookup, sine_lookup)
            .astype(bf16)
            .reshape(sequence_length, KEY_VALUE_HEADS, head_groups, HEAD_SIZE)
        )
        key_rot = apply_rotation(every_key, cosine_lookup, sine_lookup).astype(bf16)
        value_low = every_value.astype(bf16)
        causal = jnp.arange(sequence_length)[:, None] >= jnp.arange(sequence_length)[None, :]
        scores = attention_scores(query_rotated, key_rot, causal)
        peak = jnp.max(scores, axis=-1, keepdims=True)
        expo = jnp.exp(scores - peak)
        totals = jnp.sum(expo, axis=-1, keepdims=True)
        probs = expo / totals
        prob_low = probs.astype(bf16)
        heads = jnp.einsum("kgst,tkd->skgd", prob_low, value_low, preferred_element_type=f32)
        attended = heads.reshape(sequence_length, HEADS_WIDTH).astype(bf16)
        core = lax.axis_index("core")
        attended = dot(attended, order).astype(bf16)
        projected = [dot(attended, out_mine), dot(attended, out_other)]
        mid = inputs + residual_scale * jnp.where(
            core == 0,
            jnp.concatenate(projected, axis=1),
            jnp.concatenate(projected[::-1], axis=1),
        )
        factor_two = lax.rsqrt(jnp.mean(mid * mid, axis=-1, keepdims=True) + norm_eps)
        hidden_two = (mid * factor_two * gain_two).astype(bf16)
        logits = dot(hidden_two, router_w)
        named = jnp.any(
            routes[..., None] == jnp.arange(EXPERTS, dtype=routes.dtype)[None, None, :], axis=1
        )
        shown = jnp.where(named, logits, -jnp.inf)
        raised = jnp.exp(shown - jnp.max(shown, axis=-1, keepdims=True))
        gates = raised / jnp.sum(raised, axis=-1, keepdims=True)

        gate_high = gates.astype(bf16)
        gate_rest = (gates - gate_high.astype(f32)).astype(bf16)
        sent = jnp.concatenate(
            [hidden_two, pad_lanes(jnp.concatenate([gate_high, gate_rest], axis=1))], axis=1
        )
        sent_line = line_of(sent)
        more_own = after(more_own, sent)
        own = [None, more_own]
        if whole:
            own[0] = all_to_all_plane(after(full, sent_line[-1])).reshape(D, -1)
        more_other, low_other = swap_core(more_own), swap_core(low_own)
        down_own, down_other = down_of(more_own, low_own), down_of(more_other, low_other)
        reach = [dot_nt(cot_all, down_own), dot_nt(cot_all, down_other)]
        sent_sets = [gather_set(sent_line, s) for s in sets]
        other = [None, more_other]
        if whole:
            own[0] = after(own[0], sent_sets[-1])
            other[0] = swap_core(own[0])
        rows_all = jnp.concatenate([s[:, :D] for s in sent_sets], axis=0)

        behind = jnp.concatenate([unit_experts(group, place), unit_experts(partner, place)])
        numbers = jnp.arange(LANES)[:, None]
        real = behind[None, :] >= 0
        once = ((numbers == behind[None, :]) & real).astype(bf16)
        twice = once + ((numbers == behind[None, :] + EXPERTS) & real).astype(bf16)
        kept = None
        firsts = []
        for at, sent_set in enumerate(sent_sets):
            *kept, two = run_experts(at, sent_set, reach, own, other, twice, once, kept)
            firsts.append(scatter_first(two))
        two_blocks = [b for packs in firsts for b in scatter_second(packs)]
        gated, grad_both = kept
        two_sum = sum_line(two_blocks)
        mixed = (dot(gated[:, :units], down_own) + dot(gated[:, units:], down_other)).astype(bf16)
        mixed = after(mixed, two_blocks[-1])
        half = mixed.shape[0] // 2
        mixed_blocks = [
            b for v in (mixed[:half], mixed[half:]) for b in scatter_second(scatter_first(v))
        ]
        mixed_blocks[-1] = after(mixed_blocks[-1], two_sum)
        mixed = sum_line(mixed_blocks)
        layer_out = (mid + residual_scale * mixed).astype(bf16)

        grad_both = after(grad_both, *firsts[-1])
        came_gate_up = swap_core(dot_tn(rows_all, grad_both[:, 2 * units :]).astype(bf16))
        came_down = swap_core(dot_tn(gated[:, units:], cot_all).astype(bf16))
        full, more, low = combine_grads(
            dot_tn(rows_all, grad_both[:, : 2 * units]).astype(bf16),
            came_gate_up,
            dot_tn(gated[:, :units], cot_all).astype(bf16),
            came_down,
        )
        home_full = all_to_all_plane(after(full, two_sum)) if whole else None
        home_rest = all_to_all_plane(after(more, two_sum))
        two_sum = after(two_sum, full, more)
        grad_two, grad_gates = two_sum[:, :D], two_sum[:, D : D + EXPERTS]

        grad_out = cotangent.astype(f32)
        grad_chosen = gates * (grad_gates - jnp.sum(gates * grad_gates, axis=-1, keepdims=True))
        grad_logits = grad_chosen.astype(bf16)
        grad_router = dot_tn(hidden_two, grad_logits)
        grad_two = grad_two + dot_nt(grad_logits, router_w)
        grad_mid, grad_gain_two = norm_backward(grad_two, mid, factor_two, gain_two)
        grad_mid = grad_out + grad_mid
        grad_att = (residual_scale * grad_mid).astype(bf16)
        att_left, att_right = grad_att[:, : D // 2], grad_att[:, D // 2 :]
        grad_heads = (
            (
                dot_nt(jnp.where(core == 0, att_left, att_right), out_mine)
                + dot_nt(jnp.where(core == 0, att_right, att_left), out_other)
            )
            .astype(bf16)
        )
        grad_heads = (
            dot_nt(grad_heads, order)
            .astype(bf16)
            .reshape(sequence_length, KEY_VALUE_HEADS, head_groups, HEAD_SIZE)
        )
        out_left, out_right = scatter_halves(
            dot_tn(attended, att_left).astype(bf16), dot_tn(attended, att_right).astype(bf16)
        )
        grad_probs = jnp.einsum(
            "skgd,tkd->kgst", grad_heads, value_low, preferred_element_type=f32
        )
        value_gradient = jnp.einsum(
            "kgst,skgd->tkd", prob_low, grad_heads, preferred_element_type=f32
        )
        row_dot = jnp.sum(probs * grad_probs, axis=-1, keepdims=True)
        grad_scores = (probs * (grad_probs - row_dot)).astype(bf16)
        grad_qrot = (
            jnp.einsum("kgst,tkd->skgd", grad_scores, key_rot, preferred_element_type=f32)
            * score_scale
        )
        grad_krot = (
            jnp.einsum("kgst,skgd->tkd", grad_scores, query_rotated, preferred_element_type=f32)
            * score_scale
        )
        grad_queries = apply_rotation(
            grad_qrot.reshape(sequence_length, QUERY_HEADS, HEAD_SIZE), cosine_lookup, -sine_lookup
        )
        key_gradient = apply_rotation(grad_krot, cosine_lookup, -sine_lookup)
        grad_joined = jnp.concatenate(
            [
                grad_queries.reshape(sequence_length, HEADS_WIDTH),
                key_gradient.reshape(sequence_length, KEYS_WIDTH),
                value_gradient.reshape(sequence_length, KEYS_WIDTH),
            ],
            axis=1,
        ).astype(bf16)
        grad_one = dot_nt(grad_joined, qkv_w)
        grad_inputs, grad_gain_one = norm_backward(grad_one, inputs, factor_one, gain_one)
        token_grad = grad_mid + grad_inputs
        small_sent = pad_lanes(
            jnp.concatenate([grad_router, grad_gain_one[:, None], grad_gain_two[:, None]], axis=1)
        )
        small_sent = dot_tn(order, small_sent.astype(bf16))
        qkv_left, qkv_right = scatter_halves(
            jnp.concatenate(
                [dot_tn(hidden_here, grad_joined[:, : QKV // 2]), small_sent], axis=1
            ).astype(bf16),
            jnp.concatenate(
                [dot_tn(hidden_here, grad_joined[:, QKV // 2 :]), jnp.zeros_like(small_sent)], axis=1
            ).astype(bf16),
        )
        sum_out = jnp.concatenate([out_left, out_right], axis=1)
        sum_qkv = jnp.concatenate([qkv_left[:, : QKV // 2], qkv_right[:, : QKV // 2]], axis=1)
        sum_router = qkv_left[:, QKV // 2 : QKV // 2 + EXPERTS]
        sum_gains = qkv_left[:, QKV // 2 + EXPERTS : QKV // 2 + EXPERTS + 2].T

        new_gate_up, new_down = update_experts(
            home_full,
            home_rest,
            low,
            (weight_gate_up, moment_gate_up, square_gate_up),
            (weight_down, moment_down, square_down),
        )
        new_qkv = adam_step(weight_qkv, moment_qkv, square_qkv, sum_qkv, D ** (-0.5), weight_decay)
        new_out = adam_step(
            weight_out,
            moment_out,
            square_out,
            sum_out,
            max(4, QUERY_HEADS * HEAD_SIZE // 256) ** (-0.5),
            weight_decay,
        )
        new_router = adam_step(
            weight_router, moment_router, square_router, sum_router, (4 * D) ** (-0.5), weight_decay
        )
        new_gains = adam_step(gains, moment_gains, square_gains, sum_gains, 0.75, 0.0)
        return (
            layer_out,
            token_grad,
            *new_qkv,
            *new_out,
            *new_router,
            *new_gains,
            *new_gate_up,
            *new_down,
        )

    return shards


def solution(mesh):
    n_dp, n_expert = mesh.shape["dp"], mesh.shape["expert"]
    nz = 4
    nx, ny = n_dp // nz, n_expert // 2
    fine = Mesh(mesh.devices.reshape(nz, nx, ny, 2), ALL)
    rows = P(ALL, None)
    columns = P(None, ALL)
    experts = P(("y", "core"), ("z", "x"), None)
    dense = (rows,) * 9 + (columns,) * 3 + (experts,) * 6
    return jax.shard_map(
        make_shards((nz, nx, ny)),
        mesh=fine,
        in_specs=(rows,) * 3 + dense,
        out_specs=(rows,) * 2 + dense,
        check_vma=False,
    )
```

```python
import functools

import jax
import jax.numpy as jnp
import numpy as np
from jax import lax
from jax.experimental import pallas as pl
from jax.experimental.pallas import tpu as pltpu
from jax.sharding import Mesh, PartitionSpec as P

D = 1536
QUERY_HEADS = 24
KEY_VALUE_HEADS = 8
HEAD_SIZE = 64
FF = 512
EXPERTS = 40
TOPK = 8
STEP = 10
QKV = 2560
LANES = 128
HEADS_WIDTH = QUERY_HEADS * HEAD_SIZE
KEYS_WIDTH = KEY_VALUE_HEADS * HEAD_SIZE

norm_eps = 1e-06
residual_scale = 0.22
score_scale = 0.125
beta_one = 0.9
beta_two = 0.95
adam_eps = 1e-08
weight_decay = 0.1

f32 = jnp.float32
bf16 = jnp.bfloat16
ALL = ("z", "x", "y", "core")
PLANE = ("z", "x")


def rotary_tables(sequence_length, size):
    half = size // 2
    places = jnp.arange(sequence_length).astype(f32)[:, None]
    inverse = 10000.0 ** (-jnp.arange(half).astype(f32) * 2.0 / size)
    angles = places * inverse[None, :]
    return (jnp.cos(angles)[:, None, :], jnp.sin(angles)[:, None, :])


def apply_rotation(values, cosine_lookup, sine_lookup):
    half = values.shape[-1] // 2
    first = values[..., :half]
    second = values[..., half:]
    return jnp.concatenate(
        [
            first * cosine_lookup - second * sine_lookup,
            second * cosine_lookup + first * sine_lookup,
        ],
        axis=-1,
    )


def attention_scores(query_rotated, key_rot, causal):
    scores = (
        jnp.einsum("skgd,tkd->kgst", query_rotated, key_rot, preferred_element_type=f32)
        * score_scale
    )
    return jnp.where(causal, scores, -1e30)


def norm_backward(grad_normed, values, factor, gain):
    scaled = grad_normed * gain
    grad_gain = jnp.sum(grad_normed * values * factor, axis=0)
    value_gradient = factor * scaled - values * factor * factor * factor * jnp.mean(
        scaled * values, axis=-1, keepdims=True
    )
    return (value_gradient, grad_gain)


def adam_step(weight, moment, square, grad, rate, decay):
    moment = beta_one * moment + (1.0 - beta_one) * grad
    square = beta_two * square + (1.0 - beta_two) * grad * grad
    fixed_one = moment / (1.0 - beta_one**STEP)
    fixed_two = square / (1.0 - beta_two**STEP)
    weight = weight - rate * (fixed_one / (jnp.sqrt(fixed_two) + adam_eps) + decay * weight)
    return (weight, moment, square)


def dot(a, b):
    return jnp.dot(a, b, preferred_element_type=f32)


def dot_nt(a, b):
    return lax.dot_general(a, b, (((1,), (1,)), ((), ())), preferred_element_type=f32)


def dot_tn(a, b):
    return lax.dot_general(a, b, (((0,), (0,)), ((), ())), preferred_element_type=f32)


def pad_lanes(values):
    extra = -values.shape[-1] % LANES
    return jnp.pad(values, ((0, 0), (0, extra)))


def swap_core(values):
    return lax.ppermute(values, "core", [(0, 1), (1, 0)])


def keep_kernel(*refs):
    pass


def ring_order(n):
    return [0] + list(range(1, n, 2)) + list(range(n - 2 + n % 2, 0, -2))


def home_table(n):
    order = ring_order(n)
    place = {chip: at for at, chip in enumerate(order)}
    return np.array([[order[(place[i] - s) % n] for s in range(n)] for i in range(n)], np.int32)


def make_shards(sizes):
    nz, nx, ny = sizes
    length = {"z": nz, "x": nx, "y": ny}
    planes = nz * nx
    per_group = EXPERTS // (2 * ny)
    whole = per_group // planes
    spare = per_group - whole * planes
    piece = FF // planes
    wide = whole * FF
    narrow = spare * piece
    narrow_pad = narrow + -narrow % LANES
    units = wide + narrow_pad

    rings = {axis: ring_order(n) for axis, n in length.items()}
    places = {axis: i for i, axis in enumerate(("z", "x", "y", "core"))}
    shape = (nz, nx, ny, 2)

    def pairs_of(axes, step):
        pairs = []
        for at in np.ndindex(*shape):
            axis = axes[at[3]]
            ring = rings[axis]
            to = list(at)
            to[places[axis]] = ring[(ring.index(at[places[axis]]) + step) % len(ring)]
            pairs.append(
                (int(np.ravel_multi_index(at, shape)), int(np.ravel_multi_index(to, shape)))
            )
        return pairs

    def move(values, axes, step):
        return lax.ppermute(values, ALL, pairs_of(axes, step))

    def row_order():
        found = {}
        for axis, n, form in (("z", nz, (1, 1, nz, 1)), ("x", nx, (1, nx, 1, 1)), ("y", ny, (ny, 1, 1, 1))):
            here = jnp.arange(n)[:, None] == lax.axis_index(axis)
            row = jnp.sum(jnp.where(here, jnp.asarray(home_table(n)), 0), axis=0)
            found[axis] = row.reshape(form)
        block = ((found["z"] * nx + found["x"]) * ny + found["y"]) * 2 + jnp.arange(2)
        block = block.reshape(-1, 1)
        rows = D // block.shape[0]
        kept = (block * rows + jnp.arange(rows)[None, :]).reshape(1, D)
        return (jnp.arange(D)[:, None] == kept).astype(bf16)

    def add_low(a, b):
        return (a.astype(f32) + b.astype(f32)).astype(bf16)

    parts = ((0, "x", "y"), (1, "y", "x"))

    def line_of(own):
        line = [own]
        for _ in range(nz - 1):
            line.append(move(line[-1], "zz", 1))
        return line

    def gather_tokens(line):
        half = line[0].shape[0] // 2
        packs = [
            jnp.concatenate([b[part * half : (part + 1) * half] for b in line], axis=0)
            for part, _, _ in parts
        ]
        for level in (1, 2):
            grown = []
            for pack, names in zip(packs, parts):
                axis = names[level]
                steps = [pack]
                for _ in range(length[axis] - 1):
                    steps.append(move(steps[-1], axis * 2, 1))
                grown.append(jnp.concatenate(steps, axis=0))
            packs = grown
        return jnp.concatenate(packs, axis=0)

    def sum_level(packs, level):
        summed = []
        for pack, names in zip(packs, parts):
            n = length[names[level]]
            pack = pack.reshape(n, pack.shape[0] // n, *pack.shape[1:])
            acc = None
            for s in reversed(range(n)):
                acc = pack[s] if acc is None else add_low(move(acc, names[level] * 2, -1), pack[s])
            summed.append(acc)
        return summed

    def scatter_first(values):
        count = values.shape[0] // 2
        return sum_level([values[:count], values[count:]], 2)

    def scatter_second(halves):
        packs = [jnp.concatenate(same, axis=1) for same in zip(*halves)]
        packs = [p[0] for p in sum_level(packs, 1)]
        half = packs[0].shape[0] // nz
        return [
            jnp.concatenate([p[s * half : (s + 1) * half] for p in packs], axis=0)
            for s in range(nz)
        ]

    def sum_line(blocks):
        total = blocks[-1]
        for mine in reversed(blocks[:-1]):
            total = add_low(move(total, "zz", -1), mine)
        return total.astype(f32)

    def chip_half(own):
        half = own.shape[1] // 2
        core = lax.axis_index("core")
        left, right = own[:, :half], own[:, half:]
        kept = jnp.where(core == 0, left, right)
        came = swap_core(jnp.where(core == 0, right, left))
        return jnp.where(
            core == 0, jnp.concatenate([kept, came], axis=0), jnp.concatenate([came, kept], axis=0)
        )

    def gather_halves(line):
        rows, half = line[0].shape
        steps = [jnp.concatenate(line, axis=0)]
        for _ in range(nx - 1):
            steps.append(move(steps[-1], "xy", 1))
        packs = [jnp.concatenate(steps, axis=0)]
        for _ in range(nx - 1):
            packs.append(move(packs[-1], "yx", 1))
        result = jnp.concatenate(packs, axis=0).reshape(nx, nx, nz * rows, half)
        result = jnp.where(lax.axis_index("core") == 0, result, result.swapaxes(0, 1))
        result = result.reshape(nz * nx * ny * rows, half)
        return result, swap_core(result)

    def scatter_halves_first(left, right):
        core = lax.axis_index("core")
        came = swap_core(jnp.where(core == 0, right, left))
        both = add_low(came, jnp.where(core == 0, left, right))
        grid = both.reshape(ny, nx, both.shape[0] // (ny * nx), both.shape[1])
        acc = None
        for s in reversed(range(nx)):
            mine = jnp.where(core == 0, grid[s], grid[:, s])
            acc = mine if acc is None else add_low(move(acc, "yx", -1), mine)
        return acc

    def scatter_halves_second(acc):
        core = lax.axis_index("core")
        rows = acc.shape[1] // (nz * 2)
        two = None
        for s in reversed(range(nx)):
            two = acc[s] if two is None else add_low(move(two, "xy", -1), acc[s])
        total = None
        for s in reversed(range(nz)):
            mine = two[s * 2 * rows : (s + 1) * 2 * rows]
            total = mine if total is None else add_low(move(total, "zz", -1), mine)
        kept = jnp.where(core == 0, total[:rows], total[rows:])
        came = swap_core(jnp.where(core == 0, total[rows:], total[:rows]))
        return (
            jnp.where(core == 0, kept, came).astype(f32),
            jnp.where(core == 0, came, kept).astype(f32),
        )

    def after(values, *first, always=False):
        if not (whole or always):
            return values
        anywhere = pl.BlockSpec(memory_space=pl.ANY)
        return pl.pallas_call(
            keep_kernel,
            in_specs=[anywhere] * (1 + len(first)),
            out_specs=anywhere,
            out_shape=jax.ShapeDtypeStruct(values.shape, values.dtype),
            input_output_aliases={0: 0},
        )(values, *first)

    def all_to_all_plane(values):
        return lax.all_to_all(values, PLANE, split_axis=0, concat_axis=0, tiled=True)

    rows_home = D // planes
    across = rows_home // piece
    rest = 2 * narrow_pad + wide

    def cut_spare(part):
        part = part.reshape(spare, rows_home, 2, planes, piece)
        part = part.transpose(3, 1, 2, 0, 4).reshape(planes, rows_home, 2, narrow)
        part = jnp.pad(part, ((0, 0), (0, 0), (0, 0), (0, narrow_pad - narrow)))
        return part.reshape(planes, rows_home, 2 * narrow_pad)

    def join_spare(part):
        part = part.reshape(planes, rows_home, 2, narrow_pad)[..., :narrow]
        part = part.reshape(planes, rows_home, 2, spare, piece).transpose(3, 1, 2, 0, 4)
        return part.reshape(spare, rows_home, 2 * FF)

    def lanes(values, first, width=piece):
        return values[:, first : first + width]

    packed_columns = 2 * units + wide

    def pack_kernel(gate_up_ref, spare_ref, down_ref, spare_down_ref, out_ref, low_ref):
        step = pl.program_id(0)
        out_ref[step, :, pl.ds(0, 2 * wide)] = gate_up_ref[0].astype(bf16)
        for j in range(across):
            out_ref[step, pl.ds(j * piece, piece), pl.ds(2 * units, wide)] = down_ref[
                0, :, pl.ds(j * wide, wide)
            ].astype(bf16)

        @pl.when(step == 0)
        def _():
            for to in range(planes):
                taken = [
                    lanes(spare_ref[s], g * FF + to * piece) for g in range(2) for s in range(spare)
                ]
                out_ref[to, :, pl.ds(2 * wide, 2 * narrow)] = jnp.concatenate(taken, axis=1).astype(
                    bf16
                )
            for s in range(spare):
                low_ref[pl.ds(s * piece, piece), :] = spare_down_ref[s].astype(bf16)

    def pack_experts(gate_up, down):
        if not whole:
            low = down.astype(bf16).reshape(narrow, D)
            low = jnp.pad(low, ((0, narrow_pad - narrow), (0, 0)))
            return cut_spare(gate_up.astype(bf16)), low
        return pl.pallas_call(
            pack_kernel,
            grid=(planes,),
            in_specs=[
                pl.BlockSpec((1, rows_home, 2 * FF), lambda i: (i, 0, 0)),
                pl.BlockSpec((spare, rows_home, 2 * FF), lambda i: (planes // spare, 0, 0)),
                pl.BlockSpec((1, piece, D), lambda i: (i, 0, 0)),
                pl.BlockSpec((spare, piece, D), lambda i: (planes // spare, 0, 0)),
            ],
            out_specs=[
                pl.BlockSpec((planes, rows_home, packed_columns), lambda i: (0, 0, 0)),
                pl.BlockSpec((narrow, D), lambda i: (0, 0)),
            ],
            out_shape=[
                jax.ShapeDtypeStruct((planes, rows_home, packed_columns), bf16),
                jax.ShapeDtypeStruct((narrow, D), bf16),
            ],
            cost_estimate=pl.CostEstimate(flops=0, bytes_accessed=2**24, transcendentals=0),
            compiler_params=pltpu.CompilerParams(vmem_limit_bytes=48 * 2**20),
        )(gate_up, gate_up, down, down)

    def down_of(packed, low):
        if not whole:
            return low
        mine = packed[:, 2 * units :].reshape(planes, across, piece, wide)
        mine = mine.transpose(0, 2, 1, 3).reshape(wide, D)
        return jnp.concatenate([mine, low], axis=0)

    def combine_kernel(a_ref, came_a_ref, b_ref, came_b_ref, c_ref, came_c_ref, full_ref, rest_ref, low_ref):
        total = a_ref[...].astype(f32) + came_a_ref[...].astype(f32)
        full_ref[0] = total[:, : 2 * wide].astype(bf16)
        rest_ref[0, :, pl.ds(0, 2 * narrow_pad)] = total[:, 2 * wide :].astype(bf16)
        total = residual_scale * (b_ref[...].astype(f32) + came_b_ref[...].astype(f32))
        for j in range(across):
            rest_ref[0, pl.ds(j * piece, piece), pl.ds(2 * narrow_pad, wide)] = total[
                :, j * wide : (j + 1) * wide
            ].astype(bf16)
        low_ref[...] = residual_scale * (c_ref[...].astype(f32) + came_c_ref[...].astype(f32))

    def combine_grads(gate_up, came_gate_up, down, came_down):
        if not whole:
            total = (gate_up.astype(f32) + came_gate_up.astype(f32)).astype(bf16)
            low = residual_scale * (down.astype(f32) + came_down.astype(f32))
            return None, total.reshape(planes, rows_home, rest), low
        return pl.pallas_call(
            combine_kernel,
            grid=(planes,),
            in_specs=[pl.BlockSpec((rows_home, 2 * units), lambda i: (i, 0))] * 2
            + [pl.BlockSpec((piece, D), lambda i: (i, 0))] * 2
            + [pl.BlockSpec((narrow, D), lambda i: (wide // narrow, 0))] * 2,
            out_specs=[
                pl.BlockSpec((1, rows_home, 2 * FF), lambda i: (i, 0, 0)),
                pl.BlockSpec((1, rows_home, rest), lambda i: (i, 0, 0)),
                pl.BlockSpec((narrow, D), lambda i: (0, 0)),
            ],
            out_shape=[
                jax.ShapeDtypeStruct((planes, rows_home, 2 * FF), bf16),
                jax.ShapeDtypeStruct((planes, rows_home, rest), bf16),
                jax.ShapeDtypeStruct((narrow, D), f32),
            ],
            cost_estimate=pl.CostEstimate(flops=0, bytes_accessed=2**24, transcendentals=0),
            compiler_params=pltpu.CompilerParams(vmem_limit_bytes=48 * 2**20),
        )(gate_up, came_gate_up, down, came_down, down, came_down)

    gate_up_rate = D ** (-0.5)
    down_rate = max(2, FF // 128) ** (-0.5)

    def full_kernel(home_ref, w_ref, m_ref, s_ref, *outs):
        done = adam_step(
            w_ref[0], m_ref[0], s_ref[0], home_ref[0].astype(f32), gate_up_rate, weight_decay
        )
        for ref, value in zip(outs, done):
            ref[0] = value

    def spare_kernel(home_ref, w_ref, m_ref, s_ref, a_ref, b_ref, c_ref, *outs):
        for s in range(spare):

            @pl.when(pl.program_id(0) == s)
            def _():
                grad = jnp.concatenate(
                    [
                        lanes(home_ref[p], g * narrow_pad + s * piece)
                        for g in range(2)
                        for p in range(planes)
                    ],
                    axis=1,
                ).astype(f32)
                done = adam_step(w_ref[0], m_ref[0], s_ref[0], grad, gate_up_rate, weight_decay)
                for ref, value in zip(outs, done):
                    ref[0] = value

    def down_kernel(home_ref, low_ref, w_ref, m_ref, s_ref, *outs):
        def update(grad):
            done = adam_step(w_ref[0], m_ref[0], s_ref[0], grad, down_rate, weight_decay)
            for ref, value in zip(outs, done):
                ref[0] = value

        @pl.when(pl.program_id(0) < planes)
        def _():
            update(
                jnp.concatenate(
                    [
                        home_ref[0, pl.ds(j * piece, piece), pl.ds(2 * narrow_pad, wide)]
                        for j in range(across)
                    ],
                    axis=1,
                ).astype(f32)
            )

        @pl.when(pl.program_id(0) >= planes)
        def _():
            update(low_ref[...])

    def update_experts(home_full, home_rest, low, gate_up, down):
        if not whole:
            grad = join_spare(home_rest).astype(f32)
            return (
                adam_step(*gate_up, grad, gate_up_rate, weight_decay),
                adam_step(
                    *down, low[:narrow].reshape(spare, piece, D), down_rate, weight_decay
                ),
            )
        params = pltpu.CompilerParams(vmem_limit_bytes=48 * 2**20)
        shapes = [jax.ShapeDtypeStruct(gate_up[0].shape, f32)] * 3
        one = pl.BlockSpec((1, rows_home, 2 * FF), lambda i: (i, 0, 0))
        last = pl.BlockSpec((1, rows_home, 2 * FF), lambda i: (planes + i, 0, 0))
        new_gate_up = pl.pallas_call(
            full_kernel,
            grid=(planes,),
            in_specs=[one] * 4,
            out_specs=[one] * 3,
            cost_estimate=pl.CostEstimate(flops=0, bytes_accessed=2**25, transcendentals=0),
            out_shape=shapes,
            compiler_params=params,
        )(home_full, *gate_up)
        new_gate_up = pl.pallas_call(
            spare_kernel,
            grid=(spare,),
            in_specs=[pl.BlockSpec((planes, rows_home, 2 * narrow_pad), lambda i: (0, 0, 0))]
            + [last] * 3
            + [pl.BlockSpec(memory_space=pl.ANY)] * 3,
            out_specs=[last] * 3,
            out_shape=shapes,
            input_output_aliases={4: 0, 5: 1, 6: 2},
            compiler_params=params,
        )(home_rest, *gate_up, *new_gate_up)
        row = pl.BlockSpec((1, piece, D), lambda i: (i, 0, 0))
        new_down = pl.pallas_call(
            down_kernel,
            grid=(per_group,),
            in_specs=[
                pl.BlockSpec((1, rows_home, rest), lambda i: (jnp.minimum(i, planes - 1), 0, 0)),
                pl.BlockSpec((piece, D), lambda i: (jnp.maximum(i - planes, 0), 0)),
            ]
            + [row] * 3,
            out_specs=[row] * 3,
            cost_estimate=pl.CostEstimate(flops=0, bytes_accessed=2**24, transcendentals=0),
            out_shape=[jax.ShapeDtypeStruct(down[0].shape, f32)] * 3,
            compiler_params=params,
        )(home_rest, low, *down)
        return new_gate_up, new_down

    def unit_experts(group, place):
        base = group * per_group
        sets = []
        if whole:
            sets.append(jnp.full((wide,), base + place))
        behind = base + whole * planes + jnp.arange(narrow_pad) // piece
        sets.append(jnp.where(jnp.arange(narrow_pad) < narrow, behind, -1))
        return jnp.concatenate(sets)

    def columns_of():
        pieces = []
        for first in range(0, wide, 256):
            pieces.append((first, wide + first, first, min(256, wide - first)))
        pieces.append((2 * wide, 2 * wide + narrow_pad, wide, narrow_pad))
        return pieces

    def expert_kernel(first_call, *refs):
        rows_ref, gates_ref = refs[:2]
        reaches, weights = refs[2:4], refs[4:6]
        twice_ref, once_ref = refs[6:8]
        gated_ref, grad_ref, two_ref = refs[8 + (0 if first_call else 2) :]
        blocks, rows_of, _ = rows_ref.shape
        count = blocks * rows_of
        rows = rows_ref[...].reshape(count, D)
        gates = gates_ref[...].reshape(count, LANES)
        dgate = jnp.zeros((count, LANES), f32)
        for k in range(2):
            for gate_at, up_at, unit_at, width in columns_of():
                unit = pl.ds(k * units + unit_at, width)
                gate_w = weights[k][:, pl.ds(gate_at, width)]
                up_w = weights[k][:, pl.ds(up_at, width)]
                gate_part = jnp.dot(rows, gate_w, preferred_element_type=f32)
                up_part = jnp.dot(rows, up_w, preferred_element_type=f32)
                gate_wide = jnp.dot(gates, twice_ref[:, unit], preferred_element_type=f32)
                reach = reaches[k][:, :, pl.ds(unit_at, width)].reshape(count, width)
                reach = residual_scale * reach
                squash = 1.0 / (1.0 + jnp.exp(-gate_part))
                swish = gate_part * squash
                hidden = swish * up_part
                gated = (hidden * gate_wide).astype(bf16)
                gated_ref[:, :, unit] = gated.reshape(blocks, rows_of, width)
                dgate += dot_nt((hidden * reach).astype(bf16), once_ref[:, unit])
                grad_hidden = reach * gate_wide
                grad_gate = grad_hidden * up_part * squash * (1.0 + gate_part * (1.0 - squash))
                for at, value in ((gate_at, grad_gate), (up_at, grad_hidden * swish)):
                    grad_ref[:, :, pl.ds(k * 2 * units + at, width)] = value.astype(bf16).reshape(
                        blocks, rows_of, width
                    )
        two = jnp.zeros((count, D), f32)
        for k in range(2):
            grad = grad_ref[:, :, pl.ds(k * 2 * units, 2 * units)].reshape(count, 2 * units)
            two += dot_nt(grad, weights[k][...])
        two_ref[:, :, pl.ds(0, D)] = two.astype(bf16).reshape(blocks, rows_of, D)
        two_ref[:, :, pl.ds(D, LANES)] = dgate.astype(bf16).reshape(blocks, rows_of, LANES)

    def run_experts(at, sent, reach, own, other, twice, once, before):
        blocks, rows_of, _ = sent.shape
        rows_of = rows_of // 2
        tile = max(1, 512 // rows_of)

        def by_rows(columns, column=0):
            return pl.BlockSpec((tile, rows_of, columns), lambda i: (i, at, column))

        def fixed(rows, columns):
            return pl.BlockSpec((rows, columns), lambda i: (0, 0), pipeline_mode=pl.Buffered(1))

        kept = list(before) if before else []
        count = blocks * rows_of
        return pl.pallas_call(
            functools.partial(expert_kernel, not kept),
            grid=(blocks // tile,),
            in_specs=[by_rows(D), by_rows(LANES, D // LANES)]
            + [by_rows(units)] * 2
            + [fixed(D, 2 * units)] * 2
            + [fixed(LANES, 2 * units)] * 2
            + [pl.BlockSpec(memory_space=pl.ANY)] * len(kept),
            out_specs=[
                by_rows(2 * units),
                by_rows(4 * units),
                pl.BlockSpec((tile, rows_of, D + LANES), lambda i: (i, 0, 0)),
            ],
            out_shape=[
                jax.ShapeDtypeStruct((blocks, 2 * rows_of, 2 * units), bf16),
                jax.ShapeDtypeStruct((blocks, 2 * rows_of, 4 * units), bf16),
                jax.ShapeDtypeStruct((blocks, rows_of, D + LANES), bf16),
            ],
            input_output_aliases={8 + i: i for i in range(len(kept))},
            cost_estimate=pl.CostEstimate(
                flops=16 * count * D * units, bytes_accessed=2**25, transcendentals=2 * count * units
            ),
            compiler_params=pltpu.CompilerParams(vmem_limit_bytes=60 * 2**20),
        )(sent, sent, *reach, own, other, twice, once, *kept)

    def shards(
        tokens,
        cotangent,
        routes,
        weight_qkv,
        moment_qkv,
        square_qkv,
        weight_out,
        moment_out,
        square_out,
        weight_router,
        moment_router,
        square_router,
        gains,
        moment_gains,
        square_gains,
        weight_gate_up,
        moment_gate_up,
        square_gate_up,
        weight_down,
        moment_down,
        square_down,
    ):
        sequence_length = tokens.shape[0]
        head_groups = QUERY_HEADS // KEY_VALUE_HEADS
        place = lax.axis_index(PLANE)
        group = lax.axis_index("y") * 2 + lax.axis_index("core")
        partner = lax.axis_index("y") * 2 + 1 - lax.axis_index("core")

        small = pad_lanes(jnp.concatenate([weight_router, gains.T], axis=1))
        first_pack = jnp.concatenate([weight_qkv, small], axis=1).astype(bf16)
        first_all = lax.all_gather(first_pack, ALL, axis=0, tiled=True)

        packed, low_own = pack_experts(weight_gate_up, weight_down)
        chip = chip_half(weight_out.astype(bf16))
        chip_rows = chip.size // D
        line = line_of(jnp.concatenate([chip.reshape(chip_rows, D), cotangent], axis=0))
        own = all_to_all_plane(after(packed, line[-1])).reshape(D, -1)
        out_mine, out_other = gather_halves([b[:chip_rows].reshape(chip.shape) for b in line])
        cot_all = gather_tokens([b[chip_rows:] for b in line])
        order = row_order()

        qkv_w = first_all[:, :QKV]
        router_w = first_all[:, QKV : QKV + EXPERTS]
        gain_one = first_all[:, QKV + EXPERTS].astype(f32)
        gain_two = first_all[:, QKV + EXPERTS + 1].astype(f32)

        inputs = tokens.astype(f32)
        factor_one = lax.rsqrt(jnp.mean(inputs * inputs, axis=-1, keepdims=True) + norm_eps)
        hidden_one = (inputs * factor_one * gain_one).astype(bf16)
        joined_heads = dot(hidden_one, qkv_w)
        hidden_here = dot(hidden_one, order).astype(bf16)
        query_rows = joined_heads[:, :HEADS_WIDTH].reshape(sequence_length, QUERY_HEADS, HEAD_SIZE)
        every_key = joined_heads[:, HEADS_WIDTH : HEADS_WIDTH + KEYS_WIDTH].reshape(
            sequence_length, KEY_VALUE_HEADS, HEAD_SIZE
        )
        every_value = joined_heads[:, HEADS_WIDTH + KEYS_WIDTH :].reshape(
            sequence_length, KEY_VALUE_HEADS, HEAD_SIZE
        )
        cosine_lookup, sine_lookup = rotary_tables(sequence_length, HEAD_SIZE)
        query_rotated = (
            apply_rotation(query_rows, cosine_lookup, sine_lookup)
            .astype(bf16)
            .reshape(sequence_length, KEY_VALUE_HEADS, head_groups, HEAD_SIZE)
        )
        key_rot = apply_rotation(every_key, cosine_lookup, sine_lookup).astype(bf16)
        value_low = every_value.astype(bf16)
        causal = jnp.arange(sequence_length)[:, None] >= jnp.arange(sequence_length)[None, :]
        scores = attention_scores(query_rotated, key_rot, causal)
        peak = jnp.max(scores, axis=-1, keepdims=True)
        expo = jnp.exp(scores - peak)
        totals = jnp.sum(expo, axis=-1, keepdims=True)
        probs = expo / totals
        prob_low = probs.astype(bf16)
        heads = jnp.einsum("kgst,tkd->skgd", prob_low, value_low, preferred_element_type=f32)
        attended = heads.reshape(sequence_length, HEADS_WIDTH).astype(bf16)
        core = lax.axis_index("core")
        attended = dot(attended, order).astype(bf16)
        projected = [dot(attended, out_mine), dot(attended, out_other)]
        mid = inputs + residual_scale * jnp.where(
            core == 0,
            jnp.concatenate(projected, axis=1),
            jnp.concatenate(projected[::-1], axis=1),
        )
        factor_two = lax.rsqrt(jnp.mean(mid * mid, axis=-1, keepdims=True) + norm_eps)
        hidden_two = (mid * factor_two * gain_two).astype(bf16)
        logits = dot(hidden_two, router_w)
        named = jnp.any(
            routes[..., None] == jnp.arange(EXPERTS, dtype=routes.dtype)[None, None, :], axis=1
        )
        shown = jnp.where(named, logits, -jnp.inf)
        raised = jnp.exp(shown - jnp.max(shown, axis=-1, keepdims=True))
        gates = raised / jnp.sum(raised, axis=-1, keepdims=True)

        gate_high = gates.astype(bf16)
        gate_rest = (gates - gate_high.astype(f32)).astype(bf16)
        sent = jnp.concatenate(
            [hidden_two, pad_lanes(jnp.concatenate([gate_high, gate_rest], axis=1))], axis=1
        )
        sent_all = gather_tokens(line_of(sent))
        own = after(own, sent)
        other, low_other = swap_core(own), swap_core(low_own)
        down_own, down_other = down_of(own, low_own), down_of(other, low_other)
        blocks = 2 * nx * ny
        reach = [dot_nt(cot_all, d).reshape(blocks, -1, units) for d in (down_own, down_other)]

        behind = jnp.concatenate([unit_experts(group, place), unit_experts(partner, place)])
        numbers = jnp.arange(LANES)[:, None]
        real = behind[None, :] >= 0
        once = ((numbers == behind[None, :]) & real).astype(bf16)
        twice = once + ((numbers == behind[None, :] + EXPERTS) & real).astype(bf16)
        kept = None
        firsts = []
        sent_blocks = sent_all.reshape(blocks, -1, sent_all.shape[1])
        for at in range(2):
            *kept, two = run_experts(at, sent_blocks, reach, own, other, twice, once, kept)
            firsts.append(scatter_first(two))
        two_sum = sum_line(scatter_second(firsts))

        gated, grad_both = (k.reshape(-1, k.shape[2]) for k in kept)
        gated, grad_both = after(gated, *firsts[-1], always=True), after(grad_both, *firsts[-1])
        rows_all = after(sent_all, *firsts[-1], always=True)[:, :D]
        mixed = (dot(gated[:, :units], down_own) + dot(gated[:, units:], down_other)).astype(bf16)
        mixed = after(mixed, two_sum, always=True).reshape(blocks, -1, D)
        mixed = sum_line(scatter_second([scatter_first(mixed)]))
        layer_out = (mid + residual_scale * mixed).astype(bf16)

        came_gate_up = swap_core(dot_tn(rows_all, grad_both[:, 2 * units :]).astype(bf16))
        came_down = swap_core(dot_tn(gated[:, units:], cot_all).astype(bf16))
        full, more, low = combine_grads(
            dot_tn(rows_all, grad_both[:, : 2 * units]).astype(bf16),
            came_gate_up,
            dot_tn(gated[:, :units], cot_all).astype(bf16),
            came_down,
        )
        home_full = all_to_all_plane(after(full, two_sum)) if whole else None
        home_rest = all_to_all_plane(after(more, two_sum))
        two_sum = after(two_sum, low)
        grad_two, grad_gates = two_sum[:, :D], two_sum[:, D : D + EXPERTS]

        grad_out = cotangent.astype(f32)
        grad_chosen = gates * (grad_gates - jnp.sum(gates * grad_gates, axis=-1, keepdims=True))
        grad_logits = grad_chosen.astype(bf16)
        grad_router = dot_tn(hidden_two, grad_logits)
        grad_two = grad_two + dot_nt(grad_logits, router_w)
        grad_mid, grad_gain_two = norm_backward(grad_two, mid, factor_two, gain_two)
        grad_mid = grad_out + grad_mid
        grad_att = (residual_scale * grad_mid).astype(bf16)
        att_left, att_right = grad_att[:, : D // 2], grad_att[:, D // 2 :]
        grad_heads = (
            (
                dot_nt(jnp.where(core == 0, att_left, att_right), out_mine)
                + dot_nt(jnp.where(core == 0, att_right, att_left), out_other)
            )
            .astype(bf16)
        )
        grad_heads = (
            dot_nt(grad_heads, order)
            .astype(bf16)
            .reshape(sequence_length, KEY_VALUE_HEADS, head_groups, HEAD_SIZE)
        )
        out_first = scatter_halves_first(
            dot_tn(attended, att_left).astype(bf16), dot_tn(attended, att_right).astype(bf16)
        )
        out_left, out_right = scatter_halves_second(out_first)
        grad_probs = jnp.einsum(
            "skgd,tkd->kgst", grad_heads, value_low, preferred_element_type=f32
        )
        value_gradient = jnp.einsum(
            "kgst,skgd->tkd", prob_low, grad_heads, preferred_element_type=f32
        )
        row_dot = jnp.sum(probs * grad_probs, axis=-1, keepdims=True)
        grad_scores = (probs * (grad_probs - row_dot)).astype(bf16)
        grad_qrot = (
            jnp.einsum("kgst,tkd->skgd", grad_scores, key_rot, preferred_element_type=f32)
            * score_scale
        )
        grad_krot = (
            jnp.einsum("kgst,skgd->tkd", grad_scores, query_rotated, preferred_element_type=f32)
            * score_scale
        )
        grad_queries = apply_rotation(
            grad_qrot.reshape(sequence_length, QUERY_HEADS, HEAD_SIZE), cosine_lookup, -sine_lookup
        )
        key_gradient = apply_rotation(grad_krot, cosine_lookup, -sine_lookup)
        grad_joined = jnp.concatenate(
            [
                grad_queries.reshape(sequence_length, HEADS_WIDTH),
                key_gradient.reshape(sequence_length, KEYS_WIDTH),
                value_gradient.reshape(sequence_length, KEYS_WIDTH),
            ],
            axis=1,
        ).astype(bf16)
        grad_one = dot_nt(grad_joined, qkv_w)
        grad_inputs, grad_gain_one = norm_backward(grad_one, inputs, factor_one, gain_one)
        token_grad = grad_mid + grad_inputs
        small_sent = pad_lanes(
            jnp.concatenate([grad_router, grad_gain_one[:, None], grad_gain_two[:, None]], axis=1)
        )
        small_sent = dot_tn(order, small_sent.astype(bf16))
        qkv_first = scatter_halves_first(
            after(
                jnp.concatenate(
                    [dot_tn(hidden_here, grad_joined[:, : QKV // 2]), small_sent], axis=1
                ).astype(bf16),
                out_first,
                home_full,
            ),
            jnp.concatenate(
                [dot_tn(hidden_here, grad_joined[:, QKV // 2 :]), jnp.zeros_like(small_sent)], axis=1
            ).astype(bf16),
        )
        qkv_left, qkv_right = scatter_halves_second(qkv_first)
        sum_out = jnp.concatenate([out_left, out_right], axis=1)
        sum_qkv = jnp.concatenate([qkv_left[:, : QKV // 2], qkv_right[:, : QKV // 2]], axis=1)
        sum_router = qkv_left[:, QKV // 2 : QKV // 2 + EXPERTS]
        sum_gains = qkv_left[:, QKV // 2 + EXPERTS : QKV // 2 + EXPERTS + 2].T

        new_gate_up, new_down = update_experts(
            home_full,
            home_rest,
            low,
            (weight_gate_up, moment_gate_up, square_gate_up),
            (weight_down, moment_down, square_down),
        )
        new_qkv = adam_step(weight_qkv, moment_qkv, square_qkv, sum_qkv, D ** (-0.5), weight_decay)
        new_out = adam_step(
            weight_out,
            moment_out,
            square_out,
            sum_out,
            max(4, QUERY_HEADS * HEAD_SIZE // 256) ** (-0.5),
            weight_decay,
        )
        new_router = adam_step(
            weight_router, moment_router, square_router, sum_router, (4 * D) ** (-0.5), weight_decay
        )
        new_gains = adam_step(gains, moment_gains, square_gains, sum_gains, 0.75, 0.0)
        return (
            layer_out,
            token_grad,
            *new_qkv,
            *new_out,
            *new_router,
            *new_gains,
            *new_gate_up,
            *new_down,
        )

    return shards


def solution(mesh):
    n_dp, n_expert = mesh.shape["dp"], mesh.shape["expert"]
    nz = 4
    nx, ny = n_dp // nz, n_expert // 2
    fine = Mesh(mesh.devices.reshape(nz, nx, ny, 2), ALL)
    rows = P(ALL, None)
    columns = P(None, ALL)
    experts = P(("y", "core"), ("z", "x"), None)
    dense = (rows,) * 9 + (columns,) * 3 + (experts,) * 6
    return jax.shard_map(
        make_shards((nz, nx, ny)),
        mesh=fine,
        in_specs=(rows,) * 3 + dense,
        out_specs=(rows,) * 2 + dense,
        check_vma=False,
    )
```

```python
import functools

import jax
import jax.numpy as jnp
import numpy as np
from jax import lax
from jax.experimental import pallas as pl
from jax.experimental.pallas import tpu as pltpu
from jax.sharding import Mesh, PartitionSpec as P

D = 1536
QUERY_HEADS = 24
KEY_VALUE_HEADS = 8
HEAD_SIZE = 64
FF = 512
EXPERTS = 40
TOPK = 8
STEP = 10
QKV = 2560
LANES = 128
HEADS_WIDTH = QUERY_HEADS * HEAD_SIZE
KEYS_WIDTH = KEY_VALUE_HEADS * HEAD_SIZE

norm_eps = 1e-06
residual_scale = 0.22
score_scale = 0.125
beta_one = 0.9
beta_two = 0.95
adam_eps = 1e-08
weight_decay = 0.1

f32 = jnp.float32
bf16 = jnp.bfloat16
ALL = ("z", "x", "y", "core")
PLANE = ("z", "x")


def rotary_tables(sequence_length, size):
    half = size // 2
    places = jnp.arange(sequence_length).astype(f32)[:, None]
    inverse = 10000.0 ** (-jnp.arange(half).astype(f32) * 2.0 / size)
    angles = places * inverse[None, :]
    return (jnp.cos(angles)[:, None, :], jnp.sin(angles)[:, None, :])


def apply_rotation(values, cosine_lookup, sine_lookup):
    half = values.shape[-1] // 2
    first = values[..., :half]
    second = values[..., half:]
    return jnp.concatenate(
        [
            first * cosine_lookup - second * sine_lookup,
            second * cosine_lookup + first * sine_lookup,
        ],
        axis=-1,
    )


def attention_scores(query_rotated, key_rot, causal):
    scores = (
        jnp.einsum("skgd,tkd->kgst", query_rotated, key_rot, preferred_element_type=f32)
        * score_scale
    )
    return jnp.where(causal, scores, -1e30)


def norm_backward(grad_normed, values, factor, gain):
    scaled = grad_normed * gain
    grad_gain = jnp.sum(grad_normed * values * factor, axis=0)
    value_gradient = factor * scaled - values * factor * factor * factor * jnp.mean(
        scaled * values, axis=-1, keepdims=True
    )
    return (value_gradient, grad_gain)


def adam_step(weight, moment, square, grad, rate, decay):
    moment = beta_one * moment + (1.0 - beta_one) * grad
    square = beta_two * square + (1.0 - beta_two) * grad * grad
    fixed_one = moment / (1.0 - beta_one**STEP)
    fixed_two = square / (1.0 - beta_two**STEP)
    weight = weight - rate * (fixed_one / (jnp.sqrt(fixed_two) + adam_eps) + decay * weight)
    return (weight, moment, square)


def dot(a, b):
    return jnp.dot(a, b, preferred_element_type=f32)


def dot_nt(a, b):
    return lax.dot_general(a, b, (((1,), (1,)), ((), ())), preferred_element_type=f32)


def dot_tn(a, b):
    return lax.dot_general(a, b, (((0,), (0,)), ((), ())), preferred_element_type=f32)


def pad_lanes(values):
    extra = -values.shape[-1] % LANES
    return jnp.pad(values, ((0, 0), (0, extra)))


def swap_core(values):
    return lax.ppermute(values, "core", [(0, 1), (1, 0)])


def keep_kernel(*refs):
    pass


def ring_order(n):
    return [0] + list(range(1, n, 2)) + list(range(n - 2 + n % 2, 0, -2))


def home_table(n):
    order = ring_order(n)
    place = {chip: at for at, chip in enumerate(order)}
    return np.array([[order[(place[i] - s) % n] for s in range(n)] for i in range(n)], np.int32)


def make_shards(sizes):
    nz, nx, ny = sizes
    length = {"z": nz, "x": nx, "y": ny}
    planes = nz * nx
    per_group = EXPERTS // (2 * ny)
    whole = per_group // planes
    spare = per_group - whole * planes
    piece = FF // planes
    wide = whole * FF
    narrow = spare * piece
    narrow_pad = narrow + -narrow % LANES
    units = wide + narrow_pad

    rings = {axis: ring_order(n) for axis, n in length.items()}
    places = {axis: i for i, axis in enumerate(("z", "x", "y", "core"))}
    shape = (nz, nx, ny, 2)

    def pairs_of(axes, step):
        pairs = []
        for at in np.ndindex(*shape):
            axis = axes[at[3]]
            ring = rings[axis]
            to = list(at)
            to[places[axis]] = ring[(ring.index(at[places[axis]]) + step) % len(ring)]
            pairs.append(
                (int(np.ravel_multi_index(at, shape)), int(np.ravel_multi_index(to, shape)))
            )
        return pairs

    def move(values, axes, step):
        return lax.ppermute(values, ALL, pairs_of(axes, step))

    def row_order(core):
        found = {}
        for axis, n in length.items():
            here = jnp.arange(n)[:, None] == lax.axis_index(axis)
            found[axis] = jnp.sum(jnp.where(here, jnp.asarray(home_table(n)), 0), axis=0)
        x = jnp.where(core == 0, found["x"][None, :], found["x"][:, None])
        y = jnp.where(core == 0, found["y"][:, None], found["y"][None, :])
        chip = (found["z"] * nx + x[:, :, None]) * ny + y[:, :, None]
        block = (chip[..., None] * 2 + jnp.arange(2)).reshape(-1, 1)
        rows = D // block.shape[0]
        kept = (block * rows + jnp.arange(rows)[None, :]).reshape(1, D)
        return (jnp.arange(D)[:, None] == kept).astype(bf16)

    def add_low(a, b):
        return (a.astype(f32) + b.astype(f32)).astype(bf16)

    parts = ((0, "x", "y"), (1, "y", "x"))

    def line_of(own):
        line = [own]
        for _ in range(nz - 1):
            line.append(move(line[-1], "zz", 1))
        return line

    def gather_tokens(line, late=None):
        half = line[0].shape[0] // 2
        packs = [
            jnp.concatenate([b[part * half : (part + 1) * half] for b in line], axis=0)
            for part, _, _ in parts
        ]
        for level in (1, 2):
            grown = []
            if level == 2 and late is not None:
                packs = [after(p, late) for p in packs]
            for pack, names in zip(packs, parts):
                axis = names[level]
                steps = [pack]
                for _ in range(length[axis] - 1):
                    steps.append(move(steps[-1], axis * 2, 1))
                grown.append(jnp.concatenate(steps, axis=0))
            packs = grown
        return jnp.concatenate(packs, axis=0)

    def sum_level(packs, level):
        summed = []
        for pack, names in zip(packs, parts):
            n = length[names[level]]
            pack = pack.reshape(n, pack.shape[0] // n, *pack.shape[1:])
            acc = None
            for s in reversed(range(n)):
                acc = pack[s] if acc is None else add_low(move(acc, names[level] * 2, -1), pack[s])
            summed.append(acc)
        return summed

    def scatter_first(values):
        count = values.shape[0] // 2
        return sum_level([values[:count], values[count:]], 2)

    def scatter_second(halves):
        packs = [jnp.concatenate(same, axis=1) for same in zip(*halves)]
        packs = [p[0] for p in sum_level(packs, 1)]
        half = packs[0].shape[0] // nz
        return [
            jnp.concatenate([p[s * half : (s + 1) * half] for p in packs], axis=0)
            for s in range(nz)
        ]

    def sum_line(blocks):
        total = blocks[-1]
        for mine in reversed(blocks[:-1]):
            total = add_low(move(total, "zz", -1), mine)
        return total.astype(f32)

    def chip_half(own):
        half = own.shape[1] // 2
        core = lax.axis_index("core")
        left, right = own[:, :half], own[:, half:]
        kept = jnp.where(core == 0, left, right)
        came = swap_core(jnp.where(core == 0, right, left))
        return jnp.where(
            core == 0, jnp.concatenate([kept, came], axis=0), jnp.concatenate([came, kept], axis=0)
        )

    def gather_halves(line):
        rows, half = line[0].shape
        steps = [jnp.concatenate(line, axis=0)]
        for _ in range(nx - 1):
            steps.append(move(steps[-1], "xy", 1))
        packs = [jnp.concatenate(steps, axis=0)]
        for _ in range(nx - 1):
            packs.append(move(packs[-1], "yx", 1))
        result = jnp.concatenate(packs, axis=0)
        return result, swap_core(result)

    def scatter_halves_first(mine, other):
        both = add_low(swap_core(other), mine)
        grid = both.reshape(nx, nx, both.shape[0] // (nx * nx), both.shape[1])
        acc = None
        for s in reversed(range(nx)):
            acc = grid[s] if acc is None else add_low(move(acc, "yx", -1), grid[s])
        return acc

    def scatter_halves_second(acc, *late):
        core = lax.axis_index("core")
        rows = acc.shape[1] // (nz * 2)
        two = None
        for s in reversed(range(nx)):
            two = acc[s] if two is None else add_low(move(two, "xy", -1), acc[s])
        two = after(two, *late)
        total = None
        for s in reversed(range(nz)):
            mine = two[s * 2 * rows : (s + 1) * 2 * rows]
            total = mine if total is None else add_low(move(total, "zz", -1), mine)
        kept = jnp.where(core == 0, total[:rows], total[rows:])
        came = swap_core(jnp.where(core == 0, total[rows:], total[:rows]))
        return (
            jnp.where(core == 0, kept, came).astype(f32),
            jnp.where(core == 0, came, kept).astype(f32),
        )

    def after(values, *first, always=False):
        if not (whole or always):
            return values
        anywhere = pl.BlockSpec(memory_space=pl.ANY)
        return pl.pallas_call(
            keep_kernel,
            in_specs=[anywhere] * (1 + len(first)),
            out_specs=anywhere,
            out_shape=jax.ShapeDtypeStruct(values.shape, values.dtype),
            input_output_aliases={0: 0},
        )(values, *first)

    def all_to_all_plane(values):
        return lax.all_to_all(values, PLANE, split_axis=0, concat_axis=0, tiled=True)

    rows_home = D // planes
    across = rows_home // piece
    rest = 2 * narrow_pad + wide

    def cut_spare(part):
        part = part.reshape(spare, rows_home, 2, planes, piece)
        part = part.transpose(3, 1, 2, 0, 4).reshape(planes, rows_home, 2, narrow)
        part = jnp.pad(part, ((0, 0), (0, 0), (0, 0), (0, narrow_pad - narrow)))
        return part.reshape(planes, rows_home, 2 * narrow_pad)

    def join_spare(part):
        part = part.reshape(planes, rows_home, 2, narrow_pad)[..., :narrow]
        part = part.reshape(planes, rows_home, 2, spare, piece).transpose(3, 1, 2, 0, 4)
        return part.reshape(spare, rows_home, 2 * FF)

    def lanes(values, first, width=piece):
        return values[:, first : first + width]

    def pack_kernel(gate_up_ref, spare_ref, down_ref, spare_down_ref, full_ref, rest_ref, low_ref):
        step = pl.program_id(0)
        full_ref[0] = gate_up_ref[0].astype(bf16)
        for j in range(across):
            rest_ref[step, pl.ds(j * piece, piece), pl.ds(2 * narrow_pad, wide)] = down_ref[
                0, :, pl.ds(j * wide, wide)
            ].astype(bf16)

        @pl.when(step == 0)
        def _():
            for to in range(planes):
                taken = [
                    lanes(spare_ref[s], g * FF + to * piece) for g in range(2) for s in range(spare)
                ]
                rest_ref[to, :, pl.ds(0, 2 * narrow)] = jnp.concatenate(taken, axis=1).astype(bf16)
            for s in range(spare):
                low_ref[pl.ds(s * piece, piece), :] = spare_down_ref[s].astype(bf16)

    def pack_experts(gate_up, down):
        if not whole:
            low = down.astype(bf16).reshape(narrow, D)
            low = jnp.pad(low, ((0, narrow_pad - narrow), (0, 0)))
            return None, cut_spare(gate_up.astype(bf16)), low
        return pl.pallas_call(
            pack_kernel,
            grid=(planes,),
            in_specs=[
                pl.BlockSpec((1, rows_home, 2 * FF), lambda i: (i, 0, 0)),
                pl.BlockSpec((spare, rows_home, 2 * FF), lambda i: (planes // spare, 0, 0)),
                pl.BlockSpec((1, piece, D), lambda i: (i, 0, 0)),
                pl.BlockSpec((spare, piece, D), lambda i: (planes // spare, 0, 0)),
            ],
            out_specs=[
                pl.BlockSpec((1, rows_home, 2 * FF), lambda i: (i, 0, 0)),
                pl.BlockSpec((planes, rows_home, rest), lambda i: (0, 0, 0)),
                pl.BlockSpec((narrow, D), lambda i: (0, 0)),
            ],
            out_shape=[
                jax.ShapeDtypeStruct((planes, rows_home, 2 * FF), bf16),
                jax.ShapeDtypeStruct((planes, rows_home, rest), bf16),
                jax.ShapeDtypeStruct((narrow, D), bf16),
            ],
            cost_estimate=pl.CostEstimate(flops=0, bytes_accessed=2**24, transcendentals=0),
            compiler_params=pltpu.CompilerParams(vmem_limit_bytes=48 * 2**20),
        )(gate_up, gate_up, down, down)

    def down_of(packed, low):
        if not whole:
            return low
        mine = packed[:, 2 * narrow_pad :].reshape(planes, across, piece, wide)
        mine = mine.transpose(0, 2, 1, 3).reshape(wide, D)
        return jnp.concatenate([mine, low], axis=0)

    def combine_kernel(a_ref, came_a_ref, b_ref, came_b_ref, c_ref, came_c_ref, full_ref, rest_ref, low_ref):
        total = a_ref[...].astype(f32) + came_a_ref[...].astype(f32)
        full_ref[0] = total[:, : 2 * wide].astype(bf16)
        rest_ref[0, :, pl.ds(0, 2 * narrow_pad)] = total[:, 2 * wide :].astype(bf16)
        total = residual_scale * (b_ref[...].astype(f32) + came_b_ref[...].astype(f32))
        for j in range(across):
            rest_ref[0, pl.ds(j * piece, piece), pl.ds(2 * narrow_pad, wide)] = total[
                :, j * wide : (j + 1) * wide
            ].astype(bf16)
        low_ref[...] = residual_scale * (c_ref[...].astype(f32) + came_c_ref[...].astype(f32))

    def combine_grads(gate_up, came_gate_up, down, came_down):
        if not whole:
            total = (gate_up.astype(f32) + came_gate_up.astype(f32)).astype(bf16)
            low = residual_scale * (down.astype(f32) + came_down.astype(f32))
            return None, total.reshape(planes, rows_home, rest), low
        return pl.pallas_call(
            combine_kernel,
            grid=(planes,),
            in_specs=[pl.BlockSpec((rows_home, 2 * units), lambda i: (i, 0))] * 2
            + [pl.BlockSpec((piece, D), lambda i: (i, 0))] * 2
            + [pl.BlockSpec((narrow, D), lambda i: (wide // narrow, 0))] * 2,
            out_specs=[
                pl.BlockSpec((1, rows_home, 2 * FF), lambda i: (i, 0, 0)),
                pl.BlockSpec((1, rows_home, rest), lambda i: (i, 0, 0)),
                pl.BlockSpec((narrow, D), lambda i: (0, 0)),
            ],
            out_shape=[
                jax.ShapeDtypeStruct((planes, rows_home, 2 * FF), bf16),
                jax.ShapeDtypeStruct((planes, rows_home, rest), bf16),
                jax.ShapeDtypeStruct((narrow, D), f32),
            ],
            cost_estimate=pl.CostEstimate(flops=0, bytes_accessed=2**24, transcendentals=0),
            compiler_params=pltpu.CompilerParams(vmem_limit_bytes=48 * 2**20),
        )(gate_up, came_gate_up, down, came_down, down, came_down)

    gate_up_rate = D ** (-0.5)
    down_rate = max(2, FF // 128) ** (-0.5)

    def full_kernel(home_ref, w_ref, m_ref, s_ref, *outs):
        outs[3][...] = jnp.zeros(outs[3].shape, f32)
        done = adam_step(
            w_ref[0], m_ref[0], s_ref[0], home_ref[0].astype(f32), gate_up_rate, weight_decay
        )
        for ref, value in zip(outs, done):
            ref[0] = value

    def spare_kernel(home_ref, w_ref, m_ref, s_ref, a_ref, b_ref, c_ref, *outs):
        for s in range(spare):

            @pl.when(pl.program_id(0) == s)
            def _():
                grad = jnp.concatenate(
                    [
                        lanes(home_ref[p], g * narrow_pad + s * piece)
                        for g in range(2)
                        for p in range(planes)
                    ],
                    axis=1,
                ).astype(f32)
                done = adam_step(w_ref[0], m_ref[0], s_ref[0], grad, gate_up_rate, weight_decay)
                for ref, value in zip(outs, done):
                    ref[0] = value

    def down_kernel(home_ref, low_ref, w_ref, m_ref, s_ref, *outs):
        def update(grad):
            done = adam_step(w_ref[0], m_ref[0], s_ref[0], grad, down_rate, weight_decay)
            for ref, value in zip(outs, done):
                ref[0] = value

        @pl.when(pl.program_id(0) < planes)
        def _():
            update(
                jnp.concatenate(
                    [
                        home_ref[0, pl.ds(j * piece, piece), pl.ds(2 * narrow_pad, wide)]
                        for j in range(across)
                    ],
                    axis=1,
                ).astype(f32)
            )

        @pl.when(pl.program_id(0) >= planes)
        def _():
            update(low_ref[...])

    def update_experts(home_full, home_rest, low, gate_up, down):
        if not whole:
            grad = join_spare(home_rest).astype(f32)
            return (
                adam_step(*gate_up, grad, gate_up_rate, weight_decay),
                adam_step(
                    *down, low[:narrow].reshape(spare, piece, D), down_rate, weight_decay
                ),
                None,
            )
        params = pltpu.CompilerParams(vmem_limit_bytes=48 * 2**20)
        shapes = [jax.ShapeDtypeStruct(gate_up[0].shape, f32)] * 3
        one = pl.BlockSpec((1, rows_home, 2 * FF), lambda i: (i, 0, 0))
        last = pl.BlockSpec((1, rows_home, 2 * FF), lambda i: (planes + i, 0, 0))
        *new_gate_up, marker = pl.pallas_call(
            full_kernel,
            grid=(planes,),
            in_specs=[one] * 4,
            out_specs=[one] * 3 + [pl.BlockSpec((8, LANES), lambda i: (0, 0))],
            cost_estimate=pl.CostEstimate(flops=0, bytes_accessed=2**25, transcendentals=0),
            out_shape=shapes + [jax.ShapeDtypeStruct((8, LANES), f32)],
            compiler_params=params,
        )(home_full, *gate_up)
        new_gate_up = pl.pallas_call(
            spare_kernel,
            grid=(spare,),
            in_specs=[pl.BlockSpec((planes, rows_home, 2 * narrow_pad), lambda i: (0, 0, 0))]
            + [last] * 3
            + [pl.BlockSpec(memory_space=pl.ANY)] * 3,
            out_specs=[last] * 3,
            out_shape=shapes,
            input_output_aliases={4: 0, 5: 1, 6: 2},
            compiler_params=params,
        )(home_rest, *gate_up, *new_gate_up)
        row = pl.BlockSpec((1, piece, D), lambda i: (i, 0, 0))
        new_down = pl.pallas_call(
            down_kernel,
            grid=(per_group,),
            in_specs=[
                pl.BlockSpec((1, rows_home, rest), lambda i: (jnp.minimum(i, planes - 1), 0, 0)),
                pl.BlockSpec((piece, D), lambda i: (jnp.maximum(i - planes, 0), 0)),
            ]
            + [row] * 3,
            out_specs=[row] * 3,
            cost_estimate=pl.CostEstimate(flops=0, bytes_accessed=2**24, transcendentals=0),
            out_shape=[jax.ShapeDtypeStruct(down[0].shape, f32)] * 3,
            compiler_params=params,
        )(home_rest, low, *down)
        return new_gate_up, new_down, marker

    def unit_experts(group, place):
        base = group * per_group
        sets = []
        if whole:
            sets.append(jnp.full((wide,), base + place))
        behind = base + whole * planes + jnp.arange(narrow_pad) // piece
        sets.append(jnp.where(jnp.arange(narrow_pad) < narrow, behind, -1))
        return jnp.concatenate(sets)

    def columns_of():
        pieces = []
        for first in range(0, wide, 256):
            pieces.append((True, first, wide + first, first, min(256, wide - first)))
        pieces.append((False, 0, narrow_pad, wide, narrow_pad))
        return pieces

    def expert_kernel(first_call, *refs):
        rows_ref, gates_ref = refs[:2]
        count = 2 if whole else 1
        reaches = refs[2:4]
        weights = (refs[4 : 4 + count], refs[4 + count : 4 + 2 * count])
        twice_ref, once_ref = refs[4 + 2 * count : 6 + 2 * count]
        gated_ref, grad_ref, two_ref = refs[6 + 2 * count + (0 if first_call else 2) :]
        blocks, rows_of, _ = rows_ref.shape
        count = blocks * rows_of
        rows = rows_ref[...].reshape(count, D)
        gates = gates_ref[...].reshape(count, LANES)
        dgate = jnp.zeros((count, LANES), f32)
        for k in range(2):
            for in_full, gate_at, up_at, unit_at, width in columns_of():
                held = weights[k][0 if in_full else -1]
                unit = pl.ds(k * units + unit_at, width)
                base = k * 2 * units + (0 if in_full else 2 * wide)
                gate_w = held[:, pl.ds(gate_at, width)]
                up_w = held[:, pl.ds(up_at, width)]
                gate_part = jnp.dot(rows, gate_w, preferred_element_type=f32)
                up_part = jnp.dot(rows, up_w, preferred_element_type=f32)
                gate_wide = jnp.dot(gates, twice_ref[:, unit], preferred_element_type=f32)
                reach = reaches[k][:, :, pl.ds(unit_at, width)].reshape(count, width)
                reach = residual_scale * reach
                squash = 1.0 / (1.0 + jnp.exp(-gate_part))
                swish = gate_part * squash
                hidden = swish * up_part
                gated = (hidden * gate_wide).astype(bf16)
                gated_ref[:, :, unit] = gated.reshape(blocks, rows_of, width)
                dgate += dot_nt((hidden * reach).astype(bf16), once_ref[:, unit])
                grad_hidden = reach * gate_wide
                grad_gate = grad_hidden * up_part * squash * (1.0 + gate_part * (1.0 - squash))
                for at, value in ((gate_at, grad_gate), (up_at, grad_hidden * swish)):
                    grad_ref[:, :, pl.ds(base + at, width)] = value.astype(bf16).reshape(
                        blocks, rows_of, width
                    )
        two = jnp.zeros((count, D), f32)
        for k in range(2):
            at = k * 2 * units
            if whole:
                grad = grad_ref[:, :, pl.ds(at, 2 * wide)].reshape(count, 2 * wide)
                two += dot_nt(grad, weights[k][0][...])
            grad = grad_ref[:, :, pl.ds(at + 2 * wide, 2 * narrow_pad)]
            two += dot_nt(grad.reshape(count, 2 * narrow_pad), weights[k][-1][...])
        two_ref[:, :, pl.ds(0, D)] = two.astype(bf16).reshape(blocks, rows_of, D)
        two_ref[:, :, pl.ds(D, LANES)] = dgate.astype(bf16).reshape(blocks, rows_of, LANES)

    def run_experts(at, sent, reach, own, other, twice, once, before):
        blocks, rows_of, _ = sent.shape
        rows_of = rows_of // 2
        tile = max(1, 512 // rows_of)

        def by_rows(columns, column=0):
            return pl.BlockSpec((tile, rows_of, columns), lambda i: (i, at, column))

        def fixed(rows, columns):
            return pl.BlockSpec((rows, columns), lambda i: (0, 0), pipeline_mode=pl.Buffered(1))

        held = []
        for full, more in (own, other):
            if whole:
                held.append((full, fixed(D, 2 * wide)))
            held.append((more, fixed(D, 2 * narrow_pad)))
        kept = list(before) if before else []
        count = blocks * rows_of
        return pl.pallas_call(
            functools.partial(expert_kernel, not kept),
            grid=(blocks // tile,),
            in_specs=[by_rows(D), by_rows(LANES, D // LANES)]
            + [by_rows(units)] * 2
            + [spec for _, spec in held]
            + [fixed(LANES, 2 * units)] * 2
            + [pl.BlockSpec(memory_space=pl.ANY)] * len(kept),
            out_specs=[
                by_rows(2 * units),
                by_rows(4 * units),
                pl.BlockSpec((tile, rows_of, D + LANES), lambda i: (i, 0, 0)),
            ],
            out_shape=[
                jax.ShapeDtypeStruct((blocks, 2 * rows_of, 2 * units), bf16),
                jax.ShapeDtypeStruct((blocks, 2 * rows_of, 4 * units), bf16),
                jax.ShapeDtypeStruct((blocks, rows_of, D + LANES), bf16),
            ],
            input_output_aliases={6 + len(held) + i: i for i in range(len(kept))},
            cost_estimate=pl.CostEstimate(
                flops=16 * count * D * units, bytes_accessed=2**25, transcendentals=2 * count * units
            ),
            compiler_params=pltpu.CompilerParams(vmem_limit_bytes=60 * 2**20),
        )(sent, sent, *reach, *[w for w, _ in held], twice, once, *kept)

    def shards(
        tokens,
        cotangent,
        routes,
        weight_qkv,
        moment_qkv,
        square_qkv,
        weight_out,
        moment_out,
        square_out,
        weight_router,
        moment_router,
        square_router,
        gains,
        moment_gains,
        square_gains,
        weight_gate_up,
        moment_gate_up,
        square_gate_up,
        weight_down,
        moment_down,
        square_down,
    ):
        sequence_length = tokens.shape[0]
        head_groups = QUERY_HEADS // KEY_VALUE_HEADS
        place = lax.axis_index(PLANE)
        group = lax.axis_index("y") * 2 + lax.axis_index("core")
        partner = lax.axis_index("y") * 2 + 1 - lax.axis_index("core")

        small = pad_lanes(jnp.concatenate([weight_router, gains.T], axis=1))
        first_pack = jnp.concatenate([weight_qkv, small], axis=1).astype(bf16)
        first_all = lax.all_gather(first_pack, ALL, axis=0, tiled=True)

        full, more, low_own = pack_experts(weight_gate_up, weight_down)
        chip = chip_half(weight_out.astype(bf16))
        chip_rows = chip.size // D
        line = line_of(
            jnp.concatenate([chip.reshape(chip_rows, D), after(cotangent, low_own)], axis=0)
        )
        more_own = all_to_all_plane(after(more, line[-1])).reshape(D, -1)
        out_mine, out_other = gather_halves([b[:chip_rows].reshape(chip.shape) for b in line])
        core = lax.axis_index("core")
        order_mine, order_other = row_order(core), row_order(1 - core)

        qkv_w = first_all[:, :QKV]
        router_w = first_all[:, QKV : QKV + EXPERTS]
        gain_one = first_all[:, QKV + EXPERTS].astype(f32)
        gain_two = first_all[:, QKV + EXPERTS + 1].astype(f32)

        inputs = tokens.astype(f32)
        factor_one = lax.rsqrt(jnp.mean(inputs * inputs, axis=-1, keepdims=True) + norm_eps)
        hidden_one = (inputs * factor_one * gain_one).astype(bf16)
        joined_heads = dot(hidden_one, qkv_w)
        cot_all = gather_tokens([b[chip_rows:] for b in line], joined_heads)
        hidden_mine = dot(hidden_one, order_mine).astype(bf16)
        hidden_other = dot(hidden_one, order_other).astype(bf16)
        query_rows = joined_heads[:, :HEADS_WIDTH].reshape(sequence_length, QUERY_HEADS, HEAD_SIZE)
        every_key = joined_heads[:, HEADS_WIDTH : HEADS_WIDTH + KEYS_WIDTH].reshape(
            sequence_length, KEY_VALUE_HEADS, HEAD_SIZE
        )
        every_value = joined_heads[:, HEADS_WIDTH + KEYS_WIDTH :].reshape(
            sequence_length, KEY_VALUE_HEADS, HEAD_SIZE
        )
        cosine_lookup, sine_lookup = rotary_tables(sequence_length, HEAD_SIZE)
        query_rotated = (
            apply_rotation(query_rows, cosine_lookup, sine_lookup)
            .astype(bf16)
            .reshape(sequence_length, KEY_VALUE_HEADS, head_groups, HEAD_SIZE)
        )
        key_rot = apply_rotation(every_key, cosine_lookup, sine_lookup).astype(bf16)
        value_low = every_value.astype(bf16)
        causal = jnp.arange(sequence_length)[:, None] >= jnp.arange(sequence_length)[None, :]
        scores = attention_scores(query_rotated, key_rot, causal)
        peak = jnp.max(scores, axis=-1, keepdims=True)
        expo = jnp.exp(scores - peak)
        totals = jnp.sum(expo, axis=-1, keepdims=True)
        probs = expo / totals
        prob_low = probs.astype(bf16)
        heads = jnp.einsum("kgst,tkd->skgd", prob_low, value_low, preferred_element_type=f32)
        attended = heads.reshape(sequence_length, HEADS_WIDTH).astype(bf16)
        attended_mine = dot(attended, order_mine).astype(bf16)
        attended_other = dot(attended, order_other).astype(bf16)
        projected = [dot(attended_mine, out_mine), dot(attended_other, out_other)]
        mid = inputs + residual_scale * jnp.where(
            core == 0,
            jnp.concatenate(projected, axis=1),
            jnp.concatenate(projected[::-1], axis=1),
        )
        factor_two = lax.rsqrt(jnp.mean(mid * mid, axis=-1, keepdims=True) + norm_eps)
        hidden_two = (mid * factor_two * gain_two).astype(bf16)
        logits = dot(hidden_two, router_w)
        named = jnp.any(
            routes[..., None] == jnp.arange(EXPERTS, dtype=routes.dtype)[None, None, :], axis=1
        )
        shown = jnp.where(named, logits, -jnp.inf)
        raised = jnp.exp(shown - jnp.max(shown, axis=-1, keepdims=True))
        gates = raised / jnp.sum(raised, axis=-1, keepdims=True)

        gate_high = gates.astype(bf16)
        gate_rest = (gates - gate_high.astype(f32)).astype(bf16)
        sent = jnp.concatenate(
            [hidden_two, pad_lanes(jnp.concatenate([gate_high, gate_rest], axis=1))], axis=1
        )
        sent_line = line_of(sent)
        full_own = all_to_all_plane(after(full, sent_line[-1])).reshape(D, -1) if whole else None
        sent_all = gather_tokens(sent_line)
        more_own = after(more_own, sent)
        more_other, low_other = swap_core(more_own), swap_core(low_own)
        down_own, down_other = down_of(more_own, low_own), down_of(more_other, low_other)
        full_other = None
        if whole:
            full_own = after(full_own, sent_all)
            full_other = swap_core(full_own)
        own, other = (full_own, more_own), (full_other, more_other)
        blocks = 2 * nx * ny
        reach = [dot_nt(cot_all, d).reshape(blocks, -1, units) for d in (down_own, down_other)]

        behind = jnp.concatenate([unit_experts(group, place), unit_experts(partner, place)])
        numbers = jnp.arange(LANES)[:, None]
        real = behind[None, :] >= 0
        once = ((numbers == behind[None, :]) & real).astype(bf16)
        twice = once + ((numbers == behind[None, :] + EXPERTS) & real).astype(bf16)
        kept = None
        firsts = []
        sent_blocks = sent_all.reshape(blocks, -1, sent_all.shape[1])
        for at in range(2):
            *kept, two = run_experts(at, sent_blocks, reach, own, other, twice, once, kept)
            firsts.append(scatter_first(two))
        two_sum = sum_line(scatter_second(firsts))

        gated, grad_both = (k.reshape(-1, k.shape[2]) for k in kept)
        gated, grad_both = after(gated, *firsts[-1], always=True), after(grad_both, *firsts[-1])
        rows_all = after(sent_all, *firsts[-1], always=True)[:, :D]
        mixed = (dot(gated[:, :units], down_own) + dot(gated[:, units:], down_other)).astype(bf16)
        mixed = after(mixed, two_sum, always=True).reshape(blocks, -1, D)
        mixed_first = scatter_first(mixed)

        came_gate_up = swap_core(dot_tn(rows_all, grad_both[:, 2 * units :]).astype(bf16))
        came_down = swap_core(dot_tn(gated[:, units:], cot_all).astype(bf16))
        full, more, low = combine_grads(
            dot_tn(rows_all, grad_both[:, : 2 * units]).astype(bf16),
            came_gate_up,
            dot_tn(gated[:, :units], cot_all).astype(bf16),
            came_down,
        )
        home_full = all_to_all_plane(after(full, two_sum)) if whole else None
        home_rest = all_to_all_plane(after(more, two_sum))
        two_sum = after(two_sum, low)
        grad_two, grad_gates = two_sum[:, :D], two_sum[:, D : D + EXPERTS]

        grad_out = cotangent.astype(f32)
        grad_chosen = gates * (grad_gates - jnp.sum(gates * grad_gates, axis=-1, keepdims=True))
        grad_logits = grad_chosen.astype(bf16)
        grad_router = dot_tn(hidden_two, grad_logits)
        grad_two = grad_two + dot_nt(grad_logits, router_w)
        grad_mid, grad_gain_two = norm_backward(grad_two, mid, factor_two, gain_two)
        grad_mid = grad_out + grad_mid
        grad_att = (residual_scale * grad_mid).astype(bf16)
        att_left, att_right = grad_att[:, : D // 2], grad_att[:, D // 2 :]
        att_mine = jnp.where(core == 0, att_left, att_right)
        att_other = jnp.where(core == 0, att_right, att_left)
        grad_heads = (
            dot_nt(dot_nt(att_mine, out_mine).astype(bf16), order_mine)
            + dot_nt(dot_nt(att_other, out_other).astype(bf16), order_other)
        )
        grad_heads = grad_heads.astype(bf16).reshape(
            sequence_length, KEY_VALUE_HEADS, head_groups, HEAD_SIZE
        )
        out_first = scatter_halves_first(
            dot_tn(attended_mine, att_mine).astype(bf16),
            dot_tn(attended_other, att_other).astype(bf16),
        )
        out_left, out_right = scatter_halves_second(out_first)
        grad_probs = jnp.einsum(
            "skgd,tkd->kgst", grad_heads, value_low, preferred_element_type=f32
        )
        value_gradient = jnp.einsum(
            "kgst,skgd->tkd", prob_low, grad_heads, preferred_element_type=f32
        )
        row_dot = jnp.sum(probs * grad_probs, axis=-1, keepdims=True)
        grad_scores = (probs * (grad_probs - row_dot)).astype(bf16)
        grad_qrot = (
            jnp.einsum("kgst,tkd->skgd", grad_scores, key_rot, preferred_element_type=f32)
            * score_scale
        )
        grad_krot = (
            jnp.einsum("kgst,skgd->tkd", grad_scores, query_rotated, preferred_element_type=f32)
            * score_scale
        )
        grad_queries = apply_rotation(
            grad_qrot.reshape(sequence_length, QUERY_HEADS, HEAD_SIZE), cosine_lookup, -sine_lookup
        )
        key_gradient = apply_rotation(grad_krot, cosine_lookup, -sine_lookup)
        grad_joined = jnp.concatenate(
            [
                grad_queries.reshape(sequence_length, HEADS_WIDTH),
                key_gradient.reshape(sequence_length, KEYS_WIDTH),
                value_gradient.reshape(sequence_length, KEYS_WIDTH),
            ],
            axis=1,
        ).astype(bf16)
        grad_one = dot_nt(grad_joined, qkv_w)
        grad_inputs, grad_gain_one = norm_backward(grad_one, inputs, factor_one, gain_one)
        token_grad = grad_mid + grad_inputs
        small_sent = pad_lanes(
            jnp.concatenate([grad_router, grad_gain_one[:, None], grad_gain_two[:, None]], axis=1)
        )
        small_sent = small_sent.astype(bf16)
        joined_left, joined_right = grad_joined[:, : QKV // 2], grad_joined[:, QKV // 2 :]
        qkv_sent = []
        for hidden, rows_order, at in (
            (hidden_mine, order_mine, core),
            (hidden_other, order_other, 1 - core),
        ):
            product = dot_tn(hidden, jnp.where(at == 0, joined_left, joined_right))
            extra = jnp.where(at == 0, dot_tn(rows_order, small_sent), 0.0)
            qkv_sent.append(jnp.concatenate([product, extra], axis=1).astype(bf16))
        qkv_first = scatter_halves_first(qkv_sent[0], after(qkv_sent[1], out_first))
        mixed = sum_line(scatter_second([[after(m, qkv_first) for m in mixed_first]]))
        layer_out = (mid + residual_scale * mixed).astype(bf16)
        new_gate_up, new_down, marker = update_experts(
            home_full,
            home_rest,
            low,
            (weight_gate_up, moment_gate_up, square_gate_up),
            (weight_down, moment_down, square_down),
        )
        late = (marker, home_rest) if whole else ()
        qkv_left, qkv_right = scatter_halves_second(qkv_first, *late)
        sum_out = jnp.concatenate([out_left, out_right], axis=1)
        sum_qkv = jnp.concatenate([qkv_left[:, : QKV // 2], qkv_right[:, : QKV // 2]], axis=1)
        sum_router = qkv_left[:, QKV // 2 : QKV // 2 + EXPERTS]
        sum_gains = qkv_left[:, QKV // 2 + EXPERTS : QKV // 2 + EXPERTS + 2].T

        new_qkv = adam_step(weight_qkv, moment_qkv, square_qkv, sum_qkv, D ** (-0.5), weight_decay)
        new_out = adam_step(
            weight_out,
            moment_out,
            square_out,
            sum_out,
            max(4, QUERY_HEADS * HEAD_SIZE // 256) ** (-0.5),
            weight_decay,
        )
        new_router = adam_step(
            weight_router, moment_router, square_router, sum_router, (4 * D) ** (-0.5), weight_decay
        )
        new_gains = adam_step(gains, moment_gains, square_gains, sum_gains, 0.75, 0.0)
        return (
            layer_out,
            token_grad,
            *new_qkv,
            *new_out,
            *new_router,
            *new_gains,
            *new_gate_up,
            *new_down,
        )

    return shards


def solution(mesh):
    n_dp, n_expert = mesh.shape["dp"], mesh.shape["expert"]
    nz = 4
    nx, ny = n_dp // nz, n_expert // 2
    fine = Mesh(mesh.devices.reshape(nz, nx, ny, 2), ALL)
    rows = P(ALL, None)
    columns = P(None, ALL)
    experts = P(("y", "core"), ("z", "x"), None)
    dense = (rows,) * 9 + (columns,) * 3 + (experts,) * 6
    return jax.shard_map(
        make_shards((nz, nx, ny)),
        mesh=fine,
        in_specs=(rows,) * 3 + dense,
        out_specs=(rows,) * 2 + dense,
        check_vma=False,
    )
```

```python
import functools

import jax
import jax.numpy as jnp
import numpy as np
from jax import lax
from jax.experimental import pallas as pl
from jax.experimental.pallas import tpu as pltpu
from jax.sharding import Mesh, PartitionSpec as P

D = 1536
QUERY_HEADS = 24
KEY_VALUE_HEADS = 8
HEAD_SIZE = 64
FF = 512
EXPERTS = 40
TOPK = 8
STEP = 10
QKV = 2560
LANES = 128
HEADS_WIDTH = QUERY_HEADS * HEAD_SIZE
KEYS_WIDTH = KEY_VALUE_HEADS * HEAD_SIZE

norm_eps = 1e-06
residual_scale = 0.22
score_scale = 0.125
beta_one = 0.9
beta_two = 0.95
adam_eps = 1e-08
weight_decay = 0.1

f32 = jnp.float32
bf16 = jnp.bfloat16
ALL = ("z", "x", "y", "core")
PLANE = ("z", "x")
SAME_CORE = ("z", "x", "y")


def rotary_tables(sequence_length, size):
    half = size // 2
    places = jnp.arange(sequence_length).astype(f32)[:, None]
    inverse = 10000.0 ** (-jnp.arange(half).astype(f32) * 2.0 / size)
    angles = places * inverse[None, :]
    return (jnp.cos(angles)[:, None, :], jnp.sin(angles)[:, None, :])


def apply_rotation(values, cosine_lookup, sine_lookup):
    half = values.shape[-1] // 2
    first = values[..., :half]
    second = values[..., half:]
    return jnp.concatenate(
        [
            first * cosine_lookup - second * sine_lookup,
            second * cosine_lookup + first * sine_lookup,
        ],
        axis=-1,
    )


def attention_scores(query_rotated, key_rot, causal):
    scores = (
        jnp.einsum("skgd,tkd->kgst", query_rotated, key_rot, preferred_element_type=f32)
        * score_scale
    )
    return jnp.where(causal, scores, -1e30)


def norm_backward(grad_normed, values, factor, gain):
    scaled = grad_normed * gain
    grad_gain = jnp.sum(grad_normed * values * factor, axis=0)
    value_gradient = factor * scaled - values * factor * factor * factor * jnp.mean(
        scaled * values, axis=-1, keepdims=True
    )
    return (value_gradient, grad_gain)


def adam_step(weight, moment, square, grad, rate, decay):
    moment = beta_one * moment + (1.0 - beta_one) * grad
    square = beta_two * square + (1.0 - beta_two) * grad * grad
    fixed_one = moment / (1.0 - beta_one**STEP)
    fixed_two = square / (1.0 - beta_two**STEP)
    weight = weight - rate * (fixed_one / (jnp.sqrt(fixed_two) + adam_eps) + decay * weight)
    return (weight, moment, square)


def dot(a, b):
    return jnp.dot(a, b, preferred_element_type=f32)


def dot_nt(a, b):
    return lax.dot_general(a, b, (((1,), (1,)), ((), ())), preferred_element_type=f32)


def dot_tn(a, b):
    return lax.dot_general(a, b, (((0,), (0,)), ((), ())), preferred_element_type=f32)


def pad_lanes(values):
    extra = -values.shape[-1] % LANES
    return jnp.pad(values, ((0, 0), (0, extra)))


def swap_core(values):
    return lax.ppermute(values, "core", [(0, 1), (1, 0)])


def keep_kernel(*refs):
    pass


def ring_order(n):
    return [0] + list(range(1, n, 2)) + list(range(n - 2 + n % 2, 0, -2))


def home_table(n):
    order = ring_order(n)
    place = {chip: at for at, chip in enumerate(order)}
    return np.array([[order[(place[i] - s) % n] for s in range(n)] for i in range(n)], np.int32)


def make_shards(sizes):
    nz, nx, ny = sizes
    length = {"z": nz, "x": nx, "y": ny}
    planes = nz * nx
    per_group = EXPERTS // (2 * ny)
    whole = per_group // planes
    spare = per_group - whole * planes
    piece = FF // planes
    wide = whole * FF
    narrow = spare * piece
    narrow_pad = narrow + -narrow % LANES
    units = wide + narrow_pad

    rings = {axis: ring_order(n) for axis, n in length.items()}
    places = {axis: i for i, axis in enumerate(("z", "x", "y", "core"))}
    shape = (nz, nx, ny, 2)

    def pairs_of(axes, step):
        pairs = []
        for at in np.ndindex(*shape):
            axis = axes[at[3]]
            ring = rings[axis]
            to = list(at)
            to[places[axis]] = ring[(ring.index(at[places[axis]]) + step) % len(ring)]
            pairs.append(
                (int(np.ravel_multi_index(at, shape)), int(np.ravel_multi_index(to, shape)))
            )
        return pairs

    def move(values, axes, step):
        return lax.ppermute(values, ALL, pairs_of(axes, step))

    def row_order(core):
        found = {}
        for axis, n in length.items():
            here = jnp.arange(n)[:, None] == lax.axis_index(axis)
            found[axis] = jnp.sum(jnp.where(here, jnp.asarray(home_table(n)), 0), axis=0)
        x = jnp.where(core == 0, found["x"][None, :], found["x"][:, None])
        y = jnp.where(core == 0, found["y"][:, None], found["y"][None, :])
        chip = (found["z"] * nx + x[:, :, None]) * ny + y[:, :, None]
        block = (chip[..., None] * 2 + jnp.arange(2)).reshape(-1, 1)
        rows = D // block.shape[0]
        kept = (block * rows + jnp.arange(rows)[None, :]).reshape(1, D)
        return (jnp.arange(D)[:, None] == kept).astype(bf16)

    def add_low(a, b):
        return (a.astype(f32) + b.astype(f32)).astype(bf16)

    parts = ((0, "x", "y"), (1, "y", "x"))

    def line_of(own):
        line = [own]
        for _ in range(nz - 1):
            line.append(move(line[-1], "zz", 1))
        return line

    def gather_tokens(line, late):
        half = line[0].shape[0] // 2
        packs = [
            jnp.concatenate([b[part * half : (part + 1) * half] for b in line], axis=0)
            for part, _, _ in parts
        ]
        packs = [after(p, late) for p in packs]
        for level in (1, 2):
            grown = []
            for pack, names in zip(packs, parts):
                axis = names[level]
                steps = [pack]
                for _ in range(length[axis] - 1):
                    steps.append(move(steps[-1], axis * 2, 1))
                grown.append(jnp.concatenate(steps, axis=0))
            packs = grown
        return jnp.concatenate(packs, axis=0)

    def block_order():
        found = {}
        for axis, n in length.items():
            here = jnp.arange(n)[:, None] == lax.axis_index(axis)
            found[axis] = jnp.sum(jnp.where(here, jnp.asarray(home_table(n)), 0), axis=0)
        z = found["z"][None, None, :]
        blocks = []
        for part, second, third in parts:
            at = {second: found[second][None, :, None], third: found[third][:, None, None]}
            chip = (z * nx + at["x"]) * ny + at["y"]
            blocks.append((chip * 2 + part).reshape(-1))
        return jnp.concatenate(blocks)

    def copy_kernel(order_ref, values_ref, out_ref):
        out_ref[...] = values_ref[...]

    def permute_blocks(values, order, back=False):
        count = order.shape[0]
        rows = values.shape[0] // count
        here = pl.BlockSpec((1, rows, values.shape[1]), lambda i, order: (i, 0, 0))
        there = pl.BlockSpec((1, rows, values.shape[1]), lambda i, order: (order[i], 0, 0))
        size = 2 * values.size * values.dtype.itemsize
        result = pl.pallas_call(
            copy_kernel,
            grid_spec=pltpu.PrefetchScalarGridSpec(
                num_scalar_prefetch=1,
                grid=(count,),
                in_specs=[here if back else there],
                out_specs=there if back else here,
            ),
            out_shape=jax.ShapeDtypeStruct((count, rows, values.shape[1]), values.dtype),
            cost_estimate=pl.CostEstimate(flops=0, bytes_accessed=size, transcendentals=0),
        )(order, values.reshape(count, rows, values.shape[1]))
        return result.reshape(values.shape)

    def sum_level(packs, level):
        summed = []
        for pack, names in zip(packs, parts):
            n = length[names[level]]
            pack = pack.reshape(n, pack.shape[0] // n, *pack.shape[1:])
            acc = None
            for s in reversed(range(n)):
                acc = pack[s] if acc is None else add_low(move(acc, names[level] * 2, -1), pack[s])
            summed.append(acc)
        return summed

    def scatter_first(values):
        count = values.shape[0] // 2
        return sum_level([values[:count], values[count:]], 2)

    def scatter_second(halves):
        packs = [jnp.concatenate(same, axis=1) for same in zip(*halves)]
        packs = [p[0] for p in sum_level(packs, 1)]
        half = packs[0].shape[0] // nz
        return [
            jnp.concatenate([p[s * half : (s + 1) * half] for p in packs], axis=0)
            for s in range(nz)
        ]

    def sum_line(blocks):
        total = blocks[-1]
        for mine in reversed(blocks[:-1]):
            total = add_low(move(total, "zz", -1), mine)
        return total.astype(f32)

    def chip_half(own):
        half = own.shape[1] // 2
        core = lax.axis_index("core")
        left, right = own[:, :half], own[:, half:]
        kept = jnp.where(core == 0, left, right)
        came = swap_core(jnp.where(core == 0, right, left))
        return jnp.where(
            core == 0, jnp.concatenate([kept, came], axis=0), jnp.concatenate([came, kept], axis=0)
        )

    def gather_halves(line):
        rows, half = line[0].shape
        steps = [jnp.concatenate(line, axis=0)]
        for _ in range(nx - 1):
            steps.append(move(steps[-1], "xy", 1))
        packs = [jnp.concatenate(steps, axis=0)]
        for _ in range(nx - 1):
            packs.append(move(packs[-1], "yx", 1))
        result = jnp.concatenate(packs, axis=0)
        return result, swap_core(result)

    def scatter_halves_first(mine, other):
        both = add_low(swap_core(other), mine)
        grid = both.reshape(nx, nx, both.shape[0] // (nx * nx), both.shape[1])
        acc = None
        for s in reversed(range(nx)):
            acc = grid[s] if acc is None else add_low(move(acc, "yx", -1), grid[s])
        return acc

    def scatter_halves_second(acc, *late):
        core = lax.axis_index("core")
        rows = acc.shape[1] // (nz * 2)
        two = None
        for s in reversed(range(nx)):
            two = acc[s] if two is None else add_low(move(two, "xy", -1), acc[s])
        two = after(two, *late)
        total = None
        for s in reversed(range(nz)):
            mine = two[s * 2 * rows : (s + 1) * 2 * rows]
            total = mine if total is None else add_low(move(total, "zz", -1), mine)
        kept = jnp.where(core == 0, total[:rows], total[rows:])
        came = swap_core(jnp.where(core == 0, total[rows:], total[:rows]))
        return (
            jnp.where(core == 0, kept, came).astype(f32),
            jnp.where(core == 0, came, kept).astype(f32),
        )

    def after(values, *first, always=False):
        if not (whole or always):
            return values
        anywhere = pl.BlockSpec(memory_space=pl.ANY)
        return pl.pallas_call(
            keep_kernel,
            in_specs=[anywhere] * (1 + len(first)),
            out_specs=anywhere,
            out_shape=jax.ShapeDtypeStruct(values.shape, values.dtype),
            input_output_aliases={0: 0},
        )(values, *first)

    def all_to_all_plane(values):
        return lax.all_to_all(values, PLANE, split_axis=0, concat_axis=0, tiled=True)

    rows_home = D // planes
    across = rows_home // piece
    rest = 2 * narrow_pad + wide

    def cut_spare(part):
        part = part.reshape(spare, rows_home, 2, planes, piece)
        part = part.transpose(3, 1, 2, 0, 4).reshape(planes, rows_home, 2, narrow)
        part = jnp.pad(part, ((0, 0), (0, 0), (0, 0), (0, narrow_pad - narrow)))
        return part.reshape(planes, rows_home, 2 * narrow_pad)

    def join_spare(part):
        part = part.reshape(planes, rows_home, 2, narrow_pad)[..., :narrow]
        part = part.reshape(planes, rows_home, 2, spare, piece).transpose(3, 1, 2, 0, 4)
        return part.reshape(spare, rows_home, 2 * FF)

    def lanes(values, first, width=piece):
        return values[:, first : first + width]

    packed_columns = 2 * units + wide

    def pack_kernel(gate_up_ref, spare_ref, down_ref, spare_down_ref, out_ref, low_ref):
        step = pl.program_id(0)
        out_ref[step, :, pl.ds(0, 2 * wide)] = gate_up_ref[0].astype(bf16)
        for j in range(across):
            out_ref[step, pl.ds(j * piece, piece), pl.ds(2 * units, wide)] = down_ref[
                0, :, pl.ds(j * wide, wide)
            ].astype(bf16)

        @pl.when(step == 0)
        def _():
            for to in range(planes):
                taken = [
                    lanes(spare_ref[s], g * FF + to * piece) for g in range(2) for s in range(spare)
                ]
                out_ref[to, :, pl.ds(2 * wide, 2 * narrow)] = jnp.concatenate(taken, axis=1).astype(
                    bf16
                )
            for s in range(spare):
                low_ref[pl.ds(s * piece, piece), :] = spare_down_ref[s].astype(bf16)

    def pack_experts(gate_up, down):
        if not whole:
            low = down.astype(bf16).reshape(narrow, D)
            low = jnp.pad(low, ((0, narrow_pad - narrow), (0, 0)))
            return cut_spare(gate_up.astype(bf16)), low
        return pl.pallas_call(
            pack_kernel,
            grid=(planes,),
            in_specs=[
                pl.BlockSpec((1, rows_home, 2 * FF), lambda i: (i, 0, 0)),
                pl.BlockSpec((spare, rows_home, 2 * FF), lambda i: (planes // spare, 0, 0)),
                pl.BlockSpec((1, piece, D), lambda i: (i, 0, 0)),
                pl.BlockSpec((spare, piece, D), lambda i: (planes // spare, 0, 0)),
            ],
            out_specs=[
                pl.BlockSpec((planes, rows_home, packed_columns), lambda i: (0, 0, 0)),
                pl.BlockSpec((narrow, D), lambda i: (0, 0)),
            ],
            out_shape=[
                jax.ShapeDtypeStruct((planes, rows_home, packed_columns), bf16),
                jax.ShapeDtypeStruct((narrow, D), bf16),
            ],
            cost_estimate=pl.CostEstimate(flops=0, bytes_accessed=2**24, transcendentals=0),
            compiler_params=pltpu.CompilerParams(vmem_limit_bytes=48 * 2**20),
        )(gate_up, gate_up, down, down)

    def down_of(packed, low):
        if not whole:
            return low
        mine = packed[:, 2 * units :].reshape(planes, across, piece, wide)
        mine = mine.transpose(0, 2, 1, 3).reshape(wide, D)
        return jnp.concatenate([mine, low], axis=0)

    def combine_kernel(a_ref, came_a_ref, b_ref, came_b_ref, c_ref, came_c_ref, out_ref, low_ref):
        total = a_ref[...].astype(f32) + came_a_ref[...].astype(f32)
        out_ref[0, :, pl.ds(0, 2 * units)] = total.astype(bf16)
        total = residual_scale * (b_ref[...].astype(f32) + came_b_ref[...].astype(f32))
        for j in range(across):
            out_ref[0, pl.ds(j * piece, piece), pl.ds(2 * units, wide)] = total[
                :, j * wide : (j + 1) * wide
            ].astype(bf16)
        low_ref[...] = residual_scale * (c_ref[...].astype(f32) + came_c_ref[...].astype(f32))

    def combine_grads(gate_up, came_gate_up, down, came_down):
        if not whole:
            total = (gate_up.astype(f32) + came_gate_up.astype(f32)).astype(bf16)
            low = residual_scale * (down.astype(f32) + came_down.astype(f32))
            return total.reshape(planes, rows_home, rest), low
        return pl.pallas_call(
            combine_kernel,
            grid=(planes,),
            in_specs=[pl.BlockSpec((rows_home, 2 * units), lambda i: (i, 0))] * 2
            + [pl.BlockSpec((piece, D), lambda i: (i, 0))] * 2
            + [pl.BlockSpec((narrow, D), lambda i: (wide // narrow, 0))] * 2,
            out_specs=[
                pl.BlockSpec((1, rows_home, packed_columns), lambda i: (i, 0, 0)),
                pl.BlockSpec((narrow, D), lambda i: (0, 0)),
            ],
            out_shape=[
                jax.ShapeDtypeStruct((planes, rows_home, packed_columns), bf16),
                jax.ShapeDtypeStruct((narrow, D), f32),
            ],
            cost_estimate=pl.CostEstimate(flops=0, bytes_accessed=2**24, transcendentals=0),
            compiler_params=pltpu.CompilerParams(vmem_limit_bytes=48 * 2**20),
        )(gate_up, came_gate_up, down, came_down, down, came_down)

    gate_up_rate = D ** (-0.5)
    down_rate = max(2, FF // 128) ** (-0.5)

    def full_kernel(home_ref, w_ref, m_ref, s_ref, *outs):
        done = adam_step(
            w_ref[0], m_ref[0], s_ref[0], home_ref[0].astype(f32), gate_up_rate, weight_decay
        )
        for ref, value in zip(outs, done):
            ref[0] = value

    def spare_kernel(home_ref, w_ref, m_ref, s_ref, a_ref, b_ref, c_ref, *outs):
        for s in range(spare):

            @pl.when(pl.program_id(0) == s)
            def _():
                grad = jnp.concatenate(
                    [
                        lanes(home_ref[p], g * narrow_pad + s * piece)
                        for g in range(2)
                        for p in range(planes)
                    ],
                    axis=1,
                ).astype(f32)
                done = adam_step(w_ref[0], m_ref[0], s_ref[0], grad, gate_up_rate, weight_decay)
                for ref, value in zip(outs, done):
                    ref[0] = value

    def down_kernel(home_ref, low_ref, w_ref, m_ref, s_ref, *outs):
        def update(grad):
            done = adam_step(w_ref[0], m_ref[0], s_ref[0], grad, down_rate, weight_decay)
            for ref, value in zip(outs, done):
                ref[0] = value

        @pl.when(pl.program_id(0) < planes)
        def _():
            update(
                jnp.concatenate(
                    [
                        home_ref[0, pl.ds(j * piece, piece), pl.ds(2 * units, wide)]
                        for j in range(across)
                    ],
                    axis=1,
                ).astype(f32)
            )

        @pl.when(pl.program_id(0) >= planes)
        def _():
            update(low_ref[...])

    def update_experts(home, low, gate_up, down):
        if not whole:
            grad = join_spare(home).astype(f32)
            return (
                adam_step(*gate_up, grad, gate_up_rate, weight_decay),
                adam_step(
                    *down, low[:narrow].reshape(spare, piece, D), down_rate, weight_decay
                ),
            )
        params = pltpu.CompilerParams(vmem_limit_bytes=48 * 2**20)
        shapes = [jax.ShapeDtypeStruct(gate_up[0].shape, f32)] * 3
        one = pl.BlockSpec((1, rows_home, 2 * FF), lambda i: (i, 0, 0))
        last = pl.BlockSpec((1, rows_home, 2 * FF), lambda i: (planes + i, 0, 0))
        new_gate_up = pl.pallas_call(
            full_kernel,
            grid=(planes,),
            in_specs=[one] * 4,
            out_specs=[one] * 3,
            cost_estimate=pl.CostEstimate(flops=0, bytes_accessed=2**25, transcendentals=0),
            out_shape=shapes,
            compiler_params=params,
        )(home, *gate_up)
        new_gate_up = pl.pallas_call(
            spare_kernel,
            grid=(spare,),
            in_specs=[pl.BlockSpec((planes, rows_home, 2 * narrow_pad), lambda i: (0, 0, wide // narrow_pad))]
            + [last] * 3
            + [pl.BlockSpec(memory_space=pl.ANY)] * 3,
            out_specs=[last] * 3,
            out_shape=shapes,
            input_output_aliases={4: 0, 5: 1, 6: 2},
            compiler_params=params,
        )(home, *gate_up, *new_gate_up)
        row = pl.BlockSpec((1, piece, D), lambda i: (i, 0, 0))
        new_down = pl.pallas_call(
            down_kernel,
            grid=(per_group,),
            in_specs=[
                pl.BlockSpec((1, rows_home, packed_columns), lambda i: (jnp.minimum(i, planes - 1), 0, 0)),
                pl.BlockSpec((piece, D), lambda i: (jnp.maximum(i - planes, 0), 0)),
            ]
            + [row] * 3,
            out_specs=[row] * 3,
            cost_estimate=pl.CostEstimate(flops=0, bytes_accessed=2**24, transcendentals=0),
            out_shape=[jax.ShapeDtypeStruct(down[0].shape, f32)] * 3,
            compiler_params=params,
        )(home, low, *down)
        return new_gate_up, new_down

    def unit_experts(group, place):
        base = group * per_group
        sets = []
        if whole:
            sets.append(jnp.full((wide,), base + place))
        behind = base + whole * planes + jnp.arange(narrow_pad) // piece
        sets.append(jnp.where(jnp.arange(narrow_pad) < narrow, behind, -1))
        return jnp.concatenate(sets)

    def columns_of():
        pieces = []
        for first in range(0, wide, 256):
            pieces.append((first, wide + first, first, min(256, wide - first)))
        pieces.append((2 * wide, 2 * wide + narrow_pad, wide, narrow_pad))
        return pieces

    def expert_kernel(first_call, *refs):
        rows_ref, gates_ref = refs[:2]
        reaches, weights = refs[2:4], refs[4:6]
        twice_ref, once_ref = refs[6:8]
        gated_ref, grad_ref, two_ref = refs[8 + (0 if first_call else 2) :]
        blocks, rows_of, _ = rows_ref.shape
        count = blocks * rows_of
        rows = rows_ref[...].reshape(count, D)
        gates = gates_ref[...].reshape(count, LANES)
        dgate = jnp.zeros((count, LANES), f32)
        for k in range(2):
            for gate_at, up_at, unit_at, width in columns_of():
                unit = pl.ds(k * units + unit_at, width)
                gate_w = weights[k][:, pl.ds(gate_at, width)]
                up_w = weights[k][:, pl.ds(up_at, width)]
                gate_part = jnp.dot(rows, gate_w, preferred_element_type=f32)
                up_part = jnp.dot(rows, up_w, preferred_element_type=f32)
                gate_wide = jnp.dot(gates, twice_ref[:, unit], preferred_element_type=f32)
                reach = reaches[k][:, :, pl.ds(unit_at, width)].reshape(count, width)
                reach = residual_scale * reach
                squash = 1.0 / (1.0 + jnp.exp(-gate_part))
                swish = gate_part * squash
                hidden = swish * up_part
                gated = (hidden * gate_wide).astype(bf16)
                gated_ref[:, :, unit] = gated.reshape(blocks, rows_of, width)
                dgate += dot_nt((hidden * reach).astype(bf16), once_ref[:, unit])
                grad_hidden = reach * gate_wide
                grad_gate = grad_hidden * up_part * squash * (1.0 + gate_part * (1.0 - squash))
                for at, value in ((gate_at, grad_gate), (up_at, grad_hidden * swish)):
                    grad_ref[:, :, pl.ds(k * 2 * units + at, width)] = value.astype(bf16).reshape(
                        blocks, rows_of, width
                    )
        two = jnp.zeros((count, D), f32)
        for k in range(2):
            grad = grad_ref[:, :, pl.ds(k * 2 * units, 2 * units)].reshape(count, 2 * units)
            two += dot_nt(grad, weights[k][...])
        two_ref[:, :, pl.ds(0, D)] = two.astype(bf16).reshape(blocks, rows_of, D)
        two_ref[:, :, pl.ds(D, LANES)] = dgate.astype(bf16).reshape(blocks, rows_of, LANES)

    def run_experts(at, sent, reach, own, other, twice, once, before):
        blocks, rows_of, _ = sent.shape
        rows_of = rows_of // 2
        tile = max(1, 512 // rows_of)

        def by_rows(columns, column=0):
            return pl.BlockSpec((tile, rows_of, columns), lambda i: (i, at, column))

        def fixed(rows, columns):
            return pl.BlockSpec((rows, columns), lambda i: (0, 0), pipeline_mode=pl.Buffered(1))

        kept = list(before) if before else []
        count = blocks * rows_of
        return pl.pallas_call(
            functools.partial(expert_kernel, not kept),
            grid=(blocks // tile,),
            in_specs=[by_rows(D), by_rows(LANES, D // LANES)]
            + [by_rows(units)] * 2
            + [fixed(D, 2 * units)] * 2
            + [fixed(LANES, 2 * units)] * 2
            + [pl.BlockSpec(memory_space=pl.ANY)] * len(kept),
            out_specs=[
                by_rows(2 * units),
                by_rows(4 * units),
                pl.BlockSpec((tile, rows_of, D + LANES), lambda i: (i, 0, 0)),
            ],
            out_shape=[
                jax.ShapeDtypeStruct((blocks, 2 * rows_of, 2 * units), bf16),
                jax.ShapeDtypeStruct((blocks, 2 * rows_of, 4 * units), bf16),
                jax.ShapeDtypeStruct((blocks, rows_of, D + LANES), bf16),
            ],
            input_output_aliases={8 + i: i for i in range(len(kept))},
            cost_estimate=pl.CostEstimate(
                flops=16 * count * D * units, bytes_accessed=2**25, transcendentals=2 * count * units
            ),
            compiler_params=pltpu.CompilerParams(vmem_limit_bytes=60 * 2**20),
        )(sent, sent, *reach, own, other, twice, once, *kept)

    def shards(
        tokens,
        cotangent,
        routes,
        weight_qkv,
        moment_qkv,
        square_qkv,
        weight_out,
        moment_out,
        square_out,
        weight_router,
        moment_router,
        square_router,
        gains,
        moment_gains,
        square_gains,
        weight_gate_up,
        moment_gate_up,
        square_gate_up,
        weight_down,
        moment_down,
        square_down,
    ):
        sequence_length = tokens.shape[0]
        head_groups = QUERY_HEADS // KEY_VALUE_HEADS
        place = lax.axis_index(PLANE)
        group = lax.axis_index("y") * 2 + lax.axis_index("core")
        partner = lax.axis_index("y") * 2 + 1 - lax.axis_index("core")

        small = pad_lanes(jnp.concatenate([weight_router, gains.T], axis=1))
        first_pack = jnp.concatenate([weight_qkv, small], axis=1).astype(bf16)
        first_all = lax.all_gather(first_pack, ALL, axis=0, tiled=True)

        packed, low_own = pack_experts(weight_gate_up, weight_down)
        out_line = line_of(chip_half(weight_out.astype(bf16)))
        cot_line = line_of(after(cotangent, low_own, out_line[1]))
        own = all_to_all_plane(after(packed, cot_line[-1], out_line[-1])).reshape(D, -1)
        out_mine, out_other = gather_halves(out_line)
        core = lax.axis_index("core")
        order_mine, order_other = row_order(core), row_order(1 - core)
        blocks_order = block_order()

        qkv_w = first_all[:, :QKV]
        router_w = first_all[:, QKV : QKV + EXPERTS]
        gain_one = first_all[:, QKV + EXPERTS].astype(f32)
        gain_two = first_all[:, QKV + EXPERTS + 1].astype(f32)

        inputs = tokens.astype(f32)
        factor_one = lax.rsqrt(jnp.mean(inputs * inputs, axis=-1, keepdims=True) + norm_eps)
        hidden_one = (inputs * factor_one * gain_one).astype(bf16)
        joined_heads = dot(hidden_one, qkv_w)
        cot_all = gather_tokens(cot_line, joined_heads)
        hidden_mine = dot(hidden_one, order_mine).astype(bf16)
        hidden_other = dot(hidden_one, order_other).astype(bf16)
        query_rows = joined_heads[:, :HEADS_WIDTH].reshape(sequence_length, QUERY_HEADS, HEAD_SIZE)
        every_key = joined_heads[:, HEADS_WIDTH : HEADS_WIDTH + KEYS_WIDTH].reshape(
            sequence_length, KEY_VALUE_HEADS, HEAD_SIZE
        )
        every_value = joined_heads[:, HEADS_WIDTH + KEYS_WIDTH :].reshape(
            sequence_length, KEY_VALUE_HEADS, HEAD_SIZE
        )
        cosine_lookup, sine_lookup = rotary_tables(sequence_length, HEAD_SIZE)
        query_rotated = (
            apply_rotation(query_rows, cosine_lookup, sine_lookup)
            .astype(bf16)
            .reshape(sequence_length, KEY_VALUE_HEADS, head_groups, HEAD_SIZE)
        )
        key_rot = apply_rotation(every_key, cosine_lookup, sine_lookup).astype(bf16)
        value_low = every_value.astype(bf16)
        causal = jnp.arange(sequence_length)[:, None] >= jnp.arange(sequence_length)[None, :]
        scores = attention_scores(query_rotated, key_rot, causal)
        peak = jnp.max(scores, axis=-1, keepdims=True)
        expo = jnp.exp(scores - peak)
        totals = jnp.sum(expo, axis=-1, keepdims=True)
        probs = expo / totals
        prob_low = probs.astype(bf16)
        heads = jnp.einsum("kgst,tkd->skgd", prob_low, value_low, preferred_element_type=f32)
        attended = heads.reshape(sequence_length, HEADS_WIDTH).astype(bf16)
        attended_mine = dot(attended, order_mine).astype(bf16)
        attended_other = dot(attended, order_other).astype(bf16)
        projected = [dot(attended_mine, out_mine), dot(attended_other, out_other)]
        mid = inputs + residual_scale * jnp.where(
            core == 0,
            jnp.concatenate(projected, axis=1),
            jnp.concatenate(projected[::-1], axis=1),
        )
        factor_two = lax.rsqrt(jnp.mean(mid * mid, axis=-1, keepdims=True) + norm_eps)
        hidden_two = (mid * factor_two * gain_two).astype(bf16)
        logits = dot(hidden_two, router_w)
        named = jnp.any(
            routes[..., None] == jnp.arange(EXPERTS, dtype=routes.dtype)[None, None, :], axis=1
        )
        shown = jnp.where(named, logits, -jnp.inf)
        raised = jnp.exp(shown - jnp.max(shown, axis=-1, keepdims=True))
        gates = raised / jnp.sum(raised, axis=-1, keepdims=True)

        gate_high = gates.astype(bf16)
        gate_rest = (gates - gate_high.astype(f32)).astype(bf16)
        sent = jnp.concatenate(
            [hidden_two, pad_lanes(jnp.concatenate([gate_high, gate_rest], axis=1))], axis=1
        )
        sent_all = lax.all_gather(sent, SAME_CORE, axis=0, tiled=True)
        sent_all = permute_blocks(sent_all, blocks_order)
        own = after(own, sent)
        other, low_other = swap_core(own), swap_core(low_own)
        down_own, down_other = down_of(own, low_own), down_of(other, low_other)
        blocks = 2 * nx * ny
        reach = [dot_nt(cot_all, d).reshape(blocks, -1, units) for d in (down_own, down_other)]

        behind = jnp.concatenate([unit_experts(group, place), unit_experts(partner, place)])
        numbers = jnp.arange(LANES)[:, None]
        real = behind[None, :] >= 0
        once = ((numbers == behind[None, :]) & real).astype(bf16)
        twice = once + ((numbers == behind[None, :] + EXPERTS) & real).astype(bf16)
        kept = None
        firsts = []
        sent_blocks = sent_all.reshape(blocks, -1, sent_all.shape[1])
        for at in range(2):
            *kept, two = run_experts(at, sent_blocks, reach, own, other, twice, once, kept)
            firsts.append(scatter_first(two))
        two_sum = sum_line(scatter_second(firsts))

        gated, grad_both = (k.reshape(-1, k.shape[2]) for k in kept)
        gated, grad_both = after(gated, *firsts[-1], always=True), after(grad_both, *firsts[-1])
        rows_all = after(sent_all, *firsts[-1], always=True)[:, :D]
        mixed = (dot(gated[:, :units], down_own) + dot(gated[:, units:], down_other)).astype(bf16)
        mixed = permute_blocks(after(mixed, two_sum, always=True), blocks_order, back=True)
        mixed = lax.psum_scatter(mixed, SAME_CORE, scatter_dimension=0, tiled=True).astype(f32)
        layer_out = (mid + residual_scale * mixed).astype(bf16)

        came_gate_up = swap_core(dot_tn(rows_all, grad_both[:, 2 * units :]).astype(bf16))
        came_down = swap_core(dot_tn(gated[:, units:], cot_all).astype(bf16))
        packed, low = combine_grads(
            dot_tn(rows_all, grad_both[:, : 2 * units]).astype(bf16),
            came_gate_up,
            dot_tn(gated[:, :units], cot_all).astype(bf16),
            came_down,
        )
        home = all_to_all_plane(after(packed, two_sum))
        two_sum = after(two_sum, low)
        grad_two, grad_gates = two_sum[:, :D], two_sum[:, D : D + EXPERTS]

        grad_out = cotangent.astype(f32)
        grad_chosen = gates * (grad_gates - jnp.sum(gates * grad_gates, axis=-1, keepdims=True))
        grad_logits = grad_chosen.astype(bf16)
        grad_router = dot_tn(hidden_two, grad_logits)
        grad_two = grad_two + dot_nt(grad_logits, router_w)
        grad_mid, grad_gain_two = norm_backward(grad_two, mid, factor_two, gain_two)
        grad_mid = grad_out + grad_mid
        grad_att = (residual_scale * grad_mid).astype(bf16)
        att_left, att_right = grad_att[:, : D // 2], grad_att[:, D // 2 :]
        att_mine = jnp.where(core == 0, att_left, att_right)
        att_other = jnp.where(core == 0, att_right, att_left)
        grad_heads = (
            dot_nt(dot_nt(att_mine, out_mine).astype(bf16), order_mine)
            + dot_nt(dot_nt(att_other, out_other).astype(bf16), order_other)
        )
        grad_heads = grad_heads.astype(bf16).reshape(
            sequence_length, KEY_VALUE_HEADS, head_groups, HEAD_SIZE
        )
        out_first = scatter_halves_first(
            dot_tn(attended_mine, att_mine).astype(bf16),
            dot_tn(attended_other, att_other).astype(bf16),
        )
        out_left, out_right = scatter_halves_second(out_first)
        grad_probs = jnp.einsum(
            "skgd,tkd->kgst", grad_heads, value_low, preferred_element_type=f32
        )
        value_gradient = jnp.einsum(
            "kgst,skgd->tkd", prob_low, grad_heads, preferred_element_type=f32
        )
        row_dot = jnp.sum(probs * grad_probs, axis=-1, keepdims=True)
        grad_scores = (probs * (grad_probs - row_dot)).astype(bf16)
        grad_qrot = (
            jnp.einsum("kgst,tkd->skgd", grad_scores, key_rot, preferred_element_type=f32)
            * score_scale
        )
        grad_krot = (
            jnp.einsum("kgst,skgd->tkd", grad_scores, query_rotated, preferred_element_type=f32)
            * score_scale
        )
        grad_queries = apply_rotation(
            grad_qrot.reshape(sequence_length, QUERY_HEADS, HEAD_SIZE), cosine_lookup, -sine_lookup
        )
        key_gradient = apply_rotation(grad_krot, cosine_lookup, -sine_lookup)
        grad_joined = jnp.concatenate(
            [
                grad_queries.reshape(sequence_length, HEADS_WIDTH),
                key_gradient.reshape(sequence_length, KEYS_WIDTH),
                value_gradient.reshape(sequence_length, KEYS_WIDTH),
            ],
            axis=1,
        ).astype(bf16)
        grad_one = dot_nt(grad_joined, qkv_w)
        grad_inputs, grad_gain_one = norm_backward(grad_one, inputs, factor_one, gain_one)
        token_grad = grad_mid + grad_inputs
        small_sent = pad_lanes(
            jnp.concatenate([grad_router, grad_gain_one[:, None], grad_gain_two[:, None]], axis=1)
        )
        small_sent = small_sent.astype(bf16)
        joined_left, joined_right = grad_joined[:, : QKV // 2], grad_joined[:, QKV // 2 :]
        qkv_sent = []
        for hidden, rows_order, at in (
            (hidden_mine, order_mine, core),
            (hidden_other, order_other, 1 - core),
        ):
            product = dot_tn(hidden, jnp.where(at == 0, joined_left, joined_right))
            extra = jnp.where(at == 0, dot_tn(rows_order, small_sent), 0.0)
            qkv_sent.append(jnp.concatenate([product, extra], axis=1).astype(bf16))
        qkv_first = scatter_halves_first(qkv_sent[0], after(qkv_sent[1], out_first))
        qkv_left, qkv_right = scatter_halves_second(qkv_first, home)
        sum_out = jnp.concatenate([out_left, out_right], axis=1)
        sum_qkv = jnp.concatenate([qkv_left[:, : QKV // 2], qkv_right[:, : QKV // 2]], axis=1)
        sum_router = qkv_left[:, QKV // 2 : QKV // 2 + EXPERTS]
        sum_gains = qkv_left[:, QKV // 2 + EXPERTS : QKV // 2 + EXPERTS + 2].T

        new_gate_up, new_down = update_experts(
            home,
            low,
            (weight_gate_up, moment_gate_up, square_gate_up),
            (weight_down, moment_down, square_down),
        )
        new_qkv = adam_step(weight_qkv, moment_qkv, square_qkv, sum_qkv, D ** (-0.5), weight_decay)
        new_out = adam_step(
            weight_out,
            moment_out,
            square_out,
            sum_out,
            max(4, QUERY_HEADS * HEAD_SIZE // 256) ** (-0.5),
            weight_decay,
        )
        new_router = adam_step(
            weight_router, moment_router, square_router, sum_router, (4 * D) ** (-0.5), weight_decay
        )
        new_gains = adam_step(gains, moment_gains, square_gains, sum_gains, 0.75, 0.0)
        return (
            layer_out,
            token_grad,
            *new_qkv,
            *new_out,
            *new_router,
            *new_gains,
            *new_gate_up,
            *new_down,
        )

    return shards


def solution(mesh):
    n_dp, n_expert = mesh.shape["dp"], mesh.shape["expert"]
    nz = 4
    nx, ny = n_dp // nz, n_expert // 2
    fine = Mesh(mesh.devices.reshape(nz, nx, ny, 2), ALL)
    rows = P(ALL, None)
    columns = P(None, ALL)
    experts = P(("y", "core"), ("z", "x"), None)
    dense = (rows,) * 9 + (columns,) * 3 + (experts,) * 6
    return jax.shard_map(
        make_shards((nz, nx, ny)),
        mesh=fine,
        in_specs=(rows,) * 3 + dense,
        out_specs=(rows,) * 2 + dense,
        check_vma=False,
    )
```

```python
import functools

import jax
import jax.numpy as jnp
import numpy as np
from jax import lax
from jax.experimental import pallas as pl
from jax.experimental.pallas import tpu as pltpu
from jax.sharding import Mesh, PartitionSpec as P

D = 1536
QUERY_HEADS = 24
KEY_VALUE_HEADS = 8
HEAD_SIZE = 64
FF = 512
EXPERTS = 40
TOPK = 8
STEP = 10
QKV = 2560
LANES = 128
HEADS_WIDTH = QUERY_HEADS * HEAD_SIZE
KEYS_WIDTH = KEY_VALUE_HEADS * HEAD_SIZE

norm_eps = 1e-06
residual_scale = 0.22
score_scale = 0.125
beta_one = 0.9
beta_two = 0.95
adam_eps = 1e-08
weight_decay = 0.1

f32 = jnp.float32
bf16 = jnp.bfloat16
ALL = ("z", "x", "y", "core")
PLANE = ("z", "x")
SAME_CORE = ("z", "x", "y")


def rotary_tables(sequence_length, size):
    half = size // 2
    places = jnp.arange(sequence_length).astype(f32)[:, None]
    inverse = 10000.0 ** (-jnp.arange(half).astype(f32) * 2.0 / size)
    angles = places * inverse[None, :]
    return (jnp.cos(angles)[:, None, :], jnp.sin(angles)[:, None, :])


def apply_rotation(values, cosine_lookup, sine_lookup):
    half = values.shape[-1] // 2
    first = values[..., :half]
    second = values[..., half:]
    return jnp.concatenate(
        [
            first * cosine_lookup - second * sine_lookup,
            second * cosine_lookup + first * sine_lookup,
        ],
        axis=-1,
    )


def attention_scores(query_rotated, key_rot, causal):
    scores = (
        jnp.einsum("skgd,tkd->kgst", query_rotated, key_rot, preferred_element_type=f32)
        * score_scale
    )
    return jnp.where(causal, scores, -1e30)


def norm_backward(grad_normed, values, factor, gain):
    scaled = grad_normed * gain
    grad_gain = jnp.sum(grad_normed * values * factor, axis=0)
    value_gradient = factor * scaled - values * factor * factor * factor * jnp.mean(
        scaled * values, axis=-1, keepdims=True
    )
    return (value_gradient, grad_gain)


def adam_step(weight, moment, square, grad, rate, decay):
    moment = beta_one * moment + (1.0 - beta_one) * grad
    square = beta_two * square + (1.0 - beta_two) * grad * grad
    fixed_one = moment / (1.0 - beta_one**STEP)
    fixed_two = square / (1.0 - beta_two**STEP)
    weight = weight - rate * (fixed_one / (jnp.sqrt(fixed_two) + adam_eps) + decay * weight)
    return (weight, moment, square)


def dot(a, b):
    return jnp.dot(a, b, preferred_element_type=f32)


def dot_nt(a, b):
    return lax.dot_general(a, b, (((1,), (1,)), ((), ())), preferred_element_type=f32)


def dot_tn(a, b):
    return lax.dot_general(a, b, (((0,), (0,)), ((), ())), preferred_element_type=f32)


def pad_lanes(values):
    extra = -values.shape[-1] % LANES
    return jnp.pad(values, ((0, 0), (0, extra)))


def swap_core(values):
    return lax.ppermute(values, "core", [(0, 1), (1, 0)])


def keep_kernel(*refs):
    pass


def ring_order(n):
    return [0] + list(range(1, n, 2)) + list(range(n - 2 + n % 2, 0, -2))


def home_table(n):
    order = ring_order(n)
    place = {chip: at for at, chip in enumerate(order)}
    return np.array([[order[(place[i] - s) % n] for s in range(n)] for i in range(n)], np.int32)


def make_shards(sizes):
    nz, nx, ny = sizes
    length = {"z": nz, "x": nx, "y": ny}
    planes = nz * nx
    per_group = EXPERTS // (2 * ny)
    whole = per_group // planes
    spare = per_group - whole * planes
    piece = FF // planes
    wide = whole * FF
    narrow = spare * piece
    narrow_pad = narrow + -narrow % LANES
    units = wide + narrow_pad

    rings = {axis: ring_order(n) for axis, n in length.items()}
    places = {axis: i for i, axis in enumerate(("z", "x", "y", "core"))}
    shape = (nz, nx, ny, 2)

    def pairs_of(axes, step):
        pairs = []
        for at in np.ndindex(*shape):
            axis = axes[at[3]]
            ring = rings[axis]
            to = list(at)
            to[places[axis]] = ring[(ring.index(at[places[axis]]) + step) % len(ring)]
            pairs.append(
                (int(np.ravel_multi_index(at, shape)), int(np.ravel_multi_index(to, shape)))
            )
        return pairs

    def move(values, axes, step):
        return lax.ppermute(values, ALL, pairs_of(axes, step))

    def row_order(core):
        found = {}
        for axis, n in length.items():
            here = jnp.arange(n)[:, None] == lax.axis_index(axis)
            found[axis] = jnp.sum(jnp.where(here, jnp.asarray(home_table(n)), 0), axis=0)
        x = jnp.where(core == 0, found["x"][None, :], found["x"][:, None])
        y = jnp.where(core == 0, found["y"][:, None], found["y"][None, :])
        chip = (found["z"] * nx + x[:, :, None]) * ny + y[:, :, None]
        block = (chip[..., None] * 2 + jnp.arange(2)).reshape(-1, 1)
        rows = D // block.shape[0]
        kept = (block * rows + jnp.arange(rows)[None, :]).reshape(1, D)
        return (jnp.arange(D)[:, None] == kept).astype(bf16)

    def add_low(a, b):
        return (a.astype(f32) + b.astype(f32)).astype(bf16)

    parts = ((0, "x", "y"), (1, "y", "x"))

    def line_of(own):
        line = [own]
        for _ in range(nz - 1):
            line.append(move(line[-1], "zz", 1))
        return line

    def gather_tokens(line, late):
        half = line[0].shape[0] // 2
        packs = [
            jnp.concatenate([b[part * half : (part + 1) * half] for b in line], axis=0)
            for part, _, _ in parts
        ]
        packs = [after(p, late) for p in packs]
        for level in (1, 2):
            grown = []
            for pack, names in zip(packs, parts):
                axis = names[level]
                steps = [pack]
                for _ in range(length[axis] - 1):
                    steps.append(move(steps[-1], axis * 2, 1))
                grown.append(jnp.concatenate(steps, axis=0))
            packs = grown
        return jnp.concatenate(packs, axis=0)

    def block_order():
        found = {}
        for axis, n in length.items():
            here = jnp.arange(n)[:, None] == lax.axis_index(axis)
            found[axis] = jnp.sum(jnp.where(here, jnp.asarray(home_table(n)), 0), axis=0)
        z = found["z"][None, None, :]
        blocks = []
        for part, second, third in parts:
            at = {second: found[second][None, :, None], third: found[third][:, None, None]}
            chip = (z * nx + at["x"]) * ny + at["y"]
            blocks.append((chip * 2 + part).reshape(-1))
        return jnp.concatenate(blocks)

    def copy_kernel(order_ref, *refs):
        out_ref = refs[-1]
        for i, ref in enumerate(refs[:-1]):
            out_ref[i] = ref[0]

    def permute_blocks(values, order):
        count, each = order.shape[0], 4
        rows, columns = values.shape[0] // count, values.shape[1]
        values = values.reshape(count, rows, columns)
        result = pl.pallas_call(
            copy_kernel,
            grid_spec=pltpu.PrefetchScalarGridSpec(
                num_scalar_prefetch=1,
                grid=(count // each,),
                in_specs=[
                    pl.BlockSpec(
                        (1, rows, columns), lambda i, order, j=j: (order[i * each + j], 0, 0)
                    )
                    for j in range(each)
                ],
                out_specs=pl.BlockSpec((each, rows, columns), lambda i, order: (i, 0, 0)),
            ),
            out_shape=jax.ShapeDtypeStruct((count, rows, columns), values.dtype),
            cost_estimate=pl.CostEstimate(flops=0, bytes_accessed=2**24, transcendentals=0),
            compiler_params=pltpu.CompilerParams(vmem_limit_bytes=32 * 2**20),
        )(order, *[values] * each)
        return result.reshape(count * rows, columns)

    def sum_level(packs, level):
        summed = []
        for pack, names in zip(packs, parts):
            n = length[names[level]]
            pack = pack.reshape(n, pack.shape[0] // n, *pack.shape[1:])
            acc = None
            for s in reversed(range(n)):
                acc = pack[s] if acc is None else add_low(move(acc, names[level] * 2, -1), pack[s])
            summed.append(acc)
        return summed

    def scatter_first(values):
        count = values.shape[0] // 2
        return sum_level([values[:count], values[count:]], 2)

    def scatter_second(halves):
        packs = [jnp.concatenate(same, axis=1) for same in zip(*halves)]
        packs = [p[0] for p in sum_level(packs, 1)]
        half = packs[0].shape[0] // nz
        return [
            jnp.concatenate([p[s * half : (s + 1) * half] for p in packs], axis=0)
            for s in range(nz)
        ]

    def sum_line(blocks):
        total = blocks[-1]
        for mine in reversed(blocks[:-1]):
            total = add_low(move(total, "zz", -1), mine)
        return total.astype(f32)

    def chip_half(own):
        half = own.shape[1] // 2
        core = lax.axis_index("core")
        left, right = own[:, :half], own[:, half:]
        kept = jnp.where(core == 0, left, right)
        came = swap_core(jnp.where(core == 0, right, left))
        return jnp.where(
            core == 0, jnp.concatenate([kept, came], axis=0), jnp.concatenate([came, kept], axis=0)
        )

    def gather_halves(line):
        rows, half = line[0].shape
        steps = [jnp.concatenate(line, axis=0)]
        for _ in range(nx - 1):
            steps.append(move(steps[-1], "xy", 1))
        packs = [jnp.concatenate(steps, axis=0)]
        for _ in range(nx - 1):
            packs.append(move(packs[-1], "yx", 1))
        result = jnp.concatenate(packs, axis=0)
        return result, swap_core(result)

    def scatter_halves_first(mine, other):
        both = add_low(swap_core(other), mine)
        grid = both.reshape(nx, nx, both.shape[0] // (nx * nx), both.shape[1])
        acc = None
        for s in reversed(range(nx)):
            acc = grid[s] if acc is None else add_low(move(acc, "yx", -1), grid[s])
        return acc

    def scatter_halves_second(acc, *late):
        core = lax.axis_index("core")
        rows = acc.shape[1] // (nz * 2)
        two = None
        for s in reversed(range(nx)):
            two = acc[s] if two is None else add_low(move(two, "xy", -1), acc[s])
        two = after(two, *late)
        total = None
        for s in reversed(range(nz)):
            mine = two[s * 2 * rows : (s + 1) * 2 * rows]
            total = mine if total is None else add_low(move(total, "zz", -1), mine)
        kept = jnp.where(core == 0, total[:rows], total[rows:])
        came = swap_core(jnp.where(core == 0, total[rows:], total[:rows]))
        return (
            jnp.where(core == 0, kept, came).astype(f32),
            jnp.where(core == 0, came, kept).astype(f32),
        )

    def after(values, *first, always=False):
        if not (whole or always):
            return values
        anywhere = pl.BlockSpec(memory_space=pl.ANY)
        return pl.pallas_call(
            keep_kernel,
            in_specs=[anywhere] * (1 + len(first)),
            out_specs=anywhere,
            out_shape=jax.ShapeDtypeStruct(values.shape, values.dtype),
            input_output_aliases={0: 0},
        )(values, *first)

    def all_to_all_plane(values):
        return lax.all_to_all(values, PLANE, split_axis=0, concat_axis=0, tiled=True)

    rows_home = D // planes
    across = rows_home // piece
    rest = 2 * narrow_pad + wide

    def cut_spare(part):
        part = part.reshape(spare, rows_home, 2, planes, piece)
        part = part.transpose(3, 1, 2, 0, 4).reshape(planes, rows_home, 2, narrow)
        part = jnp.pad(part, ((0, 0), (0, 0), (0, 0), (0, narrow_pad - narrow)))
        return part.reshape(planes, rows_home, 2 * narrow_pad)

    def join_spare(part):
        part = part.reshape(planes, rows_home, 2, narrow_pad)[..., :narrow]
        part = part.reshape(planes, rows_home, 2, spare, piece).transpose(3, 1, 2, 0, 4)
        return part.reshape(spare, rows_home, 2 * FF)

    def lanes(values, first, width=piece):
        return values[:, first : first + width]

    packed_columns = 2 * units + wide

    def pack_kernel(gate_up_ref, spare_ref, down_ref, spare_down_ref, out_ref, low_ref):
        step = pl.program_id(0)
        out_ref[step, :, pl.ds(0, 2 * wide)] = gate_up_ref[0].astype(bf16)
        for j in range(across):
            out_ref[step, pl.ds(j * piece, piece), pl.ds(2 * units, wide)] = down_ref[
                0, :, pl.ds(j * wide, wide)
            ].astype(bf16)

        @pl.when(step == 0)
        def _():
            for to in range(planes):
                taken = [
                    lanes(spare_ref[s], g * FF + to * piece) for g in range(2) for s in range(spare)
                ]
                out_ref[to, :, pl.ds(2 * wide, 2 * narrow)] = jnp.concatenate(taken, axis=1).astype(
                    bf16
                )
            for s in range(spare):
                low_ref[pl.ds(s * piece, piece), :] = spare_down_ref[s].astype(bf16)

    def pack_experts(gate_up, down):
        if not whole:
            low = down.astype(bf16).reshape(narrow, D)
            low = jnp.pad(low, ((0, narrow_pad - narrow), (0, 0)))
            return cut_spare(gate_up.astype(bf16)), low
        return pl.pallas_call(
            pack_kernel,
            grid=(planes,),
            in_specs=[
                pl.BlockSpec((1, rows_home, 2 * FF), lambda i: (i, 0, 0)),
                pl.BlockSpec((spare, rows_home, 2 * FF), lambda i: (planes // spare, 0, 0)),
                pl.BlockSpec((1, piece, D), lambda i: (i, 0, 0)),
                pl.BlockSpec((spare, piece, D), lambda i: (planes // spare, 0, 0)),
            ],
            out_specs=[
                pl.BlockSpec((planes, rows_home, packed_columns), lambda i: (0, 0, 0)),
                pl.BlockSpec((narrow, D), lambda i: (0, 0)),
            ],
            out_shape=[
                jax.ShapeDtypeStruct((planes, rows_home, packed_columns), bf16),
                jax.ShapeDtypeStruct((narrow, D), bf16),
            ],
            cost_estimate=pl.CostEstimate(flops=0, bytes_accessed=2**24, transcendentals=0),
            compiler_params=pltpu.CompilerParams(vmem_limit_bytes=48 * 2**20),
        )(gate_up, gate_up, down, down)

    def down_of(packed, low):
        if not whole:
            return low
        mine = packed[:, 2 * units :].reshape(planes, across, piece, wide)
        mine = mine.transpose(0, 2, 1, 3).reshape(wide, D)
        return jnp.concatenate([mine, low], axis=0)

    def combine_kernel(a_ref, came_a_ref, b_ref, came_b_ref, c_ref, came_c_ref, full_ref, rest_ref, low_ref):
        total = a_ref[...].astype(f32) + came_a_ref[...].astype(f32)
        full_ref[0] = total[:, : 2 * wide].astype(bf16)
        rest_ref[0, :, pl.ds(0, 2 * narrow_pad)] = total[:, 2 * wide :].astype(bf16)
        total = residual_scale * (b_ref[...].astype(f32) + came_b_ref[...].astype(f32))
        for j in range(across):
            rest_ref[0, pl.ds(j * piece, piece), pl.ds(2 * narrow_pad, wide)] = total[
                :, j * wide : (j + 1) * wide
            ].astype(bf16)
        low_ref[...] = residual_scale * (c_ref[...].astype(f32) + came_c_ref[...].astype(f32))

    def combine_grads(gate_up, came_gate_up, down, came_down):
        if not whole:
            total = (gate_up.astype(f32) + came_gate_up.astype(f32)).astype(bf16)
            low = residual_scale * (down.astype(f32) + came_down.astype(f32))
            return None, total.reshape(planes, rows_home, rest), low
        return pl.pallas_call(
            combine_kernel,
            grid=(planes,),
            in_specs=[pl.BlockSpec((rows_home, 2 * units), lambda i: (i, 0))] * 2
            + [pl.BlockSpec((piece, D), lambda i: (i, 0))] * 2
            + [pl.BlockSpec((narrow, D), lambda i: (wide // narrow, 0))] * 2,
            out_specs=[
                pl.BlockSpec((1, rows_home, 2 * FF), lambda i: (i, 0, 0)),
                pl.BlockSpec((1, rows_home, rest), lambda i: (i, 0, 0)),
                pl.BlockSpec((narrow, D), lambda i: (0, 0)),
            ],
            out_shape=[
                jax.ShapeDtypeStruct((planes, rows_home, 2 * FF), bf16),
                jax.ShapeDtypeStruct((planes, rows_home, rest), bf16),
                jax.ShapeDtypeStruct((narrow, D), f32),
            ],
            cost_estimate=pl.CostEstimate(flops=0, bytes_accessed=2**24, transcendentals=0),
            compiler_params=pltpu.CompilerParams(vmem_limit_bytes=48 * 2**20),
        )(gate_up, came_gate_up, down, came_down, down, came_down)

    gate_up_rate = D ** (-0.5)
    down_rate = max(2, FF // 128) ** (-0.5)

    def full_kernel(home_ref, w_ref, m_ref, s_ref, *outs):
        done = adam_step(
            w_ref[0], m_ref[0], s_ref[0], home_ref[0].astype(f32), gate_up_rate, weight_decay
        )
        for ref, value in zip(outs, done):
            ref[0] = value

    def spare_kernel(home_ref, w_ref, m_ref, s_ref, a_ref, b_ref, c_ref, *outs):
        for s in range(spare):

            @pl.when(pl.program_id(0) == s)
            def _():
                grad = jnp.concatenate(
                    [
                        lanes(home_ref[p], g * narrow_pad + s * piece)
                        for g in range(2)
                        for p in range(planes)
                    ],
                    axis=1,
                ).astype(f32)
                done = adam_step(w_ref[0], m_ref[0], s_ref[0], grad, gate_up_rate, weight_decay)
                for ref, value in zip(outs, done):
                    ref[0] = value

    def down_kernel(home_ref, low_ref, w_ref, m_ref, s_ref, *outs):
        def update(grad):
            done = adam_step(w_ref[0], m_ref[0], s_ref[0], grad, down_rate, weight_decay)
            for ref, value in zip(outs, done):
                ref[0] = value

        @pl.when(pl.program_id(0) < planes)
        def _():
            update(
                jnp.concatenate(
                    [
                        home_ref[0, pl.ds(j * piece, piece), pl.ds(2 * narrow_pad, wide)]
                        for j in range(across)
                    ],
                    axis=1,
                ).astype(f32)
            )

        @pl.when(pl.program_id(0) >= planes)
        def _():
            update(low_ref[...])

    def update_experts(home_full, home_rest, low, gate_up, down):
        if not whole:
            grad = join_spare(home_rest).astype(f32)
            return (
                adam_step(*gate_up, grad, gate_up_rate, weight_decay),
                adam_step(
                    *down, low[:narrow].reshape(spare, piece, D), down_rate, weight_decay
                ),
            )
        params = pltpu.CompilerParams(vmem_limit_bytes=48 * 2**20)
        shapes = [jax.ShapeDtypeStruct(gate_up[0].shape, f32)] * 3
        one = pl.BlockSpec((1, rows_home, 2 * FF), lambda i: (i, 0, 0))
        last = pl.BlockSpec((1, rows_home, 2 * FF), lambda i: (planes + i, 0, 0))
        new_gate_up = pl.pallas_call(
            full_kernel,
            grid=(planes,),
            in_specs=[one] * 4,
            out_specs=[one] * 3,
            cost_estimate=pl.CostEstimate(flops=0, bytes_accessed=2**25, transcendentals=0),
            out_shape=shapes,
            compiler_params=params,
        )(home_full, *gate_up)
        new_gate_up = pl.pallas_call(
            spare_kernel,
            grid=(spare,),
            in_specs=[pl.BlockSpec((planes, rows_home, 2 * narrow_pad), lambda i: (0, 0, 0))]
            + [last] * 3
            + [pl.BlockSpec(memory_space=pl.ANY)] * 3,
            out_specs=[last] * 3,
            out_shape=shapes,
            input_output_aliases={4: 0, 5: 1, 6: 2},
            compiler_params=params,
        )(home_rest, *gate_up, *new_gate_up)
        row = pl.BlockSpec((1, piece, D), lambda i: (i, 0, 0))
        new_down = pl.pallas_call(
            down_kernel,
            grid=(per_group,),
            in_specs=[
                pl.BlockSpec((1, rows_home, rest), lambda i: (jnp.minimum(i, planes - 1), 0, 0)),
                pl.BlockSpec((piece, D), lambda i: (jnp.maximum(i - planes, 0), 0)),
            ]
            + [row] * 3,
            out_specs=[row] * 3,
            cost_estimate=pl.CostEstimate(flops=0, bytes_accessed=2**24, transcendentals=0),
            out_shape=[jax.ShapeDtypeStruct(down[0].shape, f32)] * 3,
            compiler_params=params,
        )(home_rest, low, *down)
        return new_gate_up, new_down

    def unit_experts(group, place):
        base = group * per_group
        sets = []
        if whole:
            sets.append(jnp.full((wide,), base + place))
        behind = base + whole * planes + jnp.arange(narrow_pad) // piece
        sets.append(jnp.where(jnp.arange(narrow_pad) < narrow, behind, -1))
        return jnp.concatenate(sets)

    def columns_of():
        pieces = []
        for first in range(0, wide, 256):
            pieces.append((first, wide + first, first, min(256, wide - first)))
        pieces.append((2 * wide, 2 * wide + narrow_pad, wide, narrow_pad))
        return pieces

    def expert_kernel(first_call, *refs):
        rows_ref, gates_ref = refs[:2]
        reaches, weights = refs[2:4], refs[4:6]
        twice_ref, once_ref = refs[6:8]
        gated_ref, grad_ref, two_ref = refs[8 + (0 if first_call else 2) :]
        blocks, rows_of, _ = rows_ref.shape
        count = blocks * rows_of
        rows = rows_ref[...].reshape(count, D)
        gates = gates_ref[...].reshape(count, LANES)
        dgate = jnp.zeros((count, LANES), f32)
        for k in range(2):
            for gate_at, up_at, unit_at, width in columns_of():
                unit = pl.ds(k * units + unit_at, width)
                gate_w = weights[k][:, pl.ds(gate_at, width)]
                up_w = weights[k][:, pl.ds(up_at, width)]
                gate_part = jnp.dot(rows, gate_w, preferred_element_type=f32)
                up_part = jnp.dot(rows, up_w, preferred_element_type=f32)
                gate_wide = jnp.dot(gates, twice_ref[:, unit], preferred_element_type=f32)
                reach = reaches[k][:, :, pl.ds(unit_at, width)].reshape(count, width)
                reach = residual_scale * reach
                squash = 1.0 / (1.0 + jnp.exp(-gate_part))
                swish = gate_part * squash
                hidden = swish * up_part
                gated = (hidden * gate_wide).astype(bf16)
                gated_ref[:, :, unit] = gated.reshape(blocks, rows_of, width)
                dgate += dot_nt((hidden * reach).astype(bf16), once_ref[:, unit])
                grad_hidden = reach * gate_wide
                grad_gate = grad_hidden * up_part * squash * (1.0 + gate_part * (1.0 - squash))
                for at, value in ((gate_at, grad_gate), (up_at, grad_hidden * swish)):
                    grad_ref[:, :, pl.ds(k * 2 * units + at, width)] = value.astype(bf16).reshape(
                        blocks, rows_of, width
                    )
        two = jnp.zeros((count, D), f32)
        for k in range(2):
            grad = grad_ref[:, :, pl.ds(k * 2 * units, 2 * units)].reshape(count, 2 * units)
            two += dot_nt(grad, weights[k][...])
        two_ref[:, :, pl.ds(0, D)] = two.astype(bf16).reshape(blocks, rows_of, D)
        two_ref[:, :, pl.ds(D, LANES)] = dgate.astype(bf16).reshape(blocks, rows_of, LANES)

    def run_experts(at, sent, reach, own, other, twice, once, before):
        blocks, rows_of, _ = sent.shape
        rows_of = rows_of // 2
        tile = max(1, 512 // rows_of)

        def by_rows(columns, column=0):
            return pl.BlockSpec((tile, rows_of, columns), lambda i: (i, at, column))

        def fixed(rows, columns):
            return pl.BlockSpec((rows, columns), lambda i: (0, 0), pipeline_mode=pl.Buffered(1))

        kept = list(before) if before else []
        count = blocks * rows_of
        return pl.pallas_call(
            functools.partial(expert_kernel, not kept),
            grid=(blocks // tile,),
            in_specs=[by_rows(D), by_rows(LANES, D // LANES)]
            + [by_rows(units)] * 2
            + [fixed(D, 2 * units)] * 2
            + [fixed(LANES, 2 * units)] * 2
            + [pl.BlockSpec(memory_space=pl.ANY)] * len(kept),
            out_specs=[
                by_rows(2 * units),
                by_rows(4 * units),
                pl.BlockSpec((tile, rows_of, D + LANES), lambda i: (i, 0, 0)),
            ],
            out_shape=[
                jax.ShapeDtypeStruct((blocks, 2 * rows_of, 2 * units), bf16),
                jax.ShapeDtypeStruct((blocks, 2 * rows_of, 4 * units), bf16),
                jax.ShapeDtypeStruct((blocks, rows_of, D + LANES), bf16),
            ],
            input_output_aliases={8 + i: i for i in range(len(kept))},
            cost_estimate=pl.CostEstimate(
                flops=16 * count * D * units, bytes_accessed=2**25, transcendentals=2 * count * units
            ),
            compiler_params=pltpu.CompilerParams(vmem_limit_bytes=60 * 2**20),
        )(sent, sent, *reach, own, other, twice, once, *kept)

    def shards(
        tokens,
        cotangent,
        routes,
        weight_qkv,
        moment_qkv,
        square_qkv,
        weight_out,
        moment_out,
        square_out,
        weight_router,
        moment_router,
        square_router,
        gains,
        moment_gains,
        square_gains,
        weight_gate_up,
        moment_gate_up,
        square_gate_up,
        weight_down,
        moment_down,
        square_down,
    ):
        sequence_length = tokens.shape[0]
        head_groups = QUERY_HEADS // KEY_VALUE_HEADS
        place = lax.axis_index(PLANE)
        group = lax.axis_index("y") * 2 + lax.axis_index("core")
        partner = lax.axis_index("y") * 2 + 1 - lax.axis_index("core")

        small = pad_lanes(jnp.concatenate([weight_router, gains.T], axis=1))
        first_pack = jnp.concatenate([weight_qkv, small], axis=1).astype(bf16)
        first_all = lax.all_gather(first_pack, ALL, axis=0, tiled=True)

        packed, low_own = pack_experts(weight_gate_up, weight_down)
        out_line = line_of(chip_half(weight_out.astype(bf16)))
        cot_line = line_of(after(cotangent, low_own, out_line[1]))
        own = all_to_all_plane(after(packed, cot_line[-1], out_line[-1])).reshape(D, -1)
        out_mine, out_other = gather_halves(out_line)
        core = lax.axis_index("core")
        order_mine, order_other = row_order(core), row_order(1 - core)
        blocks_order = block_order()

        qkv_w = first_all[:, :QKV]
        router_w = first_all[:, QKV : QKV + EXPERTS]
        gain_one = first_all[:, QKV + EXPERTS].astype(f32)
        gain_two = first_all[:, QKV + EXPERTS + 1].astype(f32)

        inputs = tokens.astype(f32)
        factor_one = lax.rsqrt(jnp.mean(inputs * inputs, axis=-1, keepdims=True) + norm_eps)
        hidden_one = (inputs * factor_one * gain_one).astype(bf16)
        joined_heads = dot(hidden_one, qkv_w)
        cot_all = gather_tokens(cot_line, joined_heads)
        hidden_mine = dot(hidden_one, order_mine).astype(bf16)
        hidden_other = dot(hidden_one, order_other).astype(bf16)
        query_rows = joined_heads[:, :HEADS_WIDTH].reshape(sequence_length, QUERY_HEADS, HEAD_SIZE)
        every_key = joined_heads[:, HEADS_WIDTH : HEADS_WIDTH + KEYS_WIDTH].reshape(
            sequence_length, KEY_VALUE_HEADS, HEAD_SIZE
        )
        every_value = joined_heads[:, HEADS_WIDTH + KEYS_WIDTH :].reshape(
            sequence_length, KEY_VALUE_HEADS, HEAD_SIZE
        )
        cosine_lookup, sine_lookup = rotary_tables(sequence_length, HEAD_SIZE)
        query_rotated = (
            apply_rotation(query_rows, cosine_lookup, sine_lookup)
            .astype(bf16)
            .reshape(sequence_length, KEY_VALUE_HEADS, head_groups, HEAD_SIZE)
        )
        key_rot = apply_rotation(every_key, cosine_lookup, sine_lookup).astype(bf16)
        value_low = every_value.astype(bf16)
        causal = jnp.arange(sequence_length)[:, None] >= jnp.arange(sequence_length)[None, :]
        scores = attention_scores(query_rotated, key_rot, causal)
        peak = jnp.max(scores, axis=-1, keepdims=True)
        expo = jnp.exp(scores - peak)
        totals = jnp.sum(expo, axis=-1, keepdims=True)
        probs = expo / totals
        prob_low = probs.astype(bf16)
        heads = jnp.einsum("kgst,tkd->skgd", prob_low, value_low, preferred_element_type=f32)
        attended = heads.reshape(sequence_length, HEADS_WIDTH).astype(bf16)
        attended_mine = dot(attended, order_mine).astype(bf16)
        attended_other = dot(attended, order_other).astype(bf16)
        projected = [dot(attended_mine, out_mine), dot(attended_other, out_other)]
        mid = inputs + residual_scale * jnp.where(
            core == 0,
            jnp.concatenate(projected, axis=1),
            jnp.concatenate(projected[::-1], axis=1),
        )
        factor_two = lax.rsqrt(jnp.mean(mid * mid, axis=-1, keepdims=True) + norm_eps)
        hidden_two = (mid * factor_two * gain_two).astype(bf16)
        logits = dot(hidden_two, router_w)
        named = jnp.any(
            routes[..., None] == jnp.arange(EXPERTS, dtype=routes.dtype)[None, None, :], axis=1
        )
        shown = jnp.where(named, logits, -jnp.inf)
        raised = jnp.exp(shown - jnp.max(shown, axis=-1, keepdims=True))
        gates = raised / jnp.sum(raised, axis=-1, keepdims=True)

        gate_high = gates.astype(bf16)
        gate_rest = (gates - gate_high.astype(f32)).astype(bf16)
        sent = jnp.concatenate(
            [hidden_two, pad_lanes(jnp.concatenate([gate_high, gate_rest], axis=1))], axis=1
        )
        sent_all = lax.all_gather(sent, SAME_CORE, axis=0, tiled=True)
        sent_all = permute_blocks(sent_all, blocks_order)
        own = after(own, cot_all)
        other, low_other = swap_core(own), swap_core(low_own)
        down_own, down_other = down_of(own, low_own), down_of(other, low_other)
        blocks = 2 * nx * ny
        reach = [dot_nt(cot_all, d).reshape(blocks, -1, units) for d in (down_own, down_other)]

        behind = jnp.concatenate([unit_experts(group, place), unit_experts(partner, place)])
        numbers = jnp.arange(LANES)[:, None]
        real = behind[None, :] >= 0
        once = ((numbers == behind[None, :]) & real).astype(bf16)
        twice = once + ((numbers == behind[None, :] + EXPERTS) & real).astype(bf16)
        kept = None
        firsts = []
        sent_blocks = sent_all.reshape(blocks, -1, sent_all.shape[1])
        for at in range(2):
            *kept, two = run_experts(at, sent_blocks, reach, own, other, twice, once, kept)
            firsts.append(scatter_first(two))
        two_sum = sum_line(scatter_second(firsts))

        gated, grad_both = (k.reshape(-1, k.shape[2]) for k in kept)
        gated, grad_both = after(gated, *firsts[-1], always=True), after(grad_both, *firsts[-1])
        rows_all = after(sent_all, *firsts[-1], always=True)[:, :D]
        mixed = (dot(gated[:, :units], down_own) + dot(gated[:, units:], down_other)).astype(bf16)
        mixed = after(mixed, two_sum, always=True).reshape(blocks, -1, D)
        mixed_first = scatter_first(mixed)

        came_gate_up = swap_core(dot_tn(rows_all, grad_both[:, 2 * units :]).astype(bf16))
        came_down = swap_core(dot_tn(gated[:, units:], cot_all).astype(bf16))
        full, more, low = combine_grads(
            dot_tn(rows_all, grad_both[:, : 2 * units]).astype(bf16),
            came_gate_up,
            dot_tn(gated[:, :units], cot_all).astype(bf16),
            came_down,
        )
        home_full = all_to_all_plane(after(full, two_sum)) if whole else None
        home_rest = all_to_all_plane(after(more, two_sum))
        two_sum = after(two_sum, low)
        grad_two, grad_gates = two_sum[:, :D], two_sum[:, D : D + EXPERTS]

        grad_out = cotangent.astype(f32)
        grad_chosen = gates * (grad_gates - jnp.sum(gates * grad_gates, axis=-1, keepdims=True))
        grad_logits = grad_chosen.astype(bf16)
        grad_router = dot_tn(hidden_two, grad_logits)
        grad_two = grad_two + dot_nt(grad_logits, router_w)
        grad_mid, grad_gain_two = norm_backward(grad_two, mid, factor_two, gain_two)
        grad_mid = grad_out + grad_mid
        grad_att = (residual_scale * grad_mid).astype(bf16)
        att_left, att_right = grad_att[:, : D // 2], grad_att[:, D // 2 :]
        att_mine = jnp.where(core == 0, att_left, att_right)
        att_other = jnp.where(core == 0, att_right, att_left)
        grad_heads = (
            dot_nt(dot_nt(att_mine, out_mine).astype(bf16), order_mine)
            + dot_nt(dot_nt(att_other, out_other).astype(bf16), order_other)
        )
        grad_heads = grad_heads.astype(bf16).reshape(
            sequence_length, KEY_VALUE_HEADS, head_groups, HEAD_SIZE
        )
        out_first = scatter_halves_first(
            dot_tn(attended_mine, att_mine).astype(bf16),
            dot_tn(attended_other, att_other).astype(bf16),
        )
        out_left, out_right = scatter_halves_second(out_first)
        grad_probs = jnp.einsum(
            "skgd,tkd->kgst", grad_heads, value_low, preferred_element_type=f32
        )
        value_gradient = jnp.einsum(
            "kgst,skgd->tkd", prob_low, grad_heads, preferred_element_type=f32
        )
        row_dot = jnp.sum(probs * grad_probs, axis=-1, keepdims=True)
        grad_scores = (probs * (grad_probs - row_dot)).astype(bf16)
        grad_qrot = (
            jnp.einsum("kgst,tkd->skgd", grad_scores, key_rot, preferred_element_type=f32)
            * score_scale
        )
        grad_krot = (
            jnp.einsum("kgst,skgd->tkd", grad_scores, query_rotated, preferred_element_type=f32)
            * score_scale
        )
        grad_queries = apply_rotation(
            grad_qrot.reshape(sequence_length, QUERY_HEADS, HEAD_SIZE), cosine_lookup, -sine_lookup
        )
        key_gradient = apply_rotation(grad_krot, cosine_lookup, -sine_lookup)
        grad_joined = jnp.concatenate(
            [
                grad_queries.reshape(sequence_length, HEADS_WIDTH),
                key_gradient.reshape(sequence_length, KEYS_WIDTH),
                value_gradient.reshape(sequence_length, KEYS_WIDTH),
            ],
            axis=1,
        ).astype(bf16)
        grad_one = dot_nt(grad_joined, qkv_w)
        grad_inputs, grad_gain_one = norm_backward(grad_one, inputs, factor_one, gain_one)
        token_grad = grad_mid + grad_inputs
        small_sent = pad_lanes(
            jnp.concatenate([grad_router, grad_gain_one[:, None], grad_gain_two[:, None]], axis=1)
        )
        small_sent = small_sent.astype(bf16)
        joined_left, joined_right = grad_joined[:, : QKV // 2], grad_joined[:, QKV // 2 :]
        qkv_sent = []
        for hidden, rows_order, at in (
            (hidden_mine, order_mine, core),
            (hidden_other, order_other, 1 - core),
        ):
            product = dot_tn(hidden, jnp.where(at == 0, joined_left, joined_right))
            extra = jnp.where(at == 0, dot_tn(rows_order, small_sent), 0.0)
            qkv_sent.append(jnp.concatenate([product, extra], axis=1).astype(bf16))
        qkv_first = scatter_halves_first(qkv_sent[0], after(qkv_sent[1], out_first, home_full))
        mixed = sum_line(scatter_second([[after(m, qkv_first) for m in mixed_first]]))
        layer_out = (mid + residual_scale * mixed).astype(bf16)
        qkv_left, qkv_right = scatter_halves_second(qkv_first, home_rest)
        sum_out = jnp.concatenate([out_left, out_right], axis=1)
        sum_qkv = jnp.concatenate([qkv_left[:, : QKV // 2], qkv_right[:, : QKV // 2]], axis=1)
        sum_router = qkv_left[:, QKV // 2 : QKV // 2 + EXPERTS]
        sum_gains = qkv_left[:, QKV // 2 + EXPERTS : QKV // 2 + EXPERTS + 2].T

        new_gate_up, new_down = update_experts(
            home_full,
            home_rest,
            low,
            (weight_gate_up, moment_gate_up, square_gate_up),
            (weight_down, moment_down, square_down),
        )
        new_qkv = adam_step(weight_qkv, moment_qkv, square_qkv, sum_qkv, D ** (-0.5), weight_decay)
        new_out = adam_step(
            weight_out,
            moment_out,
            square_out,
            sum_out,
            max(4, QUERY_HEADS * HEAD_SIZE // 256) ** (-0.5),
            weight_decay,
        )
        new_router = adam_step(
            weight_router, moment_router, square_router, sum_router, (4 * D) ** (-0.5), weight_decay
        )
        new_gains = adam_step(gains, moment_gains, square_gains, sum_gains, 0.75, 0.0)
        return (
            layer_out,
            token_grad,
            *new_qkv,
            *new_out,
            *new_router,
            *new_gains,
            *new_gate_up,
            *new_down,
        )

    return shards


def solution(mesh):
    n_dp, n_expert = mesh.shape["dp"], mesh.shape["expert"]
    nz = 4
    nx, ny = n_dp // nz, n_expert // 2
    fine = Mesh(mesh.devices.reshape(nz, nx, ny, 2), ALL)
    rows = P(ALL, None)
    columns = P(None, ALL)
    experts = P(("y", "core"), ("z", "x"), None)
    dense = (rows,) * 9 + (columns,) * 3 + (experts,) * 6
    return jax.shard_map(
        make_shards((nz, nx, ny)),
        mesh=fine,
        in_specs=(rows,) * 3 + dense,
        out_specs=(rows,) * 2 + dense,
        check_vma=False,
    )
```

```python
import functools

import jax
import jax.numpy as jnp
import numpy as np
from jax import lax
from jax.experimental import pallas as pl
from jax.experimental.pallas import tpu as pltpu
from jax.sharding import Mesh, PartitionSpec as P

D = 1536
QUERY_HEADS = 24
KEY_VALUE_HEADS = 8
HEAD_SIZE = 64
FF = 512
EXPERTS = 40
TOPK = 8
STEP = 10
QKV = 2560
LANES = 128
HEADS_WIDTH = QUERY_HEADS * HEAD_SIZE
KEYS_WIDTH = KEY_VALUE_HEADS * HEAD_SIZE

norm_eps = 1e-06
residual_scale = 0.22
score_scale = 0.125
beta_one = 0.9
beta_two = 0.95
adam_eps = 1e-08
weight_decay = 0.1

f32 = jnp.float32
bf16 = jnp.bfloat16
ALL = ("z", "x", "y", "core")
PLANE = ("z", "x")
SAME_CORE = ("z", "x", "y")


def rotary_tables(sequence_length, size):
    half = size // 2
    places = jnp.arange(sequence_length).astype(f32)[:, None]
    inverse = 10000.0 ** (-jnp.arange(half).astype(f32) * 2.0 / size)
    angles = places * inverse[None, :]
    return (jnp.cos(angles)[:, None, :], jnp.sin(angles)[:, None, :])


def apply_rotation(values, cosine_lookup, sine_lookup):
    half = values.shape[-1] // 2
    first = values[..., :half]
    second = values[..., half:]
    return jnp.concatenate(
        [
            first * cosine_lookup - second * sine_lookup,
            second * cosine_lookup + first * sine_lookup,
        ],
        axis=-1,
    )


def attention_scores(query_rotated, key_rot, causal):
    scores = (
        jnp.einsum("skgd,tkd->kgst", query_rotated, key_rot, preferred_element_type=f32)
        * score_scale
    )
    return jnp.where(causal, scores, -1e30)


def norm_backward(grad_normed, values, factor, gain):
    scaled = grad_normed * gain
    grad_gain = jnp.sum(grad_normed * values * factor, axis=0)
    value_gradient = factor * scaled - values * factor * factor * factor * jnp.mean(
        scaled * values, axis=-1, keepdims=True
    )
    return (value_gradient, grad_gain)


def adam_step(weight, moment, square, grad, rate, decay):
    moment = beta_one * moment + (1.0 - beta_one) * grad
    square = beta_two * square + (1.0 - beta_two) * grad * grad
    fixed_one = moment / (1.0 - beta_one**STEP)
    fixed_two = square / (1.0 - beta_two**STEP)
    weight = weight - rate * (fixed_one / (jnp.sqrt(fixed_two) + adam_eps) + decay * weight)
    return (weight, moment, square)


def dot(a, b):
    return jnp.dot(a, b, preferred_element_type=f32)


def dot_nt(a, b):
    return lax.dot_general(a, b, (((1,), (1,)), ((), ())), preferred_element_type=f32)


def dot_tn(a, b):
    return lax.dot_general(a, b, (((0,), (0,)), ((), ())), preferred_element_type=f32)


def pad_lanes(values):
    extra = -values.shape[-1] % LANES
    return jnp.pad(values, ((0, 0), (0, extra)))


def swap_core(values):
    return lax.ppermute(values, "core", [(0, 1), (1, 0)])


def keep_kernel(*refs):
    pass


def ring_order(n):
    return [0] + list(range(1, n, 2)) + list(range(n - 2 + n % 2, 0, -2))


def home_table(n):
    order = ring_order(n)
    place = {chip: at for at, chip in enumerate(order)}
    return np.array([[order[(place[i] - s) % n] for s in range(n)] for i in range(n)], np.int32)


def make_shards(sizes):
    nz, nx, ny = sizes
    length = {"z": nz, "x": nx, "y": ny}
    planes = nz * nx
    per_group = EXPERTS // (2 * ny)
    whole = per_group // planes
    spare = per_group - whole * planes
    piece = FF // planes
    wide = whole * FF
    narrow = spare * piece
    narrow_pad = narrow + -narrow % LANES
    units = wide + narrow_pad

    rings = {axis: ring_order(n) for axis, n in length.items()}
    places = {axis: i for i, axis in enumerate(("z", "x", "y", "core"))}
    shape = (nz, nx, ny, 2)

    def pairs_of(axes, step):
        pairs = []
        for at in np.ndindex(*shape):
            axis = axes[at[3]]
            ring = rings[axis]
            to = list(at)
            to[places[axis]] = ring[(ring.index(at[places[axis]]) + step) % len(ring)]
            pairs.append(
                (int(np.ravel_multi_index(at, shape)), int(np.ravel_multi_index(to, shape)))
            )
        return pairs

    def move(values, axes, step):
        return lax.ppermute(values, ALL, pairs_of(axes, step))

    def row_order(core):
        found = {}
        for axis, n in length.items():
            here = jnp.arange(n)[:, None] == lax.axis_index(axis)
            found[axis] = jnp.sum(jnp.where(here, jnp.asarray(home_table(n)), 0), axis=0)
        x = jnp.where(core == 0, found["x"][None, :], found["x"][:, None])
        y = jnp.where(core == 0, found["y"][:, None], found["y"][None, :])
        chip = (found["z"] * nx + x[:, :, None]) * ny + y[:, :, None]
        block = (chip[..., None] * 2 + jnp.arange(2)).reshape(-1, 1)
        rows = D // block.shape[0]
        kept = (block * rows + jnp.arange(rows)[None, :]).reshape(1, D)
        return (jnp.arange(D)[:, None] == kept).astype(bf16)

    def add_low(a, b):
        return (a.astype(f32) + b.astype(f32)).astype(bf16)

    parts = ((0, "x", "y"), (1, "y", "x"))

    def line_of(own):
        line = [own]
        for _ in range(nz - 1):
            line.append(move(line[-1], "zz", 1))
        return line

    def gather_tokens(line, late):
        half = line[0].shape[0] // 2
        packs = [
            jnp.concatenate([b[part * half : (part + 1) * half] for b in line], axis=0)
            for part, _, _ in parts
        ]
        packs = [after(p, late) for p in packs]
        for level in (1, 2):
            grown = []
            for pack, names in zip(packs, parts):
                axis = names[level]
                steps = [pack]
                for _ in range(length[axis] - 1):
                    steps.append(move(steps[-1], axis * 2, 1))
                grown.append(jnp.concatenate(steps, axis=0))
            packs = grown
        return jnp.concatenate(packs, axis=0)

    def block_order():
        found = {}
        for axis, n in length.items():
            here = jnp.arange(n)[:, None] == lax.axis_index(axis)
            found[axis] = jnp.sum(jnp.where(here, jnp.asarray(home_table(n)), 0), axis=0)
        z = found["z"][None, None, :]
        blocks = []
        for part, second, third in parts:
            at = {second: found[second][None, :, None], third: found[third][:, None, None]}
            chip = (z * nx + at["x"]) * ny + at["y"]
            blocks.append((chip * 2 + part).reshape(-1))
        return jnp.concatenate(blocks)

    def copy_kernel(order_ref, *refs):
        out_ref = refs[-1]
        for i, ref in enumerate(refs[:-1]):
            out_ref[i] = ref[0]

    def permute_blocks(values, order):
        count, each = order.shape[0], 4
        rows, columns = values.shape[0] // count, values.shape[1]
        values = values.reshape(count, rows, columns)
        result = pl.pallas_call(
            copy_kernel,
            grid_spec=pltpu.PrefetchScalarGridSpec(
                num_scalar_prefetch=1,
                grid=(count // each,),
                in_specs=[
                    pl.BlockSpec(
                        (1, rows, columns), lambda i, order, j=j: (order[i * each + j], 0, 0)
                    )
                    for j in range(each)
                ],
                out_specs=pl.BlockSpec((each, rows, columns), lambda i, order: (i, 0, 0)),
            ),
            out_shape=jax.ShapeDtypeStruct((count, rows, columns), values.dtype),
            cost_estimate=pl.CostEstimate(flops=0, bytes_accessed=2**24, transcendentals=0),
            compiler_params=pltpu.CompilerParams(vmem_limit_bytes=32 * 2**20),
        )(order, *[values] * each)
        return result.reshape(count * rows, columns)

    def sum_level(packs, level):
        summed = []
        for pack, names in zip(packs, parts):
            n = length[names[level]]
            pack = pack.reshape(n, pack.shape[0] // n, *pack.shape[1:])
            acc = None
            for s in reversed(range(n)):
                acc = pack[s] if acc is None else add_low(move(acc, names[level] * 2, -1), pack[s])
            summed.append(acc)
        return summed

    def scatter_first(values):
        count = values.shape[0] // 2
        return sum_level([values[:count], values[count:]], 2)

    def scatter_second(halves):
        packs = [jnp.concatenate(same, axis=1) for same in zip(*halves)]
        packs = [p[0] for p in sum_level(packs, 1)]
        half = packs[0].shape[0] // nz
        return [
            jnp.concatenate([p[s * half : (s + 1) * half] for p in packs], axis=0)
            for s in range(nz)
        ]

    def sum_line(blocks):
        total = blocks[-1]
        for mine in reversed(blocks[:-1]):
            total = add_low(move(total, "zz", -1), mine)
        return total.astype(f32)

    def chip_half(own):
        half = own.shape[1] // 2
        core = lax.axis_index("core")
        left, right = own[:, :half], own[:, half:]
        kept = jnp.where(core == 0, left, right)
        came = swap_core(jnp.where(core == 0, right, left))
        return jnp.where(
            core == 0, jnp.concatenate([kept, came], axis=0), jnp.concatenate([came, kept], axis=0)
        )

    def gather_halves(line):
        rows, half = line[0].shape
        steps = [jnp.concatenate(line, axis=0)]
        for _ in range(nx - 1):
            steps.append(move(steps[-1], "xy", 1))
        packs = [jnp.concatenate(steps, axis=0)]
        for _ in range(nx - 1):
            packs.append(move(packs[-1], "yx", 1))
        result = jnp.concatenate(packs, axis=0)
        return result, swap_core(result)

    def scatter_halves_first(mine, other):
        both = add_low(swap_core(other), mine)
        grid = both.reshape(nx, nx, both.shape[0] // (nx * nx), both.shape[1])
        acc = None
        for s in reversed(range(nx)):
            acc = grid[s] if acc is None else add_low(move(acc, "yx", -1), grid[s])
        return acc

    def scatter_halves_second(acc):
        two = None
        for s in reversed(range(nx)):
            two = acc[s] if two is None else add_low(move(two, "xy", -1), acc[s])
        return two

    def scatter_halves_line(twos, *late):
        core = lax.axis_index("core")
        two = after(jnp.concatenate(twos, axis=1), *late)
        rows = two.shape[0] // (nz * 2)
        total = None
        for s in reversed(range(nz)):
            mine = two[s * 2 * rows : (s + 1) * 2 * rows]
            total = mine if total is None else add_low(move(total, "zz", -1), mine)
        kept = jnp.where(core == 0, total[:rows], total[rows:])
        came = swap_core(jnp.where(core == 0, total[rows:], total[:rows]))
        left = jnp.where(core == 0, kept, came).astype(f32)
        right = jnp.where(core == 0, came, kept).astype(f32)
        found = []
        at = 0
        for part in twos:
            end = at + part.shape[1]
            found.append((left[:, at:end], right[:, at:end]))
            at = end
        return found

    def after(values, *first, always=False):
        if not (whole or always):
            return values
        anywhere = pl.BlockSpec(memory_space=pl.ANY)
        return pl.pallas_call(
            keep_kernel,
            in_specs=[anywhere] * (1 + len(first)),
            out_specs=anywhere,
            out_shape=jax.ShapeDtypeStruct(values.shape, values.dtype),
            input_output_aliases={0: 0},
        )(values, *first)

    def all_to_all_plane(values):
        return lax.all_to_all(values, PLANE, split_axis=0, concat_axis=0, tiled=True)

    rows_home = D // planes
    across = rows_home // piece
    rest = 2 * narrow_pad + wide

    def cut_spare(part):
        part = part.reshape(spare, rows_home, 2, planes, piece)
        part = part.transpose(3, 1, 2, 0, 4).reshape(planes, rows_home, 2, narrow)
        part = jnp.pad(part, ((0, 0), (0, 0), (0, 0), (0, narrow_pad - narrow)))
        return part.reshape(planes, rows_home, 2 * narrow_pad)

    def join_spare(part):
        part = part.reshape(planes, rows_home, 2, narrow_pad)[..., :narrow]
        part = part.reshape(planes, rows_home, 2, spare, piece).transpose(3, 1, 2, 0, 4)
        return part.reshape(spare, rows_home, 2 * FF)

    def lanes(values, first, width=piece):
        return values[:, first : first + width]

    packed_columns = 2 * units + wide

    def pack_kernel(gate_up_ref, spare_ref, down_ref, spare_down_ref, out_ref, low_ref):
        step = pl.program_id(0)
        out_ref[step, :, pl.ds(0, 2 * wide)] = gate_up_ref[0].astype(bf16)
        for j in range(across):
            out_ref[step, pl.ds(j * piece, piece), pl.ds(2 * units, wide)] = down_ref[
                0, :, pl.ds(j * wide, wide)
            ].astype(bf16)

        @pl.when(step == 0)
        def _():
            for to in range(planes):
                taken = [
                    lanes(spare_ref[s], g * FF + to * piece) for g in range(2) for s in range(spare)
                ]
                out_ref[to, :, pl.ds(2 * wide, 2 * narrow)] = jnp.concatenate(taken, axis=1).astype(
                    bf16
                )
            for s in range(spare):
                low_ref[pl.ds(s * piece, piece), :] = spare_down_ref[s].astype(bf16)

    def pack_experts(gate_up, down):
        if not whole:
            low = down.astype(bf16).reshape(narrow, D)
            low = jnp.pad(low, ((0, narrow_pad - narrow), (0, 0)))
            return cut_spare(gate_up.astype(bf16)), low
        return pl.pallas_call(
            pack_kernel,
            grid=(planes,),
            in_specs=[
                pl.BlockSpec((1, rows_home, 2 * FF), lambda i: (i, 0, 0)),
                pl.BlockSpec((spare, rows_home, 2 * FF), lambda i: (planes // spare, 0, 0)),
                pl.BlockSpec((1, piece, D), lambda i: (i, 0, 0)),
                pl.BlockSpec((spare, piece, D), lambda i: (planes // spare, 0, 0)),
            ],
            out_specs=[
                pl.BlockSpec((planes, rows_home, packed_columns), lambda i: (0, 0, 0)),
                pl.BlockSpec((narrow, D), lambda i: (0, 0)),
            ],
            out_shape=[
                jax.ShapeDtypeStruct((planes, rows_home, packed_columns), bf16),
                jax.ShapeDtypeStruct((narrow, D), bf16),
            ],
            cost_estimate=pl.CostEstimate(flops=0, bytes_accessed=2**24, transcendentals=0),
            compiler_params=pltpu.CompilerParams(vmem_limit_bytes=48 * 2**20),
        )(gate_up, gate_up, down, down)

    def down_of(packed, low):
        if not whole:
            return low
        mine = packed[:, 2 * units :].reshape(planes, across, piece, wide)
        mine = mine.transpose(0, 2, 1, 3).reshape(wide, D)
        return jnp.concatenate([mine, low], axis=0)

    def combine_kernel(a_ref, came_a_ref, b_ref, came_b_ref, c_ref, came_c_ref, full_ref, rest_ref, low_ref):
        total = a_ref[...].astype(f32) + came_a_ref[...].astype(f32)
        full_ref[0] = total[:, : 2 * wide].astype(bf16)
        rest_ref[0, :, pl.ds(0, 2 * narrow_pad)] = total[:, 2 * wide :].astype(bf16)
        total = residual_scale * (b_ref[...].astype(f32) + came_b_ref[...].astype(f32))
        for j in range(across):
            rest_ref[0, pl.ds(j * piece, piece), pl.ds(2 * narrow_pad, wide)] = total[
                :, j * wide : (j + 1) * wide
            ].astype(bf16)
        low_ref[...] = residual_scale * (c_ref[...].astype(f32) + came_c_ref[...].astype(f32))

    def combine_grads(gate_up, came_gate_up, down, came_down):
        if not whole:
            total = (gate_up.astype(f32) + came_gate_up.astype(f32)).astype(bf16)
            low = residual_scale * (down.astype(f32) + came_down.astype(f32))
            return None, total.reshape(planes, rows_home, rest), low
        return pl.pallas_call(
            combine_kernel,
            grid=(planes,),
            in_specs=[pl.BlockSpec((rows_home, 2 * units), lambda i: (i, 0))] * 2
            + [pl.BlockSpec((piece, D), lambda i: (i, 0))] * 2
            + [pl.BlockSpec((narrow, D), lambda i: (wide // narrow, 0))] * 2,
            out_specs=[
                pl.BlockSpec((1, rows_home, 2 * FF), lambda i: (i, 0, 0)),
                pl.BlockSpec((1, rows_home, rest), lambda i: (i, 0, 0)),
                pl.BlockSpec((narrow, D), lambda i: (0, 0)),
            ],
            out_shape=[
                jax.ShapeDtypeStruct((planes, rows_home, 2 * FF), bf16),
                jax.ShapeDtypeStruct((planes, rows_home, rest), bf16),
                jax.ShapeDtypeStruct((narrow, D), f32),
            ],
            cost_estimate=pl.CostEstimate(flops=0, bytes_accessed=2**24, transcendentals=0),
            compiler_params=pltpu.CompilerParams(vmem_limit_bytes=48 * 2**20),
        )(gate_up, came_gate_up, down, came_down, down, came_down)

    gate_up_rate = D ** (-0.5)
    down_rate = max(2, FF // 128) ** (-0.5)

    def full_kernel(home_ref, w_ref, m_ref, s_ref, *outs):
        done = adam_step(
            w_ref[0], m_ref[0], s_ref[0], home_ref[0].astype(f32), gate_up_rate, weight_decay
        )
        for ref, value in zip(outs, done):
            ref[0] = value

    def spare_kernel(home_ref, w_ref, m_ref, s_ref, a_ref, b_ref, c_ref, *outs):
        for s in range(spare):

            @pl.when(pl.program_id(0) == s)
            def _():
                grad = jnp.concatenate(
                    [
                        lanes(home_ref[p], g * narrow_pad + s * piece)
                        for g in range(2)
                        for p in range(planes)
                    ],
                    axis=1,
                ).astype(f32)
                done = adam_step(w_ref[0], m_ref[0], s_ref[0], grad, gate_up_rate, weight_decay)
                for ref, value in zip(outs, done):
                    ref[0] = value

    def down_kernel(home_ref, low_ref, w_ref, m_ref, s_ref, *outs):
        def update(grad):
            done = adam_step(w_ref[0], m_ref[0], s_ref[0], grad, down_rate, weight_decay)
            for ref, value in zip(outs, done):
                ref[0] = value

        @pl.when(pl.program_id(0) < planes)
        def _():
            update(
                jnp.concatenate(
                    [
                        home_ref[0, pl.ds(j * piece, piece), pl.ds(2 * narrow_pad, wide)]
                        for j in range(across)
                    ],
                    axis=1,
                ).astype(f32)
            )

        @pl.when(pl.program_id(0) >= planes)
        def _():
            update(low_ref[...])

    def update_experts(home_full, home_rest, low, gate_up, down):
        if not whole:
            grad = join_spare(home_rest).astype(f32)
            return (
                adam_step(*gate_up, grad, gate_up_rate, weight_decay),
                adam_step(
                    *down, low[:narrow].reshape(spare, piece, D), down_rate, weight_decay
                ),
            )
        params = pltpu.CompilerParams(vmem_limit_bytes=48 * 2**20)
        shapes = [jax.ShapeDtypeStruct(gate_up[0].shape, f32)] * 3
        one = pl.BlockSpec((1, rows_home, 2 * FF), lambda i: (i, 0, 0))
        last = pl.BlockSpec((1, rows_home, 2 * FF), lambda i: (planes + i, 0, 0))
        new_gate_up = pl.pallas_call(
            full_kernel,
            grid=(planes,),
            in_specs=[one] * 4,
            out_specs=[one] * 3,
            cost_estimate=pl.CostEstimate(flops=0, bytes_accessed=2**25, transcendentals=0),
            out_shape=shapes,
            compiler_params=params,
        )(home_full, *gate_up)
        new_gate_up = pl.pallas_call(
            spare_kernel,
            grid=(spare,),
            in_specs=[pl.BlockSpec((planes, rows_home, 2 * narrow_pad), lambda i: (0, 0, 0))]
            + [last] * 3
            + [pl.BlockSpec(memory_space=pl.ANY)] * 3,
            out_specs=[last] * 3,
            out_shape=shapes,
            input_output_aliases={4: 0, 5: 1, 6: 2},
            compiler_params=params,
        )(home_rest, *gate_up, *new_gate_up)
        row = pl.BlockSpec((1, piece, D), lambda i: (i, 0, 0))
        new_down = pl.pallas_call(
            down_kernel,
            grid=(per_group,),
            in_specs=[
                pl.BlockSpec((1, rows_home, rest), lambda i: (jnp.minimum(i, planes - 1), 0, 0)),
                pl.BlockSpec((piece, D), lambda i: (jnp.maximum(i - planes, 0), 0)),
            ]
            + [row] * 3,
            out_specs=[row] * 3,
            cost_estimate=pl.CostEstimate(flops=0, bytes_accessed=2**24, transcendentals=0),
            out_shape=[jax.ShapeDtypeStruct(down[0].shape, f32)] * 3,
            compiler_params=params,
        )(home_rest, low, *down)
        return new_gate_up, new_down

    def unit_experts(group, place):
        base = group * per_group
        sets = []
        if whole:
            sets.append(jnp.full((wide,), base + place))
        behind = base + whole * planes + jnp.arange(narrow_pad) // piece
        sets.append(jnp.where(jnp.arange(narrow_pad) < narrow, behind, -1))
        return jnp.concatenate(sets)

    def columns_of():
        pieces = []
        for first in range(0, wide, 256):
            pieces.append((first, wide + first, first, min(256, wide - first)))
        pieces.append((2 * wide, 2 * wide + narrow_pad, wide, narrow_pad))
        return pieces

    def expert_kernel(first_call, *refs):
        rows_ref, gates_ref = refs[:2]
        reaches, weights = refs[2:4], refs[4:6]
        twice_ref, once_ref = refs[6:8]
        gated_ref, grad_ref, two_ref = refs[8 + (0 if first_call else 2) :]
        blocks, rows_of, _ = rows_ref.shape
        count = blocks * rows_of
        rows = rows_ref[...].reshape(count, D)
        gates = gates_ref[...].reshape(count, LANES)
        dgate = jnp.zeros((count, LANES), f32)
        for k in range(2):
            for gate_at, up_at, unit_at, width in columns_of():
                unit = pl.ds(k * units + unit_at, width)
                gate_w = weights[k][:, pl.ds(gate_at, width)]
                up_w = weights[k][:, pl.ds(up_at, width)]
                gate_part = jnp.dot(rows, gate_w, preferred_element_type=f32)
                up_part = jnp.dot(rows, up_w, preferred_element_type=f32)
                gate_wide = jnp.dot(gates, twice_ref[:, unit], preferred_element_type=f32)
                reach = reaches[k][:, :, pl.ds(unit_at, width)].reshape(count, width)
                reach = residual_scale * reach
                squash = 1.0 / (1.0 + jnp.exp(-gate_part))
                swish = gate_part * squash
                hidden = swish * up_part
                gated = (hidden * gate_wide).astype(bf16)
                gated_ref[:, :, unit] = gated.reshape(blocks, rows_of, width)
                dgate += dot_nt((hidden * reach).astype(bf16), once_ref[:, unit])
                grad_hidden = reach * gate_wide
                grad_gate = grad_hidden * up_part * squash * (1.0 + gate_part * (1.0 - squash))
                for at, value in ((gate_at, grad_gate), (up_at, grad_hidden * swish)):
                    grad_ref[:, :, pl.ds(k * 2 * units + at, width)] = value.astype(bf16).reshape(
                        blocks, rows_of, width
                    )
        two = jnp.zeros((count, D), f32)
        for k in range(2):
            grad = grad_ref[:, :, pl.ds(k * 2 * units, 2 * units)].reshape(count, 2 * units)
            two += dot_nt(grad, weights[k][...])
        two_ref[:, :, pl.ds(0, D)] = two.astype(bf16).reshape(blocks, rows_of, D)
        two_ref[:, :, pl.ds(D, LANES)] = dgate.astype(bf16).reshape(blocks, rows_of, LANES)

    def run_experts(at, sent, reach, own, other, twice, once, before):
        blocks, rows_of, _ = sent.shape
        rows_of = rows_of // 2
        tile = max(1, 512 // rows_of)

        def by_rows(columns, column=0):
            return pl.BlockSpec((tile, rows_of, columns), lambda i: (i, at, column))

        def fixed(rows, columns):
            return pl.BlockSpec((rows, columns), lambda i: (0, 0), pipeline_mode=pl.Buffered(1))

        kept = list(before) if before else []
        count = blocks * rows_of
        return pl.pallas_call(
            functools.partial(expert_kernel, not kept),
            grid=(blocks // tile,),
            in_specs=[by_rows(D), by_rows(LANES, D // LANES)]
            + [by_rows(units)] * 2
            + [fixed(D, 2 * units)] * 2
            + [fixed(LANES, 2 * units)] * 2
            + [pl.BlockSpec(memory_space=pl.ANY)] * len(kept),
            out_specs=[
                by_rows(2 * units),
                by_rows(4 * units),
                pl.BlockSpec((tile, rows_of, D + LANES), lambda i: (i, 0, 0)),
            ],
            out_shape=[
                jax.ShapeDtypeStruct((blocks, 2 * rows_of, 2 * units), bf16),
                jax.ShapeDtypeStruct((blocks, 2 * rows_of, 4 * units), bf16),
                jax.ShapeDtypeStruct((blocks, rows_of, D + LANES), bf16),
            ],
            input_output_aliases={8 + i: i for i in range(len(kept))},
            cost_estimate=pl.CostEstimate(
                flops=16 * count * D * units, bytes_accessed=2**25, transcendentals=2 * count * units
            ),
            compiler_params=pltpu.CompilerParams(vmem_limit_bytes=60 * 2**20),
        )(sent, sent, *reach, own, other, twice, once, *kept)

    def shards(
        tokens,
        cotangent,
        routes,
        weight_qkv,
        moment_qkv,
        square_qkv,
        weight_out,
        moment_out,
        square_out,
        weight_router,
        moment_router,
        square_router,
        gains,
        moment_gains,
        square_gains,
        weight_gate_up,
        moment_gate_up,
        square_gate_up,
        weight_down,
        moment_down,
        square_down,
    ):
        sequence_length = tokens.shape[0]
        head_groups = QUERY_HEADS // KEY_VALUE_HEADS
        place = lax.axis_index(PLANE)
        group = lax.axis_index("y") * 2 + lax.axis_index("core")
        partner = lax.axis_index("y") * 2 + 1 - lax.axis_index("core")

        small = pad_lanes(jnp.concatenate([weight_router, gains.T], axis=1))
        first_pack = jnp.concatenate([weight_qkv, small], axis=1).astype(bf16)
        first_all = lax.all_gather(first_pack, ALL, axis=0, tiled=True)

        packed, low_own = pack_experts(weight_gate_up, weight_down)
        out_line = line_of(chip_half(weight_out.astype(bf16)))
        cot_line = line_of(after(cotangent, low_own, out_line[1]))
        own = all_to_all_plane(after(packed, cot_line[-1], out_line[-1])).reshape(D, -1)
        out_mine, out_other = gather_halves(out_line)
        core = lax.axis_index("core")
        order_mine, order_other = row_order(core), row_order(1 - core)
        blocks_order = block_order()

        qkv_w = first_all[:, :QKV]
        router_w = first_all[:, QKV : QKV + EXPERTS]
        gain_one = first_all[:, QKV + EXPERTS].astype(f32)
        gain_two = first_all[:, QKV + EXPERTS + 1].astype(f32)

        inputs = tokens.astype(f32)
        factor_one = lax.rsqrt(jnp.mean(inputs * inputs, axis=-1, keepdims=True) + norm_eps)
        hidden_one = (inputs * factor_one * gain_one).astype(bf16)
        joined_heads = dot(hidden_one, qkv_w)
        cot_all = gather_tokens(cot_line, joined_heads)
        hidden_mine = dot(hidden_one, order_mine).astype(bf16)
        hidden_other = dot(hidden_one, order_other).astype(bf16)
        query_rows = joined_heads[:, :HEADS_WIDTH].reshape(sequence_length, QUERY_HEADS, HEAD_SIZE)
        every_key = joined_heads[:, HEADS_WIDTH : HEADS_WIDTH + KEYS_WIDTH].reshape(
            sequence_length, KEY_VALUE_HEADS, HEAD_SIZE
        )
        every_value = joined_heads[:, HEADS_WIDTH + KEYS_WIDTH :].reshape(
            sequence_length, KEY_VALUE_HEADS, HEAD_SIZE
        )
        cosine_lookup, sine_lookup = rotary_tables(sequence_length, HEAD_SIZE)
        query_rotated = (
            apply_rotation(query_rows, cosine_lookup, sine_lookup)
            .astype(bf16)
            .reshape(sequence_length, KEY_VALUE_HEADS, head_groups, HEAD_SIZE)
        )
        key_rot = apply_rotation(every_key, cosine_lookup, sine_lookup).astype(bf16)
        value_low = every_value.astype(bf16)
        causal = jnp.arange(sequence_length)[:, None] >= jnp.arange(sequence_length)[None, :]
        scores = attention_scores(query_rotated, key_rot, causal)
        peak = jnp.max(scores, axis=-1, keepdims=True)
        expo = jnp.exp(scores - peak)
        totals = jnp.sum(expo, axis=-1, keepdims=True)
        probs = expo / totals
        prob_low = probs.astype(bf16)
        heads = jnp.einsum("kgst,tkd->skgd", prob_low, value_low, preferred_element_type=f32)
        attended = heads.reshape(sequence_length, HEADS_WIDTH).astype(bf16)
        attended_mine = dot(attended, order_mine).astype(bf16)
        attended_other = dot(attended, order_other).astype(bf16)
        projected = [dot(attended_mine, out_mine), dot(attended_other, out_other)]
        mid = inputs + residual_scale * jnp.where(
            core == 0,
            jnp.concatenate(projected, axis=1),
            jnp.concatenate(projected[::-1], axis=1),
        )
        factor_two = lax.rsqrt(jnp.mean(mid * mid, axis=-1, keepdims=True) + norm_eps)
        hidden_two = (mid * factor_two * gain_two).astype(bf16)
        logits = dot(hidden_two, router_w)
        named = jnp.any(
            routes[..., None] == jnp.arange(EXPERTS, dtype=routes.dtype)[None, None, :], axis=1
        )
        shown = jnp.where(named, logits, -jnp.inf)
        raised = jnp.exp(shown - jnp.max(shown, axis=-1, keepdims=True))
        gates = raised / jnp.sum(raised, axis=-1, keepdims=True)

        gate_high = gates.astype(bf16)
        gate_rest = (gates - gate_high.astype(f32)).astype(bf16)
        sent = jnp.concatenate(
            [hidden_two, pad_lanes(jnp.concatenate([gate_high, gate_rest], axis=1))], axis=1
        )
        sent_all = lax.all_gather(sent, SAME_CORE, axis=0, tiled=True)
        sent_all = permute_blocks(sent_all, blocks_order)
        own = after(own, cot_all)
        other, low_other = swap_core(own), swap_core(low_own)
        down_own, down_other = down_of(own, low_own), down_of(other, low_other)
        blocks = 2 * nx * ny
        reach = [dot_nt(cot_all, d).reshape(blocks, -1, units) for d in (down_own, down_other)]

        behind = jnp.concatenate([unit_experts(group, place), unit_experts(partner, place)])
        numbers = jnp.arange(LANES)[:, None]
        real = behind[None, :] >= 0
        once = ((numbers == behind[None, :]) & real).astype(bf16)
        twice = once + ((numbers == behind[None, :] + EXPERTS) & real).astype(bf16)
        kept = None
        firsts = []
        sent_blocks = sent_all.reshape(blocks, -1, sent_all.shape[1])
        for at in range(2):
            *kept, two = run_experts(at, sent_blocks, reach, own, other, twice, once, kept)
            firsts.append(scatter_first(two))
        two_sum = sum_line(scatter_second(firsts))

        gated, grad_both = (k.reshape(-1, k.shape[2]) for k in kept)
        gated, grad_both = after(gated, *firsts[-1], always=True), after(grad_both, *firsts[-1])
        rows_all = after(sent_all, *firsts[-1], always=True)[:, :D]
        mixed = (dot(gated[:, :units], down_own) + dot(gated[:, units:], down_other)).astype(bf16)
        mixed = after(mixed, two_sum, always=True).reshape(blocks, -1, D)
        mixed_first = scatter_first(mixed)

        came_gate_up = swap_core(dot_tn(rows_all, grad_both[:, 2 * units :]).astype(bf16))
        came_down = swap_core(dot_tn(gated[:, units:], cot_all).astype(bf16))
        full, more, low = combine_grads(
            dot_tn(rows_all, grad_both[:, : 2 * units]).astype(bf16),
            came_gate_up,
            dot_tn(gated[:, :units], cot_all).astype(bf16),
            came_down,
        )
        home_full = all_to_all_plane(after(full, two_sum)) if whole else None
        home_rest = all_to_all_plane(after(more, two_sum))
        two_sum = after(two_sum, low)
        grad_two, grad_gates = two_sum[:, :D], two_sum[:, D : D + EXPERTS]

        grad_out = cotangent.astype(f32)
        grad_chosen = gates * (grad_gates - jnp.sum(gates * grad_gates, axis=-1, keepdims=True))
        grad_logits = grad_chosen.astype(bf16)
        grad_router = dot_tn(hidden_two, grad_logits)
        grad_two = grad_two + dot_nt(grad_logits, router_w)
        grad_mid, grad_gain_two = norm_backward(grad_two, mid, factor_two, gain_two)
        grad_mid = grad_out + grad_mid
        grad_att = (residual_scale * grad_mid).astype(bf16)
        att_left, att_right = grad_att[:, : D // 2], grad_att[:, D // 2 :]
        att_mine = jnp.where(core == 0, att_left, att_right)
        att_other = jnp.where(core == 0, att_right, att_left)
        grad_heads = (
            dot_nt(dot_nt(att_mine, out_mine).astype(bf16), order_mine)
            + dot_nt(dot_nt(att_other, out_other).astype(bf16), order_other)
        )
        grad_heads = grad_heads.astype(bf16).reshape(
            sequence_length, KEY_VALUE_HEADS, head_groups, HEAD_SIZE
        )
        out_first = scatter_halves_first(
            dot_tn(attended_mine, att_mine).astype(bf16),
            dot_tn(attended_other, att_other).astype(bf16),
        )
        out_two = scatter_halves_second(out_first)
        grad_probs = jnp.einsum(
            "skgd,tkd->kgst", grad_heads, value_low, preferred_element_type=f32
        )
        value_gradient = jnp.einsum(
            "kgst,skgd->tkd", prob_low, grad_heads, preferred_element_type=f32
        )
        row_dot = jnp.sum(probs * grad_probs, axis=-1, keepdims=True)
        grad_scores = (probs * (grad_probs - row_dot)).astype(bf16)
        grad_qrot = (
            jnp.einsum("kgst,tkd->skgd", grad_scores, key_rot, preferred_element_type=f32)
            * score_scale
        )
        grad_krot = (
            jnp.einsum("kgst,skgd->tkd", grad_scores, query_rotated, preferred_element_type=f32)
            * score_scale
        )
        grad_queries = apply_rotation(
            grad_qrot.reshape(sequence_length, QUERY_HEADS, HEAD_SIZE), cosine_lookup, -sine_lookup
        )
        key_gradient = apply_rotation(grad_krot, cosine_lookup, -sine_lookup)
        grad_joined = jnp.concatenate(
            [
                grad_queries.reshape(sequence_length, HEADS_WIDTH),
                key_gradient.reshape(sequence_length, KEYS_WIDTH),
                value_gradient.reshape(sequence_length, KEYS_WIDTH),
            ],
            axis=1,
        ).astype(bf16)
        grad_one = dot_nt(grad_joined, qkv_w)
        grad_inputs, grad_gain_one = norm_backward(grad_one, inputs, factor_one, gain_one)
        token_grad = grad_mid + grad_inputs
        small_sent = pad_lanes(
            jnp.concatenate([grad_router, grad_gain_one[:, None], grad_gain_two[:, None]], axis=1)
        )
        small_sent = small_sent.astype(bf16)
        joined_left, joined_right = grad_joined[:, : QKV // 2], grad_joined[:, QKV // 2 :]
        qkv_sent = []
        for hidden, rows_order, at in (
            (hidden_mine, order_mine, core),
            (hidden_other, order_other, 1 - core),
        ):
            product = dot_tn(hidden, jnp.where(at == 0, joined_left, joined_right))
            extra = jnp.where(at == 0, dot_tn(rows_order, small_sent), 0.0)
            qkv_sent.append(jnp.concatenate([product, extra], axis=1).astype(bf16))
        qkv_first = scatter_halves_first(qkv_sent[0], after(qkv_sent[1], out_two, home_full, *mixed_first))
        mixed = sum_line(scatter_second([[after(m, qkv_first) for m in mixed_first]]))
        layer_out = (mid + residual_scale * mixed).astype(bf16)
        (out_left, out_right), (qkv_left, qkv_right) = scatter_halves_line(
            [out_two, scatter_halves_second(qkv_first)], home_rest
        )
        sum_out = jnp.concatenate([out_left, out_right], axis=1)
        sum_qkv = jnp.concatenate([qkv_left[:, : QKV // 2], qkv_right[:, : QKV // 2]], axis=1)
        sum_router = qkv_left[:, QKV // 2 : QKV // 2 + EXPERTS]
        sum_gains = qkv_left[:, QKV // 2 + EXPERTS : QKV // 2 + EXPERTS + 2].T

        new_gate_up, new_down = update_experts(
            home_full,
            home_rest,
            low,
            (weight_gate_up, moment_gate_up, square_gate_up),
            (weight_down, moment_down, square_down),
        )
        new_qkv = adam_step(weight_qkv, moment_qkv, square_qkv, sum_qkv, D ** (-0.5), weight_decay)
        new_out = adam_step(
            weight_out,
            moment_out,
            square_out,
            sum_out,
            max(4, QUERY_HEADS * HEAD_SIZE // 256) ** (-0.5),
            weight_decay,
        )
        new_router = adam_step(
            weight_router, moment_router, square_router, sum_router, (4 * D) ** (-0.5), weight_decay
        )
        new_gains = adam_step(gains, moment_gains, square_gains, sum_gains, 0.75, 0.0)
        return (
            layer_out,
            token_grad,
            *new_qkv,
            *new_out,
            *new_router,
            *new_gains,
            *new_gate_up,
            *new_down,
        )

    return shards


def solution(mesh):
    n_dp, n_expert = mesh.shape["dp"], mesh.shape["expert"]
    nz = 4
    nx, ny = n_dp // nz, n_expert // 2
    fine = Mesh(mesh.devices.reshape(nz, nx, ny, 2), ALL)
    rows = P(ALL, None)
    columns = P(None, ALL)
    experts = P(("y", "core"), ("z", "x"), None)
    dense = (rows,) * 9 + (columns,) * 3 + (experts,) * 6
    return jax.shard_map(
        make_shards((nz, nx, ny)),
        mesh=fine,
        in_specs=(rows,) * 3 + dense,
        out_specs=(rows,) * 2 + dense,
        check_vma=False,
    )
```

```python
import functools

import jax
import jax.numpy as jnp
import numpy as np
from jax import lax
from jax.experimental import pallas as pl
from jax.experimental.pallas import tpu as pltpu
from jax.sharding import Mesh, PartitionSpec as P

D = 1536
QUERY_HEADS = 24
KEY_VALUE_HEADS = 8
HEAD_SIZE = 64
FF = 512
EXPERTS = 40
TOPK = 8
STEP = 10
QKV = 2560
LANES = 128
HEADS_WIDTH = QUERY_HEADS * HEAD_SIZE
KEYS_WIDTH = KEY_VALUE_HEADS * HEAD_SIZE

norm_eps = 1e-06
residual_scale = 0.22
score_scale = 0.125
beta_one = 0.9
beta_two = 0.95
adam_eps = 1e-08
weight_decay = 0.1

f32 = jnp.float32
bf16 = jnp.bfloat16
ALL = ("z", "x", "y", "core")
PLANE = ("z", "x")
SAME_CORE = ("z", "x", "y")


def rotary_tables(sequence_length, size):
    half = size // 2
    places = jnp.arange(sequence_length).astype(f32)[:, None]
    inverse = 10000.0 ** (-jnp.arange(half).astype(f32) * 2.0 / size)
    angles = places * inverse[None, :]
    return (jnp.cos(angles)[:, None, :], jnp.sin(angles)[:, None, :])


def apply_rotation(values, cosine_lookup, sine_lookup):
    half = values.shape[-1] // 2
    first = values[..., :half]
    second = values[..., half:]
    return jnp.concatenate(
        [
            first * cosine_lookup - second * sine_lookup,
            second * cosine_lookup + first * sine_lookup,
        ],
        axis=-1,
    )


def attention_scores(query_rotated, key_rot, causal):
    scores = (
        jnp.einsum("skgd,tkd->kgst", query_rotated, key_rot, preferred_element_type=f32)
        * score_scale
    )
    return jnp.where(causal, scores, -1e30)


def norm_backward(grad_normed, values, factor, gain):
    scaled = grad_normed * gain
    grad_gain = jnp.sum(grad_normed * values * factor, axis=0)
    value_gradient = factor * scaled - values * factor * factor * factor * jnp.mean(
        scaled * values, axis=-1, keepdims=True
    )
    return (value_gradient, grad_gain)


def adam_step(weight, moment, square, grad, rate, decay):
    moment = beta_one * moment + (1.0 - beta_one) * grad
    square = beta_two * square + (1.0 - beta_two) * grad * grad
    fixed_one = moment / (1.0 - beta_one**STEP)
    fixed_two = square / (1.0 - beta_two**STEP)
    weight = weight - rate * (fixed_one / (jnp.sqrt(fixed_two) + adam_eps) + decay * weight)
    return (weight, moment, square)


def dot(a, b):
    return jnp.dot(a, b, preferred_element_type=f32)


def dot_nt(a, b):
    return lax.dot_general(a, b, (((1,), (1,)), ((), ())), preferred_element_type=f32)


def dot_tn(a, b):
    return lax.dot_general(a, b, (((0,), (0,)), ((), ())), preferred_element_type=f32)


def pad_lanes(values):
    extra = -values.shape[-1] % LANES
    return jnp.pad(values, ((0, 0), (0, extra)))


def swap_core(values):
    return lax.ppermute(values, "core", [(0, 1), (1, 0)])


def keep_kernel(*refs):
    pass


def ring_order(n):
    return [0] + list(range(1, n, 2)) + list(range(n - 2 + n % 2, 0, -2))


def home_table(n):
    order = ring_order(n)
    place = {chip: at for at, chip in enumerate(order)}
    return np.array([[order[(place[i] - s) % n] for s in range(n)] for i in range(n)], np.int32)


def make_shards(sizes):
    nz, nx, ny = sizes
    length = {"z": nz, "x": nx, "y": ny}
    planes = nz * nx
    per_group = EXPERTS // (2 * ny)
    whole = per_group // planes
    spare = per_group - whole * planes
    piece = FF // planes
    wide = whole * FF
    narrow = spare * piece
    narrow_pad = narrow + -narrow % LANES
    units = wide + narrow_pad

    rings = {axis: ring_order(n) for axis, n in length.items()}
    places = {axis: i for i, axis in enumerate(("z", "x", "y", "core"))}
    shape = (nz, nx, ny, 2)

    def pairs_of(axes, step):
        pairs = []
        for at in np.ndindex(*shape):
            axis = axes[at[3]]
            ring = rings[axis]
            to = list(at)
            to[places[axis]] = ring[(ring.index(at[places[axis]]) + step) % len(ring)]
            pairs.append(
                (int(np.ravel_multi_index(at, shape)), int(np.ravel_multi_index(to, shape)))
            )
        return pairs

    def move(values, axes, step):
        return lax.ppermute(values, ALL, pairs_of(axes, step))

    def row_order(core):
        found = {}
        for axis, n in length.items():
            here = jnp.arange(n)[:, None] == lax.axis_index(axis)
            found[axis] = jnp.sum(jnp.where(here, jnp.asarray(home_table(n)), 0), axis=0)
        x = jnp.where(core == 0, found["x"][None, :], found["x"][:, None])
        y = jnp.where(core == 0, found["y"][:, None], found["y"][None, :])
        chip = (found["z"] * nx + x[:, :, None]) * ny + y[:, :, None]
        block = (chip[..., None] * 2 + jnp.arange(2)).reshape(-1, 1)
        rows = D // block.shape[0]
        kept = (block * rows + jnp.arange(rows)[None, :]).reshape(1, D)
        return (jnp.arange(D)[:, None] == kept).astype(bf16)

    def add_low(a, b):
        return (a.astype(f32) + b.astype(f32)).astype(bf16)

    parts = ((0, "x", "y"), (1, "y", "x"))

    def line_of(own):
        line = [own]
        for _ in range(nz - 1):
            line.append(move(line[-1], "zz", 1))
        return line

    def gather_tokens(line, late):
        half = line[0].shape[0] // 2
        packs = [
            jnp.concatenate([b[part * half : (part + 1) * half] for b in line], axis=0)
            for part, _, _ in parts
        ]
        packs = [after(p, late) for p in packs]
        for level in (1, 2):
            grown = []
            for pack, names in zip(packs, parts):
                axis = names[level]
                steps = [pack]
                for _ in range(length[axis] - 1):
                    steps.append(move(steps[-1], axis * 2, 1))
                grown.append(jnp.concatenate(steps, axis=0))
            packs = grown
        return jnp.concatenate(packs, axis=0)

    def block_order():
        found = {}
        for axis, n in length.items():
            here = jnp.arange(n)[:, None] == lax.axis_index(axis)
            found[axis] = jnp.sum(jnp.where(here, jnp.asarray(home_table(n)), 0), axis=0)
        z = found["z"][None, None, :]
        blocks = []
        for part, second, third in parts:
            at = {second: found[second][None, :, None], third: found[third][:, None, None]}
            chip = (z * nx + at["x"]) * ny + at["y"]
            blocks.append((chip * 2 + part).reshape(-1))
        return jnp.concatenate(blocks)

    def copy_kernel(order_ref, *refs):
        out_ref = refs[-1]
        for i, ref in enumerate(refs[:-1]):
            out_ref[i] = ref[0]

    def permute_blocks(values, order):
        count, each = order.shape[0], 4
        rows, columns = values.shape[0] // count, values.shape[1]
        values = values.reshape(count, rows, columns)
        result = pl.pallas_call(
            copy_kernel,
            grid_spec=pltpu.PrefetchScalarGridSpec(
                num_scalar_prefetch=1,
                grid=(count // each,),
                in_specs=[
                    pl.BlockSpec(
                        (1, rows, columns), lambda i, order, j=j: (order[i * each + j], 0, 0)
                    )
                    for j in range(each)
                ],
                out_specs=pl.BlockSpec((each, rows, columns), lambda i, order: (i, 0, 0)),
            ),
            out_shape=jax.ShapeDtypeStruct((count, rows, columns), values.dtype),
            cost_estimate=pl.CostEstimate(flops=0, bytes_accessed=2**24, transcendentals=0),
            compiler_params=pltpu.CompilerParams(vmem_limit_bytes=32 * 2**20),
        )(order, *[values] * each)
        return result.reshape(count * rows, columns)

    def sum_level(packs, level):
        summed = []
        for pack, names in zip(packs, parts):
            n = length[names[level]]
            pack = pack.reshape(n, pack.shape[0] // n, *pack.shape[1:])
            acc = None
            for s in reversed(range(n)):
                acc = pack[s] if acc is None else add_low(move(acc, names[level] * 2, -1), pack[s])
            summed.append(acc)
        return summed

    def scatter_first(values):
        count = values.shape[0] // 2
        return sum_level([values[:count], values[count:]], 2)

    def scatter_second(halves):
        packs = [jnp.concatenate(same, axis=1) for same in zip(*halves)]
        packs = [p[0] for p in sum_level(packs, 1)]
        half = packs[0].shape[0] // nz
        return [
            jnp.concatenate([p[s * half : (s + 1) * half] for p in packs], axis=0)
            for s in range(nz)
        ]

    def sum_line(blocks):
        total = blocks[-1]
        for mine in reversed(blocks[:-1]):
            total = add_low(move(total, "zz", -1), mine)
        return total.astype(f32)

    def chip_half(own):
        half = own.shape[1] // 2
        core = lax.axis_index("core")
        left, right = own[:, :half], own[:, half:]
        kept = jnp.where(core == 0, left, right)
        came = swap_core(jnp.where(core == 0, right, left))
        return jnp.where(
            core == 0, jnp.concatenate([kept, came], axis=0), jnp.concatenate([came, kept], axis=0)
        )

    def gather_halves(line):
        rows, half = line[0].shape
        steps = [jnp.concatenate(line, axis=0)]
        for _ in range(nx - 1):
            steps.append(move(steps[-1], "xy", 1))
        packs = [jnp.concatenate(steps, axis=0)]
        for _ in range(nx - 1):
            packs.append(move(packs[-1], "yx", 1))
        result = jnp.concatenate(packs, axis=0)
        return result, swap_core(result)

    def scatter_halves_first(mine, other):
        both = add_low(swap_core(other), mine)
        grid = both.reshape(nx, nx, both.shape[0] // (nx * nx), both.shape[1])
        acc = None
        for s in reversed(range(nx)):
            acc = grid[s] if acc is None else add_low(move(acc, "yx", -1), grid[s])
        return acc

    def scatter_halves_second(acc):
        two = None
        for s in reversed(range(nx)):
            two = acc[s] if two is None else add_low(move(two, "xy", -1), acc[s])
        return two

    def scatter_halves_line(twos, *late):
        core = lax.axis_index("core")
        two = after(jnp.concatenate(twos, axis=1), *late)
        rows = two.shape[0] // (nz * 2)
        total = None
        for s in reversed(range(nz)):
            mine = two[s * 2 * rows : (s + 1) * 2 * rows]
            total = mine if total is None else add_low(move(total, "zz", -1), mine)
        kept = jnp.where(core == 0, total[:rows], total[rows:])
        came = swap_core(jnp.where(core == 0, total[rows:], total[:rows]))
        left = jnp.where(core == 0, kept, came).astype(f32)
        right = jnp.where(core == 0, came, kept).astype(f32)
        found = []
        at = 0
        for part in twos:
            end = at + part.shape[1]
            found.append((left[:, at:end], right[:, at:end]))
            at = end
        return found

    def after(values, *first, always=False):
        if not (whole or always):
            return values
        anywhere = pl.BlockSpec(memory_space=pl.ANY)
        return pl.pallas_call(
            keep_kernel,
            in_specs=[anywhere] * (1 + len(first)),
            out_specs=anywhere,
            out_shape=jax.ShapeDtypeStruct(values.shape, values.dtype),
            input_output_aliases={0: 0},
        )(values, *first)

    def all_to_all_plane(values):
        return lax.all_to_all(values, PLANE, split_axis=0, concat_axis=0, tiled=True)

    rows_home = D // planes
    across = rows_home // piece
    rest = 2 * narrow_pad + wide

    def cut_spare(part):
        part = part.reshape(spare, rows_home, 2, planes, piece)
        part = part.transpose(3, 1, 2, 0, 4).reshape(planes, rows_home, 2, narrow)
        part = jnp.pad(part, ((0, 0), (0, 0), (0, 0), (0, narrow_pad - narrow)))
        return part.reshape(planes, rows_home, 2 * narrow_pad)

    def join_spare(part):
        part = part.reshape(planes, rows_home, 2, narrow_pad)[..., :narrow]
        part = part.reshape(planes, rows_home, 2, spare, piece).transpose(3, 1, 2, 0, 4)
        return part.reshape(spare, rows_home, 2 * FF)

    def lanes(values, first, width=piece):
        return values[:, first : first + width]

    packed_columns = 2 * units + wide

    def pack_kernel(gate_up_ref, spare_ref, down_ref, spare_down_ref, out_ref, low_ref):
        step = pl.program_id(0)
        out_ref[step, :, pl.ds(0, 2 * wide)] = gate_up_ref[0].astype(bf16)
        for j in range(across):
            out_ref[step, pl.ds(j * piece, piece), pl.ds(2 * units, wide)] = down_ref[
                0, :, pl.ds(j * wide, wide)
            ].astype(bf16)

        @pl.when(step == 0)
        def _():
            for to in range(planes):
                taken = [
                    lanes(spare_ref[s], g * FF + to * piece) for g in range(2) for s in range(spare)
                ]
                out_ref[to, :, pl.ds(2 * wide, 2 * narrow)] = jnp.concatenate(taken, axis=1).astype(
                    bf16
                )
            for s in range(spare):
                low_ref[pl.ds(s * piece, piece), :] = spare_down_ref[s].astype(bf16)

    def pack_experts(gate_up, down):
        if not whole:
            low = down.astype(bf16).reshape(narrow, D)
            low = jnp.pad(low, ((0, narrow_pad - narrow), (0, 0)))
            return cut_spare(gate_up.astype(bf16)), low
        return pl.pallas_call(
            pack_kernel,
            grid=(planes,),
            in_specs=[
                pl.BlockSpec((1, rows_home, 2 * FF), lambda i: (i, 0, 0)),
                pl.BlockSpec((spare, rows_home, 2 * FF), lambda i: (planes // spare, 0, 0)),
                pl.BlockSpec((1, piece, D), lambda i: (i, 0, 0)),
                pl.BlockSpec((spare, piece, D), lambda i: (planes // spare, 0, 0)),
            ],
            out_specs=[
                pl.BlockSpec((planes, rows_home, packed_columns), lambda i: (0, 0, 0)),
                pl.BlockSpec((narrow, D), lambda i: (0, 0)),
            ],
            out_shape=[
                jax.ShapeDtypeStruct((planes, rows_home, packed_columns), bf16),
                jax.ShapeDtypeStruct((narrow, D), bf16),
            ],
            cost_estimate=pl.CostEstimate(flops=0, bytes_accessed=2**24, transcendentals=0),
            compiler_params=pltpu.CompilerParams(vmem_limit_bytes=48 * 2**20),
        )(gate_up, gate_up, down, down)

    def down_of(packed, low):
        if not whole:
            return low
        mine = packed[:, 2 * units :].reshape(planes, across, piece, wide)
        mine = mine.transpose(0, 2, 1, 3).reshape(wide, D)
        return jnp.concatenate([mine, low], axis=0)

    def combine_kernel(a_ref, came_a_ref, b_ref, came_b_ref, c_ref, came_c_ref, full_ref, rest_ref, low_ref):
        total = a_ref[...].astype(f32) + came_a_ref[...].astype(f32)
        full_ref[0] = total[:, : 2 * wide].astype(bf16)
        rest_ref[0, :, pl.ds(0, 2 * narrow_pad)] = total[:, 2 * wide :].astype(bf16)
        total = residual_scale * (b_ref[...].astype(f32) + came_b_ref[...].astype(f32))
        for j in range(across):
            rest_ref[0, pl.ds(j * piece, piece), pl.ds(2 * narrow_pad, wide)] = total[
                :, j * wide : (j + 1) * wide
            ].astype(bf16)
        low_ref[...] = residual_scale * (c_ref[...].astype(f32) + came_c_ref[...].astype(f32))

    def combine_grads(gate_up, came_gate_up, down, came_down):
        if not whole:
            total = (gate_up.astype(f32) + came_gate_up.astype(f32)).astype(bf16)
            low = residual_scale * (down.astype(f32) + came_down.astype(f32))
            return None, total.reshape(planes, rows_home, rest), low
        return pl.pallas_call(
            combine_kernel,
            grid=(planes,),
            in_specs=[pl.BlockSpec((rows_home, 2 * units), lambda i: (i, 0))] * 2
            + [pl.BlockSpec((piece, D), lambda i: (i, 0))] * 2
            + [pl.BlockSpec((narrow, D), lambda i: (wide // narrow, 0))] * 2,
            out_specs=[
                pl.BlockSpec((1, rows_home, 2 * FF), lambda i: (i, 0, 0)),
                pl.BlockSpec((1, rows_home, rest), lambda i: (i, 0, 0)),
                pl.BlockSpec((narrow, D), lambda i: (0, 0)),
            ],
            out_shape=[
                jax.ShapeDtypeStruct((planes, rows_home, 2 * FF), bf16),
                jax.ShapeDtypeStruct((planes, rows_home, rest), bf16),
                jax.ShapeDtypeStruct((narrow, D), f32),
            ],
            cost_estimate=pl.CostEstimate(flops=0, bytes_accessed=2**24, transcendentals=0),
            compiler_params=pltpu.CompilerParams(vmem_limit_bytes=48 * 2**20),
        )(gate_up, came_gate_up, down, came_down, down, came_down)

    gate_up_rate = D ** (-0.5)
    down_rate = max(2, FF // 128) ** (-0.5)

    def full_kernel(home_ref, w_ref, m_ref, s_ref, *outs):
        done = adam_step(
            w_ref[0], m_ref[0], s_ref[0], home_ref[0].astype(f32), gate_up_rate, weight_decay
        )
        for ref, value in zip(outs, done):
            ref[0] = value

    def spare_kernel(home_ref, w_ref, m_ref, s_ref, a_ref, b_ref, c_ref, *outs):
        for s in range(spare):

            @pl.when(pl.program_id(0) == s)
            def _():
                grad = jnp.concatenate(
                    [
                        lanes(home_ref[p], g * narrow_pad + s * piece)
                        for g in range(2)
                        for p in range(planes)
                    ],
                    axis=1,
                ).astype(f32)
                done = adam_step(w_ref[0], m_ref[0], s_ref[0], grad, gate_up_rate, weight_decay)
                for ref, value in zip(outs, done):
                    ref[0] = value

    def down_kernel(home_ref, low_ref, w_ref, m_ref, s_ref, *outs):
        def update(grad):
            done = adam_step(w_ref[0], m_ref[0], s_ref[0], grad, down_rate, weight_decay)
            for ref, value in zip(outs, done):
                ref[0] = value

        @pl.when(pl.program_id(0) < planes)
        def _():
            update(
                jnp.concatenate(
                    [
                        home_ref[0, pl.ds(j * piece, piece), pl.ds(2 * narrow_pad, wide)]
                        for j in range(across)
                    ],
                    axis=1,
                ).astype(f32)
            )

        @pl.when(pl.program_id(0) >= planes)
        def _():
            update(low_ref[...])

    def update_experts(home_full, home_rest, low, gate_up, down):
        if not whole:
            grad = join_spare(home_rest).astype(f32)
            return (
                adam_step(*gate_up, grad, gate_up_rate, weight_decay),
                adam_step(
                    *down, low[:narrow].reshape(spare, piece, D), down_rate, weight_decay
                ),
            )
        params = pltpu.CompilerParams(vmem_limit_bytes=48 * 2**20)
        shapes = [jax.ShapeDtypeStruct(gate_up[0].shape, f32)] * 3
        one = pl.BlockSpec((1, rows_home, 2 * FF), lambda i: (i, 0, 0))
        last = pl.BlockSpec((1, rows_home, 2 * FF), lambda i: (planes + i, 0, 0))
        new_gate_up = pl.pallas_call(
            full_kernel,
            grid=(planes,),
            in_specs=[one] * 4,
            out_specs=[one] * 3,
            cost_estimate=pl.CostEstimate(flops=0, bytes_accessed=2**25, transcendentals=0),
            out_shape=shapes,
            compiler_params=params,
        )(home_full, *gate_up)
        new_gate_up = pl.pallas_call(
            spare_kernel,
            grid=(spare,),
            in_specs=[pl.BlockSpec((planes, rows_home, 2 * narrow_pad), lambda i: (0, 0, 0))]
            + [last] * 3
            + [pl.BlockSpec(memory_space=pl.ANY)] * 3,
            out_specs=[last] * 3,
            out_shape=shapes,
            input_output_aliases={4: 0, 5: 1, 6: 2},
            compiler_params=params,
        )(home_rest, *gate_up, *new_gate_up)
        row = pl.BlockSpec((1, piece, D), lambda i: (i, 0, 0))
        new_down = pl.pallas_call(
            down_kernel,
            grid=(per_group,),
            in_specs=[
                pl.BlockSpec((1, rows_home, rest), lambda i: (jnp.minimum(i, planes - 1), 0, 0)),
                pl.BlockSpec((piece, D), lambda i: (jnp.maximum(i - planes, 0), 0)),
            ]
            + [row] * 3,
            out_specs=[row] * 3,
            cost_estimate=pl.CostEstimate(flops=0, bytes_accessed=2**24, transcendentals=0),
            out_shape=[jax.ShapeDtypeStruct(down[0].shape, f32)] * 3,
            compiler_params=params,
        )(home_rest, low, *down)
        return new_gate_up, new_down

    def unit_experts(group, place):
        base = group * per_group
        sets = []
        if whole:
            sets.append(jnp.full((wide,), base + place))
        behind = base + whole * planes + jnp.arange(narrow_pad) // piece
        sets.append(jnp.where(jnp.arange(narrow_pad) < narrow, behind, -1))
        return jnp.concatenate(sets)

    def columns_of():
        pieces = []
        for first in range(0, wide, 256):
            pieces.append((first, wide + first, first, min(256, wide - first)))
        pieces.append((2 * wide, 2 * wide + narrow_pad, wide, narrow_pad))
        return pieces

    def expert_kernel(first_call, *refs):
        rows_ref, gates_ref = refs[:2]
        reaches, weights = refs[2:4], refs[4:6]
        twice_ref, once_ref = refs[6:8]
        gated_ref, grad_ref, two_ref = refs[8 + (0 if first_call else 2) :]
        blocks, rows_of, _ = rows_ref.shape
        count = blocks * rows_of
        rows = rows_ref[...].reshape(count, D)
        gates = gates_ref[...].reshape(count, LANES)
        dgate = jnp.zeros((count, LANES), f32)
        for k in range(2):
            for gate_at, up_at, unit_at, width in columns_of():
                unit = pl.ds(k * units + unit_at, width)
                gate_w = weights[k][:, pl.ds(gate_at, width)]
                up_w = weights[k][:, pl.ds(up_at, width)]
                gate_part = jnp.dot(rows, gate_w, preferred_element_type=f32)
                up_part = jnp.dot(rows, up_w, preferred_element_type=f32)
                gate_wide = jnp.dot(gates, twice_ref[:, unit], preferred_element_type=f32)
                reach = reaches[k][:, :, pl.ds(unit_at, width)].reshape(count, width)
                reach = residual_scale * reach
                squash = 1.0 / (1.0 + jnp.exp(-gate_part))
                swish = gate_part * squash
                hidden = swish * up_part
                gated = (hidden * gate_wide).astype(bf16)
                gated_ref[:, :, unit] = gated.reshape(blocks, rows_of, width)
                dgate += dot_nt((hidden * reach).astype(bf16), once_ref[:, unit])
                grad_hidden = reach * gate_wide
                grad_gate = grad_hidden * up_part * squash * (1.0 + gate_part * (1.0 - squash))
                for at, value in ((gate_at, grad_gate), (up_at, grad_hidden * swish)):
                    grad_ref[:, :, pl.ds(k * 2 * units + at, width)] = value.astype(bf16).reshape(
                        blocks, rows_of, width
                    )
        two = jnp.zeros((count, D), f32)
        for k in range(2):
            grad = grad_ref[:, :, pl.ds(k * 2 * units, 2 * units)].reshape(count, 2 * units)
            two += dot_nt(grad, weights[k][...])
        two_ref[:, :, pl.ds(0, D)] = two.astype(bf16).reshape(blocks, rows_of, D)
        two_ref[:, :, pl.ds(D, LANES)] = dgate.astype(bf16).reshape(blocks, rows_of, LANES)

    def run_experts(at, sent, reach, own, other, twice, once, before):
        blocks, rows_of, _ = sent.shape
        rows_of = rows_of // 2
        tile = max(1, 512 // rows_of)

        def by_rows(columns, column=0):
            return pl.BlockSpec((tile, rows_of, columns), lambda i: (i, at, column))

        def fixed(rows, columns):
            return pl.BlockSpec((rows, columns), lambda i: (0, 0), pipeline_mode=pl.Buffered(1))

        kept = list(before) if before else []
        count = blocks * rows_of
        return pl.pallas_call(
            functools.partial(expert_kernel, not kept),
            grid=(blocks // tile,),
            in_specs=[by_rows(D), by_rows(LANES, D // LANES)]
            + [by_rows(units)] * 2
            + [fixed(D, 2 * units)] * 2
            + [fixed(LANES, 2 * units)] * 2
            + [pl.BlockSpec(memory_space=pl.ANY)] * len(kept),
            out_specs=[
                by_rows(2 * units),
                by_rows(4 * units),
                pl.BlockSpec((tile, rows_of, D + LANES), lambda i: (i, 0, 0)),
            ],
            out_shape=[
                jax.ShapeDtypeStruct((blocks, 2 * rows_of, 2 * units), bf16),
                jax.ShapeDtypeStruct((blocks, 2 * rows_of, 4 * units), bf16),
                jax.ShapeDtypeStruct((blocks, rows_of, D + LANES), bf16),
            ],
            input_output_aliases={8 + i: i for i in range(len(kept))},
            cost_estimate=pl.CostEstimate(
                flops=16 * count * D * units, bytes_accessed=2**25, transcendentals=2 * count * units
            ),
            compiler_params=pltpu.CompilerParams(vmem_limit_bytes=60 * 2**20),
        )(sent, sent, *reach, own, other, twice, once, *kept)

    def shards(
        tokens,
        cotangent,
        routes,
        weight_qkv,
        moment_qkv,
        square_qkv,
        weight_out,
        moment_out,
        square_out,
        weight_router,
        moment_router,
        square_router,
        gains,
        moment_gains,
        square_gains,
        weight_gate_up,
        moment_gate_up,
        square_gate_up,
        weight_down,
        moment_down,
        square_down,
    ):
        sequence_length = tokens.shape[0]
        head_groups = QUERY_HEADS // KEY_VALUE_HEADS
        place = lax.axis_index(PLANE)
        group = lax.axis_index("y") * 2 + lax.axis_index("core")
        partner = lax.axis_index("y") * 2 + 1 - lax.axis_index("core")

        small = pad_lanes(jnp.concatenate([weight_router, gains.T], axis=1))
        first_pack = jnp.concatenate([weight_qkv, small], axis=1).astype(bf16)
        first_all = lax.all_gather(first_pack, ALL, axis=0, tiled=True)

        packed, low_own = pack_experts(weight_gate_up, weight_down)
        out_line = line_of(chip_half(weight_out.astype(bf16)))
        cot_line = line_of(after(cotangent, low_own, out_line[1]))
        own = all_to_all_plane(after(packed, cot_line[-1], out_line[-1])).reshape(D, -1)
        out_mine, out_other = gather_halves(out_line)
        core = lax.axis_index("core")
        order_mine, order_other = row_order(core), row_order(1 - core)
        blocks_order = block_order()

        qkv_w = first_all[:, :QKV]
        router_w = first_all[:, QKV : QKV + EXPERTS]
        gain_one = first_all[:, QKV + EXPERTS].astype(f32)
        gain_two = first_all[:, QKV + EXPERTS + 1].astype(f32)

        inputs = tokens.astype(f32)
        factor_one = lax.rsqrt(jnp.mean(inputs * inputs, axis=-1, keepdims=True) + norm_eps)
        hidden_one = (inputs * factor_one * gain_one).astype(bf16)
        joined_heads = dot(hidden_one, qkv_w)
        cot_all = gather_tokens(cot_line, joined_heads)
        hidden_mine = dot(hidden_one, order_mine).astype(bf16)
        hidden_other = dot(hidden_one, order_other).astype(bf16)
        query_rows = joined_heads[:, :HEADS_WIDTH].reshape(sequence_length, QUERY_HEADS, HEAD_SIZE)
        every_key = joined_heads[:, HEADS_WIDTH : HEADS_WIDTH + KEYS_WIDTH].reshape(
            sequence_length, KEY_VALUE_HEADS, HEAD_SIZE
        )
        every_value = joined_heads[:, HEADS_WIDTH + KEYS_WIDTH :].reshape(
            sequence_length, KEY_VALUE_HEADS, HEAD_SIZE
        )
        cosine_lookup, sine_lookup = rotary_tables(sequence_length, HEAD_SIZE)
        query_rotated = (
            apply_rotation(query_rows, cosine_lookup, sine_lookup)
            .astype(bf16)
            .reshape(sequence_length, KEY_VALUE_HEADS, head_groups, HEAD_SIZE)
        )
        key_rot = apply_rotation(every_key, cosine_lookup, sine_lookup).astype(bf16)
        value_low = every_value.astype(bf16)
        causal = jnp.arange(sequence_length)[:, None] >= jnp.arange(sequence_length)[None, :]
        scores = attention_scores(query_rotated, key_rot, causal)
        peak = jnp.max(scores, axis=-1, keepdims=True)
        expo = jnp.exp(scores - peak)
        totals = jnp.sum(expo, axis=-1, keepdims=True)
        probs = expo / totals
        prob_low = probs.astype(bf16)
        heads = jnp.einsum("kgst,tkd->skgd", prob_low, value_low, preferred_element_type=f32)
        attended = heads.reshape(sequence_length, HEADS_WIDTH).astype(bf16)
        attended_mine = dot(attended, order_mine).astype(bf16)
        attended_other = dot(attended, order_other).astype(bf16)
        projected = [dot(attended_mine, out_mine), dot(attended_other, out_other)]
        mid = inputs + residual_scale * jnp.where(
            core == 0,
            jnp.concatenate(projected, axis=1),
            jnp.concatenate(projected[::-1], axis=1),
        )
        factor_two = lax.rsqrt(jnp.mean(mid * mid, axis=-1, keepdims=True) + norm_eps)
        hidden_two = (mid * factor_two * gain_two).astype(bf16)
        logits = dot(hidden_two, router_w)
        named = jnp.any(
            routes[..., None] == jnp.arange(EXPERTS, dtype=routes.dtype)[None, None, :], axis=1
        )
        shown = jnp.where(named, logits, -jnp.inf)
        raised = jnp.exp(shown - jnp.max(shown, axis=-1, keepdims=True))
        gates = raised / jnp.sum(raised, axis=-1, keepdims=True)

        gate_high = gates.astype(bf16)
        gate_rest = (gates - gate_high.astype(f32)).astype(bf16)
        sent = jnp.concatenate(
            [hidden_two, pad_lanes(jnp.concatenate([gate_high, gate_rest], axis=1))], axis=1
        )
        sent_all = lax.all_gather(sent, SAME_CORE, axis=0, tiled=True)
        sent_all = permute_blocks(sent_all, blocks_order)
        own = after(own, cot_all)
        other, low_other = swap_core(own), swap_core(low_own)
        down_own, down_other = down_of(own, low_own), down_of(other, low_other)
        blocks = 2 * nx * ny
        reach = [dot_nt(cot_all, d).reshape(blocks, -1, units) for d in (down_own, down_other)]

        behind = jnp.concatenate([unit_experts(group, place), unit_experts(partner, place)])
        numbers = jnp.arange(LANES)[:, None]
        real = behind[None, :] >= 0
        once = ((numbers == behind[None, :]) & real).astype(bf16)
        twice = once + ((numbers == behind[None, :] + EXPERTS) & real).astype(bf16)
        kept = None
        firsts = []
        sent_blocks = sent_all.reshape(blocks, -1, sent_all.shape[1])
        for at in range(2):
            *kept, two = run_experts(at, sent_blocks, reach, own, other, twice, once, kept)
            firsts.append(scatter_first(two))
        two_sum = sum_line(scatter_second(firsts))

        gated, grad_both = (k.reshape(-1, k.shape[2]) for k in kept)
        gated, grad_both = after(gated, *firsts[-1], always=True), after(grad_both, *firsts[-1])
        rows_all = after(sent_all, *firsts[-1], always=True)[:, :D]
        mixed = (dot(gated[:, :units], down_own) + dot(gated[:, units:], down_other)).astype(bf16)
        mixed = after(mixed, two_sum, always=True)

        came_gate_up = swap_core(dot_tn(rows_all, grad_both[:, 2 * units :]).astype(bf16))
        came_down = swap_core(dot_tn(gated[:, units:], cot_all).astype(bf16))
        full, more, low = combine_grads(
            dot_tn(rows_all, grad_both[:, : 2 * units]).astype(bf16),
            came_gate_up,
            dot_tn(gated[:, :units], cot_all).astype(bf16),
            came_down,
        )
        home_full = all_to_all_plane(after(full, two_sum)) if whole else None
        home_rest = all_to_all_plane(after(more, two_sum))
        two_sum = after(two_sum, low)
        grad_two, grad_gates = two_sum[:, :D], two_sum[:, D : D + EXPERTS]

        grad_out = cotangent.astype(f32)
        grad_chosen = gates * (grad_gates - jnp.sum(gates * grad_gates, axis=-1, keepdims=True))
        grad_logits = grad_chosen.astype(bf16)
        grad_router = dot_tn(hidden_two, grad_logits)
        grad_two = grad_two + dot_nt(grad_logits, router_w)
        grad_mid, grad_gain_two = norm_backward(grad_two, mid, factor_two, gain_two)
        grad_mid = grad_out + grad_mid
        grad_att = (residual_scale * grad_mid).astype(bf16)
        att_left, att_right = grad_att[:, : D // 2], grad_att[:, D // 2 :]
        att_mine = jnp.where(core == 0, att_left, att_right)
        att_other = jnp.where(core == 0, att_right, att_left)
        grad_heads = (
            dot_nt(dot_nt(att_mine, out_mine).astype(bf16), order_mine)
            + dot_nt(dot_nt(att_other, out_other).astype(bf16), order_other)
        )
        grad_heads = grad_heads.astype(bf16).reshape(
            sequence_length, KEY_VALUE_HEADS, head_groups, HEAD_SIZE
        )
        out_first = scatter_halves_first(
            dot_tn(attended_mine, att_mine).astype(bf16),
            dot_tn(attended_other, att_other).astype(bf16),
        )
        out_two = scatter_halves_second(out_first)
        grad_probs = jnp.einsum(
            "skgd,tkd->kgst", grad_heads, value_low, preferred_element_type=f32
        )
        value_gradient = jnp.einsum(
            "kgst,skgd->tkd", prob_low, grad_heads, preferred_element_type=f32
        )
        row_dot = jnp.sum(probs * grad_probs, axis=-1, keepdims=True)
        grad_scores = (probs * (grad_probs - row_dot)).astype(bf16)
        grad_qrot = (
            jnp.einsum("kgst,tkd->skgd", grad_scores, key_rot, preferred_element_type=f32)
            * score_scale
        )
        grad_krot = (
            jnp.einsum("kgst,skgd->tkd", grad_scores, query_rotated, preferred_element_type=f32)
            * score_scale
        )
        grad_queries = apply_rotation(
            grad_qrot.reshape(sequence_length, QUERY_HEADS, HEAD_SIZE), cosine_lookup, -sine_lookup
        )
        key_gradient = apply_rotation(grad_krot, cosine_lookup, -sine_lookup)
        grad_joined = jnp.concatenate(
            [
                grad_queries.reshape(sequence_length, HEADS_WIDTH),
                key_gradient.reshape(sequence_length, KEYS_WIDTH),
                value_gradient.reshape(sequence_length, KEYS_WIDTH),
            ],
            axis=1,
        ).astype(bf16)
        grad_one = dot_nt(grad_joined, qkv_w)
        grad_inputs, grad_gain_one = norm_backward(grad_one, inputs, factor_one, gain_one)
        token_grad = grad_mid + grad_inputs
        small_sent = pad_lanes(
            jnp.concatenate([grad_router, grad_gain_one[:, None], grad_gain_two[:, None]], axis=1)
        )
        small_sent = small_sent.astype(bf16)
        joined_left, joined_right = grad_joined[:, : QKV // 2], grad_joined[:, QKV // 2 :]
        qkv_sent = []
        for hidden, rows_order, at in (
            (hidden_mine, order_mine, core),
            (hidden_other, order_other, 1 - core),
        ):
            product = dot_tn(hidden, jnp.where(at == 0, joined_left, joined_right))
            extra = jnp.where(at == 0, dot_tn(rows_order, small_sent), 0.0)
            qkv_sent.append(jnp.concatenate([product, extra], axis=1).astype(bf16))
        qkv_first = scatter_halves_first(qkv_sent[0], after(qkv_sent[1], out_two, home_full))
        mixed = after(mixed, qkv_first).reshape(blocks, -1, D)
        mixed = sum_line(scatter_second([scatter_first(mixed)]))
        layer_out = (mid + residual_scale * mixed).astype(bf16)
        qkv_two = scatter_halves_second(qkv_first)
        if whole:
            home_full = after(home_full, qkv_two)
        (out_left, out_right), (qkv_left, qkv_right) = scatter_halves_line(
            [out_two, qkv_two], home_rest
        )
        new_gate_up, new_down = update_experts(
            home_full,
            home_rest,
            low,
            (weight_gate_up, moment_gate_up, square_gate_up),
            (weight_down, moment_down, square_down),
        )
        sum_out = jnp.concatenate([out_left, out_right], axis=1)
        sum_qkv = jnp.concatenate([qkv_left[:, : QKV // 2], qkv_right[:, : QKV // 2]], axis=1)
        sum_router = qkv_left[:, QKV // 2 : QKV // 2 + EXPERTS]
        sum_gains = qkv_left[:, QKV // 2 + EXPERTS : QKV // 2 + EXPERTS + 2].T

        new_qkv = adam_step(weight_qkv, moment_qkv, square_qkv, sum_qkv, D ** (-0.5), weight_decay)
        new_out = adam_step(
            weight_out,
            moment_out,
            square_out,
            sum_out,
            max(4, QUERY_HEADS * HEAD_SIZE // 256) ** (-0.5),
            weight_decay,
        )
        new_router = adam_step(
            weight_router, moment_router, square_router, sum_router, (4 * D) ** (-0.5), weight_decay
        )
        new_gains = adam_step(gains, moment_gains, square_gains, sum_gains, 0.75, 0.0)
        return (
            layer_out,
            token_grad,
            *new_qkv,
            *new_out,
            *new_router,
            *new_gains,
            *new_gate_up,
            *new_down,
        )

    return shards


def solution(mesh):
    n_dp, n_expert = mesh.shape["dp"], mesh.shape["expert"]
    nz = 4
    nx, ny = n_dp // nz, n_expert // 2
    fine = Mesh(mesh.devices.reshape(nz, nx, ny, 2), ALL)
    rows = P(ALL, None)
    columns = P(None, ALL)
    experts = P(("y", "core"), ("z", "x"), None)
    dense = (rows,) * 9 + (columns,) * 3 + (experts,) * 6
    return jax.shard_map(
        make_shards((nz, nx, ny)),
        mesh=fine,
        in_specs=(rows,) * 3 + dense,
        out_specs=(rows,) * 2 + dense,
        check_vma=False,
    )
```
